32 devices in a mesh: rep: 8 (over z, core), shard: 4 (over y, x).
Axes of the slice: x: 2, y: 2, z: 4, core: 2. Of those that a mesh axis runs over, the one named last changes fastest.
Arguments:
- inputs: bfloat16 [8, 512, 8192], P('rep', 'shard'), may hold values from -6 to 6
- target: bfloat16 [8, 512, 512], P('rep', 'shard'), may hold values from -6 to 6
- weights: bfloat16 [8, 8192, 512], P('rep', 'shard'), may hold values from -0.0625 to 0.0625
- feedback: bfloat16 [8, 8192, 512], P('rep', 'shard'), may hold values from -6 to 6
- counts: int32 [8, 4], P('rep', 'shard'), may hold values from 16 to 128, as said below
- blocks: int32 [8, 4, 128], P('rep', 'shard'), may hold values from 0 to 8191, as said below
Outputs:
- outer_update: float32 [8192, 512], P('shard')
- new_feedback: bfloat16 [8, 8192, 512], P('rep', 'shard')
The draws below stay inside these ranges and needn't reach their ends.
Inputs may be any that keep to these rules, and one draw needn't show every extreme that they name: `counts`: in every shard index some replica keeps exactly 128 blocks. The 128 slots of one device hold distinct block numbers; only the first counts slots are kept; the others hold block numbers that this device does not keep (other replicas may keep them). All replicas of one shard index draw all their slots from a common set of 512 blocks.
All inputs are finite; a program needn't handle non-finite values.
Results may differ from the reference program's by a relative error of at most 0.0034.
Values may be sent and summed in bfloat16 or wider, within the bound.
No kernel may reach another device: no remote copies, remote signals or barrier semaphores. Data moves between devices by JAX's collectives and lax.ppermute only.
A program may use at most 64 MiB of HBM per device.

```python
import jax
import jax.numpy as jnp
from jax import lax

D = 8192
KW = 512
TOK_DEV = 128
CAP = 128
BLOCK = 128
TOK_REP = 512
NBLK = 8192
POOL = 512
N_REP = 8
N_SHARD = 4


def draw_counts(key, part):
    key = jax.random.fold_in(key, 11)
    key_base, key_full = jax.random.split(key)
    lowest = max(CAP // 8, 1)
    base = jax.random.randint(key_base, (N_REP, N_SHARD), lowest, CAP + 1)
    full_rep = jax.random.randint(key_full, (N_SHARD,), 0, N_REP)
    replica = jnp.arange(N_REP)[:, None]
    return jnp.where(replica == full_rep[None, :], CAP, base).astype(jnp.int32)


def draw_blocks(key, part):
    key = jax.random.fold_in(key, 23)

    def column(shard_id):
        common = jax.random.permutation(jax.random.fold_in(key, shard_id), NBLK)[:POOL]

        def single(rep_id):
            inner = jax.random.fold_in(jax.random.fold_in(key, shard_id + N_SHARD), rep_id)
            picked = jax.random.permutation(inner, POOL)[:CAP]
            return common[picked]
        return jax.vmap(single)(jnp.arange(N_REP))
    table = jax.vmap(column)(jnp.arange(N_SHARD))
    return jnp.transpose(table, (1, 0, 2)).astype(jnp.int32)


def block_levels(own_key, extent, shards, smallest, high):
    gain, own = 1.0, jax.random.fold_in(own_key, 6)
    for position, shards_of in shards:
        heights = jnp.exp(jax.random.uniform(jax.random.fold_in(own, position), (shards_of,), jnp.float32, smallest / len(shards), high / len(shards)))
        gain = gain * jnp.repeat(heights, extent[position] // shards_of).reshape([-1 if axis == position else 1 for axis in range(len(extent))])
    return gain


def noise(key, shape, deviation, limit, cuts=(), kind=jnp.bfloat16):
    entries = jax.random.normal(key, shape, jnp.float32) * deviation
    if len(cuts) > 0:
        entries = block_levels(key, shape, cuts, -0.22, 0.18) * entries
    return jnp.clip(entries, min=-limit, max=limit).astype(kind)


def setup_inputs(seed: int = 0) -> dict:
    key_list = jax.random.split(jax.random.key(seed), 7)
    inputs = noise(key_list[0], (N_REP, TOK_REP, D), 1.0, 6.0, ((0, 8), (1, 4)))
    target = noise(key_list[1], (N_REP, TOK_REP, KW), 1.0, 6.0, ((0, 8), (1, 4)))
    weights = noise(key_list[2], (N_REP, D, KW), D ** -0.5, 0.0625, ((0, 8), (1, 4)))
    feedback = noise(key_list[3], (N_REP, D, KW), 1.0, 6.0, ((0, 8), (1, 4)))
    counts = draw_counts(jax.random.fold_in(key_list[6], 71), 0)
    blocks = draw_blocks(jax.random.fold_in(key_list[6], 71), 0)
    return {"inputs": inputs, "target": target, "weights": weights, "feedback": feedback, "counts": counts, "blocks": blocks}


def replica_step(summed, items):
    inputs, target, weights, feedback, counts, blocks = items
    key_proj = jnp.dot(inputs, weights, preferred_element_type=jnp.float32)
    slopes = ((key_proj - target.astype(jnp.float32)) / TOK_DEV).astype(jnp.bfloat16)
    gradient = jnp.dot(inputs.T, slopes, preferred_element_type=jnp.float32)
    pseudo = gradient + feedback.astype(jnp.float32)
    blocked = pseudo.reshape(N_SHARD, NBLK, BLOCK)
    in_use = (jnp.arange(CAP, dtype=jnp.int32)[None, :] < counts[:, None]).astype(jnp.float32)
    shard_ids = jnp.broadcast_to(jnp.arange(N_SHARD, dtype=jnp.int32)[:, None], blocks.shape)
    kept_mask = jnp.zeros((N_SHARD, NBLK), jnp.float32).at[shard_ids, blocks].add(in_use)
    chosen = kept_mask[..., None] > 0
    kept = jnp.where(chosen, blocked, jnp.zeros_like(blocked))
    residue = jnp.where(chosen, jnp.zeros_like(blocked), blocked)
    summed = summed + kept.reshape(D, KW)
    return summed, residue.reshape(D, KW).astype(jnp.bfloat16)


def reference(inputs, target, weights, feedback, counts, blocks):
    start = jnp.zeros((D, KW), jnp.float32)
    summed, residues = lax.scan(replica_step, start, (inputs, target, weights, feedback, counts, blocks))
    return summed / N_REP, residues
```

```python
import functools

import jax
import jax.numpy as jnp
from jax import lax
from jax.experimental import pallas as pl
from jax.experimental.pallas import tpu as pltpu
from jax.sharding import PartitionSpec as P

LANES = 128
CHUNKS = 1
MIB = 1024 * 1024


def params(mib):
    return pltpu.CompilerParams(vmem_limit_bytes=mib * MIB)


def cost(flops, nbytes):
    return pl.CostEstimate(flops=int(flops), bytes_accessed=int(nbytes), transcendentals=0)


def swap(x, axis, n, d):
    return lax.ppermute(x, axis, [(i, i ^ d) for i in range(n)])


def project_kernel(*refs):
    n = (len(refs) - 2) // 2
    pieces, w, outs, x = refs[:n], refs[n], refs[n + 1 : 2 * n + 1], refs[-1]
    rows = pieces[0].shape[0]
    for d in range(n):
        x[d * rows : (d + 1) * rows, :] = pieces[d][...]
    full = jnp.dot(x[...], w[...], preferred_element_type=jnp.float32)
    for d in range(n):
        outs[d][...] = full[d * rows : (d + 1) * rows, :].astype(outs[d].dtype)


def project(pieces, w):
    n = len(pieces)
    rows, depth = pieces[0].shape
    kw = w.shape[1]
    return pl.pallas_call(
        project_kernel,
        out_shape=[
            jax.ShapeDtypeStruct((rows, kw), jnp.float32 if d == 0 else jnp.bfloat16)
            for d in range(n)
        ],
        scratch_shapes=[pltpu.VMEM((n * rows, depth), jnp.bfloat16)],
        compiler_params=params(24),
        cost_estimate=cost(2 * n * rows * depth * kw, 2 * depth * (n * rows + kw)),
        name="project",
    )(*pieces, w)


def pick_columns(wide, column):
    out = jnp.zeros((wide.shape[0], LANES), jnp.float32)
    for c in range(wide.shape[1] // LANES):
        out += jnp.where(column == c, wide[:, c * LANES : (c + 1) * LANES], 0.0)
    return out


def prepare_kernel(per_row, *refs):
    pieces, (slots, fb, xg, fbk, x) = refs[:-5], refs[-5:]
    rows, depth = pieces[0].shape
    for d in range(len(pieces)):
        x[d * rows : (d + 1) * rows, :] = pieces[d][...]
    cap = slots.shape[0]
    slot = slots[...]
    hot = slot // per_row == lax.broadcasted_iota(jnp.int32, (cap, depth), 1)
    hot = hot.astype(jnp.float32).astype(jnp.bfloat16)
    xg[...] = lax.dot_general(
        hot, x[...], (((1,), (1,)), ((), ())), preferred_element_type=jnp.float32
    ).astype(jnp.bfloat16)
    wide = jnp.dot(hot, fb[...], preferred_element_type=jnp.float32)
    fbk[...] = pick_columns(wide, slot % per_row)


def prepare(pieces, slots, fb):
    n = len(pieces)
    rows, depth = pieces[0].shape
    cap = slots.shape[0]
    kw = fb.shape[1]
    return pl.pallas_call(
        functools.partial(prepare_kernel, kw // LANES),
        out_shape=[
            jax.ShapeDtypeStruct((cap, n * rows), jnp.bfloat16),
            jax.ShapeDtypeStruct((cap, LANES), jnp.float32),
        ],
        scratch_shapes=[pltpu.VMEM((n * rows, depth), jnp.bfloat16)],
        compiler_params=params(24),
        cost_estimate=cost(2 * cap * depth * (n * rows + kw), 2 * depth * (n * rows + kw)),
        name="prepare",
    )(*pieces, slots, fb)


def kept_kernel(per_row, *refs):
    parts, (xg, fbk, slots, slot_row, count, out, s) = refs[:-7], refs[-7:]
    rows = parts[0].shape[0]
    cap = xg.shape[0]
    for d in range(len(parts)):
        s[d * rows : (d + 1) * rows, :] = parts[d][...]
    wide = jnp.dot(xg[...], s[...], preferred_element_type=jnp.float32)
    value = pick_columns(wide, slots[...] % per_row) + fbk[...]
    used = lax.broadcasted_iota(jnp.int32, (cap, LANES), 0) < count[0, 0]
    out[:cap, :] = jnp.where(used, value, 0.0).astype(jnp.bfloat16)
    tail = out.shape[0] - cap
    number = jnp.broadcast_to(slot_row[...], (tail, cap))
    line = lax.broadcasted_iota(jnp.int32, (tail, cap), 0)
    number = jnp.where(line == 0, number // LANES, number % LANES)
    out[cap:, :] = number.astype(jnp.float32).astype(jnp.bfloat16)


def kept(parts, xg, fbk, slots, slot_row, count):
    cap = slots.shape[0]
    rows, kw = parts[0].shape
    vmem = pl.BlockSpec(memory_space=pltpu.VMEM)
    return pl.pallas_call(
        functools.partial(kept_kernel, kw // LANES),
        out_shape=jax.ShapeDtypeStruct((cap + 16, LANES), jnp.bfloat16),
        in_specs=[vmem] * (len(parts) + 4) + [pl.BlockSpec(memory_space=pltpu.SMEM)],
        scratch_shapes=[pltpu.VMEM((len(parts) * rows, kw), jnp.bfloat16)],
        compiler_params=params(8),
        cost_estimate=cost(2 * cap * len(parts) * rows * kw, 2 * len(parts) * rows * kw),
        name="kept",
    )(*parts, xg, fbk, slots, slot_row, count)


def residue_kernel(n, per_row, *refs):
    pieces, parts = refs[:n], refs[n : 2 * n]
    fb, slots, slot_row, count, out, x, s = refs[2 * n :]
    step = pl.program_id(0)
    rows = pieces[0].shape[0]
    cap = slots.shape[0]
    tile, kw = out.shape

    @pl.when(step == 0)
    def _():
        for d in range(n):
            s[d * rows : (d + 1) * rows, :] = parts[d][...]

    for d in range(n):
        x[d * rows : (d + 1) * rows, :] = pieces[d][...]
    gradient = lax.dot_general(
        x[...], s[...], (((0,), (0,)), ((), ())), preferred_element_type=jnp.float32
    )
    pseudo = gradient + fb[...].astype(jnp.float32)
    line = lax.broadcasted_iota(jnp.int32, (tile, cap), 0) + step * tile
    hot = (slot_row[...] // per_row == line).astype(jnp.float32).astype(jnp.bfloat16)
    used = lax.broadcasted_iota(jnp.int32, (cap, kw), 0) < count[0, 0]
    group = lax.broadcasted_iota(jnp.int32, (cap, kw), 1) // LANES
    mark = jnp.where(used & (slots[...] % per_row == group), 1.0, 0.0).astype(jnp.bfloat16)
    mask = jnp.dot(hot, mark, preferred_element_type=jnp.float32)
    out[...] = jnp.where(mask > 0, 0.0, pseudo).astype(jnp.bfloat16)


def residue(pieces, parts, fb, slots, slot_row, count):
    n = len(pieces)
    rows, depth = pieces[0].shape
    kw = fb.shape[1]
    tile = min(depth, 512)
    full = lambda a: pl.BlockSpec(a.shape, lambda i: (0, 0))
    return pl.pallas_call(
        functools.partial(residue_kernel, n, kw // LANES),
        grid=(depth // tile,),
        out_shape=jax.ShapeDtypeStruct((depth, kw), jnp.bfloat16),
        in_specs=[pl.BlockSpec((rows, tile), lambda i: (0, i))] * n
        + [full(parts[0])] * n
        + [pl.BlockSpec((tile, kw), lambda i: (i, 0)), full(slots), full(slot_row)]
        + [pl.BlockSpec(memory_space=pltpu.SMEM)],
        out_specs=pl.BlockSpec((tile, kw), lambda i: (i, 0)),
        scratch_shapes=[
            pltpu.VMEM((n * rows, tile), jnp.bfloat16),
            pltpu.VMEM((n * rows, kw), jnp.bfloat16),
        ],
        compiler_params=params(24),
        cost_estimate=cost(2 * n * rows * depth * kw, 2 * depth * (n * rows + 2 * kw)),
        name="residue",
    )(*pieces, *parts, fb, slots, slot_row, count)


def outer_kernel(n, per_row, *refs):
    messages, (out, wide, lines) = refs[:n], refs[n:]
    step = pl.program_id(0)
    cap = messages[0].shape[0] - 16
    tile, kw = out.shape

    @pl.when(step == 0)
    def _():
        for k in range(n):
            tail = messages[k][cap:, :].astype(jnp.float32)
            number = (tail[0:1, :] * LANES + tail[1:2, :]).astype(jnp.int32)
            lines[:, k * cap : (k + 1) * cap] = jnp.broadcast_to(number // per_row, (8, cap))
            column = jnp.broadcast_to((number % per_row).astype(jnp.float32), (LANES, cap)).T
            value = messages[k][:cap, :].astype(jnp.float32)
            for c in range(per_row):
                wide[k * cap : (k + 1) * cap, c * LANES : (c + 1) * LANES] = jnp.where(
                    column == c, value, 0.0
                ).astype(jnp.bfloat16)

    line = lax.broadcasted_iota(jnp.int32, (tile, n * cap), 0) + step * tile
    hot = (lines[0:1, :] == line).astype(jnp.float32).astype(jnp.bfloat16)
    out[...] = jnp.dot(hot, wide[...], preferred_element_type=jnp.float32) / n


def outer(messages, depth, kw):
    n = len(messages)
    cap = messages[0].shape[0] - 16
    tile = min(depth, 256)
    return pl.pallas_call(
        functools.partial(outer_kernel, n, kw // LANES),
        grid=(depth // tile,),
        out_shape=jax.ShapeDtypeStruct((depth, kw), jnp.float32),
        in_specs=[pl.BlockSpec(messages[0].shape, lambda i: (0, 0))] * n,
        out_specs=pl.BlockSpec((tile, kw), lambda i: (i, 0)),
        scratch_shapes=[
            pltpu.VMEM((n * cap, kw), jnp.bfloat16),
            pltpu.VMEM((8, n * cap), jnp.int32),
        ],
        compiler_params=params(24),
        cost_estimate=cost(2 * n * cap * depth * kw, 4 * depth * kw),
        name="outer",
    )(*messages)


def on_device(inputs, target, weights, feedback, counts, blocks):
    tokens, w, fb = inputs[0], weights[0], feedback[0]
    n_shard, n_rep = lax.axis_size("shard"), lax.axis_size("rep")
    me = lax.axis_index("shard")
    tok_dev = tokens.shape[0]
    depth, kw = w.shape
    rows = tok_dev // CHUNKS
    slot_row = blocks[0]
    slots = blocks.reshape(-1, 1)

    pieces = []
    for c in range(CHUNKS):
        mine = [
            lax.dynamic_slice(tokens, (c * rows, (me ^ d) * depth), (rows, depth))
            for d in range(n_shard)
        ]
        pieces.append(mine[:1] + [swap(mine[d], "shard", n_shard, d) for d in range(1, n_shard)])
    parts = []
    for c in range(CHUNKS):
        products = project(pieces[c], w)
        key_proj = products[0]
        for d in range(1, n_shard):
            key_proj = key_proj + swap(products[d], "shard", n_shard, d).astype(jnp.float32)
        goal = target[0, c * rows : (c + 1) * rows].astype(jnp.float32)
        slope = ((key_proj - goal) / tok_dev).astype(jnp.bfloat16)
        parts += [slope] + [swap(slope, "shard", n_shard, d) for d in range(1, n_shard)]
    pieces = [p for chunk in pieces for p in chunk]
    xg, fbk = prepare(pieces, slots, fb)
    message = kept(parts, xg, fbk, slots, slot_row, counts)
    messages = [message] + [swap(message, "rep", n_rep, d) for d in range(1, n_rep)]
    new_feedback = residue(pieces, parts, fb, slots, slot_row, counts)
    return outer(messages, depth, kw), new_feedback[None]


def solution(mesh):
    placed = (
        P("rep", "shard", None),
        P("rep", "shard", None),
        P("rep", "shard", None),
        P("rep", "shard", None),
        P("rep", "shard"),
        P("rep", "shard", None),
    )
    return jax.shard_map(
        on_device,
        mesh=mesh,
        in_specs=placed,
        out_specs=(P("shard", None), P("rep", "shard", None)),
        check_vma=False,
    )
```

```python
import functools

import jax
import jax.numpy as jnp
from jax import lax
from jax.experimental import pallas as pl
from jax.experimental.pallas import tpu as pltpu
from jax.sharding import PartitionSpec as P

LANES = 128
CHUNKS = (4, 4)
ANY = pl.BlockSpec(memory_space=pl.ANY)
VMEM = pl.BlockSpec(memory_space=pltpu.VMEM)
SMEM = pl.BlockSpec(memory_space=pltpu.SMEM)
MIB = 1024 * 1024


def params(mib):
    return pltpu.CompilerParams(vmem_limit_bytes=mib * MIB)


def cost(flops, nbytes):
    return pl.CostEstimate(flops=int(flops), bytes_accessed=int(nbytes), transcendentals=0)


def swap(x, axis, n, d):
    return lax.ppermute(x, axis, [(i, i ^ d) for i in range(n)])


def project_kernel(n, *refs):
    pieces, w, outs, x = refs[:n], refs[n], refs[-n - 1 : -1], refs[-1]
    rows = x.shape[0] // n
    for d in range(n):
        x[d * rows : (d + 1) * rows, :] = pieces[d][...]
    full = jnp.dot(x[...], w[...], preferred_element_type=jnp.float32)
    for d in range(n):
        outs[d][...] = full[d * rows : (d + 1) * rows, :].astype(outs[d].dtype)


def project(pieces, w, after):
    n = len(pieces)
    rows, depth = pieces[0].shape
    kw = w.shape[1]
    result = pl.pallas_call(
        functools.partial(project_kernel, n),
        out_shape=[
            jax.ShapeDtypeStruct((rows, kw), jnp.float32 if d == 0 else jnp.bfloat16)
            for d in range(n)
        ]
        + [jax.ShapeDtypeStruct((n * rows, depth), jnp.bfloat16)],
        in_specs=[VMEM] * (n + 1) + [ANY] * len(after),
        compiler_params=params(24),
        cost_estimate=cost(2 * n * rows * depth * kw, 2 * depth * (n * rows + kw)),
        name="project",
    )(*pieces, w, *after)
    return result[:n], result[n]


def slope_kernel(low, tok_dev, *refs):
    products, goal, out = refs[:-3], refs[-3], refs[-1]
    key_proj = products[0][...]
    for product in products[1:]:
        key_proj += product[...].astype(jnp.float32)
    goal = goal[low : low + out.shape[0], :].astype(jnp.float32)
    out[...] = ((key_proj - goal) / tok_dev).astype(jnp.bfloat16)


def slope(products, goal, low, after):
    return pl.pallas_call(
        functools.partial(slope_kernel, low, goal.shape[0]),
        out_shape=jax.ShapeDtypeStruct(products[0].shape, jnp.bfloat16),
        in_specs=[VMEM] * (len(products) + 1) + [ANY],
        compiler_params=params(8),
        cost_estimate=cost(4 * products[0].size, 12 * products[0].size),
        name="slope",
    )(*products, goal, after)


def pick_columns(wide, column):
    out = jnp.zeros((wide.shape[0], LANES), jnp.float32)
    for c in range(wide.shape[1] // LANES):
        out += jnp.where(column == c, wide[:, c * LANES : (c + 1) * LANES], 0.0)
    return out


def early_kernel(per_row, slots, slot_row, count, fb, fbk, keep):
    depth, kw = fb.shape
    cap = slots.shape[0]
    slot = slots[...]
    hot = slot // per_row == lax.broadcasted_iota(jnp.int32, (cap, depth), 1)
    hot = hot.astype(jnp.float32).astype(jnp.bfloat16)
    used = lax.broadcasted_iota(jnp.int32, (cap, 1), 0) < count[0, 0]
    wide = jnp.dot(hot, fb[...], preferred_element_type=jnp.float32)
    fbk[...] = jnp.where(used, pick_columns(wide, slot % per_row), 0.0)
    group = lax.broadcasted_iota(jnp.int32, (cap, kw), 1) // LANES
    mark = jnp.where(used & (slot % per_row == group), 1.0, 0.0).astype(jnp.bfloat16)
    tile = min(depth, 512)
    for t in range(depth // tile):
        line = lax.broadcasted_iota(jnp.int32, (tile, cap), 0) + t * tile
        hot = (slot_row[...] // per_row == line).astype(jnp.float32).astype(jnp.bfloat16)
        mask = jnp.dot(hot, mark, preferred_element_type=jnp.float32)
        keep[t * tile : (t + 1) * tile, :] = (1.0 - mask).astype(jnp.bfloat16)


def early(slots, slot_row, count, fb):
    depth, kw = fb.shape
    cap = slots.shape[0]
    return pl.pallas_call(
        functools.partial(early_kernel, kw // LANES),
        out_shape=[
            jax.ShapeDtypeStruct((cap, LANES), jnp.float32),
            jax.ShapeDtypeStruct((depth, kw), jnp.bfloat16),
        ],
        in_specs=[VMEM, VMEM, SMEM, VMEM],
        compiler_params=params(24),
        cost_estimate=cost(4 * cap * depth * kw, 4 * depth * kw),
        name="early",
    )(slots, slot_row, count, fb)


def prepare_kernel(per_row, x, slots, count, after, xg, xt):
    depth = x.shape[1]
    cap = slots.shape[0]
    used = lax.broadcasted_iota(jnp.int32, (cap, 1), 0) < count[0, 0]
    line = jnp.where(used, slots[...] // per_row, depth)
    hot = line == lax.broadcasted_iota(jnp.int32, (cap, depth), 1)
    hot = hot.astype(jnp.float32).astype(jnp.bfloat16)
    xg[...] = lax.dot_general(
        hot, x[...], (((1,), (1,)), ((), ())), preferred_element_type=jnp.float32
    ).astype(jnp.bfloat16)
    xt[...] = x[...].T


def prepare(x, slots, count, per_row, after):
    rows, depth = x.shape
    cap = slots.shape[0]
    return pl.pallas_call(
        functools.partial(prepare_kernel, per_row),
        out_shape=[
            jax.ShapeDtypeStruct((cap, rows), jnp.bfloat16),
            jax.ShapeDtypeStruct((depth, rows), jnp.bfloat16),
        ],
        in_specs=[VMEM, VMEM, SMEM, ANY],
        compiler_params=params(24),
        cost_estimate=cost(2 * cap * depth * rows, 4 * depth * rows),
        name="prepare",
    )(x, slots, count, after)


def stack(parts, s):
    rows = parts[0].shape[0]
    for d in range(len(parts)):
        s[d * rows : (d + 1) * rows, :] = parts[d][...]
    return s[...]


def kept_kernel(per_row, n, *refs):
    chunks = (len(refs) - 4) // (n + 2)
    parts, xgs = refs[: n * chunks], refs[n * chunks : (n + 1) * chunks]
    fbk, slots, slot_row, out = refs[(n + 1) * chunks : (n + 1) * chunks + 4]
    scratch = refs[(n + 1) * chunks + 4 :]
    cap = slots.shape[0]
    wide = 0.0
    for c in range(chunks):
        s = stack(parts[c * n : (c + 1) * n], scratch[c])
        wide += jnp.dot(xgs[c][...], s, preferred_element_type=jnp.float32)
    value = pick_columns(wide, slots[...] % per_row) + fbk[...]
    out[:cap, :] = value.astype(jnp.bfloat16)
    tail = out.shape[0] - cap
    number = jnp.broadcast_to(slot_row[...], (tail, cap))
    line = lax.broadcasted_iota(jnp.int32, (tail, cap), 0)
    number = jnp.where(line == 0, number // LANES, number % LANES)
    out[cap:, :] = number.astype(jnp.float32).astype(jnp.bfloat16)


def kept(parts, xgs, fbk, slots, slot_row):
    cap = slots.shape[0]
    n, kw = len(parts[0]), parts[0][0].shape[1]
    total = sum(xg.shape[1] for xg in xgs)
    return pl.pallas_call(
        functools.partial(kept_kernel, kw // LANES, n),
        out_shape=jax.ShapeDtypeStruct((cap + 16, LANES), jnp.bfloat16),
        scratch_shapes=[pltpu.VMEM((xg.shape[1], kw), jnp.bfloat16) for xg in xgs],
        compiler_params=params(8),
        cost_estimate=cost(2 * cap * total * kw, 2 * total * kw),
        name="kept",
    )(*sum(parts, []), *xgs, fbk, slots, slot_row)


def residue_kernel(n, *refs):
    chunks = (len(refs) - 3) // (n + 2)
    parts, xts = refs[: n * chunks], refs[n * chunks : (n + 1) * chunks]
    fb, keep, out = refs[(n + 1) * chunks : (n + 1) * chunks + 3]
    scratch = refs[(n + 1) * chunks + 3 :]

    @pl.when(pl.program_id(0) == 0)
    def _():
        for c in range(chunks):
            stack(parts[c * n : (c + 1) * n], scratch[c])

    pseudo = fb[...].astype(jnp.float32)
    for c in range(chunks):
        pseudo += jnp.dot(xts[c][...], scratch[c][...], preferred_element_type=jnp.float32)
    out[...] = jnp.where(keep[...] > 0, pseudo, 0.0).astype(jnp.bfloat16)


def residue(parts, xts, fb, keep):
    depth, kw = fb.shape
    n = len(parts[0])
    total = sum(xt.shape[1] for xt in xts)
    tile = min(depth, 512)
    rows = pl.BlockSpec((tile, kw), lambda i: (i, 0))
    flat = sum(parts, [])
    return pl.pallas_call(
        functools.partial(residue_kernel, n),
        grid=(depth // tile,),
        out_shape=jax.ShapeDtypeStruct((depth, kw), jnp.bfloat16),
        in_specs=[pl.BlockSpec(p.shape, lambda i: (0, 0)) for p in flat]
        + [pl.BlockSpec((tile, xt.shape[1]), lambda i: (i, 0)) for xt in xts]
        + [rows, rows],
        out_specs=rows,
        scratch_shapes=[pltpu.VMEM((xt.shape[1], kw), jnp.bfloat16) for xt in xts],
        compiler_params=params(24),
        cost_estimate=cost(2 * total * depth * kw, 2 * depth * (total + 3 * kw)),
        name="residue",
    )(*flat, *xts, fb, keep)


def outer_kernel(n, per_row, *refs):
    messages, (out, wide, lines) = refs[:n], refs[n:]
    step = pl.program_id(0)
    cap = messages[0].shape[0] - 16
    tile, kw = out.shape

    @pl.when(step == 0)
    def _():
        for k in range(n):
            tail = messages[k][cap:, :].astype(jnp.float32)
            number = (tail[0:1, :] * LANES + tail[1:2, :]).astype(jnp.int32)
            lines[:, k * cap : (k + 1) * cap] = jnp.broadcast_to(number // per_row, (8, cap))
            column = jnp.broadcast_to((number % per_row).astype(jnp.float32), (LANES, cap)).T
            value = messages[k][:cap, :].astype(jnp.float32)
            for c in range(per_row):
                wide[k * cap : (k + 1) * cap, c * LANES : (c + 1) * LANES] = jnp.where(
                    column == c, value, 0.0
                ).astype(jnp.bfloat16)

    line = lax.broadcasted_iota(jnp.int32, (tile, n * cap), 0) + step * tile
    hot = (lines[0:1, :] == line).astype(jnp.float32).astype(jnp.bfloat16)
    out[...] = jnp.dot(hot, wide[...], preferred_element_type=jnp.float32) / n


def outer(messages, depth, kw):
    n = len(messages)
    cap = messages[0].shape[0] - 16
    tile = min(depth, 512)
    return pl.pallas_call(
        functools.partial(outer_kernel, n, kw // LANES),
        grid=(depth // tile,),
        out_shape=jax.ShapeDtypeStruct((depth, kw), jnp.float32),
        in_specs=[pl.BlockSpec(messages[0].shape, lambda i: (0, 0))] * n,
        out_specs=pl.BlockSpec((tile, kw), lambda i: (i, 0)),
        scratch_shapes=[
            pltpu.VMEM((n * cap, kw), jnp.bfloat16),
            pltpu.VMEM((8, n * cap), jnp.int32),
        ],
        compiler_params=params(24),
        cost_estimate=cost(2 * n * cap * depth * kw, 4 * depth * kw),
        name="outer",
    )(*messages)


def on_device(inputs, target, weights, feedback, counts, blocks):
    tokens, w, fb = inputs[0], weights[0], feedback[0]
    n_shard, n_rep = lax.axis_size("shard"), lax.axis_size("rep")
    me = lax.axis_index("shard")
    tok_dev = tokens.shape[0]
    depth, kw = w.shape
    slot_row = blocks[0]
    slots = blocks.reshape(-1, 1)

    pieces, parts, xgs, xts, spans = [], [], [], [], []
    start = 0
    for share in CHUNKS:
        rows = tok_dev * share // sum(CHUNKS)
        mine = [
            lax.dynamic_slice(tokens, (start, (me ^ d) * depth), (rows, depth))
            for d in range(n_shard)
        ]
        moved = [swap(mine[d], "shard", n_shard, d) for d in range(1, n_shard)]
        pieces.append(mine[:1] + moved)
        spans.append(start)
        start += rows
    fbk, keep = early(slots, slot_row, counts, fb)
    after = []
    for c, low in enumerate(spans):
        products, x = project(pieces[c], w, after)
        moved = [swap(products[d], "shard", n_shard, d) for d in range(1, n_shard)]
        xg, xt = prepare(x, slots, counts, kw // LANES, products[1])
        xgs.append(xg)
        xts.append(xt)
        mine = slope([products[0]] + moved, target[0], low, xt)
        parts.append([mine] + [swap(mine, "shard", n_shard, d) for d in range(1, n_shard)])
        after = [keep] + parts[-1]
    message = kept(parts, xgs, fbk, slots, slot_row)
    messages = [message] + [swap(message, "rep", n_rep, d) for d in range(1, n_rep)]
    new_feedback = residue(parts, xts, fb, keep)
    return outer(messages, depth, kw), new_feedback[None]


def solution(mesh):
    placed = (
        P("rep", "shard", None),
        P("rep", "shard", None),
        P("rep", "shard", None),
        P("rep", "shard", None),
        P("rep", "shard"),
        P("rep", "shard", None),
    )
    return jax.shard_map(
        on_device,
        mesh=mesh,
        in_specs=placed,
        out_specs=(P("shard", None), P("rep", "shard", None)),
        check_vma=False,
    )
```

```python
import functools

import jax
import jax.numpy as jnp
from jax import lax
from jax.experimental import pallas as pl
from jax.experimental.pallas import tpu as pltpu
from jax.sharding import PartitionSpec as P

LANES = 128
ANY = pl.BlockSpec(memory_space=pl.ANY)
VMEM = pl.BlockSpec(memory_space=pltpu.VMEM)
SMEM = pl.BlockSpec(memory_space=pltpu.SMEM)
MIB = 1024 * 1024


def params(mib):
    return pltpu.CompilerParams(vmem_limit_bytes=mib * MIB)


def cost(flops, nbytes):
    return pl.CostEstimate(flops=int(flops), bytes_accessed=int(nbytes), transcendentals=0)


def swap(x, axis, n, d):
    return lax.ppermute(x, axis, [(i, i ^ d) for i in range(n)])


def cut_kernel(cuts, tokens, *refs):
    outs, sems = refs[-len(cuts) - 1 : -1], refs[-1]
    me = lax.axis_index("shard")
    copies = []
    for k, (d, low, rows) in enumerate(cuts):
        depth = outs[k].shape[1]
        columns = pl.ds(pl.multiple_of((me ^ d) * depth, LANES), depth)
        copy = pltpu.make_async_copy(tokens.at[pl.ds(low, rows), columns], outs[k], sems.at[k])
        copy.start()
        copies.append(copy)
    for copy in copies:
        copy.wait()


def cut(tokens, depth, cuts, after):
    return pl.pallas_call(
        functools.partial(cut_kernel, cuts),
        out_shape=[jax.ShapeDtypeStruct((rows, depth), tokens.dtype) for _, _, rows in cuts],
        in_specs=[ANY] * (1 + len(after)),
        scratch_shapes=[pltpu.SemaphoreType.DMA((len(cuts),))],
        compiler_params=params(16),
        cost_estimate=cost(0, 4 * depth * sum(rows for _, _, rows in cuts)),
        name="cut",
    )(tokens, *after)


def project_kernel(n, *refs):
    pieces, w, outs, x = refs[:n], refs[n], refs[-n - 1 : -1], refs[-1]
    start = 0
    for piece in pieces:
        x[start : start + piece.shape[0], :] = piece[...]
        start += piece.shape[0]
    full = jnp.dot(x[...], w[...], preferred_element_type=jnp.float32)
    start = 0
    for out in outs:
        out[...] = full[start : start + out.shape[0], :].astype(out.dtype)
        start += out.shape[0]


def project(pieces, types, w, after):
    n = len(pieces)
    rows, depth = sum(p.shape[0] for p in pieces), pieces[0].shape[1]
    kw = w.shape[1]
    result = pl.pallas_call(
        functools.partial(project_kernel, n),
        out_shape=[jax.ShapeDtypeStruct((p.shape[0], kw), t) for p, t in zip(pieces, types)]
        + [jax.ShapeDtypeStruct((rows, depth), jnp.bfloat16)],
        in_specs=[VMEM] * (n + 1) + [ANY] * len(after),
        compiler_params=params(24),
        cost_estimate=cost(2 * rows * depth * kw, 2 * depth * (rows + kw)),
        name="project",
    )(*pieces, w, *after)
    return result[:n], result[n]


def slope_kernel(tok_dev, n, *refs):
    goal, mine, out = refs[0], refs[1], refs[-1]
    whole = refs[2 : 2 + n]
    halves = refs[2 + n : -2]
    half = out.shape[0] // 2
    for part in range(2):
        rows = slice(part * half, (part + 1) * half)
        key_proj = mine[rows, :]
        for product in whole:
            key_proj += product[rows, :].astype(jnp.float32)
        for product in halves[part::2]:
            key_proj += product[...].astype(jnp.float32)
        gap = key_proj - goal[rows, :].astype(jnp.float32)
        out[rows, :] = (gap / tok_dev).astype(jnp.bfloat16)


def slope(goal, mine, whole, halves, after):
    return pl.pallas_call(
        functools.partial(slope_kernel, goal.shape[0], len(whole)),
        out_shape=jax.ShapeDtypeStruct(mine.shape, jnp.bfloat16),
        in_specs=[VMEM] * (2 + len(whole) + len(halves)) + [ANY],
        compiler_params=params(8),
        cost_estimate=cost(4 * mine.size, 12 * mine.size),
        name="slope",
    )(goal, mine, *whole, *halves, after)


def pick_columns(wide, column):
    out = jnp.zeros((wide.shape[0], LANES), jnp.float32)
    for c in range(wide.shape[1] // LANES):
        out += jnp.where(column == c, wide[:, c * LANES : (c + 1) * LANES], 0.0)
    return out


def early_kernel(per_row, slots, slot_row, count, fb, after, fbk, keep):
    depth, kw = fb.shape
    cap = slots.shape[0]
    slot = slots[...]
    hot = slot // per_row == lax.broadcasted_iota(jnp.int32, (cap, depth), 1)
    hot = hot.astype(jnp.float32).astype(jnp.bfloat16)
    used = lax.broadcasted_iota(jnp.int32, (cap, 1), 0) < count[0, 0]
    wide = jnp.dot(hot, fb[...], preferred_element_type=jnp.float32)
    fbk[...] = jnp.where(used, pick_columns(wide, slot % per_row), 0.0)
    group = lax.broadcasted_iota(jnp.int32, (cap, kw), 1) // LANES
    mark = jnp.where(used & (slot % per_row == group), 1.0, 0.0).astype(jnp.bfloat16)
    tile = min(depth, 512)
    for t in range(depth // tile):
        line = lax.broadcasted_iota(jnp.int32, (tile, cap), 0) + t * tile
        hot = (slot_row[...] // per_row == line).astype(jnp.float32).astype(jnp.bfloat16)
        mask = jnp.dot(hot, mark, preferred_element_type=jnp.float32)
        keep[t * tile : (t + 1) * tile, :] = (1.0 - mask).astype(jnp.bfloat16)


def early(slots, slot_row, count, fb, after):
    depth, kw = fb.shape
    cap = slots.shape[0]
    return pl.pallas_call(
        functools.partial(early_kernel, kw // LANES),
        out_shape=[
            jax.ShapeDtypeStruct((cap, LANES), jnp.float32),
            jax.ShapeDtypeStruct((depth, kw), jnp.bfloat16),
        ],
        in_specs=[VMEM, VMEM, SMEM, VMEM, ANY],
        compiler_params=params(24),
        cost_estimate=cost(4 * cap * depth * kw, 4 * depth * kw),
        name="early",
    )(slots, slot_row, count, fb, after)


def prepare_kernel(per_row, n, *refs):
    xs, (slots, count), (xg, xt) = refs[:n], refs[n : n + 2], refs[-2:]
    depth = xs[0].shape[1]
    cap = slots.shape[0]
    used = lax.broadcasted_iota(jnp.int32, (cap, 1), 0) < count[0, 0]
    line = jnp.where(used, slots[...] // per_row, depth)
    hot = line == lax.broadcasted_iota(jnp.int32, (cap, depth), 1)
    hot = hot.astype(jnp.float32).astype(jnp.bfloat16)
    start = 0
    for x in xs:
        rows = x.shape[0]
        xg[:, start : start + rows] = lax.dot_general(
            hot, x[...], (((1,), (1,)), ((), ())), preferred_element_type=jnp.float32
        ).astype(jnp.bfloat16)
        xt[:, start : start + rows] = x[...].T
        start += rows


def prepare(xs, slots, count, per_row, after):
    rows, depth = sum(x.shape[0] for x in xs), xs[0].shape[1]
    cap = slots.shape[0]
    return pl.pallas_call(
        functools.partial(prepare_kernel, per_row, len(xs)),
        out_shape=[
            jax.ShapeDtypeStruct((cap, rows), jnp.bfloat16),
            jax.ShapeDtypeStruct((depth, rows), jnp.bfloat16),
        ],
        in_specs=[VMEM] * (len(xs) + 1) + [SMEM] + [ANY] * len(after),
        compiler_params=params(24),
        cost_estimate=cost(2 * cap * depth * rows, 4 * depth * rows),
        name="prepare",
    )(*xs, slots, count, *after)


def stack(slopes, order, s):
    start = 0
    for d, low, high in order:
        s[start : start + high - low, :] = slopes[d][low:high, :]
        start += high - low


def kept_kernel(per_row, order, *refs):
    n = len({d for d, _, _ in order})
    slopes, (fbk, slots, slot_row), out, s = refs[:n], refs[-5:-2], refs[-2], refs[-1]
    xgs = refs[n:-5]
    cap = slots.shape[0]
    stack(slopes, order, s)
    wide, start = 0.0, 0
    for xg in xgs:
        rows = xg.shape[1]
        wide += jnp.dot(xg[...], s[start : start + rows, :], preferred_element_type=jnp.float32)
        start += rows
    value = pick_columns(wide, slots[...] % per_row) + fbk[...]
    out[:cap, :] = value.astype(jnp.bfloat16)
    tail = out.shape[0] - cap
    number = jnp.broadcast_to(slot_row[...], (tail, cap))
    line = lax.broadcasted_iota(jnp.int32, (tail, cap), 0)
    number = jnp.where(line == 0, number // LANES, number % LANES)
    out[cap:, :] = number.astype(jnp.float32).astype(jnp.bfloat16)


def kept(slopes, order, xgs, fbk, slots, slot_row):
    cap = slots.shape[0]
    rows, kw = slopes[0].shape
    total = len(slopes) * rows
    return pl.pallas_call(
        functools.partial(kept_kernel, kw // LANES, order),
        out_shape=jax.ShapeDtypeStruct((cap + 16, LANES), jnp.bfloat16),
        scratch_shapes=[pltpu.VMEM((total, kw), jnp.bfloat16)],
        compiler_params=params(8),
        cost_estimate=cost(2 * cap * total * kw, 2 * total * kw),
        name="kept",
    )(*slopes, *xgs, fbk, slots, slot_row)


def residue_kernel(order, tile, *refs):
    n = len({d for d, _, _ in order})
    slopes, xts, (fb, keep, out, s, held, sems) = refs[:n], refs[n:-6], refs[-6:]
    stack(slopes, order, s)
    copies = []
    for t in range(out.shape[0] // tile):
        rows = slice(t * tile, (t + 1) * tile)
        pseudo, start = fb[rows, :].astype(jnp.float32), 0
        for xt in xts:
            part = s[start : start + xt.shape[1], :]
            pseudo += jnp.dot(xt[rows, :], part, preferred_element_type=jnp.float32)
            start += xt.shape[1]
        held[rows, :] = jnp.where(keep[rows, :] > 0, pseudo, 0.0).astype(jnp.bfloat16)
        copy = pltpu.make_async_copy(held.at[rows, :], out.at[rows, :], sems.at[t])
        copy.start()
        copies.append(copy)
    for copy in copies:
        copy.wait()


def residue(slopes, order, xts, fb, keep):
    depth, kw = fb.shape
    total = sum(xt.shape[1] for xt in xts)
    tile = min(depth, 512)
    return pl.pallas_call(
        functools.partial(residue_kernel, order, tile),
        out_shape=jax.ShapeDtypeStruct((depth, kw), jnp.bfloat16),
        in_specs=[VMEM] * (len(slopes) + len(xts) + 2),
        out_specs=ANY,
        scratch_shapes=[
            pltpu.VMEM((total, kw), jnp.bfloat16),
            pltpu.VMEM((depth, kw), jnp.bfloat16),
            pltpu.SemaphoreType.DMA((depth // tile,)),
        ],
        compiler_params=params(24),
        cost_estimate=cost(2 * total * depth * kw, 2 * depth * (total + 3 * kw)),
        name="residue",
    )(*slopes, *xts, fb, keep)


def outer_kernel(n, per_row, tile, *refs):
    messages, (out, wide, lines, held, sems) = refs[:n], refs[n:]
    cap = messages[0].shape[0] - 16
    for k in range(n):
        tail = messages[k][cap:, :].astype(jnp.float32)
        number = (tail[0:1, :] * LANES + tail[1:2, :]).astype(jnp.int32)
        lines[:, k * cap : (k + 1) * cap] = jnp.broadcast_to(number // per_row, (8, cap))
        column = jnp.broadcast_to((number % per_row).astype(jnp.float32), (LANES, cap)).T
        value = messages[k][:cap, :].astype(jnp.float32)
        for c in range(per_row):
            wide[k * cap : (k + 1) * cap, c * LANES : (c + 1) * LANES] = jnp.where(
                column == c, value, 0.0
            ).astype(jnp.bfloat16)
    copies = []
    for t in range(out.shape[0] // tile):
        rows = slice(t * tile, (t + 1) * tile)
        line = lax.broadcasted_iota(jnp.int32, (tile, n * cap), 0) + t * tile
        hot = (lines[0:1, :] == line).astype(jnp.float32).astype(jnp.bfloat16)
        held[rows, :] = jnp.dot(hot, wide[...], preferred_element_type=jnp.float32) / n
        copy = pltpu.make_async_copy(held.at[rows, :], out.at[rows, :], sems.at[t])
        copy.start()
        copies.append(copy)
    for copy in copies:
        copy.wait()


def outer(messages, depth, kw):
    n = len(messages)
    cap = messages[0].shape[0] - 16
    tile = min(depth, 512)
    return pl.pallas_call(
        functools.partial(outer_kernel, n, kw // LANES, tile),
        out_shape=jax.ShapeDtypeStruct((depth, kw), jnp.float32),
        out_specs=ANY,
        scratch_shapes=[
            pltpu.VMEM((n * cap, kw), jnp.bfloat16),
            pltpu.VMEM((8, n * cap), jnp.int32),
            pltpu.VMEM((depth, kw), jnp.float32),
            pltpu.SemaphoreType.DMA((depth // tile,)),
        ],
        compiler_params=params(24),
        cost_estimate=cost(2 * n * cap * depth * kw, 4 * depth * kw),
        name="outer",
    )(*messages)


def on_device(inputs, target, weights, feedback, counts, blocks):
    tokens, w, fb = inputs[0], weights[0], feedback[0]
    n_shard, n_rep = lax.axis_size("shard"), lax.axis_size("rep")
    tok_dev = tokens.shape[0]
    depth, kw = w.shape
    half = tok_dev // 2
    per_row = kw // LANES
    slot_row = blocks[0]
    slots = blocks.reshape(-1, 1)
    near = [d for d in range(1, n_shard) if d & (d - 1) == 0]
    far = [d for d in range(1, n_shard) if d & (d - 1) != 0]

    far_out = cut(tokens, depth, [(d, 0, tok_dev) for d in far], [])
    far_in = [swap(x, "shard", n_shard, d) for x, d in zip(far_out, far)]
    near_out, after = [], far_out[:1]
    for part in range(2):
        near_out.append(cut(tokens, depth, [(d, part * half, half) for d in near], after))
        if part == 0:
            fbk, keep = early(slots, slot_row, counts, fb, near_out[0][0])
            after = [fbk]
    near_in = [[swap(x, "shard", n_shard, d) for x, d in zip(out, near)] for out in near_out]
    (own,) = cut(tokens, depth, [(0, 0, tok_dev)], [near_out[1][0]])

    brief, wide = jnp.bfloat16, jnp.float32
    (mine, *products), x_far = project([own] + far_in, [wide] + [brief] * len(far), w, [])
    whole = [swap(p, "shard", n_shard, d) for p, d in zip(products, far)]
    xg_far, xt_far = prepare([x_far], slots, counts, per_row, [])
    after, halves, x_near = [xt_far, keep], [], []
    for part in range(2):
        products, x = project(near_in[part], [brief] * len(near), w, after)
        halves.append([swap(p, "shard", n_shard, d) for p, d in zip(products, near)])
        x_near.append(x)
        after = [products[0]]
    xg_near, xt_near = prepare(x_near, slots, counts, per_row, [products[0]])
    halves = [half_of[k] for k in range(len(near)) for half_of in halves]
    slopes = slope(target[0], mine, whole, halves, xt_near)
    slopes = [slopes] + [swap(slopes, "shard", n_shard, d) for d in range(1, n_shard)]

    order = [(d, 0, tok_dev) for d in [0] + far]
    order += [(d, part * half, (part + 1) * half) for part in range(2) for d in near]
    message = kept(slopes, order, [xg_far, xg_near], fbk, slots, slot_row)
    same_core = [message] + [swap(message, "rep", n_rep, d) for d in range(2, n_rep, 2)]
    messages = same_core + [swap(m, "rep", n_rep, 1) for m in same_core]
    new_feedback = residue(slopes, order, [xt_far, xt_near], fb, keep)
    return outer(messages, depth, kw), new_feedback[None]


def solution(mesh):
    placed = (
        P("rep", "shard", None),
        P("rep", "shard", None),
        P("rep", "shard", None),
        P("rep", "shard", None),
        P("rep", "shard"),
        P("rep", "shard", None),
    )
    return jax.shard_map(
        on_device,
        mesh=mesh,
        in_specs=placed,
        out_specs=(P("shard", None), P("rep", "shard", None)),
        check_vma=False,
    )
```

```python
import functools

import jax
import jax.numpy as jnp
from jax import lax
from jax.experimental import pallas as pl
from jax.experimental.pallas import tpu as pltpu
from jax.sharding import PartitionSpec as P

LANES = 128
ANY = pl.BlockSpec(memory_space=pl.ANY)
VMEM = pl.BlockSpec(memory_space=pltpu.VMEM)
HBM = pl.BlockSpec(memory_space=pltpu.HBM)
SMEM = pl.BlockSpec(memory_space=pltpu.SMEM)
MIB = 1024 * 1024


def params(mib):
    return pltpu.CompilerParams(vmem_limit_bytes=mib * MIB)


def cost(flops, nbytes):
    return pl.CostEstimate(flops=int(flops), bytes_accessed=int(nbytes), transcendentals=0)


def swap(x, axis, n, d):
    return lax.ppermute(x, axis, [(i, i ^ d) for i in range(n)])


def cut_kernel(cuts, tokens, *refs):
    outs, sems = refs[-len(cuts) - 1 : -1], refs[-1]
    me = lax.axis_index("shard")
    copies = []
    for k, (d, low, rows) in enumerate(cuts):
        depth = outs[k].shape[1]
        columns = pl.ds(pl.multiple_of((me ^ d) * depth, LANES), depth)
        copy = pltpu.make_async_copy(tokens.at[pl.ds(low, rows), columns], outs[k], sems.at[k])
        copy.start()
        copies.append(copy)
    for copy in copies:
        copy.wait()


def cut(tokens, depth, cuts, after):
    return pl.pallas_call(
        functools.partial(cut_kernel, cuts),
        out_shape=[jax.ShapeDtypeStruct((rows, depth), tokens.dtype) for _, _, rows in cuts],
        in_specs=[HBM] + [ANY] * len(after),
        scratch_shapes=[pltpu.SemaphoreType.DMA((len(cuts),))],
        compiler_params=params(16),
        cost_estimate=cost(0, 4 * depth * sum(rows for _, _, rows in cuts)),
        name="cut",
    )(tokens, *after)


def project_kernel(n, *refs):
    pieces, w, outs, x = refs[:n], refs[n], refs[-n - 1 : -1], refs[-1]
    start = 0
    for piece in pieces:
        x[start : start + piece.shape[0], :] = piece[...]
        start += piece.shape[0]
    full = jnp.dot(x[...], w[...], preferred_element_type=jnp.float32)
    start = 0
    for out in outs:
        out[...] = full[start : start + out.shape[0], :].astype(out.dtype)
        start += out.shape[0]


def project(pieces, types, w, after):
    n = len(pieces)
    rows, depth = sum(p.shape[0] for p in pieces), pieces[0].shape[1]
    kw = w.shape[1]
    result = pl.pallas_call(
        functools.partial(project_kernel, n),
        out_shape=[jax.ShapeDtypeStruct((p.shape[0], kw), t) for p, t in zip(pieces, types)]
        + [jax.ShapeDtypeStruct((rows, depth), jnp.bfloat16)],
        in_specs=[VMEM] * (n + 1) + [ANY] * len(after),
        compiler_params=params(24),
        cost_estimate=cost(2 * rows * depth * kw, 2 * depth * (rows + kw)),
        name="project",
    )(*pieces, w, *after)
    return result[:n], result[n]


def slope_kernel(tok_dev, n, spans, *refs):
    goal, mine, out = refs[0], refs[1], refs[-1]
    whole = refs[2 : 2 + n]
    shares = refs[2 + n : -2]
    for part, (low, high) in enumerate(spans):
        key_proj = mine[low:high, :]
        for product in whole:
            key_proj += product[low:high, :].astype(jnp.float32)
        for product in shares[part :: len(spans)]:
            key_proj += product[...].astype(jnp.float32)
        gap = key_proj - goal[low:high, :].astype(jnp.float32)
        out[low:high, :] = (gap / tok_dev).astype(jnp.bfloat16)


def slope(goal, mine, whole, shares, spans, after):
    return pl.pallas_call(
        functools.partial(slope_kernel, goal.shape[0], len(whole), spans),
        out_shape=jax.ShapeDtypeStruct(mine.shape, jnp.bfloat16),
        in_specs=[VMEM] * (2 + len(whole) + len(shares)) + [ANY],
        compiler_params=params(8),
        cost_estimate=cost(4 * mine.size, 12 * mine.size),
        name="slope",
    )(goal, mine, *whole, *shares, after)


def pick_columns(wide, column):
    out = jnp.zeros((wide.shape[0], LANES), jnp.float32)
    for c in range(wide.shape[1] // LANES):
        out += jnp.where(column == c, wide[:, c * LANES : (c + 1) * LANES], 0.0)
    return out


def early_kernel(per_row, slots, slot_row, count, fb, after, fbk, keep):
    depth, kw = fb.shape
    cap = slots.shape[0]
    slot = slots[...]
    hot = slot // per_row == lax.broadcasted_iota(jnp.int32, (cap, depth), 1)
    hot = hot.astype(jnp.float32).astype(jnp.bfloat16)
    used = lax.broadcasted_iota(jnp.int32, (cap, 1), 0) < count[0, 0]
    wide = jnp.dot(hot, fb[...], preferred_element_type=jnp.float32)
    fbk[...] = jnp.where(used, pick_columns(wide, slot % per_row), 0.0)
    group = lax.broadcasted_iota(jnp.int32, (cap, kw), 1) // LANES
    mark = jnp.where(used & (slot % per_row == group), 1.0, 0.0).astype(jnp.bfloat16)
    tile = min(depth, 512)
    for t in range(depth // tile):
        line = lax.broadcasted_iota(jnp.int32, (tile, cap), 0) + t * tile
        hot = (slot_row[...] // per_row == line).astype(jnp.float32).astype(jnp.bfloat16)
        mask = jnp.dot(hot, mark, preferred_element_type=jnp.float32)
        keep[t * tile : (t + 1) * tile, :] = (1.0 - mask).astype(jnp.bfloat16)


def early(slots, slot_row, count, fb, after):
    depth, kw = fb.shape
    cap = slots.shape[0]
    return pl.pallas_call(
        functools.partial(early_kernel, kw // LANES),
        out_shape=[
            jax.ShapeDtypeStruct((cap, LANES), jnp.float32),
            jax.ShapeDtypeStruct((depth, kw), jnp.bfloat16),
        ],
        in_specs=[VMEM, VMEM, SMEM, VMEM, ANY],
        compiler_params=params(24),
        cost_estimate=cost(4 * cap * depth * kw, 4 * depth * kw),
        name="early",
    )(slots, slot_row, count, fb, after)


def prepare_kernel(per_row, n, *refs):
    xs, (slots, count), (xg, xt) = refs[:n], refs[n : n + 2], refs[-2:]
    depth = xs[0].shape[1]
    cap = slots.shape[0]
    used = lax.broadcasted_iota(jnp.int32, (cap, 1), 0) < count[0, 0]
    line = jnp.where(used, slots[...] // per_row, depth)
    hot = line == lax.broadcasted_iota(jnp.int32, (cap, depth), 1)
    hot = hot.astype(jnp.float32).astype(jnp.bfloat16)
    start = 0
    for x in xs:
        rows = x.shape[0]
        xg[:, start : start + rows] = lax.dot_general(
            hot, x[...], (((1,), (1,)), ((), ())), preferred_element_type=jnp.float32
        ).astype(jnp.bfloat16)
        xt[:, start : start + rows] = x[...].T
        start += rows


def prepare(xs, slots, count, per_row, after):
    rows, depth = sum(x.shape[0] for x in xs), xs[0].shape[1]
    cap = slots.shape[0]
    return pl.pallas_call(
        functools.partial(prepare_kernel, per_row, len(xs)),
        out_shape=[
            jax.ShapeDtypeStruct((cap, rows), jnp.bfloat16),
            jax.ShapeDtypeStruct((depth, rows), jnp.bfloat16),
        ],
        in_specs=[VMEM] * (len(xs) + 1) + [SMEM] + [ANY] * len(after),
        compiler_params=params(24),
        cost_estimate=cost(2 * cap * depth * rows, 4 * depth * rows),
        name="prepare",
    )(*xs, slots, count, *after)


def stack(slopes, order, s):
    start = 0
    for d, low, high in order:
        s[start : start + high - low, :] = slopes[d][low:high, :]
        start += high - low


def kept_kernel(per_row, order, *refs):
    n = len({d for d, _, _ in order})
    slopes, (fbk, slots, slot_row), out, s = refs[:n], refs[-5:-2], refs[-2], refs[-1]
    xgs = refs[n:-5]
    cap = slots.shape[0]
    stack(slopes, order, s)
    wide, start = 0.0, 0
    for xg in xgs:
        rows = xg.shape[1]
        wide += jnp.dot(xg[...], s[start : start + rows, :], preferred_element_type=jnp.float32)
        start += rows
    value = pick_columns(wide, slots[...] % per_row) + fbk[...]
    out[:cap, :] = value.astype(jnp.bfloat16)
    tail = out.shape[0] - cap
    number = jnp.broadcast_to(slot_row[...], (tail, cap))
    line = lax.broadcasted_iota(jnp.int32, (tail, cap), 0)
    number = jnp.where(line == 0, number // LANES, number % LANES)
    out[cap:, :] = number.astype(jnp.float32).astype(jnp.bfloat16)


def kept(slopes, order, xgs, fbk, slots, slot_row):
    cap = slots.shape[0]
    rows, kw = slopes[0].shape
    total = len(slopes) * rows
    return pl.pallas_call(
        functools.partial(kept_kernel, kw // LANES, order),
        out_shape=jax.ShapeDtypeStruct((cap + 16, LANES), jnp.bfloat16),
        scratch_shapes=[pltpu.VMEM((total, kw), jnp.bfloat16)],
        compiler_params=params(8),
        cost_estimate=cost(2 * cap * total * kw, 2 * total * kw),
        name="kept",
    )(*slopes, *xgs, fbk, slots, slot_row)


def send_out(held, out, sems, t, tile):
    rows = pl.ds(pl.multiple_of(t * tile, tile), tile)
    return pltpu.make_async_copy(held.at[rows, :], out.at[rows, :], sems.at[t])


def residue_kernel(order, tile, *refs):
    n = len({d for d, _, _ in order})
    slopes, xts, (fb, keep, out, s, held, sems) = refs[:n], refs[n:-6], refs[-6:]
    stack(slopes, order, s)
    tiles = out.shape[0] // tile

    @pl.loop(0, tiles)
    def _(t):
        rows = pl.ds(pl.multiple_of(t * tile, tile), tile)
        pseudo, start = fb[rows, :].astype(jnp.float32), 0
        for xt in xts:
            part = s[start : start + xt.shape[1], :]
            pseudo += jnp.dot(xt[rows, :], part, preferred_element_type=jnp.float32)
            start += xt.shape[1]
        held[rows, :] = jnp.where(keep[rows, :] > 0, pseudo, 0.0).astype(jnp.bfloat16)
        send_out(held, out, sems, t, tile).start()

    @pl.loop(0, tiles)
    def _(t):
        send_out(held, out, sems, t, tile).wait()


def residue(slopes, order, xts, fb, keep):
    depth, kw = fb.shape
    total = sum(xt.shape[1] for xt in xts)
    tile = min(depth, 256)
    return pl.pallas_call(
        functools.partial(residue_kernel, order, tile),
        out_shape=jax.ShapeDtypeStruct((depth, kw), jnp.bfloat16),
        in_specs=[VMEM] * (len(slopes) + len(xts) + 2),
        out_specs=ANY,
        scratch_shapes=[
            pltpu.VMEM((total, kw), jnp.bfloat16),
            pltpu.VMEM((depth, kw), jnp.bfloat16),
            pltpu.SemaphoreType.DMA((depth // tile,)),
        ],
        compiler_params=params(24),
        cost_estimate=cost(2 * total * depth * kw, 2 * depth * (total + 3 * kw)),
        name="residue",
    )(*slopes, *xts, fb, keep)


def join_kernel(*refs):
    out = refs[-1]
    rows = refs[0].shape[0]
    for k in range(len(refs) - 2):
        out[k * rows : (k + 1) * rows, :] = refs[k][...]


def join(messages, after):
    rows, lanes = messages[0].shape
    return pl.pallas_call(
        join_kernel,
        out_shape=jax.ShapeDtypeStruct((len(messages) * rows, lanes), jnp.bfloat16),
        in_specs=[VMEM] * len(messages) + [ANY],
        compiler_params=params(8),
        cost_estimate=cost(0, 4 * len(messages) * rows * lanes),
        name="join",
    )(*messages, after)


def outer_kernel(cap, per_row, tile, *refs):
    groups, (out, wide, lines, held, sems) = refs[:-5], refs[-5:]
    n = lines.shape[1] // cap
    size = cap + 16
    k = 0
    for group in groups:
        for start in range(0, group.shape[0], size):
            tail = group[start + cap : start + size, :].astype(jnp.float32)
            number = (tail[0:1, :] * LANES + tail[1:2, :]).astype(jnp.int32)
            lines[:, k * cap : (k + 1) * cap] = jnp.broadcast_to(number // per_row, (8, cap))
            column = jnp.broadcast_to((number % per_row).astype(jnp.float32), (LANES, cap)).T
            value = group[start : start + cap, :].astype(jnp.float32)
            for c in range(per_row):
                wide[k * cap : (k + 1) * cap, c * LANES : (c + 1) * LANES] = jnp.where(
                    column == c, value, 0.0
                ).astype(jnp.bfloat16)
            k += 1
    tiles = out.shape[0] // tile

    @pl.loop(0, tiles)
    def _(t):
        rows = pl.ds(pl.multiple_of(t * tile, tile), tile)
        line = lax.broadcasted_iota(jnp.int32, (tile, n * cap), 0) + t * tile
        hot = (lines[0:1, :] == line).astype(jnp.float32).astype(jnp.bfloat16)
        held[rows, :] = jnp.dot(hot, wide[...], preferred_element_type=jnp.float32) / n
        send_out(held, out, sems, t, tile).start()

    @pl.loop(0, tiles)
    def _(t):
        send_out(held, out, sems, t, tile).wait()


def outer(groups, cap, depth, kw):
    n = sum(group.shape[0] for group in groups) // (cap + 16)
    tile = min(depth, 256)
    return pl.pallas_call(
        functools.partial(outer_kernel, cap, kw // LANES, tile),
        out_shape=jax.ShapeDtypeStruct((depth, kw), jnp.float32),
        out_specs=ANY,
        scratch_shapes=[
            pltpu.VMEM((n * cap, kw), jnp.bfloat16),
            pltpu.VMEM((8, n * cap), jnp.int32),
            pltpu.VMEM((depth, kw), jnp.float32),
            pltpu.SemaphoreType.DMA((depth // tile,)),
        ],
        compiler_params=params(24),
        cost_estimate=cost(2 * n * cap * depth * kw, 4 * depth * kw),
        name="outer",
    )(*groups)


def on_device(inputs, target, weights, feedback, counts, blocks):
    tokens, w, fb = inputs[0], weights[0], feedback[0]
    n_shard, n_rep = lax.axis_size("shard"), lax.axis_size("rep")
    tok_dev = tokens.shape[0]
    depth, kw = w.shape
    early_rows = tok_dev * 3 // 4
    spans = [(0, early_rows), (early_rows, tok_dev)]
    per_row = kw // LANES
    slot_row = blocks[0]
    slots = blocks.reshape(-1, 1)
    near = [d for d in range(1, n_shard) if d & (d - 1) == 0]
    far = [d for d in range(1, n_shard) if d & (d - 1) != 0]

    far_out = cut(tokens, depth, [(d, 0, tok_dev) for d in far], [])
    far_in = [swap(x, "shard", n_shard, d) for x, d in zip(far_out, far)]
    near_out, after = [], far_out[:1]
    for low, high in spans:
        near_out.append(cut(tokens, depth, [(d, low, high - low) for d in near], after))
        if low == 0:
            fbk, keep = early(slots, slot_row, counts, fb, near_out[0][0])
            after = [fbk]
    near_in = [[swap(x, "shard", n_shard, d) for x, d in zip(out, near)] for out in near_out]
    (own,) = cut(tokens, depth, [(0, 0, tok_dev)], [near_out[1][0]])

    brief, wide = jnp.bfloat16, jnp.float32
    (mine, *products), x_far = project([own] + far_in, [wide] + [brief] * len(far), w, [])
    whole = [swap(p, "shard", n_shard, d) for p, d in zip(products, far)]
    xg_far, xt_far = prepare([x_far], slots, counts, per_row, [])
    after, shares, x_near = [xt_far, keep], [], []
    for part in range(len(spans)):
        products, x = project(near_in[part], [brief] * len(near), w, after)
        shares.append([swap(p, "shard", n_shard, d) for p, d in zip(products, near)])
        x_near.append(x)
        after = [products[0]]
    xg_near, xt_near = prepare(x_near, slots, counts, per_row, [products[0]])
    shares = [share[k] for k in range(len(near)) for share in shares]
    slopes = slope(target[0], mine, whole, shares, spans, xt_near)
    slopes = [slopes] + [swap(slopes, "shard", n_shard, d) for d in range(1, n_shard)]

    order = [(d, 0, tok_dev) for d in [0] + far]
    order += [(d, low, high) for low, high in spans for d in near]
    message = kept(slopes, order, [xg_far, xg_near], fbk, slots, slot_row)
    same_core = [message] + [swap(message, "rep", n_rep, d) for d in range(2, n_rep, 2)]
    new_feedback = residue(slopes, order, [xt_far, xt_near], fb, keep)
    joined = join(same_core, new_feedback)
    groups = [joined, swap(joined, "rep", n_rep, 1)]
    return outer(groups, message.shape[0] - 16, depth, kw), new_feedback[None]


def solution(mesh):
    placed = (
        P("rep", "shard", None),
        P("rep", "shard", None),
        P("rep", "shard", None),
        P("rep", "shard", None),
        P("rep", "shard"),
        P("rep", "shard", None),
    )
    return jax.shard_map(
        on_device,
        mesh=mesh,
        in_specs=placed,
        out_specs=(P("shard", None), P("rep", "shard", None)),
        check_vma=False,
    )
```

```python
import functools

import jax
import jax.numpy as jnp
from jax import lax
from jax.experimental import pallas as pl
from jax.experimental.pallas import tpu as pltpu
from jax.sharding import PartitionSpec as P

LANES = 128
ANY = pl.BlockSpec(memory_space=pl.ANY)
BRIEF = pl.CostEstimate(flops=1000, bytes_accessed=1000, transcendentals=0)
VMEM = pl.BlockSpec(memory_space=pltpu.VMEM)
HBM = pl.BlockSpec(memory_space=pltpu.HBM)
SMEM = pl.BlockSpec(memory_space=pltpu.SMEM)
MIB = 1024 * 1024
TOKEN = jax.ShapeDtypeStruct((8, LANES), jnp.float32)


def params(mib):
    return pltpu.CompilerParams(vmem_limit_bytes=mib * MIB)


def swap(x, axis, n, d):
    return lax.ppermute(x, axis, [(i, i ^ d) for i in range(n)])


def cut_kernel(cuts, tokens, *refs):
    outs, (token, sems) = refs[-len(cuts) - 2 : -2], refs[-2:]
    token[...] = jnp.zeros_like(token)
    me = lax.axis_index("shard")
    copies = []
    for k, (d, low, rows) in enumerate(cuts):
        depth = outs[k].shape[1]
        columns = pl.ds(pl.multiple_of((me ^ d) * depth, LANES), depth)
        copy = pltpu.make_async_copy(tokens.at[pl.ds(low, rows), columns], outs[k], sems.at[k])
        copy.start()
        copies.append(copy)
    for copy in copies:
        copy.wait()


def cut(tokens, depth, cuts, after, mib=16):
    return pl.pallas_call(
        functools.partial(cut_kernel, cuts),
        out_shape=[jax.ShapeDtypeStruct((rows, depth), tokens.dtype) for _, _, rows in cuts]
        + [TOKEN],
        in_specs=[HBM] + [ANY] * len(after),
        scratch_shapes=[pltpu.SemaphoreType.DMA((len(cuts),))],
        compiler_params=params(mib),
        cost_estimate=BRIEF,
        name="cut",
    )(tokens, *after)


def project_kernel(n, *refs):
    pieces, w, outs, x = refs[:n], refs[n], refs[-n - 1 : -1], refs[-1]
    start = 0
    for piece in pieces:
        x[start : start + piece.shape[0], :] = piece[...]
        start += piece.shape[0]
    full = jnp.dot(x[...], w[...], preferred_element_type=jnp.float32)
    start = 0
    for out in outs:
        out[...] = full[start : start + out.shape[0], :].astype(out.dtype)
        start += out.shape[0]


def project(pieces, types, w, after):
    n = len(pieces)
    rows, depth = sum(p.shape[0] for p in pieces), pieces[0].shape[1]
    kw = w.shape[1]
    result = pl.pallas_call(
        functools.partial(project_kernel, n),
        out_shape=[jax.ShapeDtypeStruct((p.shape[0], kw), t) for p, t in zip(pieces, types)]
        + [jax.ShapeDtypeStruct((rows, depth), jnp.bfloat16)],
        in_specs=[VMEM] * (n + 1) + [ANY] * len(after),
        compiler_params=params(24),
        cost_estimate=BRIEF,
        name="project",
    )(*pieces, w, *after)
    return result[:n], result[n]


def slope_kernel(tok_dev, n, spans, *refs):
    goal, mine, out = refs[0], refs[1], refs[-1]
    whole = refs[2 : 2 + n]
    shares = refs[2 + n : -2]
    for part, (low, high) in enumerate(spans):
        key_proj = mine[low:high, :]
        for product in whole:
            key_proj += product[low:high, :].astype(jnp.float32)
        for product in shares[part :: len(spans)]:
            key_proj += product[...].astype(jnp.float32)
        gap = key_proj - goal[low:high, :].astype(jnp.float32)
        out[low:high, :] = (gap / tok_dev).astype(jnp.bfloat16)


def slope(goal, mine, whole, shares, spans, after):
    return pl.pallas_call(
        functools.partial(slope_kernel, goal.shape[0], len(whole), spans),
        out_shape=jax.ShapeDtypeStruct(mine.shape, jnp.bfloat16),
        in_specs=[VMEM] * (2 + len(whole) + len(shares)) + [ANY],
        compiler_params=params(8),
        cost_estimate=BRIEF,
        name="slope",
    )(goal, mine, *whole, *shares, after)


def pick_columns(wide, column):
    out = jnp.zeros((wide.shape[0], LANES), jnp.float32)
    for c in range(wide.shape[1] // LANES):
        out += jnp.where(column == c, wide[:, c * LANES : (c + 1) * LANES], 0.0)
    return out


def early_kernel(per_row, slots, slot_row, count, fb, after, fbk, keep, token):
    token[...] = jnp.zeros_like(token)
    depth, kw = fb.shape
    cap = slots.shape[0]
    slot = slots[...]
    hot = slot // per_row == lax.broadcasted_iota(jnp.int32, (cap, depth), 1)
    hot = hot.astype(jnp.float32).astype(jnp.bfloat16)
    used = lax.broadcasted_iota(jnp.int32, (cap, 1), 0) < count[0, 0]
    wide = jnp.dot(hot, fb[...], preferred_element_type=jnp.float32)
    fbk[...] = jnp.where(used, pick_columns(wide, slot % per_row), 0.0)
    group = lax.broadcasted_iota(jnp.int32, (cap, kw), 1) // LANES
    mark = jnp.where(used & (slot % per_row == group), 1.0, 0.0).astype(jnp.bfloat16)
    tile = min(depth, 512)
    for t in range(depth // tile):
        line = lax.broadcasted_iota(jnp.int32, (tile, cap), 0) + t * tile
        hot = (slot_row[...] // per_row == line).astype(jnp.float32).astype(jnp.bfloat16)
        mask = jnp.dot(hot, mark, preferred_element_type=jnp.float32)
        keep[t * tile : (t + 1) * tile, :] = (1.0 - mask).astype(jnp.bfloat16)


def early(slots, slot_row, count, fb, after):
    depth, kw = fb.shape
    cap = slots.shape[0]
    return pl.pallas_call(
        functools.partial(early_kernel, kw // LANES),
        out_shape=[
            jax.ShapeDtypeStruct((cap, LANES), jnp.float32),
            jax.ShapeDtypeStruct((depth, kw), jnp.bfloat16),
            TOKEN,
        ],
        in_specs=[VMEM, VMEM, SMEM, VMEM, ANY],
        compiler_params=params(24),
        cost_estimate=BRIEF,
        name="early",
    )(slots, slot_row, count, fb, after)


def prepare_kernel(per_row, n, *refs):
    xs, (slots, count), (xg, xt, token) = refs[:n], refs[n : n + 2], refs[-3:]
    token[...] = jnp.zeros_like(token)
    depth = xs[0].shape[1]
    cap = slots.shape[0]
    used = lax.broadcasted_iota(jnp.int32, (cap, 1), 0) < count[0, 0]
    line = jnp.where(used, slots[...] // per_row, depth)
    hot = line == lax.broadcasted_iota(jnp.int32, (cap, depth), 1)
    hot = hot.astype(jnp.float32).astype(jnp.bfloat16)
    start = 0
    for x in xs:
        rows = x.shape[0]
        xg[:, start : start + rows] = lax.dot_general(
            hot, x[...], (((1,), (1,)), ((), ())), preferred_element_type=jnp.float32
        ).astype(jnp.bfloat16)
        xt[:, start : start + rows] = x[...].T
        start += rows


def prepare(xs, slots, count, per_row, after):
    rows, depth = sum(x.shape[0] for x in xs), xs[0].shape[1]
    cap = slots.shape[0]
    return pl.pallas_call(
        functools.partial(prepare_kernel, per_row, len(xs)),
        out_shape=[
            jax.ShapeDtypeStruct((cap, rows), jnp.bfloat16),
            jax.ShapeDtypeStruct((depth, rows), jnp.bfloat16),
            TOKEN,
        ],
        in_specs=[VMEM] * (len(xs) + 1) + [SMEM] + [ANY] * len(after),
        compiler_params=params(24),
        cost_estimate=BRIEF,
        name="prepare",
    )(*xs, slots, count, *after)


def stack(slopes, order, s):
    start = 0
    for k, low, high in order:
        s[start : start + high - low, :] = slopes[k][low:high, :]
        start += high - low


def kept_kernel(per_row, order, *refs):
    n = len({k for k, _, _ in order})
    slopes, (fbk, slots, slot_row), out, s = refs[:n], refs[-5:-2], refs[-2], refs[-1]
    xgs = refs[n:-5]
    cap = slots.shape[0]
    stack(slopes, order, s)
    wide, start = 0.0, 0
    for xg in xgs:
        rows = xg.shape[1]
        wide += jnp.dot(xg[...], s[start : start + rows, :], preferred_element_type=jnp.float32)
        start += rows
    value = pick_columns(wide, slots[...] % per_row) + fbk[...]
    out[:cap, :] = value.astype(jnp.bfloat16)
    tail = out.shape[0] - cap
    number = jnp.broadcast_to(slot_row[...], (tail, cap))
    line = lax.broadcasted_iota(jnp.int32, (tail, cap), 0)
    number = jnp.where(line == 0, number // LANES, number % LANES)
    out[cap:, :] = number.astype(jnp.float32).astype(jnp.bfloat16)


def kept(slopes, order, xgs, fbk, slots, slot_row):
    cap = slots.shape[0]
    rows, kw = slopes[0].shape
    total = len(slopes) * rows
    return pl.pallas_call(
        functools.partial(kept_kernel, kw // LANES, order),
        out_shape=jax.ShapeDtypeStruct((cap + 16, LANES), jnp.bfloat16),
        scratch_shapes=[pltpu.VMEM((total, kw), jnp.bfloat16)],
        compiler_params=params(8),
        cost_estimate=BRIEF,
        name="kept",
    )(*slopes, *xgs, fbk, slots, slot_row)


def send_out(held, out, sems, t, tile):
    rows = pl.ds(t * tile, tile)
    return pltpu.make_async_copy(held.at[rows, :], out.at[rows, :], sems.at[t])


def residue_kernel(order, tile, *refs):
    n = len({k for k, _, _ in order})
    slopes, xts, (fb, keep, out, token, s, held, sems) = refs[:n], refs[n:-7], refs[-7:]
    token[...] = jnp.zeros_like(token)
    stack(slopes, order, s)
    tiles = out.shape[0] // tile
    for t in range(tiles):
        rows = slice(t * tile, (t + 1) * tile)
        pseudo, start = fb[rows, :].astype(jnp.float32), 0
        for xt in xts:
            part = s[start : start + xt.shape[1], :]
            pseudo += jnp.dot(xt[rows, :], part, preferred_element_type=jnp.float32)
            start += xt.shape[1]
        held[rows, :] = jnp.where(keep[rows, :] > 0, pseudo, 0.0).astype(jnp.bfloat16)
        send_out(held, out, sems, t, tile).start()
    for t in range(tiles):
        send_out(held, out, sems, t, tile).wait()


def residue(slopes, order, xts, fb, keep):
    depth, kw = fb.shape
    total = sum(xt.shape[1] for xt in xts)
    tile = min(depth, 512)
    return pl.pallas_call(
        functools.partial(residue_kernel, order, tile),
        out_shape=[
            jax.ShapeDtypeStruct((depth, kw), jnp.bfloat16),
            TOKEN,
        ],
        in_specs=[VMEM] * (len(slopes) + len(xts) + 2),
        out_specs=[ANY, VMEM],
        scratch_shapes=[
            pltpu.VMEM((total, kw), jnp.bfloat16),
            pltpu.VMEM((depth, kw), jnp.bfloat16),
            pltpu.SemaphoreType.DMA((depth // tile,)),
        ],
        compiler_params=params(24),
        cost_estimate=BRIEF,
        name="residue",
    )(*slopes, *xts, fb, keep)


def join_kernel(*refs):
    out = refs[-1]
    rows = refs[0].shape[0]
    for k in range(len(refs) - 2):
        out[k * rows : (k + 1) * rows, :] = refs[k][...]


def join(messages, after):
    rows, lanes = messages[0].shape
    return pl.pallas_call(
        join_kernel,
        out_shape=jax.ShapeDtypeStruct((len(messages) * rows, lanes), jnp.bfloat16),
        in_specs=[VMEM] * len(messages) + [ANY],
        compiler_params=params(8),
        cost_estimate=BRIEF,
        name="join",
    )(*messages, after)


def outer_kernel(cap, per_row, tile, *refs):
    groups, (out, wide, lines, held, sems) = refs[:-5], refs[-5:]
    n = lines.shape[1] // cap
    size = cap + 16
    k = 0
    for group in groups:
        for start in range(0, group.shape[0], size):
            tail = group[start + cap : start + size, :].astype(jnp.float32)
            number = (tail[0:1, :] * LANES + tail[1:2, :]).astype(jnp.int32)
            lines[:, k * cap : (k + 1) * cap] = jnp.broadcast_to(number // per_row, (8, cap))
            column = jnp.broadcast_to((number % per_row).astype(jnp.float32), (LANES, cap)).T
            value = group[start : start + cap, :].astype(jnp.float32)
            for c in range(per_row):
                wide[k * cap : (k + 1) * cap, c * LANES : (c + 1) * LANES] = jnp.where(
                    column == c, value, 0.0
                ).astype(jnp.bfloat16)
            k += 1
    tiles = out.shape[0] // tile

    for t in range(tiles):
        rows = slice(t * tile, (t + 1) * tile)
        line = lax.broadcasted_iota(jnp.int32, (tile, n * cap), 0) + t * tile
        hot = (lines[0:1, :] == line).astype(jnp.float32).astype(jnp.bfloat16)
        held[rows, :] = jnp.dot(hot, wide[...], preferred_element_type=jnp.float32) / n
        send_out(held, out, sems, t, tile).start()
    for t in range(tiles):
        send_out(held, out, sems, t, tile).wait()


def outer(groups, cap, depth, kw):
    n = sum(group.shape[0] for group in groups) // (cap + 16)
    tile = min(depth, 512)
    return pl.pallas_call(
        functools.partial(outer_kernel, cap, kw // LANES, tile),
        out_shape=jax.ShapeDtypeStruct((depth, kw), jnp.float32),
        out_specs=ANY,
        scratch_shapes=[
            pltpu.VMEM((n * cap, kw), jnp.bfloat16),
            pltpu.VMEM((8, n * cap), jnp.int32),
            pltpu.VMEM((depth, kw), jnp.float32),
            pltpu.SemaphoreType.DMA((depth // tile,)),
        ],
        compiler_params=params(24),
        cost_estimate=BRIEF,
        name="outer",
    )(*groups)


def on_device(inputs, target, weights, feedback, counts, blocks):
    tokens, w, fb = inputs[0], weights[0], feedback[0]
    n_shard, n_rep = lax.axis_size("shard"), lax.axis_size("rep")
    tok_dev = tokens.shape[0]
    depth, kw = w.shape
    early_rows = tok_dev // 2
    spans = [(0, early_rows), (early_rows, tok_dev)]
    per_row = kw // LANES
    slot_row = blocks[0]
    slots = blocks.reshape(-1, 1)
    near = [d for d in range(1, n_shard) if d & (d - 1) == 0]
    far = [d for d in range(1, n_shard) if d & (d - 1) != 0]

    *far_out, token = cut(tokens, depth, [(d, 0, tok_dev) for d in far], [], 60)
    far_in = [swap(x, "shard", n_shard, d) for x, d in zip(far_out, far)]
    near_out = []
    for low, high in spans:
        *out, token = cut(tokens, depth, [(d, low, high - low) for d in near], [token])
        near_out.append(out)
        if low == 0:
            fbk, keep, token = early(slots, slot_row, counts, fb, token)
    near_in = [[swap(x, "shard", n_shard, d) for x, d in zip(out, near)] for out in near_out]
    own, _ = cut(tokens, depth, [(0, 0, tok_dev)], [token])

    brief, wide = jnp.bfloat16, jnp.float32
    (mine, *products), x_far = project([own] + far_in, [wide] + [brief] * len(far), w, [])
    whole = [swap(p, "shard", n_shard, d) for p, d in zip(products, far)]
    xg_far, xt_far, token = prepare([x_far], slots, counts, per_row, [])
    after, shares, x_near = [token], [], []
    for part in range(len(spans)):
        products, x = project(near_in[part], [brief] * len(near), w, after)
        shares.append([swap(p, "shard", n_shard, d) for p, d in zip(products, near)])
        x_near.append(x)
        after = products[-1:]
    xg_near, xt_near, token = prepare(x_near, slots, counts, per_row, [products[0]])
    shares = [share[k] for k in range(len(near)) for share in shares]
    slopes = slope(target[0], mine, whole, shares, spans, token)
    slopes = [slopes] + [swap(slopes, "shard", n_shard, d) for d in far + near]

    order = [(k, 0, tok_dev) for k in range(1 + len(far))]
    order += [(k, low, high) for low, high in spans for k in range(1 + len(far), n_shard)]
    message = kept(slopes, order, [xg_far, xg_near], fbk, slots, slot_row)
    same_core = [message] + [swap(message, "rep", n_rep, d) for d in range(2, n_rep, 2)]
    new_feedback, token = residue(slopes, order, [xt_far, xt_near], fb, keep)
    joined = join(same_core, token)
    groups = [joined, swap(joined, "rep", n_rep, 1)]
    return outer(groups, message.shape[0] - 16, depth, kw), new_feedback[None]


def solution(mesh):
    placed = (
        P("rep", "shard", None),
        P("rep", "shard", None),
        P("rep", "shard", None),
        P("rep", "shard", None),
        P("rep", "shard"),
        P("rep", "shard", None),
    )
    return jax.shard_map(
        on_device,
        mesh=mesh,
        in_specs=placed,
        out_specs=(P("shard", None), P("rep", "shard", None)),
        check_vma=False,
    )
```

```python
import functools

import jax
import jax.numpy as jnp
from jax import lax
from jax.experimental import pallas as pl
from jax.experimental.pallas import tpu as pltpu
from jax.sharding import PartitionSpec as P

LANES = 128
ANY = pl.BlockSpec(memory_space=pl.ANY)
BRIEF = pl.CostEstimate(flops=1000, bytes_accessed=1000, transcendentals=0)
VMEM = pl.BlockSpec(memory_space=pltpu.VMEM)
SMEM = pl.BlockSpec(memory_space=pltpu.SMEM)
MIB = 1024 * 1024
TOKEN = jax.ShapeDtypeStruct((8, LANES), jnp.float32)


def params(mib):
    return pltpu.CompilerParams(vmem_limit_bytes=mib * MIB)


def swap(x, axis, n, d):
    return lax.ppermute(x, axis, [(i, i ^ d) for i in range(n)])


def cut_kernel(cuts, tokens, *refs):
    outs, (token, sems) = refs[-len(cuts) - 2 : -2], refs[-2:]
    token[...] = jnp.zeros_like(token)
    me = lax.axis_index("shard")
    copies = []
    for k, (d, low, rows) in enumerate(cuts):
        depth = outs[k].shape[1]
        columns = pl.ds(pl.multiple_of((me ^ d) * depth, LANES), depth)
        copy = pltpu.make_async_copy(tokens.at[pl.ds(low, rows), columns], outs[k], sems.at[k])
        copy.start()
        copies.append(copy)
    for copy in copies:
        copy.wait()


def cut(tokens, depth, cuts, after, mib=16):
    return pl.pallas_call(
        functools.partial(cut_kernel, cuts),
        out_shape=[jax.ShapeDtypeStruct((rows, depth), tokens.dtype) for _, _, rows in cuts]
        + [TOKEN],
        in_specs=[ANY] * (1 + len(after)),
        out_specs=[ANY] * len(cuts) + [VMEM],
        scratch_shapes=[pltpu.SemaphoreType.DMA((len(cuts),))],
        compiler_params=params(mib),
        cost_estimate=BRIEF,
        name="cut",
    )(tokens, *after)


def project_kernel(n, *refs):
    pieces, w, outs, x = refs[:n], refs[n], refs[-n - 1 : -1], refs[-1]
    start = 0
    for piece in pieces:
        x[start : start + piece.shape[0], :] = piece[...]
        start += piece.shape[0]
    full = jnp.dot(x[...], w[...], preferred_element_type=jnp.float32)
    start = 0
    for out in outs:
        out[...] = full[start : start + out.shape[0], :].astype(out.dtype)
        start += out.shape[0]


def project(pieces, types, w, after):
    n = len(pieces)
    rows, depth = sum(p.shape[0] for p in pieces), pieces[0].shape[1]
    kw = w.shape[1]
    result = pl.pallas_call(
        functools.partial(project_kernel, n),
        out_shape=[jax.ShapeDtypeStruct((p.shape[0], kw), t) for p, t in zip(pieces, types)]
        + [jax.ShapeDtypeStruct((rows, depth), jnp.bfloat16)],
        in_specs=[VMEM] * (n + 1) + [ANY] * len(after),
        compiler_params=params(24),
        cost_estimate=BRIEF,
        name="project",
    )(*pieces, w, *after)
    return result[:n], result[n]


def slope_kernel(tok_dev, n, spans, *refs):
    goal, mine, out = refs[0], refs[1], refs[-1]
    whole = refs[2 : 2 + n]
    shares = refs[2 + n : -2]
    for part, (low, high) in enumerate(spans):
        key_proj = mine[low:high, :]
        for product in whole:
            key_proj += product[low:high, :].astype(jnp.float32)
        for product in shares[part :: len(spans)]:
            key_proj += product[...].astype(jnp.float32)
        gap = key_proj - goal[low:high, :].astype(jnp.float32)
        out[low:high, :] = (gap / tok_dev).astype(jnp.bfloat16)


def slope(goal, mine, whole, shares, spans, after):
    return pl.pallas_call(
        functools.partial(slope_kernel, goal.shape[0], len(whole), spans),
        out_shape=jax.ShapeDtypeStruct(mine.shape, jnp.bfloat16),
        in_specs=[VMEM] * (2 + len(whole) + len(shares)) + [ANY],
        compiler_params=params(8),
        cost_estimate=BRIEF,
        name="slope",
    )(goal, mine, *whole, *shares, after)


def pick_columns(wide, column):
    out = jnp.zeros((wide.shape[0], LANES), jnp.float32)
    for c in range(wide.shape[1] // LANES):
        out += jnp.where(column == c, wide[:, c * LANES : (c + 1) * LANES], 0.0)
    return out


def early_kernel(per_row, slots, slot_row, count, fb, after, fbk, keep, token):
    token[...] = jnp.zeros_like(token)
    depth, kw = fb.shape
    cap = slots.shape[0]
    slot = slots[...]
    hot = slot // per_row == lax.broadcasted_iota(jnp.int32, (cap, depth), 1)
    hot = hot.astype(jnp.float32).astype(jnp.bfloat16)
    used = lax.broadcasted_iota(jnp.int32, (cap, 1), 0) < count[0, 0]
    wide = jnp.dot(hot, fb[...], preferred_element_type=jnp.float32)
    fbk[...] = jnp.where(used, pick_columns(wide, slot % per_row), 0.0)
    group = lax.broadcasted_iota(jnp.int32, (cap, kw), 1) // LANES
    mark = jnp.where(used & (slot % per_row == group), 1.0, 0.0).astype(jnp.bfloat16)
    tile = min(depth, 512)
    for t in range(depth // tile):
        line = lax.broadcasted_iota(jnp.int32, (tile, cap), 0) + t * tile
        hot = (slot_row[...] // per_row == line).astype(jnp.float32).astype(jnp.bfloat16)
        mask = jnp.dot(hot, mark, preferred_element_type=jnp.float32)
        keep[t * tile : (t + 1) * tile, :] = (1.0 - mask).astype(jnp.bfloat16)


def early(slots, slot_row, count, fb, after):
    depth, kw = fb.shape
    cap = slots.shape[0]
    return pl.pallas_call(
        functools.partial(early_kernel, kw // LANES),
        out_shape=[
            jax.ShapeDtypeStruct((cap, LANES), jnp.float32),
            jax.ShapeDtypeStruct((depth, kw), jnp.bfloat16),
            TOKEN,
        ],
        in_specs=[VMEM, VMEM, SMEM, VMEM, ANY],
        compiler_params=params(24),
        cost_estimate=BRIEF,
        name="early",
    )(slots, slot_row, count, fb, after)


def prepare_kernel(per_row, n, *refs):
    xs, (slots, count), (xg, xt, token) = refs[:n], refs[n : n + 2], refs[-3:]
    token[...] = jnp.zeros_like(token)
    depth = xs[0].shape[1]
    cap = slots.shape[0]
    used = lax.broadcasted_iota(jnp.int32, (cap, 1), 0) < count[0, 0]
    line = jnp.where(used, slots[...] // per_row, depth)
    hot = line == lax.broadcasted_iota(jnp.int32, (cap, depth), 1)
    hot = hot.astype(jnp.float32).astype(jnp.bfloat16)
    start = 0
    for x in xs:
        rows = x.shape[0]
        xg[:, start : start + rows] = lax.dot_general(
            hot, x[...], (((1,), (1,)), ((), ())), preferred_element_type=jnp.float32
        ).astype(jnp.bfloat16)
        xt[:, start : start + rows] = x[...].T
        start += rows


def prepare(xs, slots, count, per_row, after):
    rows, depth = sum(x.shape[0] for x in xs), xs[0].shape[1]
    cap = slots.shape[0]
    return pl.pallas_call(
        functools.partial(prepare_kernel, per_row, len(xs)),
        out_shape=[
            jax.ShapeDtypeStruct((cap, rows), jnp.bfloat16),
            jax.ShapeDtypeStruct((depth, rows), jnp.bfloat16),
            TOKEN,
        ],
        in_specs=[VMEM] * (len(xs) + 1) + [SMEM] + [ANY] * len(after),
        compiler_params=params(24),
        cost_estimate=BRIEF,
        name="prepare",
    )(*xs, slots, count, *after)


def stack(slopes, order, s):
    start = 0
    for k, low, high in order:
        s[start : start + high - low, :] = slopes[k][low:high, :]
        start += high - low


def kept_kernel(per_row, order, *refs):
    n = len({k for k, _, _ in order})
    slopes, (fbk, slots, slot_row), out, s = refs[:n], refs[-5:-2], refs[-2], refs[-1]
    xgs = refs[n:-5]
    cap = slots.shape[0]
    stack(slopes, order, s)
    wide, start = 0.0, 0
    for xg in xgs:
        rows = xg.shape[1]
        wide += jnp.dot(xg[...], s[start : start + rows, :], preferred_element_type=jnp.float32)
        start += rows
    value = pick_columns(wide, slots[...] % per_row) + fbk[...]
    out[:cap, :] = value.astype(jnp.bfloat16)
    tail = out.shape[0] - cap
    number = jnp.broadcast_to(slot_row[...], (tail, cap))
    line = lax.broadcasted_iota(jnp.int32, (tail, cap), 0)
    number = jnp.where(line == 0, number // LANES, number % LANES)
    out[cap:, :] = number.astype(jnp.float32).astype(jnp.bfloat16)


def kept(slopes, order, xgs, fbk, slots, slot_row):
    cap = slots.shape[0]
    rows, kw = slopes[0].shape
    total = len(slopes) * rows
    return pl.pallas_call(
        functools.partial(kept_kernel, kw // LANES, order),
        out_shape=jax.ShapeDtypeStruct((cap + 16, LANES), jnp.bfloat16),
        scratch_shapes=[pltpu.VMEM((total, kw), jnp.bfloat16)],
        compiler_params=params(8),
        cost_estimate=BRIEF,
        name="kept",
    )(*slopes, *xgs, fbk, slots, slot_row)


def send_out(held, out, sems, t, tile):
    rows = pl.ds(t * tile, tile)
    return pltpu.make_async_copy(held.at[rows, :], out.at[rows, :], sems.at[t])


def residue_kernel(order, tile, *refs):
    n = len({k for k, _, _ in order})
    slopes, xts, (fb, keep, out, token, s, held, sems) = refs[:n], refs[n:-7], refs[-7:]
    token[...] = jnp.zeros_like(token)
    stack(slopes, order, s)
    tiles = out.shape[0] // tile
    for t in range(tiles):
        rows = slice(t * tile, (t + 1) * tile)
        pseudo, start = fb[rows, :].astype(jnp.float32), 0
        for xt in xts:
            part = s[start : start + xt.shape[1], :]
            pseudo += jnp.dot(xt[rows, :], part, preferred_element_type=jnp.float32)
            start += xt.shape[1]
        held[rows, :] = jnp.where(keep[rows, :] > 0, pseudo, 0.0).astype(jnp.bfloat16)
        send_out(held, out, sems, t, tile).start()
    for t in range(tiles):
        send_out(held, out, sems, t, tile).wait()


def residue(slopes, order, xts, fb, keep):
    depth, kw = fb.shape
    total = sum(xt.shape[1] for xt in xts)
    tile = min(depth, 512)
    return pl.pallas_call(
        functools.partial(residue_kernel, order, tile),
        out_shape=[
            jax.ShapeDtypeStruct((depth, kw), jnp.bfloat16),
            TOKEN,
        ],
        in_specs=[VMEM] * (len(slopes) + len(xts) + 2),
        out_specs=[ANY, VMEM],
        scratch_shapes=[
            pltpu.VMEM((total, kw), jnp.bfloat16),
            pltpu.VMEM((depth, kw), jnp.bfloat16),
            pltpu.SemaphoreType.DMA((depth // tile,)),
        ],
        compiler_params=params(24),
        cost_estimate=BRIEF,
        name="residue",
    )(*slopes, *xts, fb, keep)


def join_kernel(*refs):
    out = refs[-1]
    rows = refs[0].shape[0]
    for k in range(len(refs) - 2):
        out[k * rows : (k + 1) * rows, :] = refs[k][...]


def join(messages, after):
    rows, lanes = messages[0].shape
    return pl.pallas_call(
        join_kernel,
        out_shape=jax.ShapeDtypeStruct((len(messages) * rows, lanes), jnp.bfloat16),
        in_specs=[VMEM] * len(messages) + [ANY],
        compiler_params=params(8),
        cost_estimate=BRIEF,
        name="join",
    )(*messages, after)


def spread(group, wide, lines, cap, per_row):
    size = cap + 16
    for k in range(group.shape[0] // size):
        start = k * size
        tail = group[start + cap : start + size, :].astype(jnp.float32)
        number = (tail[0:1, :] * LANES + tail[1:2, :]).astype(jnp.int32)
        lines[:, k * cap : (k + 1) * cap] = jnp.broadcast_to(number // per_row, (8, cap))
        column = jnp.broadcast_to((number % per_row).astype(jnp.float32), (LANES, cap)).T
        value = group[start : start + cap, :].astype(jnp.float32)
        for c in range(per_row):
            wide[k * cap : (k + 1) * cap, c * LANES : (c + 1) * LANES] = jnp.where(
                column == c, value, 0.0
            ).astype(jnp.bfloat16)


def place(lines, wide, t, tile):
    line = lax.broadcasted_iota(jnp.int32, (tile, lines.shape[1]), 0) + t * tile
    hot = (lines[0:1, :] == line).astype(jnp.float32).astype(jnp.bfloat16)
    return jnp.dot(hot, wide[...], preferred_element_type=jnp.float32)


def half_kernel(cap, per_row, tile, group, out, wide, lines):
    spread(group, wide, lines, cap, per_row)
    for t in range(out.shape[0] // tile):
        out[t * tile : (t + 1) * tile, :] = place(lines, wide, t, tile)


def outer_kernel(cap, per_row, tile, n, group, half, out, wide, lines, held, sems):
    spread(group, wide, lines, cap, per_row)
    tiles = out.shape[0] // tile
    for t in range(tiles):
        rows = slice(t * tile, (t + 1) * tile)
        held[rows, :] = (half[rows, :] + place(lines, wide, t, tile)) / n
        send_out(held, out, sems, t, tile).start()
    for t in range(tiles):
        send_out(held, out, sems, t, tile).wait()


def outer(groups, cap, depth, kw):
    slots = groups[0].shape[0] // (cap + 16) * cap
    n = 2 * slots // cap
    tile = min(depth, 512)
    shape = jax.ShapeDtypeStruct((depth, kw), jnp.float32)
    scratch = [pltpu.VMEM((slots, kw), jnp.bfloat16), pltpu.VMEM((8, slots), jnp.int32)]
    half = pl.pallas_call(
        functools.partial(half_kernel, cap, kw // LANES, tile),
        out_shape=shape,
        scratch_shapes=scratch,
        compiler_params=params(24),
        cost_estimate=BRIEF,
        name="half",
    )(groups[0])
    return pl.pallas_call(
        functools.partial(outer_kernel, cap, kw // LANES, tile, n),
        out_shape=shape,
        out_specs=ANY,
        scratch_shapes=scratch
        + [pltpu.VMEM((depth, kw), jnp.float32), pltpu.SemaphoreType.DMA((depth // tile,))],
        compiler_params=params(24),
        cost_estimate=BRIEF,
        name="outer",
    )(groups[1], half)


def on_device(inputs, target, weights, feedback, counts, blocks):
    tokens, w, fb = inputs[0], weights[0], feedback[0]
    n_shard, n_rep = lax.axis_size("shard"), lax.axis_size("rep")
    tok_dev = tokens.shape[0]
    depth, kw = w.shape
    early_rows = tok_dev * 3 // 4
    spans = [(0, early_rows), (early_rows, tok_dev)]
    per_row = kw // LANES
    slot_row = blocks[0]
    slots = blocks.reshape(-1, 1)
    near = [d for d in range(1, n_shard) if d & (d - 1) == 0]
    far = [d for d in range(1, n_shard) if d & (d - 1) != 0]

    *far_out, token = cut(tokens, depth, [(d, 0, tok_dev) for d in far], [], 60)
    far_in = [swap(x, "shard", n_shard, d) for x, d in zip(far_out, far)]
    near_out = []
    for low, high in spans:
        *out, token = cut(tokens, depth, [(d, low, high - low) for d in near], [token])
        near_out.append(out)
        if low == 0:
            fbk, keep, token = early(slots, slot_row, counts, fb, token)
    near_in = [[swap(x, "shard", n_shard, d) for x, d in zip(out, near)] for out in near_out]

    own, _ = cut(tokens, depth, [(0, 0, tok_dev)], [token])

    brief, wide = jnp.bfloat16, jnp.float32
    (mine, *products), x_far = project([own] + far_in, [wide] + [brief] * len(far), w, [])
    whole = [swap(p, "shard", n_shard, d) for p, d in zip(products, far)]
    xg_far, xt_far, token = prepare([x_far], slots, counts, per_row, [])
    after, shares, x_near = [token], [], []
    for part in range(len(spans)):
        products, x = project(near_in[part], [brief] * len(near), w, after)
        shares.append([swap(p, "shard", n_shard, d) for p, d in zip(products, near)])
        x_near.append(x)
        after = products[-1:]
    xg_near, xt_near, token = prepare(x_near, slots, counts, per_row, [products[0]])
    shares = [share[k] for k in range(len(near)) for share in shares]
    slopes = slope(target[0], mine, whole, shares, spans, token)
    slopes = [slopes] + [swap(slopes, "shard", n_shard, d) for d in far + near]

    order = [(k, 0, tok_dev) for k in range(1 + len(far))]
    order += [(k, low, high) for low, high in spans for k in range(1 + len(far), n_shard)]
    message = kept(slopes, order, [xg_far, xg_near], fbk, slots, slot_row)
    same_core = [message] + [swap(message, "rep", n_rep, d) for d in range(n_rep - 2, 0, -2)]
    new_feedback, token = residue(slopes, order, [xt_far, xt_near], fb, keep)
    joined = join(same_core, token)
    groups = [joined, swap(joined, "rep", n_rep, 1)]
    return outer(groups, message.shape[0] - 16, depth, kw), new_feedback[None]


def solution(mesh):
    placed = (
        P("rep", "shard", None),
        P("rep", "shard", None),
        P("rep", "shard", None),
        P("rep", "shard", None),
        P("rep", "shard"),
        P("rep", "shard", None),
    )
    return jax.shard_map(
        on_device,
        mesh=mesh,
        in_specs=placed,
        out_specs=(P("shard", None), P("rep", "shard", None)),
        check_vma=False,
    )
```

```python
import functools

import jax
import jax.numpy as jnp
from jax import lax
from jax.experimental import pallas as pl
from jax.experimental.pallas import tpu as pltpu
from jax.sharding import PartitionSpec as P

LANES = 128
ANY = pl.BlockSpec(memory_space=pl.ANY)
BRIEF = pl.CostEstimate(flops=1000, bytes_accessed=1000, transcendentals=0)
VMEM = pl.BlockSpec(memory_space=pltpu.VMEM)
SMEM = pl.BlockSpec(memory_space=pltpu.SMEM)
MIB = 1024 * 1024
TOKEN = jax.ShapeDtypeStruct((8, LANES), jnp.float32)


def params(mib):
    return pltpu.CompilerParams(vmem_limit_bytes=mib * MIB)


def swap(x, axis, n, d):
    return lax.ppermute(x, axis, [(i, i ^ d) for i in range(n)])


def cut_kernel(cuts, tokens, *refs):
    outs, (token, sems) = refs[-len(cuts) - 2 : -2], refs[-2:]
    token[...] = jnp.zeros_like(token)
    me = lax.axis_index("shard")
    copies = []
    for k, (d, low, rows) in enumerate(cuts):
        depth = outs[k].shape[1]
        columns = pl.ds(pl.multiple_of((me ^ d) * depth, LANES), depth)
        copy = pltpu.make_async_copy(tokens.at[pl.ds(low, rows), columns], outs[k], sems.at[k])
        copy.start()
        copies.append(copy)
    for copy in copies:
        copy.wait()


def cut(tokens, depth, cuts, after):
    return pl.pallas_call(
        functools.partial(cut_kernel, cuts),
        out_shape=[jax.ShapeDtypeStruct((rows, depth), tokens.dtype) for _, _, rows in cuts]
        + [TOKEN],
        in_specs=[ANY] * (1 + len(after)),
        out_specs=[ANY] * len(cuts) + [VMEM],
        scratch_shapes=[pltpu.SemaphoreType.DMA((len(cuts),))],
        compiler_params=params(16),
        cost_estimate=BRIEF,
        name="cut",
    )(tokens, *after)


def project_kernel(n, *refs):
    pieces, w, outs, x = refs[:n], refs[n], refs[-n - 1 : -1], refs[-1]
    start = 0
    for piece in pieces:
        x[start : start + piece.shape[0], :] = piece[...]
        start += piece.shape[0]
    full = jnp.dot(x[...], w[...], preferred_element_type=jnp.float32)
    start = 0
    for out in outs:
        out[...] = full[start : start + out.shape[0], :].astype(out.dtype)
        start += out.shape[0]


def project(pieces, types, w, after):
    n = len(pieces)
    rows, depth = sum(p.shape[0] for p in pieces), pieces[0].shape[1]
    kw = w.shape[1]
    result = pl.pallas_call(
        functools.partial(project_kernel, n),
        out_shape=[jax.ShapeDtypeStruct((p.shape[0], kw), t) for p, t in zip(pieces, types)]
        + [jax.ShapeDtypeStruct((rows, depth), jnp.bfloat16)],
        in_specs=[VMEM] * (n + 1) + [ANY] * len(after),
        compiler_params=params(24),
        cost_estimate=BRIEF,
        name="project",
    )(*pieces, w, *after)
    return result[:n], result[n]


def slope_kernel(tok_dev, n, spans, *refs):
    goal, mine, out = refs[0], refs[1], refs[-1]
    whole = refs[2 : 2 + n]
    shares = refs[2 + n : -2]
    for part, (low, high) in enumerate(spans):
        key_proj = mine[low:high, :]
        for product in whole:
            key_proj += product[low:high, :].astype(jnp.float32)
        for product in shares[part :: len(spans)]:
            key_proj += product[...].astype(jnp.float32)
        gap = key_proj - goal[low:high, :].astype(jnp.float32)
        out[low:high, :] = (gap / tok_dev).astype(jnp.bfloat16)


def slope(goal, mine, whole, shares, spans, after):
    return pl.pallas_call(
        functools.partial(slope_kernel, goal.shape[0], len(whole), spans),
        out_shape=jax.ShapeDtypeStruct(mine.shape, jnp.bfloat16),
        in_specs=[VMEM] * (2 + len(whole) + len(shares)) + [ANY],
        compiler_params=params(8),
        cost_estimate=BRIEF,
        name="slope",
    )(goal, mine, *whole, *shares, after)


def pick_columns(wide, column):
    out = jnp.zeros((wide.shape[0], LANES), jnp.float32)
    for c in range(wide.shape[1] // LANES):
        out += jnp.where(column == c, wide[:, c * LANES : (c + 1) * LANES], 0.0)
    return out


def early_kernel(per_row, slots, slot_row, count, fb, after, fbk, keep, token):
    token[...] = jnp.zeros_like(token)
    depth, kw = fb.shape
    cap = slots.shape[0]
    slot = slots[...]
    hot = slot // per_row == lax.broadcasted_iota(jnp.int32, (cap, depth), 1)
    hot = hot.astype(jnp.float32).astype(jnp.bfloat16)
    used = lax.broadcasted_iota(jnp.int32, (cap, 1), 0) < count[0, 0]
    wide = jnp.dot(hot, fb[...], preferred_element_type=jnp.float32)
    fbk[...] = jnp.where(used, pick_columns(wide, slot % per_row), 0.0)
    group = lax.broadcasted_iota(jnp.int32, (cap, kw), 1) // LANES
    mark = jnp.where(used & (slot % per_row == group), 1.0, 0.0).astype(jnp.bfloat16)
    tile = min(depth, 512)
    for t in range(depth // tile):
        line = lax.broadcasted_iota(jnp.int32, (tile, cap), 0) + t * tile
        hot = (slot_row[...] // per_row == line).astype(jnp.float32).astype(jnp.bfloat16)
        mask = jnp.dot(hot, mark, preferred_element_type=jnp.float32)
        keep[t * tile : (t + 1) * tile, :] = (1.0 - mask).astype(jnp.bfloat16)


def early(slots, slot_row, count, fb, after):
    depth, kw = fb.shape
    cap = slots.shape[0]
    return pl.pallas_call(
        functools.partial(early_kernel, kw // LANES),
        out_shape=[
            jax.ShapeDtypeStruct((cap, LANES), jnp.float32),
            jax.ShapeDtypeStruct((depth, kw), jnp.bfloat16),
            TOKEN,
        ],
        in_specs=[VMEM, VMEM, SMEM, VMEM, ANY],
        compiler_params=params(24),
        cost_estimate=BRIEF,
        name="early",
    )(slots, slot_row, count, fb, after)


def prepare_kernel(per_row, n, *refs):
    xs, (slots, count), (xg, xt, token) = refs[:n], refs[n : n + 2], refs[-3:]
    token[...] = jnp.zeros_like(token)
    depth = xs[0].shape[1]
    cap = slots.shape[0]
    used = lax.broadcasted_iota(jnp.int32, (cap, 1), 0) < count[0, 0]
    line = jnp.where(used, slots[...] // per_row, depth)
    hot = line == lax.broadcasted_iota(jnp.int32, (cap, depth), 1)
    hot = hot.astype(jnp.float32).astype(jnp.bfloat16)
    start = 0
    for x in xs:
        rows = x.shape[0]
        xg[:, start : start + rows] = lax.dot_general(
            hot, x[...], (((1,), (1,)), ((), ())), preferred_element_type=jnp.float32
        ).astype(jnp.bfloat16)
        xt[:, start : start + rows] = x[...].T
        start += rows


def prepare(xs, slots, count, per_row, after):
    rows, depth = sum(x.shape[0] for x in xs), xs[0].shape[1]
    cap = slots.shape[0]
    return pl.pallas_call(
        functools.partial(prepare_kernel, per_row, len(xs)),
        out_shape=[
            jax.ShapeDtypeStruct((cap, rows), jnp.bfloat16),
            jax.ShapeDtypeStruct((depth, rows), jnp.bfloat16),
            TOKEN,
        ],
        in_specs=[VMEM] * (len(xs) + 1) + [SMEM] + [ANY] * len(after),
        compiler_params=params(24),
        cost_estimate=BRIEF,
        name="prepare",
    )(*xs, slots, count, *after)


def stack(slopes, order, s):
    start = 0
    for k, low, high in order:
        s[start : start + high - low, :] = slopes[k][low:high, :]
        start += high - low


def gather_kernel(order, *refs):
    slopes, (xg, out, s) = refs[:-3], refs[-3:]
    stack(slopes, order, s)
    out[...] = jnp.dot(xg[...], s[...], preferred_element_type=jnp.float32)


def gather(slopes, order, xg):
    kw = slopes[0].shape[1]
    return pl.pallas_call(
        functools.partial(gather_kernel, order),
        out_shape=jax.ShapeDtypeStruct((xg.shape[0], kw), jnp.float32),
        scratch_shapes=[pltpu.VMEM((xg.shape[1], kw), jnp.bfloat16)],
        compiler_params=params(8),
        cost_estimate=BRIEF,
        name="gather",
    )(*slopes, xg)


def kept_kernel(per_row, order, *refs):
    slopes, (wide, xg, fbk, slots, slot_row, out, s) = refs[:-7], refs[-7:]
    cap = slots.shape[0]
    stack(slopes, order, s)
    total = wide[...] + jnp.dot(xg[...], s[...], preferred_element_type=jnp.float32)
    value = pick_columns(total, slots[...] % per_row) + fbk[...]
    out[:cap, :] = value.astype(jnp.bfloat16)
    tail = out.shape[0] - cap
    number = jnp.broadcast_to(slot_row[...], (tail, cap))
    line = lax.broadcasted_iota(jnp.int32, (tail, cap), 0)
    number = jnp.where(line == 0, number // LANES, number % LANES)
    out[cap:, :] = number.astype(jnp.float32).astype(jnp.bfloat16)


def kept(slopes, order, wide, xg, fbk, slots, slot_row):
    cap, kw = wide.shape
    return pl.pallas_call(
        functools.partial(kept_kernel, kw // LANES, order),
        out_shape=jax.ShapeDtypeStruct((cap + 16, LANES), jnp.bfloat16),
        scratch_shapes=[pltpu.VMEM((xg.shape[1], kw), jnp.bfloat16)],
        compiler_params=params(8),
        cost_estimate=BRIEF,
        name="kept",
    )(*slopes, wide, xg, fbk, slots, slot_row)


def send_out(held, out, sems, t, tile):
    rows = pl.ds(t * tile, tile)
    return pltpu.make_async_copy(held.at[rows, :], out.at[rows, :], sems.at[t])


def residue_kernel(order, tile, *refs):
    n = len({k for k, _, _ in order})
    slopes, xts, (fb, keep, out, token, s, held, sems) = refs[:n], refs[n:-7], refs[-7:]
    token[...] = jnp.zeros_like(token)
    stack(slopes, order, s)
    tiles = out.shape[0] // tile
    for t in range(tiles):
        rows = slice(t * tile, (t + 1) * tile)
        pseudo, start = fb[rows, :].astype(jnp.float32), 0
        for xt in xts:
            part = s[start : start + xt.shape[1], :]
            pseudo += jnp.dot(xt[rows, :], part, preferred_element_type=jnp.float32)
            start += xt.shape[1]
        held[rows, :] = jnp.where(keep[rows, :] > 0, pseudo, 0.0).astype(jnp.bfloat16)
        send_out(held, out, sems, t, tile).start()
    for t in range(tiles):
        send_out(held, out, sems, t, tile).wait()


def residue(slopes, order, xts, fb, keep):
    depth, kw = fb.shape
    total = sum(xt.shape[1] for xt in xts)
    tile = min(depth, 512)
    return pl.pallas_call(
        functools.partial(residue_kernel, order, tile),
        out_shape=[
            jax.ShapeDtypeStruct((depth, kw), jnp.bfloat16),
            TOKEN,
        ],
        in_specs=[VMEM] * (len(slopes) + len(xts) + 2),
        out_specs=[ANY, VMEM],
        scratch_shapes=[
            pltpu.VMEM((total, kw), jnp.bfloat16),
            pltpu.VMEM((depth, kw), jnp.bfloat16),
            pltpu.SemaphoreType.DMA((depth // tile,)),
        ],
        compiler_params=params(24),
        cost_estimate=BRIEF,
        name="residue",
    )(*slopes, *xts, fb, keep)


def join_kernel(n, *refs):
    out, start = refs[-1], 0
    for part in refs[:n]:
        out[start : start + part.shape[0], :] = part[...]
        start += part.shape[0]


def join(parts, after):
    rows, lanes = sum(part.shape[0] for part in parts), parts[0].shape[1]
    return pl.pallas_call(
        functools.partial(join_kernel, len(parts)),
        out_shape=jax.ShapeDtypeStruct((rows, lanes), jnp.bfloat16),
        in_specs=[VMEM] * len(parts) + [ANY] * len(after),
        compiler_params=params(8),
        cost_estimate=BRIEF,
        name="join",
    )(*parts, *after)


def spread(group, wide, lines, cap, per_row):
    size = cap + 16
    for k in range(group.shape[0] // size):
        start = k * size
        tail = group[start + cap : start + size, :].astype(jnp.float32)
        number = (tail[0:1, :] * LANES + tail[1:2, :]).astype(jnp.int32)
        lines[:, k * cap : (k + 1) * cap] = jnp.broadcast_to(number // per_row, (8, cap))
        column = jnp.broadcast_to((number % per_row).astype(jnp.float32), (LANES, cap)).T
        value = group[start : start + cap, :].astype(jnp.float32)
        for c in range(per_row):
            wide[k * cap : (k + 1) * cap, c * LANES : (c + 1) * LANES] = jnp.where(
                column == c, value, 0.0
            ).astype(jnp.bfloat16)


def place(lines, wide, t, tile):
    line = lax.broadcasted_iota(jnp.int32, (tile, lines.shape[1]), 0) + t * tile
    hot = (lines[0:1, :] == line).astype(jnp.float32).astype(jnp.bfloat16)
    return jnp.dot(hot, wide[...], preferred_element_type=jnp.float32)


def half_kernel(cap, per_row, tile, group, out, wide, lines):
    spread(group, wide, lines, cap, per_row)
    for t in range(out.shape[0] // tile):
        out[t * tile : (t + 1) * tile, :] = place(lines, wide, t, tile)


def outer_kernel(cap, per_row, tile, n, group, half, out, wide, lines, held, sems):
    spread(group, wide, lines, cap, per_row)
    tiles = out.shape[0] // tile
    for t in range(tiles):
        rows = slice(t * tile, (t + 1) * tile)
        held[rows, :] = (half[rows, :] + place(lines, wide, t, tile)) / n
        send_out(held, out, sems, t, tile).start()
    for t in range(tiles):
        send_out(held, out, sems, t, tile).wait()


def outer(groups, cap, depth, kw):
    slots = groups[0].shape[0] // (cap + 16) * cap
    n = 2 * slots // cap
    tile = min(depth, 512)
    shape = jax.ShapeDtypeStruct((depth, kw), jnp.float32)
    scratch = [pltpu.VMEM((slots, kw), jnp.bfloat16), pltpu.VMEM((8, slots), jnp.int32)]
    half = pl.pallas_call(
        functools.partial(half_kernel, cap, kw // LANES, tile),
        out_shape=shape,
        scratch_shapes=scratch,
        compiler_params=params(24),
        cost_estimate=BRIEF,
        name="half",
    )(groups[0])
    return pl.pallas_call(
        functools.partial(outer_kernel, cap, kw // LANES, tile, n),
        out_shape=shape,
        out_specs=ANY,
        scratch_shapes=scratch
        + [pltpu.VMEM((depth, kw), jnp.float32), pltpu.SemaphoreType.DMA((depth // tile,))],
        compiler_params=params(24),
        cost_estimate=BRIEF,
        name="outer",
    )(groups[1], half)


def on_device(inputs, target, weights, feedback, counts, blocks):
    tokens, w, fb = inputs[0], weights[0], feedback[0]
    n_shard, n_rep = lax.axis_size("shard"), lax.axis_size("rep")
    tok_dev = tokens.shape[0]
    depth, kw = w.shape
    early_rows = tok_dev * 3 // 4
    spans = [(0, early_rows), (early_rows, tok_dev)]
    per_row = kw // LANES
    slot_row = blocks[0]
    slots = blocks.reshape(-1, 1)
    near = [d for d in range(1, n_shard) if d & (d - 1) == 0]
    far = [d for d in range(1, n_shard) if d & (d - 1) != 0]

    me = lax.axis_index("shard")
    far_out = [lax.dynamic_slice(tokens, (0, (me ^ d) * depth), (tok_dev, depth)) for d in far]
    far_in = [swap(x, "shard", n_shard, d) for x, d in zip(far_out, far)]
    near_out, token = [], far_out[0]
    for low, high in spans:
        *out, token = cut(tokens, depth, [(d, low, high - low) for d in near], [token])
        near_out.append(out)
        if low == 0:
            fbk, keep, token = early(slots, slot_row, counts, fb, token)
    near_in = [[swap(x, "shard", n_shard, d) for x, d in zip(out, near)] for out in near_out]

    own, _ = cut(tokens, depth, [(0, 0, tok_dev)], [token])

    brief, wide = jnp.bfloat16, jnp.float32
    (mine, *products), x_far = project([own] + far_in, [wide] + [brief] * len(far), w, [])
    whole = [swap(p, "shard", n_shard, d) for p, d in zip(products, far)]
    xg_far, xt_far, token = prepare([x_far], slots, counts, per_row, [])
    after, shares, x_near = [token], [], []
    for part in range(len(spans)):
        products, x = project(near_in[part], [brief] * len(near), w, after)
        shares.append([swap(p, "shard", n_shard, d) for p, d in zip(products, near)])
        x_near.append(x)
        after = products[-1:]
    xg_near, xt_near, token = prepare(x_near, slots, counts, per_row, [products[0]])
    shares = [share[k] for k in range(len(near)) for share in shares]
    slopes = slope(target[0], mine, whole, shares, spans, token)
    slopes = [slopes] + [swap(slopes, "shard", n_shard, d) for d in far + near]

    n_far = 1 + len(far)
    order_far = [(k, 0, tok_dev) for k in range(n_far)]
    order_near = [(k, low, high) for low, high in spans for k in range(len(near))]
    wide = gather(slopes[:n_far], order_far, xg_far)
    message = kept(slopes[n_far:], order_near, wide, xg_near, fbk, slots, slot_row)
    same_core = [swap(message, "rep", n_rep, d) for d in range(n_rep - 2, 0, -2)]
    order = order_far + [(n_far + k, low, high) for k, low, high in order_near]
    new_feedback, token = residue(slopes, order, [xt_far, xt_near], fb, keep)
    joined, after = message, [token]
    for received in same_core:
        joined, after = join([joined, received], after), []
    groups = [joined, swap(joined, "rep", n_rep, 1)]
    return outer(groups, message.shape[0] - 16, depth, kw), new_feedback[None]


def solution(mesh):
    placed = (
        P("rep", "shard", None),
        P("rep", "shard", None),
        P("rep", "shard", None),
        P("rep", "shard", None),
        P("rep", "shard"),
        P("rep", "shard", None),
    )
    return jax.shard_map(
        on_device,
        mesh=mesh,
        in_specs=placed,
        out_specs=(P("shard", None), P("rep", "shard", None)),
        check_vma=False,
    )
```

```python
import functools

import jax
import jax.numpy as jnp
from jax import lax
from jax.experimental import pallas as pl
from jax.experimental.pallas import tpu as pltpu
from jax.sharding import PartitionSpec as P

LANES = 128
ANY = pl.BlockSpec(memory_space=pl.ANY)
BRIEF = pl.CostEstimate(flops=1000, bytes_accessed=1000, transcendentals=0)
VMEM = pl.BlockSpec(memory_space=pltpu.VMEM)
SMEM = pl.BlockSpec(memory_space=pltpu.SMEM)
MIB = 1024 * 1024
TOKEN = jax.ShapeDtypeStruct((8, LANES), jnp.float32)


def params(mib):
    return pltpu.CompilerParams(vmem_limit_bytes=mib * MIB)


def swap(x, axis, n, d):
    return lax.ppermute(x, axis, [(i, i ^ d) for i in range(n)])


def cut_kernel(cuts, tokens, *refs):
    outs, (token, sems) = refs[-len(cuts) - 2 : -2], refs[-2:]
    token[...] = jnp.zeros_like(token)
    me = lax.axis_index("shard")
    copies = []
    for k, (d, low, rows) in enumerate(cuts):
        depth = outs[k].shape[1]
        columns = pl.ds(pl.multiple_of((me ^ d) * depth, LANES), depth)
        copy = pltpu.make_async_copy(tokens.at[pl.ds(low, rows), columns], outs[k], sems.at[k])
        copy.start()
        copies.append(copy)
    for copy in copies:
        copy.wait()


def cut(tokens, depth, cuts, after):
    return pl.pallas_call(
        functools.partial(cut_kernel, cuts),
        out_shape=[jax.ShapeDtypeStruct((rows, depth), tokens.dtype) for _, _, rows in cuts]
        + [TOKEN],
        in_specs=[ANY] * (1 + len(after)),
        out_specs=[ANY] * len(cuts) + [VMEM],
        scratch_shapes=[pltpu.SemaphoreType.DMA((len(cuts),))],
        compiler_params=params(6),
        cost_estimate=BRIEF,
        name="cut",
    )(tokens, *after)


def project_kernel(n, *refs):
    pieces, w, outs, x = refs[:n], refs[n], refs[-n - 1 : -1], refs[-1]
    start = 0
    for piece in pieces:
        x[start : start + piece.shape[0], :] = piece[...]
        start += piece.shape[0]
    full = jnp.dot(x[...], w[...], preferred_element_type=jnp.float32)
    start = 0
    for out in outs:
        out[...] = full[start : start + out.shape[0], :].astype(out.dtype)
        start += out.shape[0]


def project(pieces, types, w, after):
    n = len(pieces)
    rows, depth = sum(p.shape[0] for p in pieces), pieces[0].shape[1]
    kw = w.shape[1]
    result = pl.pallas_call(
        functools.partial(project_kernel, n),
        out_shape=[jax.ShapeDtypeStruct((p.shape[0], kw), t) for p, t in zip(pieces, types)]
        + [jax.ShapeDtypeStruct((rows, depth), jnp.bfloat16)],
        in_specs=[VMEM] * (n + 1) + [ANY] * len(after),
        compiler_params=params(14),
        cost_estimate=BRIEF,
        name="project",
    )(*pieces, w, *after)
    return result[:n], result[n]


def slope_kernel(tok_dev, n, spans, *refs):
    goal, mine, out = refs[0], refs[1], refs[-1]
    whole = refs[2 : 2 + n]
    shares = refs[2 + n : -2]
    for part, (low, high) in enumerate(spans):
        key_proj = mine[low:high, :]
        for product in whole:
            key_proj += product[low:high, :].astype(jnp.float32)
        for product in shares[part :: len(spans)]:
            key_proj += product[...].astype(jnp.float32)
        gap = key_proj - goal[low:high, :].astype(jnp.float32)
        out[low:high, :] = (gap / tok_dev).astype(jnp.bfloat16)


def slope(goal, mine, whole, shares, spans, after):
    return pl.pallas_call(
        functools.partial(slope_kernel, goal.shape[0], len(whole), spans),
        out_shape=jax.ShapeDtypeStruct(mine.shape, jnp.bfloat16),
        in_specs=[VMEM] * (2 + len(whole) + len(shares)) + [ANY],
        compiler_params=params(8),
        cost_estimate=BRIEF,
        name="slope",
    )(goal, mine, *whole, *shares, after)


def as_column(row):
    size = row.shape[1]
    return jnp.broadcast_to(row.astype(jnp.float32), (size, size)).T.astype(jnp.int32)


def pick_columns(wide, column):
    out = jnp.zeros((wide.shape[0], LANES), jnp.float32)
    for c in range(wide.shape[1] // LANES):
        out += jnp.where(column == c, wide[:, c * LANES : (c + 1) * LANES], 0.0)
    return out


def early_kernel(per_row, slot_row, count, fb, after, fbk, keep, token):
    token[...] = jnp.zeros_like(token)
    depth, kw = fb.shape
    cap = slot_row.shape[1]
    slot = as_column(slot_row[...])[:, 0:1]
    hot = slot // per_row == lax.broadcasted_iota(jnp.int32, (cap, depth), 1)
    hot = hot.astype(jnp.float32).astype(jnp.bfloat16)
    used = lax.broadcasted_iota(jnp.int32, (cap, 1), 0) < count[0, 0]
    wide = jnp.dot(hot, fb[...], preferred_element_type=jnp.float32)
    fbk[...] = jnp.where(used, pick_columns(wide, slot % per_row), 0.0)
    group = lax.broadcasted_iota(jnp.int32, (cap, kw), 1) // LANES
    mark = jnp.where(used & (slot % per_row == group), 1.0, 0.0).astype(jnp.bfloat16)
    tile = min(depth, 512)
    for t in range(depth // tile):
        line = lax.broadcasted_iota(jnp.int32, (tile, cap), 0) + t * tile
        hot = (slot_row[...] // per_row == line).astype(jnp.float32).astype(jnp.bfloat16)
        mask = jnp.dot(hot, mark, preferred_element_type=jnp.float32)
        keep[t * tile : (t + 1) * tile, :] = (1.0 - mask).astype(jnp.bfloat16)


def early(slot_row, count, fb, after):
    depth, kw = fb.shape
    cap = slot_row.shape[1]
    return pl.pallas_call(
        functools.partial(early_kernel, kw // LANES),
        out_shape=[
            jax.ShapeDtypeStruct((cap, LANES), jnp.float32),
            jax.ShapeDtypeStruct((depth, kw), jnp.bfloat16),
            TOKEN,
        ],
        in_specs=[VMEM, SMEM, VMEM, ANY],
        compiler_params=params(14),
        cost_estimate=BRIEF,
        name="early",
    )(slot_row, count, fb, after)


def prepare_kernel(per_row, n, *refs):
    xs, (slot_row, count), (xg, xt, token) = refs[:n], refs[n : n + 2], refs[-3:]
    token[...] = jnp.zeros_like(token)
    depth = xs[0].shape[1]
    cap = slot_row.shape[1]
    used = lax.broadcasted_iota(jnp.int32, (cap, 1), 0) < count[0, 0]
    line = jnp.where(used, as_column(slot_row[...])[:, 0:1] // per_row, depth)
    hot = line == lax.broadcasted_iota(jnp.int32, (cap, depth), 1)
    hot = hot.astype(jnp.float32).astype(jnp.bfloat16)
    start = 0
    for x in xs:
        rows = x.shape[0]
        xg[:, start : start + rows] = lax.dot_general(
            hot, x[...], (((1,), (1,)), ((), ())), preferred_element_type=jnp.float32
        ).astype(jnp.bfloat16)
        xt[:, start : start + rows] = x[...].T
        start += rows


def prepare(xs, slot_row, count, per_row, after):
    rows, depth = sum(x.shape[0] for x in xs), xs[0].shape[1]
    cap = slot_row.shape[1]
    return pl.pallas_call(
        functools.partial(prepare_kernel, per_row, len(xs)),
        out_shape=[
            jax.ShapeDtypeStruct((cap, rows), jnp.bfloat16),
            jax.ShapeDtypeStruct((depth, rows), jnp.bfloat16),
            TOKEN,
        ],
        in_specs=[VMEM] * (len(xs) + 1) + [SMEM] + [ANY] * len(after),
        compiler_params=params(14),
        cost_estimate=BRIEF,
        name="prepare",
    )(*xs, slot_row, count, *after)


def stack(slopes, order, s):
    start = 0
    for k, low, high in order:
        s[start : start + high - low, :] = slopes[k][low:high, :]
        start += high - low


def gather_kernel(order, *refs):
    slopes, (xg, out, s) = refs[:-3], refs[-3:]
    stack(slopes, order, s)
    out[...] = jnp.dot(xg[...], s[...], preferred_element_type=jnp.float32)


def gather(slopes, order, xg):
    kw = slopes[0].shape[1]
    return pl.pallas_call(
        functools.partial(gather_kernel, order),
        out_shape=jax.ShapeDtypeStruct((xg.shape[0], kw), jnp.float32),
        scratch_shapes=[pltpu.VMEM((xg.shape[1], kw), jnp.bfloat16)],
        compiler_params=params(8),
        cost_estimate=BRIEF,
        name="gather",
    )(*slopes, xg)


def kept_kernel(per_row, order, *refs):
    slopes, (wide, xg, fbk, slot_row, out, s) = refs[:-6], refs[-6:]
    cap = slot_row.shape[1]
    stack(slopes, order, s)
    total = wide[...] + jnp.dot(xg[...], s[...], preferred_element_type=jnp.float32)
    value = pick_columns(total, as_column(slot_row[...])[:, 0:1] % per_row) + fbk[...]
    out[:cap, :] = value.astype(jnp.bfloat16)
    tail = out.shape[0] - cap
    number = jnp.broadcast_to(slot_row[...], (tail, cap))
    line = lax.broadcasted_iota(jnp.int32, (tail, cap), 0)
    number = jnp.where(line == 0, number // LANES, number % LANES)
    out[cap:, :] = number.astype(jnp.float32).astype(jnp.bfloat16)


def kept(slopes, order, wide, xg, fbk, slot_row):
    cap, kw = wide.shape
    return pl.pallas_call(
        functools.partial(kept_kernel, kw // LANES, order),
        out_shape=jax.ShapeDtypeStruct((cap + 16, LANES), jnp.bfloat16),
        scratch_shapes=[pltpu.VMEM((xg.shape[1], kw), jnp.bfloat16)],
        compiler_params=params(8),
        cost_estimate=BRIEF,
        name="kept",
    )(*slopes, wide, xg, fbk, slot_row)


def send_out(held, out, sems, t, tile):
    rows = pl.ds(t * tile, tile)
    return pltpu.make_async_copy(held.at[rows, :], out.at[rows, :], sems.at[t])


def residue_kernel(order, tile, *refs):
    n = len({k for k, _, _ in order})
    slopes, xts, (fb, keep, out, token, s, held, sems) = refs[:n], refs[n:-7], refs[-7:]
    token[...] = jnp.zeros_like(token)
    stack(slopes, order, s)
    tiles = out.shape[0] // tile
    for t in range(tiles):
        rows = slice(t * tile, (t + 1) * tile)
        pseudo, start = fb[rows, :].astype(jnp.float32), 0
        for xt in xts:
            part = s[start : start + xt.shape[1], :]
            pseudo += jnp.dot(xt[rows, :], part, preferred_element_type=jnp.float32)
            start += xt.shape[1]
        held[rows, :] = jnp.where(keep[rows, :] > 0, pseudo, 0.0).astype(jnp.bfloat16)
        send_out(held, out, sems, t, tile).start()
    for t in range(tiles):
        send_out(held, out, sems, t, tile).wait()


def residue(slopes, order, xts, fb, keep):
    depth, kw = fb.shape
    total = sum(xt.shape[1] for xt in xts)
    tile = min(depth, 512)
    return pl.pallas_call(
        functools.partial(residue_kernel, order, tile),
        out_shape=[
            jax.ShapeDtypeStruct((depth, kw), jnp.bfloat16),
            TOKEN,
        ],
        in_specs=[VMEM] * (len(slopes) + len(xts) + 2),
        out_specs=[ANY, VMEM],
        scratch_shapes=[
            pltpu.VMEM((total, kw), jnp.bfloat16),
            pltpu.VMEM((depth, kw), jnp.bfloat16),
            pltpu.SemaphoreType.DMA((depth // tile,)),
        ],
        compiler_params=params(14),
        cost_estimate=BRIEF,
        name="residue",
    )(*slopes, *xts, fb, keep)


def join_kernel(n, *refs):
    out, start = refs[-1], 0
    for part in refs[:n]:
        out[start : start + part.shape[0], :] = part[...]
        start += part.shape[0]


def join(parts, after):
    rows, lanes = sum(part.shape[0] for part in parts), parts[0].shape[1]
    return pl.pallas_call(
        functools.partial(join_kernel, len(parts)),
        out_shape=jax.ShapeDtypeStruct((rows, lanes), jnp.bfloat16),
        in_specs=[VMEM] * len(parts) + [ANY] * len(after),
        compiler_params=params(8),
        cost_estimate=BRIEF,
        name="join",
    )(*parts, *after)


def spread(group, wide, lines, cap, per_row):
    size = cap + 16
    for k in range(group.shape[0] // size):
        start = k * size
        tail = group[start + cap : start + size, :].astype(jnp.float32)
        number = (tail[0:1, :] * LANES + tail[1:2, :]).astype(jnp.int32)
        lines[:, k * cap : (k + 1) * cap] = jnp.broadcast_to(number // per_row, (8, cap))
        column = jnp.broadcast_to((number % per_row).astype(jnp.float32), (LANES, cap)).T
        value = group[start : start + cap, :].astype(jnp.float32)
        for c in range(per_row):
            wide[k * cap : (k + 1) * cap, c * LANES : (c + 1) * LANES] = jnp.where(
                column == c, value, 0.0
            ).astype(jnp.bfloat16)


def place(lines, wide, t, tile):
    line = lax.broadcasted_iota(jnp.int32, (tile, lines.shape[1]), 0) + t * tile
    hot = (lines[0:1, :] == line).astype(jnp.float32).astype(jnp.bfloat16)
    return jnp.dot(hot, wide[...], preferred_element_type=jnp.float32)


def half_kernel(cap, per_row, tile, group, out, wide, lines):
    spread(group, wide, lines, cap, per_row)
    for t in range(out.shape[0] // tile):
        out[t * tile : (t + 1) * tile, :] = place(lines, wide, t, tile)


def outer_kernel(cap, per_row, tile, n, group, half, out, wide, lines, held, sems):
    spread(group, wide, lines, cap, per_row)
    tiles = out.shape[0] // tile
    for t in range(tiles):
        rows = slice(t * tile, (t + 1) * tile)
        held[rows, :] = (half[rows, :] + place(lines, wide, t, tile)) / n
        send_out(held, out, sems, t, tile).start()
    for t in range(tiles):
        send_out(held, out, sems, t, tile).wait()


def outer(groups, cap, depth, kw):
    slots = groups[0].shape[0] // (cap + 16) * cap
    n = 2 * slots // cap
    tile = min(depth, 512)
    shape = jax.ShapeDtypeStruct((depth, kw), jnp.float32)
    scratch = [pltpu.VMEM((slots, kw), jnp.bfloat16), pltpu.VMEM((8, slots), jnp.int32)]
    half = pl.pallas_call(
        functools.partial(half_kernel, cap, kw // LANES, tile),
        out_shape=shape,
        scratch_shapes=scratch,
        compiler_params=params(14),
        cost_estimate=BRIEF,
        name="half",
    )(groups[0])
    return pl.pallas_call(
        functools.partial(outer_kernel, cap, kw // LANES, tile, n),
        out_shape=shape,
        out_specs=ANY,
        scratch_shapes=scratch
        + [pltpu.VMEM((depth, kw), jnp.float32), pltpu.SemaphoreType.DMA((depth // tile,))],
        compiler_params=params(14),
        cost_estimate=BRIEF,
        name="outer",
    )(groups[1], half)


def on_device(inputs, target, weights, feedback, counts, blocks):
    tokens, w, fb = inputs[0], weights[0], feedback[0]
    n_shard, n_rep = lax.axis_size("shard"), lax.axis_size("rep")
    tok_dev = tokens.shape[0]
    depth, kw = w.shape
    early_rows = tok_dev * 3 // 4
    spans = [(0, early_rows), (early_rows, tok_dev)]
    per_row = kw // LANES
    slot_row = blocks[0]
    near = [d for d in range(1, n_shard) if d & (d - 1) == 0]
    far = [d for d in range(1, n_shard) if d & (d - 1) != 0]

    me = lax.axis_index("shard")
    far_out = [lax.dynamic_slice(tokens, (0, (me ^ d) * depth), (tok_dev, depth)) for d in far]
    far_in = [swap(x, "shard", n_shard, d) for x, d in zip(far_out, far)]
    near_out, token = [], far_out[0]
    for low, high in spans:
        *out, token = cut(tokens, depth, [(d, low, high - low) for d in near], [token])
        near_out.append(out)
        if low == 0:
            fbk, keep, token = early(slot_row, counts, fb, token)
    near_in = [[swap(x, "shard", n_shard, d) for x, d in zip(out, near)] for out in near_out]

    own, _ = cut(tokens, depth, [(0, 0, tok_dev)], [token])

    brief, wide = jnp.bfloat16, jnp.float32
    (mine, *products), x_far = project([own] + far_in, [wide] + [brief] * len(far), w, [])
    whole = [swap(p, "shard", n_shard, d) for p, d in zip(products, far)]
    xg_far, xt_far, token = prepare([x_far], slot_row, counts, per_row, [])
    after, shares, x_near = [token], [], []
    for part in range(len(spans)):
        products, x = project(near_in[part], [brief] * len(near), w, after)
        shares.append([swap(p, "shard", n_shard, d) for p, d in zip(products, near)])
        x_near.append(x)
        after = products[-1:]
    xg_near, xt_near, token = prepare(x_near, slot_row, counts, per_row, [products[0]])
    shares = [share[k] for k in range(len(near)) for share in shares]
    slopes = slope(target[0], mine, whole, shares, spans, token)
    slopes = [slopes] + [swap(slopes, "shard", n_shard, d) for d in far + near]

    n_far = 1 + len(far)
    order_far = [(k, 0, tok_dev) for k in range(n_far)]
    order_near = [(k, low, high) for low, high in spans for k in range(len(near))]
    wide = gather(slopes[:n_far], order_far, xg_far)
    message = kept(slopes[n_far:], order_near, wide, xg_near, fbk, slot_row)
    same_core = [swap(message, "rep", n_rep, d) for d in range(n_rep - 2, 0, -2)]
    order = order_far + [(n_far + k, low, high) for k, low, high in order_near]
    new_feedback, token = residue(slopes, order, [xt_far, xt_near], fb, keep)
    joined, after = message, [token]
    for received in same_core:
        joined, after = join([joined, received], after), []
    groups = [joined, swap(joined, "rep", n_rep, 1)]
    return outer(groups, message.shape[0] - 16, depth, kw), new_feedback[None]


def solution(mesh):
    placed = (
        P("rep", "shard", None),
        P("rep", "shard", None),
        P("rep", "shard", None),
        P("rep", "shard", None),
        P("rep", "shard"),
        P("rep", "shard", None),
    )
    return jax.shard_map(
        on_device,
        mesh=mesh,
        in_specs=placed,
        out_specs=(P("shard", None), P("rep", "shard", None)),
        check_vma=False,
    )
```

```python
import functools

import jax
import jax.numpy as jnp
from jax import lax
from jax.experimental import pallas as pl
from jax.experimental.pallas import tpu as pltpu
from jax.sharding import PartitionSpec as P

LANES = 128
ANY = pl.BlockSpec(memory_space=pl.ANY)
BRIEF = pl.CostEstimate(flops=1000, bytes_accessed=1000, transcendentals=0)
VMEM = pl.BlockSpec(memory_space=pltpu.VMEM)
SMEM = pl.BlockSpec(memory_space=pltpu.SMEM)
MIB = 1024 * 1024
TOKEN = jax.ShapeDtypeStruct((8, LANES), jnp.float32)


def params(mib):
    return pltpu.CompilerParams(vmem_limit_bytes=mib * MIB)


def swap(x, axis, n, d):
    return lax.ppermute(x, axis, [(i, i ^ d) for i in range(n)])


def cut_kernel(cuts, tokens, *refs):
    outs, (token, sems) = refs[-len(cuts) - 2 : -2], refs[-2:]
    token[...] = jnp.zeros_like(token)
    me = lax.axis_index("shard")
    copies = []
    for k, (d, low, rows) in enumerate(cuts):
        depth = outs[k].shape[1]
        columns = pl.ds(pl.multiple_of((me ^ d) * depth, LANES), depth)
        copy = pltpu.make_async_copy(tokens.at[pl.ds(low, rows), columns], outs[k], sems.at[k])
        copy.start()
        copies.append(copy)
    for copy in copies:
        copy.wait()


def cut(tokens, depth, cuts, after):
    return pl.pallas_call(
        functools.partial(cut_kernel, cuts),
        out_shape=[jax.ShapeDtypeStruct((rows, depth), tokens.dtype) for _, _, rows in cuts]
        + [TOKEN],
        in_specs=[ANY] * (1 + len(after)),
        out_specs=[ANY] * len(cuts) + [VMEM],
        scratch_shapes=[pltpu.SemaphoreType.DMA((len(cuts),))],
        compiler_params=params(6),
        cost_estimate=BRIEF,
        name="cut",
    )(tokens, *after)


def project_kernel(n, *refs):
    pieces, w, outs, x = refs[:n], refs[n], refs[-n - 1 : -1], refs[-1]
    start = 0
    for piece in pieces:
        x[start : start + piece.shape[0], :] = piece[...]
        start += piece.shape[0]
    full = jnp.dot(x[...], w[...], preferred_element_type=jnp.float32)
    start = 0
    for out in outs:
        out[...] = full[start : start + out.shape[0], :].astype(out.dtype)
        start += out.shape[0]


def project(pieces, types, w, after):
    n = len(pieces)
    rows, depth = sum(p.shape[0] for p in pieces), pieces[0].shape[1]
    kw = w.shape[1]
    result = pl.pallas_call(
        functools.partial(project_kernel, n),
        out_shape=[jax.ShapeDtypeStruct((p.shape[0], kw), t) for p, t in zip(pieces, types)]
        + [jax.ShapeDtypeStruct((rows, depth), jnp.bfloat16)],
        in_specs=[VMEM] * (n + 1) + [ANY] * len(after),
        compiler_params=params(14),
        cost_estimate=BRIEF,
        name="project",
    )(*pieces, w, *after)
    return result[:n], result[n]


def slope_kernel(tok_dev, n, spans, *refs):
    goal, mine, out = refs[0], refs[1], refs[-1]
    whole = refs[2 : 2 + n]
    shares = refs[2 + n : -2]
    for part, (low, high) in enumerate(spans):
        key_proj = mine[low:high, :]
        for product in whole:
            key_proj += product[low:high, :].astype(jnp.float32)
        for product in shares[part :: len(spans)]:
            key_proj += product[...].astype(jnp.float32)
        gap = key_proj - goal[low:high, :].astype(jnp.float32)
        out[low:high, :] = (gap / tok_dev).astype(jnp.bfloat16)


def slope(goal, mine, whole, shares, spans, after):
    return pl.pallas_call(
        functools.partial(slope_kernel, goal.shape[0], len(whole), spans),
        out_shape=jax.ShapeDtypeStruct(mine.shape, jnp.bfloat16),
        in_specs=[VMEM] * (2 + len(whole) + len(shares)) + [ANY],
        compiler_params=params(8),
        cost_estimate=BRIEF,
        name="slope",
    )(goal, mine, *whole, *shares, after)


def as_column(row):
    size = row.shape[1]
    return jnp.broadcast_to(row.astype(jnp.float32), (size, size)).T.astype(jnp.int32)


def pick_columns(wide, column):
    out = jnp.zeros((wide.shape[0], LANES), jnp.float32)
    for c in range(wide.shape[1] // LANES):
        out += jnp.where(column == c, wide[:, c * LANES : (c + 1) * LANES], 0.0)
    return out


def early_kernel(per_row, slot_row, count, fb, after, fbk, keep, token):
    token[...] = jnp.zeros_like(token)
    depth, kw = fb.shape
    cap = slot_row.shape[1]
    slot = as_column(slot_row[...])[:, 0:1]
    hot = slot // per_row == lax.broadcasted_iota(jnp.int32, (cap, depth), 1)
    hot = hot.astype(jnp.float32).astype(jnp.bfloat16)
    used = lax.broadcasted_iota(jnp.int32, (cap, 1), 0) < count[0, 0]
    wide = jnp.dot(hot, fb[...], preferred_element_type=jnp.float32)
    fbk[...] = jnp.where(used, pick_columns(wide, slot % per_row), 0.0)
    group = lax.broadcasted_iota(jnp.int32, (cap, kw), 1) // LANES
    mark = jnp.where(used & (slot % per_row == group), 1.0, 0.0).astype(jnp.bfloat16)
    tile = min(depth, 512)
    for t in range(depth // tile):
        line = lax.broadcasted_iota(jnp.int32, (tile, cap), 0) + t * tile
        hot = (slot_row[...] // per_row == line).astype(jnp.float32).astype(jnp.bfloat16)
        mask = jnp.dot(hot, mark, preferred_element_type=jnp.float32)
        keep[t * tile : (t + 1) * tile, :] = (1.0 - mask).astype(jnp.bfloat16)


def early(slot_row, count, fb, after):
    depth, kw = fb.shape
    cap = slot_row.shape[1]
    return pl.pallas_call(
        functools.partial(early_kernel, kw // LANES),
        out_shape=[
            jax.ShapeDtypeStruct((cap, LANES), jnp.float32),
            jax.ShapeDtypeStruct((depth, kw), jnp.bfloat16),
            TOKEN,
        ],
        in_specs=[VMEM, SMEM, VMEM, ANY],
        compiler_params=params(14),
        cost_estimate=BRIEF,
        name="early",
    )(slot_row, count, fb, after)


def prepare_kernel(per_row, n, *refs):
    xs, (slot_row, count), (xg, xt, token) = refs[:n], refs[n : n + 2], refs[-3:]
    token[...] = jnp.zeros_like(token)
    depth = xs[0].shape[1]
    cap = slot_row.shape[1]
    used = lax.broadcasted_iota(jnp.int32, (cap, 1), 0) < count[0, 0]
    line = jnp.where(used, as_column(slot_row[...])[:, 0:1] // per_row, depth)
    hot = line == lax.broadcasted_iota(jnp.int32, (cap, depth), 1)
    hot = hot.astype(jnp.float32).astype(jnp.bfloat16)
    start = 0
    for x in xs:
        rows = x.shape[0]
        xg[:, start : start + rows] = lax.dot_general(
            hot, x[...], (((1,), (1,)), ((), ())), preferred_element_type=jnp.float32
        ).astype(jnp.bfloat16)
        xt[:, start : start + rows] = x[...].T
        start += rows


def prepare(xs, slot_row, count, per_row, after):
    rows, depth = sum(x.shape[0] for x in xs), xs[0].shape[1]
    cap = slot_row.shape[1]
    return pl.pallas_call(
        functools.partial(prepare_kernel, per_row, len(xs)),
        out_shape=[
            jax.ShapeDtypeStruct((cap, rows), jnp.bfloat16),
            jax.ShapeDtypeStruct((depth, rows), jnp.bfloat16),
            TOKEN,
        ],
        in_specs=[VMEM] * (len(xs) + 1) + [SMEM] + [ANY] * len(after),
        compiler_params=params(14),
        cost_estimate=BRIEF,
        name="prepare",
    )(*xs, slot_row, count, *after)


def kept_kernel(per_row, order, slopes, *refs):
    xgs, (fbk, slot_row, out, s) = refs[:-4], refs[-4:]
    cap = slot_row.shape[1]
    me = lax.axis_index("shard")
    tok_dev = slopes.shape[0] // lax.axis_size("shard")
    start = 0
    for d, low, high in order:
        rows = pl.ds(pl.multiple_of((me ^ d) * tok_dev + low, 16), high - low)
        s[start : start + high - low, :] = slopes[rows, :]
        start += high - low
    total, start = 0.0, 0
    for xg in xgs:
        part = s[start : start + xg.shape[1], :]
        total += jnp.dot(xg[...], part, preferred_element_type=jnp.float32)
        start += xg.shape[1]
    value = pick_columns(total, as_column(slot_row[...])[:, 0:1] % per_row) + fbk[...]
    out[:cap, :] = value.astype(jnp.bfloat16)
    tail = out.shape[0] - cap
    number = jnp.broadcast_to(slot_row[...], (tail, cap))
    line = lax.broadcasted_iota(jnp.int32, (tail, cap), 0)
    number = jnp.where(line == 0, number // LANES, number % LANES)
    out[cap:, :] = number.astype(jnp.float32).astype(jnp.bfloat16)


def kept(slopes, order, xgs, fbk, slot_row):
    cap = slot_row.shape[1]
    return pl.pallas_call(
        functools.partial(kept_kernel, slopes.shape[1] // LANES, order),
        out_shape=[
            jax.ShapeDtypeStruct((cap + 16, LANES), jnp.bfloat16),
            jax.ShapeDtypeStruct(slopes.shape, jnp.bfloat16),
        ],
        compiler_params=params(8),
        cost_estimate=BRIEF,
        name="kept",
    )(slopes, *xgs, fbk, slot_row)


def send_out(held, out, sems, t, tile):
    rows = pl.ds(t * tile, tile)
    return pltpu.make_async_copy(held.at[rows, :], out.at[rows, :], sems.at[t])


def residue_kernel(tile, s, *refs):
    xts, (fb, keep, out, token, held, sems) = refs[:-6], refs[-6:]
    token[...] = jnp.zeros_like(token)
    tiles = out.shape[0] // tile
    for t in range(tiles):
        rows = slice(t * tile, (t + 1) * tile)
        pseudo, start = fb[rows, :].astype(jnp.float32), 0
        for xt in xts:
            part = s[start : start + xt.shape[1], :]
            pseudo += jnp.dot(xt[rows, :], part, preferred_element_type=jnp.float32)
            start += xt.shape[1]
        held[rows, :] = jnp.where(keep[rows, :] > 0, pseudo, 0.0).astype(jnp.bfloat16)
        send_out(held, out, sems, t, tile).start()
    for t in range(tiles):
        send_out(held, out, sems, t, tile).wait()


def residue(s, xts, fb, keep):
    depth, kw = fb.shape
    tile = min(depth, 512)
    return pl.pallas_call(
        functools.partial(residue_kernel, tile),
        out_shape=[jax.ShapeDtypeStruct((depth, kw), jnp.bfloat16), TOKEN],
        in_specs=[VMEM] * (len(xts) + 3),
        out_specs=[ANY, VMEM],
        scratch_shapes=[
            pltpu.VMEM((depth, kw), jnp.bfloat16),
            pltpu.SemaphoreType.DMA((depth // tile,)),
        ],
        compiler_params=params(14),
        cost_estimate=BRIEF,
        name="residue",
    )(s, *xts, fb, keep)


def join_kernel(n, *refs):
    out, start = refs[-1], 0
    for part in refs[:n]:
        out[start : start + part.shape[0], :] = part[...]
        start += part.shape[0]


def join(parts, after):
    rows, lanes = sum(part.shape[0] for part in parts), parts[0].shape[1]
    return pl.pallas_call(
        functools.partial(join_kernel, len(parts)),
        out_shape=jax.ShapeDtypeStruct((rows, lanes), jnp.bfloat16),
        in_specs=[VMEM] * len(parts) + [ANY] * len(after),
        compiler_params=params(8),
        cost_estimate=BRIEF,
        name="join",
    )(*parts, *after)


def spread(group, wide, lines, cap, per_row):
    size = cap + 16
    for k in range(group.shape[0] // size):
        start = k * size
        tail = group[start + cap : start + size, :].astype(jnp.float32)
        number = (tail[0:1, :] * LANES + tail[1:2, :]).astype(jnp.int32)
        lines[:, k * cap : (k + 1) * cap] = jnp.broadcast_to(number // per_row, (8, cap))
        column = jnp.broadcast_to((number % per_row).astype(jnp.float32), (LANES, cap)).T
        value = group[start : start + cap, :].astype(jnp.float32)
        for c in range(per_row):
            wide[k * cap : (k + 1) * cap, c * LANES : (c + 1) * LANES] = jnp.where(
                column == c, value, 0.0
            ).astype(jnp.bfloat16)


def place(lines, wide, t, tile):
    line = lax.broadcasted_iota(jnp.int32, (tile, lines.shape[1]), 0) + t * tile
    hot = (lines[0:1, :] == line).astype(jnp.float32).astype(jnp.bfloat16)
    return jnp.dot(hot, wide[...], preferred_element_type=jnp.float32)


def half_kernel(cap, per_row, tile, group, out, wide, lines):
    spread(group, wide, lines, cap, per_row)
    for t in range(out.shape[0] // tile):
        out[t * tile : (t + 1) * tile, :] = place(lines, wide, t, tile)


def outer_kernel(cap, per_row, tile, n, group, half, out, wide, lines, held, sems):
    spread(group, wide, lines, cap, per_row)
    tiles = out.shape[0] // tile
    for t in range(tiles):
        rows = slice(t * tile, (t + 1) * tile)
        held[rows, :] = (half[rows, :] + place(lines, wide, t, tile)) / n
        send_out(held, out, sems, t, tile).start()
    for t in range(tiles):
        send_out(held, out, sems, t, tile).wait()


def outer(groups, cap, depth, kw):
    slots = groups[0].shape[0] // (cap + 16) * cap
    n = 2 * slots // cap
    tile = min(depth, 512)
    shape = jax.ShapeDtypeStruct((depth, kw), jnp.float32)
    scratch = [pltpu.VMEM((slots, kw), jnp.bfloat16), pltpu.VMEM((8, slots), jnp.int32)]
    half = pl.pallas_call(
        functools.partial(half_kernel, cap, kw // LANES, tile),
        out_shape=shape,
        scratch_shapes=scratch,
        compiler_params=params(14),
        cost_estimate=BRIEF,
        name="half",
    )(groups[0])
    return pl.pallas_call(
        functools.partial(outer_kernel, cap, kw // LANES, tile, n),
        out_shape=shape,
        out_specs=ANY,
        scratch_shapes=scratch
        + [pltpu.VMEM((depth, kw), jnp.float32), pltpu.SemaphoreType.DMA((depth // tile,))],
        compiler_params=params(14),
        cost_estimate=BRIEF,
        name="outer",
    )(groups[1], half)


def on_device(inputs, target, weights, feedback, counts, blocks):
    tokens, w, fb = inputs[0], weights[0], feedback[0]
    n_shard, n_rep = lax.axis_size("shard"), lax.axis_size("rep")
    tok_dev = tokens.shape[0]
    depth, kw = w.shape
    early_rows = tok_dev * 3 // 4
    spans = [(0, early_rows), (early_rows, tok_dev)]
    per_row = kw // LANES
    slot_row = blocks[0]
    near = [d for d in range(1, n_shard) if d & (d - 1) == 0]
    far = [d for d in range(1, n_shard) if d & (d - 1) != 0]

    me = lax.axis_index("shard")
    far_out = [lax.dynamic_slice(tokens, (0, (me ^ d) * depth), (tok_dev, depth)) for d in far]
    far_in = [swap(x, "shard", n_shard, d) for x, d in zip(far_out, far)]
    near_out, token = [], far_out[0]
    for low, high in spans:
        *out, token = cut(tokens, depth, [(d, low, high - low) for d in near], [token])
        near_out.append(out)
        if low == 0:
            fbk, keep, token = early(slot_row, counts, fb, token)
    near_in = [[swap(x, "shard", n_shard, d) for x, d in zip(out, near)] for out in near_out]

    own, _ = cut(tokens, depth, [(0, 0, tok_dev)], [token])

    brief, wide = jnp.bfloat16, jnp.float32
    (mine, *products), x_far = project([own] + far_in, [wide] + [brief] * len(far), w, [])
    whole = [swap(p, "shard", n_shard, d) for p, d in zip(products, far)]
    xg_far, xt_far, token = prepare([x_far], slot_row, counts, per_row, [])
    after, shares, x_near = [token], [], []
    for part in range(len(spans)):
        products, x = project(near_in[part], [brief] * len(near), w, after)
        shares.append([swap(p, "shard", n_shard, d) for p, d in zip(products, near)])
        x_near.append(x)
        after = products[-1:]
    xg_near, xt_near, token = prepare(x_near, slot_row, counts, per_row, [products[0]])
    shares = [share[k] for k in range(len(near)) for share in shares]
    slopes = slope(target[0], mine, whole, shares, spans, token)
    slopes = lax.all_gather(slopes, "shard", axis=0, tiled=True)

    order = [(d, 0, tok_dev) for d in [0] + far]
    order += [(d, low, high) for low, high in spans for d in near]
    message, slopes = kept(slopes, order, [xg_far, xg_near], fbk, slot_row)
    same_core = [swap(message, "rep", n_rep, d) for d in range(n_rep - 2, 0, -2)]
    new_feedback, token = residue(slopes, [xt_far, xt_near], fb, keep)
    joined, after = message, [token]
    for received in same_core:
        joined, after = join([joined, received], after), []
    groups = [joined, swap(joined, "rep", n_rep, 1)]
    return outer(groups, message.shape[0] - 16, depth, kw), new_feedback[None]


def solution(mesh):
    placed = (
        P("rep", "shard", None),
        P("rep", "shard", None),
        P("rep", "shard", None),
        P("rep", "shard", None),
        P("rep", "shard"),
        P("rep", "shard", None),
    )
    return jax.shard_map(
        on_device,
        mesh=mesh,
        in_specs=placed,
        out_specs=(P("shard", None), P("rep", "shard", None)),
        check_vma=False,
    )
```

```python
import functools

import jax
import jax.numpy as jnp
from jax import lax
from jax.experimental import pallas as pl
from jax.experimental.pallas import tpu as pltpu
from jax.sharding import PartitionSpec as P

LANES = 128
ANY = pl.BlockSpec(memory_space=pl.ANY)
BRIEF = pl.CostEstimate(flops=1000, bytes_accessed=1000, transcendentals=0)
VMEM = pl.BlockSpec(memory_space=pltpu.VMEM)
SMEM = pl.BlockSpec(memory_space=pltpu.SMEM)
MIB = 1024 * 1024
TOKEN = jax.ShapeDtypeStruct((8, LANES), jnp.float32)


def params(mib):
    return pltpu.CompilerParams(vmem_limit_bytes=mib * MIB)


def swap(x, axis, n, d):
    return lax.ppermute(x, axis, [(i, i ^ d) for i in range(n)])


def cut_kernel(cuts, tokens, *refs):
    outs, (token, sems) = refs[-len(cuts) - 2 : -2], refs[-2:]
    token[...] = jnp.zeros_like(token)
    me = lax.axis_index("shard")
    copies = []
    for k, (d, low, rows) in enumerate(cuts):
        depth = outs[k].shape[1]
        columns = pl.ds(pl.multiple_of((me ^ d) * depth, LANES), depth)
        copy = pltpu.make_async_copy(tokens.at[pl.ds(low, rows), columns], outs[k], sems.at[k])
        copy.start()
        copies.append(copy)
    for copy in copies:
        copy.wait()


def cut(tokens, depth, cuts, after):
    return pl.pallas_call(
        functools.partial(cut_kernel, cuts),
        out_shape=[jax.ShapeDtypeStruct((rows, depth), tokens.dtype) for _, _, rows in cuts]
        + [TOKEN],
        in_specs=[ANY] * (1 + len(after)),
        out_specs=[ANY] * len(cuts) + [VMEM],
        scratch_shapes=[pltpu.SemaphoreType.DMA((len(cuts),))],
        compiler_params=params(6),
        cost_estimate=BRIEF,
        name="cut",
    )(tokens, *after)


def project_kernel(n, m, *refs):
    pieces, w, outs, x = refs[:n], refs[n], refs[-m - 1 : -1], refs[-1]
    start = 0
    for piece in pieces:
        x[start : start + piece.shape[0], :] = piece[...]
        start += piece.shape[0]
    full = jnp.dot(x[...], w[...], preferred_element_type=jnp.float32)
    start = 0
    for out in outs:
        out[...] = full[start : start + out.shape[0], :].astype(out.dtype)
        start += out.shape[0]


def project(pieces, outs, w, after):
    n = len(pieces)
    rows, depth = sum(p.shape[0] for p in pieces), pieces[0].shape[1]
    kw = w.shape[1]
    result = pl.pallas_call(
        functools.partial(project_kernel, n, len(outs)),
        out_shape=[jax.ShapeDtypeStruct((r, kw), t) for r, t in outs]
        + [jax.ShapeDtypeStruct((rows, depth), jnp.bfloat16)],
        in_specs=[VMEM] * (n + 1) + [ANY] * len(after),
        compiler_params=params(14),
        cost_estimate=BRIEF,
        name="project",
    )(*pieces, w, *after)
    return result[:-1], result[-1]


def slope_kernel(tok_dev, n, spans, *refs):
    goal, mine, out = refs[0], refs[1], refs[-1]
    whole = refs[2 : 2 + n]
    shares = refs[2 + n : -2]
    for part, (low, high) in enumerate(spans):
        key_proj = mine[low:high, :]
        for product in whole:
            key_proj += product[low:high, :].astype(jnp.float32)
        for product in shares[part :: len(spans)]:
            key_proj += product[...].astype(jnp.float32)
        gap = key_proj - goal[low:high, :].astype(jnp.float32)
        out[low:high, :] = (gap / tok_dev).astype(jnp.bfloat16)


def slope(goal, mine, whole, shares, spans, after):
    return pl.pallas_call(
        functools.partial(slope_kernel, goal.shape[0], len(whole), spans),
        out_shape=jax.ShapeDtypeStruct(mine.shape, jnp.bfloat16),
        in_specs=[VMEM] * (2 + len(whole) + len(shares)) + [ANY],
        compiler_params=params(8),
        cost_estimate=BRIEF,
        name="slope",
    )(goal, mine, *whole, *shares, after)


def as_column(row):
    size = row.shape[1]
    return jnp.broadcast_to(row.astype(jnp.float32), (size, size)).T.astype(jnp.int32)


def pick_columns(wide, column):
    out = jnp.zeros((wide.shape[0], LANES), jnp.float32)
    for c in range(wide.shape[1] // LANES):
        out += jnp.where(column == c, wide[:, c * LANES : (c + 1) * LANES], 0.0)
    return out


def early_kernel(per_row, slot_row, count, fb, after, fbk, keep, token):
    token[...] = jnp.zeros_like(token)
    depth, kw = fb.shape
    cap = slot_row.shape[1]
    slot = as_column(slot_row[...])[:, 0:1]
    hot = slot // per_row == lax.broadcasted_iota(jnp.int32, (cap, depth), 1)
    hot = hot.astype(jnp.float32).astype(jnp.bfloat16)
    used = lax.broadcasted_iota(jnp.int32, (cap, 1), 0) < count[0, 0]
    wide = jnp.dot(hot, fb[...], preferred_element_type=jnp.float32)
    fbk[...] = jnp.where(used, pick_columns(wide, slot % per_row), 0.0)
    group = lax.broadcasted_iota(jnp.int32, (cap, kw), 1) // LANES
    mark = jnp.where(used & (slot % per_row == group), 1.0, 0.0).astype(jnp.bfloat16)
    tile = min(depth, 512)
    for t in range(depth // tile):
        line = lax.broadcasted_iota(jnp.int32, (tile, cap), 0) + t * tile
        hot = (slot_row[...] // per_row == line).astype(jnp.float32).astype(jnp.bfloat16)
        mask = jnp.dot(hot, mark, preferred_element_type=jnp.float32)
        keep[t * tile : (t + 1) * tile, :] = (1.0 - mask).astype(jnp.bfloat16)


def early(slot_row, count, fb, after):
    depth, kw = fb.shape
    cap = slot_row.shape[1]
    return pl.pallas_call(
        functools.partial(early_kernel, kw // LANES),
        out_shape=[
            jax.ShapeDtypeStruct((cap, LANES), jnp.float32),
            jax.ShapeDtypeStruct((depth, kw), jnp.bfloat16),
            TOKEN,
        ],
        in_specs=[VMEM, SMEM, VMEM, ANY],
        compiler_params=params(14),
        cost_estimate=BRIEF,
        name="early",
    )(slot_row, count, fb, after)


def prepare_kernel(per_row, n, *refs):
    xs, (slot_row, count), (xg, xt, token) = refs[:n], refs[n : n + 2], refs[-3:]
    token[...] = jnp.zeros_like(token)
    depth = xs[0].shape[1]
    cap = slot_row.shape[1]
    used = lax.broadcasted_iota(jnp.int32, (cap, 1), 0) < count[0, 0]
    line = jnp.where(used, as_column(slot_row[...])[:, 0:1] // per_row, depth)
    hot = line == lax.broadcasted_iota(jnp.int32, (cap, depth), 1)
    hot = hot.astype(jnp.float32).astype(jnp.bfloat16)
    start = 0
    for x in xs:
        rows = x.shape[0]
        xg[:, start : start + rows] = lax.dot_general(
            hot, x[...], (((1,), (1,)), ((), ())), preferred_element_type=jnp.float32
        ).astype(jnp.bfloat16)
        xt[:, start : start + rows] = x[...].T
        start += rows


def prepare(xs, slot_row, count, per_row, after):
    rows, depth = sum(x.shape[0] for x in xs), xs[0].shape[1]
    cap = slot_row.shape[1]
    return pl.pallas_call(
        functools.partial(prepare_kernel, per_row, len(xs)),
        out_shape=[
            jax.ShapeDtypeStruct((cap, rows), jnp.bfloat16),
            jax.ShapeDtypeStruct((depth, rows), jnp.bfloat16),
            TOKEN,
        ],
        in_specs=[VMEM] * (len(xs) + 1) + [SMEM] + [ANY] * len(after),
        compiler_params=params(14),
        cost_estimate=BRIEF,
        name="prepare",
    )(*xs, slot_row, count, *after)


def stack(slopes, order, s):
    start = 0
    for k, low, high in order:
        s[start : start + high - low, :] = slopes[k][low:high, :]
        start += high - low


def gather_kernel(order, *refs):
    slopes, (xg, out, s) = refs[:-3], refs[-3:]
    stack(slopes, order, s)
    out[...] = jnp.dot(xg[...], s[...], preferred_element_type=jnp.float32)


def gather(slopes, order, xg):
    kw = slopes[0].shape[1]
    return pl.pallas_call(
        functools.partial(gather_kernel, order),
        out_shape=jax.ShapeDtypeStruct((xg.shape[0], kw), jnp.float32),
        scratch_shapes=[pltpu.VMEM((xg.shape[1], kw), jnp.bfloat16)],
        compiler_params=params(8),
        cost_estimate=BRIEF,
        name="gather",
    )(*slopes, xg)


def kept_kernel(per_row, order, *refs):
    slopes, (wide, xg, fbk, slot_row, out, s) = refs[:-6], refs[-6:]
    cap = slot_row.shape[1]
    stack(slopes, order, s)
    total = wide[...] + jnp.dot(xg[...], s[...], preferred_element_type=jnp.float32)
    value = pick_columns(total, as_column(slot_row[...])[:, 0:1] % per_row) + fbk[...]
    out[:cap, :] = value.astype(jnp.bfloat16)
    tail = out.shape[0] - cap
    number = jnp.broadcast_to(slot_row[...], (tail, cap))
    line = lax.broadcasted_iota(jnp.int32, (tail, cap), 0)
    number = jnp.where(line == 0, number // LANES, number % LANES)
    out[cap:, :] = number.astype(jnp.float32).astype(jnp.bfloat16)


def kept(slopes, order, wide, xg, fbk, slot_row):
    cap, kw = wide.shape
    return pl.pallas_call(
        functools.partial(kept_kernel, kw // LANES, order),
        out_shape=jax.ShapeDtypeStruct((cap + 16, LANES), jnp.bfloat16),
        scratch_shapes=[pltpu.VMEM((xg.shape[1], kw), jnp.bfloat16)],
        compiler_params=params(8),
        cost_estimate=BRIEF,
        name="kept",
    )(*slopes, wide, xg, fbk, slot_row)


def send_out(held, out, sems, t, tile):
    rows = pl.ds(t * tile, tile)
    return pltpu.make_async_copy(held.at[rows, :], out.at[rows, :], sems.at[t])


def residue_kernel(order, tile, *refs):
    n = len({k for k, _, _ in order})
    slopes, xts, (fb, keep, out, token, s, held, sems) = refs[:n], refs[n:-7], refs[-7:]
    token[...] = jnp.zeros_like(token)
    stack(slopes, order, s)
    tiles = out.shape[0] // tile
    for t in range(tiles):
        rows = slice(t * tile, (t + 1) * tile)
        pseudo, start = fb[rows, :].astype(jnp.float32), 0
        for xt in xts:
            part = s[start : start + xt.shape[1], :]
            pseudo += jnp.dot(xt[rows, :], part, preferred_element_type=jnp.float32)
            start += xt.shape[1]
        held[rows, :] = jnp.where(keep[rows, :] > 0, pseudo, 0.0).astype(jnp.bfloat16)
        send_out(held, out, sems, t, tile).start()
    for t in range(tiles):
        send_out(held, out, sems, t, tile).wait()


def residue(slopes, order, xts, fb, keep):
    depth, kw = fb.shape
    total = sum(xt.shape[1] for xt in xts)
    tile = min(depth, 512)
    return pl.pallas_call(
        functools.partial(residue_kernel, order, tile),
        out_shape=[
            jax.ShapeDtypeStruct((depth, kw), jnp.bfloat16),
            TOKEN,
        ],
        in_specs=[VMEM] * (len(slopes) + len(xts) + 2),
        out_specs=[ANY, VMEM],
        scratch_shapes=[
            pltpu.VMEM((total, kw), jnp.bfloat16),
            pltpu.VMEM((depth, kw), jnp.bfloat16),
            pltpu.SemaphoreType.DMA((depth // tile,)),
        ],
        compiler_params=params(14),
        cost_estimate=BRIEF,
        name="residue",
    )(*slopes, *xts, fb, keep)


def join_kernel(n, *refs):
    out, start = refs[-1], 0
    for part in refs[:n]:
        out[start : start + part.shape[0], :] = part[...]
        start += part.shape[0]


def join(parts, after):
    rows, lanes = sum(part.shape[0] for part in parts), parts[0].shape[1]
    return pl.pallas_call(
        functools.partial(join_kernel, len(parts)),
        out_shape=jax.ShapeDtypeStruct((rows, lanes), jnp.bfloat16),
        in_specs=[VMEM] * len(parts) + [ANY] * len(after),
        compiler_params=params(8),
        cost_estimate=BRIEF,
        name="join",
    )(*parts, *after)


def spread(group, wide, lines, cap, per_row):
    size = cap + 16
    for k in range(group.shape[0] // size):
        start = k * size
        tail = group[start + cap : start + size, :].astype(jnp.float32)
        number = (tail[0:1, :] * LANES + tail[1:2, :]).astype(jnp.int32)
        lines[:, k * cap : (k + 1) * cap] = jnp.broadcast_to(number // per_row, (8, cap))
        column = jnp.broadcast_to((number % per_row).astype(jnp.float32), (LANES, cap)).T
        value = group[start : start + cap, :].astype(jnp.float32)
        for c in range(per_row):
            wide[k * cap : (k + 1) * cap, c * LANES : (c + 1) * LANES] = jnp.where(
                column == c, value, 0.0
            ).astype(jnp.bfloat16)


def place(lines, wide, t, tile):
    line = lax.broadcasted_iota(jnp.int32, (tile, lines.shape[1]), 0) + t * tile
    hot = (lines[0:1, :] == line).astype(jnp.float32).astype(jnp.bfloat16)
    return jnp.dot(hot, wide[...], preferred_element_type=jnp.float32)


def half_kernel(cap, per_row, tile, group, out, wide, lines):
    spread(group, wide, lines, cap, per_row)
    for t in range(out.shape[0] // tile):
        out[t * tile : (t + 1) * tile, :] = place(lines, wide, t, tile)


def outer_kernel(cap, per_row, tile, n, group, half, out, wide, lines, held, sems):
    spread(group, wide, lines, cap, per_row)
    tiles = out.shape[0] // tile
    for t in range(tiles):
        rows = slice(t * tile, (t + 1) * tile)
        held[rows, :] = (half[rows, :] + place(lines, wide, t, tile)) / n
        send_out(held, out, sems, t, tile).start()
    for t in range(tiles):
        send_out(held, out, sems, t, tile).wait()


def outer(groups, cap, depth, kw):
    slots = groups[0].shape[0] // (cap + 16) * cap
    n = 2 * slots // cap
    tile = min(depth, 512)
    shape = jax.ShapeDtypeStruct((depth, kw), jnp.float32)
    scratch = [pltpu.VMEM((slots, kw), jnp.bfloat16), pltpu.VMEM((8, slots), jnp.int32)]
    half = pl.pallas_call(
        functools.partial(half_kernel, cap, kw // LANES, tile),
        out_shape=shape,
        scratch_shapes=scratch,
        compiler_params=params(14),
        cost_estimate=BRIEF,
        name="half",
    )(groups[0])
    return pl.pallas_call(
        functools.partial(outer_kernel, cap, kw // LANES, tile, n),
        out_shape=shape,
        out_specs=ANY,
        scratch_shapes=scratch
        + [pltpu.VMEM((depth, kw), jnp.float32), pltpu.SemaphoreType.DMA((depth // tile,))],
        compiler_params=params(14),
        cost_estimate=BRIEF,
        name="outer",
    )(groups[1], half)


def on_device(inputs, target, weights, feedback, counts, blocks):
    tokens, w, fb = inputs[0], weights[0], feedback[0]
    n_shard, n_rep = lax.axis_size("shard"), lax.axis_size("rep")
    tok_dev = tokens.shape[0]
    depth, kw = w.shape
    early_rows = tok_dev // 2
    spans = [(0, early_rows), (early_rows, tok_dev)]
    per_row = kw // LANES
    slot_row = blocks[0]
    near = [d for d in range(1, n_shard) if d & (d - 1) == 0]
    far = [d for d in range(1, n_shard) if d & (d - 1) != 0]

    me = lax.axis_index("shard")
    rows = tok_dev // 2 if n_shard == 4 else tok_dev
    far_out = [
        [
            lax.dynamic_slice(tokens, (low, (me ^ d) * depth), (rows, depth))
            for low in range(0, tok_dev, rows)
        ]
        for d in far
    ]
    if n_shard == 4:
        ((by_x, by_y),) = far_out
        by_x, by_y = swap(by_x, "shard", n_shard, 1), swap(by_y, "shard", n_shard, 2)
        hops = [by_x, by_y]
        far_in = [swap(by_x, "shard", n_shard, 2), swap(by_y, "shard", n_shard, 1)]
    else:
        hops = []
        far_in = [swap(x, "shard", n_shard, d) for (x,), d in zip(far_out, far)]
    near_out, after = [], [far_out[0][0]]
    for low, high in spans:
        *out, token = cut(tokens, depth, [(d, low, high - low) for d in near], after)
        near_out.append(out)
        if low == 0:
            fbk, keep, token = early(slot_row, counts, fb, token)
            after = [token] + hops
    near_in = [[swap(x, "shard", n_shard, d) for x, d in zip(out, near)] for out in near_out]

    own, _ = cut(tokens, depth, [(0, 0, tok_dev)], [token])

    brief, wide = jnp.bfloat16, jnp.float32
    near_outs = [[(high - low, brief)] * len(near) for low, high in spans]
    early_near, x_early = project(near_in[0], near_outs[0], w, [])
    outs = [(tok_dev, wide)] + [(tok_dev, brief)] * len(far)
    (mine, *products), x_far = project([own] + far_in, outs, w, early_near[-1:])
    whole = [swap(p, "shard", n_shard, d) for p, d in zip(products, far)]
    xg_far, xt_far, token = prepare([x_far], slot_row, counts, per_row, products)
    late_near, x_late = project(near_in[1], near_outs[1], w, [token])
    shares = [
        [swap(p, "shard", n_shard, d) for p, d in zip(part, near)]
        for part in (early_near, late_near)
    ]
    x_near = [x_early, x_late]
    xg_near, xt_near, token = prepare(x_near, slot_row, counts, per_row, late_near[:1])
    shares = [share[k] for k in range(len(near)) for share in shares]
    slopes = slope(target[0], mine, whole, shares, spans, token)
    slopes = [slopes] + [swap(slopes, "shard", n_shard, d) for d in far + near]

    n_far = 1 + len(far)
    order_far = [(k, 0, tok_dev) for k in range(n_far)]
    order_near = [(k, low, high) for low, high in spans for k in range(len(near))]
    wide = gather(slopes[:n_far], order_far, xg_far)
    message = kept(slopes[n_far:], order_near, wide, xg_near, fbk, slot_row)
    same_core = [swap(message, "rep", n_rep, d) for d in range(n_rep - 2, 0, -2)]
    order = order_far + [(n_far + k, low, high) for k, low, high in order_near]
    new_feedback, token = residue(slopes, order, [xt_far, xt_near], fb, keep)
    joined, after = message, [token]
    for received in same_core:
        joined, after = join([joined, received], after), []
    groups = [joined, swap(joined, "rep", n_rep, 1)]
    return outer(groups, message.shape[0] - 16, depth, kw), new_feedback[None]


def solution(mesh):
    placed = (
        P("rep", "shard", None),
        P("rep", "shard", None),
        P("rep", "shard", None),
        P("rep", "shard", None),
        P("rep", "shard"),
        P("rep", "shard", None),
    )
    return jax.shard_map(
        on_device,
        mesh=mesh,
        in_specs=placed,
        out_specs=(P("shard", None), P("rep", "shard", None)),
        check_vma=False,
    )
```

```python
import functools

import jax
import jax.numpy as jnp
from jax import lax
from jax.experimental import pallas as pl
from jax.experimental.pallas import tpu as pltpu
from jax.sharding import PartitionSpec as P

LANES = 128
ANY = pl.BlockSpec(memory_space=pl.ANY)
BRIEF = pl.CostEstimate(flops=1000, bytes_accessed=1000, transcendentals=0)
VMEM = pl.BlockSpec(memory_space=pltpu.VMEM)
SMEM = pl.BlockSpec(memory_space=pltpu.SMEM)
MIB = 1024 * 1024
TOKEN = jax.ShapeDtypeStruct((8, LANES), jnp.float32)


def params(mib):
    return pltpu.CompilerParams(vmem_limit_bytes=mib * MIB)


def swap(x, axis, n, d):
    return lax.ppermute(x, axis, [(i, i ^ d) for i in range(n)])


def cut_kernel(cuts, tokens, *refs):
    outs, (token, sems) = refs[-len(cuts) - 2 : -2], refs[-2:]
    token[...] = jnp.zeros_like(token)
    me = lax.axis_index("shard")
    copies = []
    for k, (d, low, rows) in enumerate(cuts):
        depth = outs[k].shape[1]
        columns = pl.ds(pl.multiple_of((me ^ d) * depth, LANES), depth)
        copy = pltpu.make_async_copy(tokens.at[pl.ds(low, rows), columns], outs[k], sems.at[k])
        copy.start()
        copies.append(copy)
    for copy in copies:
        copy.wait()


def cut(tokens, depth, cuts, after):
    return pl.pallas_call(
        functools.partial(cut_kernel, cuts),
        out_shape=[jax.ShapeDtypeStruct((rows, depth), tokens.dtype) for _, _, rows in cuts]
        + [TOKEN],
        in_specs=[ANY] * (1 + len(after)),
        out_specs=[ANY] * len(cuts) + [VMEM],
        scratch_shapes=[pltpu.SemaphoreType.DMA((len(cuts),))],
        compiler_params=params(6),
        cost_estimate=BRIEF,
        name="cut",
    )(tokens, *after)


def project_kernel(n, *refs):
    pieces, w, outs, x = refs[:n], refs[n], refs[-n - 1 : -1], refs[-1]
    start = 0
    for piece in pieces:
        x[start : start + piece.shape[0], :] = piece[...]
        start += piece.shape[0]
    full = jnp.dot(x[...], w[...], preferred_element_type=jnp.float32)
    start = 0
    for out in outs:
        out[...] = full[start : start + out.shape[0], :].astype(out.dtype)
        start += out.shape[0]


def project(pieces, types, w, after):
    n = len(pieces)
    rows, depth = sum(p.shape[0] for p in pieces), pieces[0].shape[1]
    kw = w.shape[1]
    result = pl.pallas_call(
        functools.partial(project_kernel, n),
        out_shape=[jax.ShapeDtypeStruct((p.shape[0], kw), t) for p, t in zip(pieces, types)]
        + [jax.ShapeDtypeStruct((rows, depth), jnp.bfloat16)],
        in_specs=[VMEM] * (n + 1) + [ANY] * len(after),
        compiler_params=params(14),
        cost_estimate=BRIEF,
        name="project",
    )(*pieces, w, *after)
    return result[:n], result[n]


def slope_kernel(tok_dev, n, spans, *refs):
    goal, mine, out = refs[0], refs[1], refs[-1]
    whole = refs[2 : 2 + n]
    shares = refs[2 + n : -2]
    for part, (low, high) in enumerate(spans):
        key_proj = mine[low:high, :]
        for product in whole:
            key_proj += product[low:high, :].astype(jnp.float32)
        for product in shares[part :: len(spans)]:
            key_proj += product[...].astype(jnp.float32)
        gap = key_proj - goal[low:high, :].astype(jnp.float32)
        out[low:high, :] = (gap / tok_dev).astype(jnp.bfloat16)


def slope(goal, mine, whole, shares, spans, after):
    return pl.pallas_call(
        functools.partial(slope_kernel, goal.shape[0], len(whole), spans),
        out_shape=jax.ShapeDtypeStruct(mine.shape, jnp.bfloat16),
        in_specs=[VMEM] * (2 + len(whole) + len(shares)) + [ANY],
        compiler_params=params(8),
        cost_estimate=BRIEF,
        name="slope",
    )(goal, mine, *whole, *shares, after)


def as_column(row):
    size = row.shape[1]
    return jnp.broadcast_to(row.astype(jnp.float32), (size, size)).T.astype(jnp.int32)


def pick_columns(wide, column):
    out = jnp.zeros((wide.shape[0], LANES), jnp.float32)
    for c in range(wide.shape[1] // LANES):
        out += jnp.where(column == c, wide[:, c * LANES : (c + 1) * LANES], 0.0)
    return out


def early_kernel(per_row, slot_row, count, fb, after, fbk, keep, token):
    token[...] = jnp.zeros_like(token)
    depth, kw = fb.shape
    cap = slot_row.shape[1]
    slot = as_column(slot_row[...])[:, 0:1]
    hot = slot // per_row == lax.broadcasted_iota(jnp.int32, (cap, depth), 1)
    hot = hot.astype(jnp.float32).astype(jnp.bfloat16)
    used = lax.broadcasted_iota(jnp.int32, (cap, 1), 0) < count[0, 0]
    wide = jnp.dot(hot, fb[...], preferred_element_type=jnp.float32)
    fbk[...] = jnp.where(used, pick_columns(wide, slot % per_row), 0.0)
    group = lax.broadcasted_iota(jnp.int32, (cap, kw), 1) // LANES
    mark = jnp.where(used & (slot % per_row == group), 1.0, 0.0).astype(jnp.bfloat16)
    tile = min(depth, 512)
    for t in range(depth // tile):
        line = lax.broadcasted_iota(jnp.int32, (tile, cap), 0) + t * tile
        hot = (slot_row[...] // per_row == line).astype(jnp.float32).astype(jnp.bfloat16)
        mask = jnp.dot(hot, mark, preferred_element_type=jnp.float32)
        keep[t * tile : (t + 1) * tile, :] = (1.0 - mask).astype(jnp.bfloat16)


def early(slot_row, count, fb, after):
    depth, kw = fb.shape
    cap = slot_row.shape[1]
    return pl.pallas_call(
        functools.partial(early_kernel, kw // LANES),
        out_shape=[
            jax.ShapeDtypeStruct((cap, LANES), jnp.float32),
            jax.ShapeDtypeStruct((depth, kw), jnp.bfloat16),
            TOKEN,
        ],
        in_specs=[VMEM, SMEM, VMEM, ANY],
        compiler_params=params(14),
        cost_estimate=BRIEF,
        name="early",
    )(slot_row, count, fb, after)


def prepare_kernel(per_row, n, *refs):
    xs, (slot_row, count), (xg, xt, token) = refs[:n], refs[n : n + 2], refs[-3:]
    token[...] = jnp.zeros_like(token)
    depth = xs[0].shape[1]
    cap = slot_row.shape[1]
    used = lax.broadcasted_iota(jnp.int32, (cap, 1), 0) < count[0, 0]
    line = jnp.where(used, as_column(slot_row[...])[:, 0:1] // per_row, depth)
    hot = line == lax.broadcasted_iota(jnp.int32, (cap, depth), 1)
    hot = hot.astype(jnp.float32).astype(jnp.bfloat16)
    start = 0
    for x in xs:
        rows = x.shape[0]
        xg[:, start : start + rows] = lax.dot_general(
            hot, x[...], (((1,), (1,)), ((), ())), preferred_element_type=jnp.float32
        ).astype(jnp.bfloat16)
        xt[:, start : start + rows] = x[...].T
        start += rows


def prepare(xs, slot_row, count, per_row, after):
    rows, depth = sum(x.shape[0] for x in xs), xs[0].shape[1]
    cap = slot_row.shape[1]
    return pl.pallas_call(
        functools.partial(prepare_kernel, per_row, len(xs)),
        out_shape=[
            jax.ShapeDtypeStruct((cap, rows), jnp.bfloat16),
            jax.ShapeDtypeStruct((depth, rows), jnp.bfloat16),
            TOKEN,
        ],
        in_specs=[VMEM] * (len(xs) + 1) + [SMEM] + [ANY] * len(after),
        compiler_params=params(14),
        cost_estimate=BRIEF,
        name="prepare",
    )(*xs, slot_row, count, *after)


def stack(slopes, order, s):
    start = 0
    for k, low, high in order:
        s[start : start + high - low, :] = slopes[k][low:high, :]
        start += high - low


def gather_kernel(order, *refs):
    slopes, (xg, out, s) = refs[:-3], refs[-3:]
    stack(slopes, order, s)
    out[...] = jnp.dot(xg[...], s[...], preferred_element_type=jnp.float32)


def gather(slopes, order, xg):
    kw = slopes[0].shape[1]
    return pl.pallas_call(
        functools.partial(gather_kernel, order),
        out_shape=jax.ShapeDtypeStruct((xg.shape[0], kw), jnp.float32),
        scratch_shapes=[pltpu.VMEM((xg.shape[1], kw), jnp.bfloat16)],
        compiler_params=params(8),
        cost_estimate=BRIEF,
        name="gather",
    )(*slopes, xg)


def kept_kernel(per_row, order, *refs):
    slopes, (wide, xg, fbk, slot_row, out, s) = refs[:-6], refs[-6:]
    cap = slot_row.shape[1]
    stack(slopes, order, s)
    total = wide[...] + jnp.dot(xg[...], s[...], preferred_element_type=jnp.float32)
    value = pick_columns(total, as_column(slot_row[...])[:, 0:1] % per_row) + fbk[...]
    out[:cap, :] = value.astype(jnp.bfloat16)
    tail = out.shape[0] - cap
    number = jnp.broadcast_to(slot_row[...], (tail, cap))
    line = lax.broadcasted_iota(jnp.int32, (tail, cap), 0)
    number = jnp.where(line == 0, number // LANES, number % LANES)
    out[cap:, :] = number.astype(jnp.float32).astype(jnp.bfloat16)


def kept(slopes, order, wide, xg, fbk, slot_row):
    cap, kw = wide.shape
    return pl.pallas_call(
        functools.partial(kept_kernel, kw // LANES, order),
        out_shape=jax.ShapeDtypeStruct((cap + 16, LANES), jnp.bfloat16),
        scratch_shapes=[pltpu.VMEM((xg.shape[1], kw), jnp.bfloat16)],
        compiler_params=params(8),
        cost_estimate=BRIEF,
        name="kept",
    )(*slopes, wide, xg, fbk, slot_row)


def send_out(held, out, sems, t, tile):
    share = tile // sems.shape[1]
    spans = [pl.ds(t * tile + k * share, share) for k in range(sems.shape[1])]
    return [
        pltpu.make_async_copy(held.at[rows, :], out.at[rows, :], sems.at[t, k])
        for k, rows in enumerate(spans)
    ]


def residue_kernel(order, tile, *refs):
    n = len({k for k, _, _ in order})
    slopes, xts, (fb, keep, out, token, s, held, sems) = refs[:n], refs[n:-7], refs[-7:]
    token[...] = jnp.zeros_like(token)
    stack(slopes, order, s)
    tiles = out.shape[0] // tile
    for t in range(tiles):
        rows = slice(t * tile, (t + 1) * tile)
        pseudo, start = fb[rows, :].astype(jnp.float32), 0
        for xt in xts:
            part = s[start : start + xt.shape[1], :]
            pseudo += jnp.dot(xt[rows, :], part, preferred_element_type=jnp.float32)
            start += xt.shape[1]
        held[rows, :] = jnp.where(keep[rows, :] > 0, pseudo, 0.0).astype(jnp.bfloat16)
        for copy in send_out(held, out, sems, t, tile):
            copy.start()
    for t in range(tiles):
        for copy in send_out(held, out, sems, t, tile):
            copy.wait()


def residue(slopes, order, xts, fb, keep):
    depth, kw = fb.shape
    total = sum(xt.shape[1] for xt in xts)
    tile = min(depth, 512)
    return pl.pallas_call(
        functools.partial(residue_kernel, order, tile),
        out_shape=[
            jax.ShapeDtypeStruct((depth, kw), jnp.bfloat16),
            TOKEN,
        ],
        in_specs=[VMEM] * (len(slopes) + len(xts) + 2),
        out_specs=[ANY, VMEM],
        scratch_shapes=[
            pltpu.VMEM((total, kw), jnp.bfloat16),
            pltpu.VMEM((depth, kw), jnp.bfloat16),
            pltpu.SemaphoreType.DMA((depth // tile, 4)),
        ],
        compiler_params=params(14),
        cost_estimate=BRIEF,
        name="residue",
    )(*slopes, *xts, fb, keep)


def join_kernel(n, *refs):
    out, start = refs[-1], 0
    for part in refs[:n]:
        out[start : start + part.shape[0], :] = part[...]
        start += part.shape[0]


def join(parts, after):
    rows, lanes = sum(part.shape[0] for part in parts), parts[0].shape[1]
    return pl.pallas_call(
        functools.partial(join_kernel, len(parts)),
        out_shape=jax.ShapeDtypeStruct((rows, lanes), jnp.bfloat16),
        in_specs=[VMEM] * len(parts) + [ANY] * len(after),
        compiler_params=params(8),
        cost_estimate=BRIEF,
        name="join",
    )(*parts, *after)


def spread(group, wide, lines, cap, per_row):
    size = cap + 16
    for k in range(group.shape[0] // size):
        start = k * size
        tail = group[start + cap : start + size, :].astype(jnp.float32)
        number = (tail[0:1, :] * LANES + tail[1:2, :]).astype(jnp.int32)
        lines[:, k * cap : (k + 1) * cap] = jnp.broadcast_to(number // per_row, (8, cap))
        column = jnp.broadcast_to((number % per_row).astype(jnp.float32), (LANES, cap)).T
        value = group[start : start + cap, :].astype(jnp.float32)
        for c in range(per_row):
            wide[k * cap : (k + 1) * cap, c * LANES : (c + 1) * LANES] = jnp.where(
                column == c, value, 0.0
            ).astype(jnp.bfloat16)


def place(lines, wide, t, tile):
    line = lax.broadcasted_iota(jnp.int32, (tile, lines.shape[1]), 0) + t * tile
    hot = (lines[0:1, :] == line).astype(jnp.float32).astype(jnp.bfloat16)
    return jnp.dot(hot, wide[...], preferred_element_type=jnp.float32)


def half_kernel(cap, per_row, tile, group, out, wide, lines):
    spread(group, wide, lines, cap, per_row)
    for t in range(out.shape[0] // tile):
        out[t * tile : (t + 1) * tile, :] = place(lines, wide, t, tile)


def outer_kernel(cap, per_row, tile, n, group, half, out, wide, lines, held, sems):
    spread(group, wide, lines, cap, per_row)
    tiles = out.shape[0] // tile
    for t in range(tiles):
        rows = slice(t * tile, (t + 1) * tile)
        held[rows, :] = (half[rows, :] + place(lines, wide, t, tile)) / n
        for copy in send_out(held, out, sems, t, tile):
            copy.start()
    for t in range(tiles):
        for copy in send_out(held, out, sems, t, tile):
            copy.wait()


def outer(groups, cap, depth, kw):
    slots = groups[0].shape[0] // (cap + 16) * cap
    n = 2 * slots // cap
    tile = min(depth, 512)
    shape = jax.ShapeDtypeStruct((depth, kw), jnp.float32)
    scratch = [pltpu.VMEM((slots, kw), jnp.bfloat16), pltpu.VMEM((8, slots), jnp.int32)]
    half = pl.pallas_call(
        functools.partial(half_kernel, cap, kw // LANES, tile),
        out_shape=shape,
        scratch_shapes=scratch,
        compiler_params=params(14),
        cost_estimate=BRIEF,
        name="half",
    )(groups[0])
    return pl.pallas_call(
        functools.partial(outer_kernel, cap, kw // LANES, tile, n),
        out_shape=shape,
        out_specs=ANY,
        scratch_shapes=scratch
        + [pltpu.VMEM((depth, kw), jnp.float32), pltpu.SemaphoreType.DMA((depth // tile, 4))],
        compiler_params=params(14),
        cost_estimate=BRIEF,
        name="outer",
    )(groups[1], half)


def on_device(inputs, target, weights, feedback, counts, blocks):
    tokens, w, fb = inputs[0], weights[0], feedback[0]
    n_shard, n_rep = lax.axis_size("shard"), lax.axis_size("rep")
    tok_dev = tokens.shape[0]
    depth, kw = w.shape
    early_rows = tok_dev * 3 // 4
    spans = [(0, early_rows), (early_rows, tok_dev)]
    per_row = kw // LANES
    slot_row = blocks[0]
    near = [d for d in range(1, n_shard) if d & (d - 1) == 0]
    far = [d for d in range(1, n_shard) if d & (d - 1) != 0]

    me = lax.axis_index("shard")
    far_out = [lax.dynamic_slice(tokens, (0, (me ^ d) * depth), (tok_dev, depth)) for d in far]
    far_in = [swap(x, "shard", n_shard, d) for x, d in zip(far_out, far)]
    near_out, token = [], far_out[0]
    for low, high in spans:
        *out, token = cut(tokens, depth, [(d, low, high - low) for d in near], [token])
        near_out.append(out)
        if low == 0:
            fbk, keep, token = early(slot_row, counts, fb, token)
    near_in = [[swap(x, "shard", n_shard, d) for x, d in zip(out, near)] for out in near_out]

    own, _ = cut(tokens, depth, [(0, 0, tok_dev)], [token])

    brief, wide = jnp.bfloat16, jnp.float32
    (mine, *products), x_far = project([own] + far_in, [wide] + [brief] * len(far), w, [])
    whole = [swap(p, "shard", n_shard, d) for p, d in zip(products, far)]
    xg_far, xt_far, token = prepare([x_far], slot_row, counts, per_row, [])
    after, shares, x_near = [token], [], []
    for part in range(len(spans)):
        products, x = project(near_in[part], [brief] * len(near), w, after)
        shares.append([swap(p, "shard", n_shard, d) for p, d in zip(products, near)])
        x_near.append(x)
        after = products[-1:]
    xg_near, xt_near, token = prepare(x_near, slot_row, counts, per_row, [products[0]])
    shares = [share[k] for k in range(len(near)) for share in shares]
    slopes = slope(target[0], mine, whole, shares, spans, token)
    slopes = [slopes] + [swap(slopes, "shard", n_shard, d) for d in far + near]

    n_far = 1 + len(far)
    order_far = [(k, 0, tok_dev) for k in range(n_far)]
    order_near = [(k, low, high) for low, high in spans for k in range(len(near))]
    wide = gather(slopes[:n_far], order_far, xg_far)
    message = kept(slopes[n_far:], order_near, wide, xg_near, fbk, slot_row)
    same_core = [swap(message, "rep", n_rep, d) for d in [2, *range(n_rep - 2, 2, -2)]]
    order = order_far + [(n_far + k, low, high) for k, low, high in order_near]
    new_feedback, token = residue(slopes, order, [xt_far, xt_near], fb, keep)
    joined, after = message, [token]
    for received in same_core:
        joined, after = join([joined, received], after), []
    groups = [joined, swap(joined, "rep", n_rep, 1)]
    return outer(groups, message.shape[0] - 16, depth, kw), new_feedback[None]


def solution(mesh):
    placed = (
        P("rep", "shard", None),
        P("rep", "shard", None),
        P("rep", "shard", None),
        P("rep", "shard", None),
        P("rep", "shard"),
        P("rep", "shard", None),
    )
    return jax.shard_map(
        on_device,
        mesh=mesh,
        in_specs=placed,
        out_specs=(P("shard", None), P("rep", "shard", None)),
        check_vma=False,
    )
```

```python
import functools

import jax
import jax.numpy as jnp
from jax import lax
from jax.experimental import pallas as pl
from jax.experimental.pallas import tpu as pltpu
from jax.sharding import PartitionSpec as P

LANES = 128
ANY = pl.BlockSpec(memory_space=pl.ANY)
BRIEF = pl.CostEstimate(flops=1000, bytes_accessed=1000, transcendentals=0)
VMEM = pl.BlockSpec(memory_space=pltpu.VMEM)
SMEM = pl.BlockSpec(memory_space=pltpu.SMEM)
MIB = 1024 * 1024
TOKEN = jax.ShapeDtypeStruct((8, LANES), jnp.float32)


def params(mib):
    return pltpu.CompilerParams(vmem_limit_bytes=mib * MIB)


def swap(x, axis, n, d):
    return lax.ppermute(x, axis, [(i, i ^ d) for i in range(n)])


def cut_kernel(cuts, tokens, *refs):
    outs, (token, sems) = refs[-len(cuts) - 2 : -2], refs[-2:]
    token[...] = jnp.zeros_like(token)
    me = lax.axis_index("shard")
    copies = []
    for k, (d, low, rows) in enumerate(cuts):
        depth = outs[k].shape[1]
        columns = pl.ds(pl.multiple_of((me ^ d) * depth, LANES), depth)
        copy = pltpu.make_async_copy(tokens.at[pl.ds(low, rows), columns], outs[k], sems.at[k])
        copy.start()
        copies.append(copy)
    for copy in copies:
        copy.wait()


def cut(tokens, depth, cuts, after):
    return pl.pallas_call(
        functools.partial(cut_kernel, cuts),
        out_shape=[jax.ShapeDtypeStruct((rows, depth), tokens.dtype) for _, _, rows in cuts]
        + [TOKEN],
        in_specs=[ANY] * (1 + len(after)),
        out_specs=[ANY] * len(cuts) + [VMEM],
        scratch_shapes=[pltpu.SemaphoreType.DMA((len(cuts),))],
        compiler_params=params(6),
        cost_estimate=BRIEF,
        name="cut",
    )(tokens, *after)


def project_kernel(n, m, *refs):
    pieces, w, outs, x = refs[:n], refs[n], refs[-m - 1 : -1], refs[-1]
    start = 0
    for piece in pieces:
        x[start : start + piece.shape[0], :] = piece[...]
        start += piece.shape[0]
    full = jnp.dot(x[...], w[...], preferred_element_type=jnp.float32)
    start = 0
    for out in outs:
        out[...] = full[start : start + out.shape[0], :].astype(out.dtype)
        start += out.shape[0]


def project(pieces, outs, w, after):
    n = len(pieces)
    rows, depth = sum(p.shape[0] for p in pieces), pieces[0].shape[1]
    kw = w.shape[1]
    result = pl.pallas_call(
        functools.partial(project_kernel, n, len(outs)),
        out_shape=[jax.ShapeDtypeStruct((r, kw), t) for r, t in outs]
        + [jax.ShapeDtypeStruct((rows, depth), jnp.bfloat16)],
        in_specs=[VMEM] * (n + 1) + [ANY] * len(after),
        compiler_params=params(14),
        cost_estimate=BRIEF,
        name="project",
    )(*pieces, w, *after)
    return result[:-1], result[-1]


def slope_kernel(tok_dev, n, spans, *refs):
    goal, mine, out = refs[0], refs[1], refs[-1]
    whole = refs[2 : 2 + n]
    shares = refs[2 + n : -2]
    for part, (low, high) in enumerate(spans):
        key_proj = mine[low:high, :]
        for product in whole:
            key_proj += product[low:high, :].astype(jnp.float32)
        for product in shares[part :: len(spans)]:
            key_proj += product[...].astype(jnp.float32)
        gap = key_proj - goal[low:high, :].astype(jnp.float32)
        out[low:high, :] = (gap / tok_dev).astype(jnp.bfloat16)


def slope(goal, mine, whole, shares, spans, after):
    return pl.pallas_call(
        functools.partial(slope_kernel, goal.shape[0], len(whole), spans),
        out_shape=jax.ShapeDtypeStruct(mine.shape, jnp.bfloat16),
        in_specs=[VMEM] * (2 + len(whole) + len(shares)) + [ANY],
        compiler_params=params(8),
        cost_estimate=BRIEF,
        name="slope",
    )(goal, mine, *whole, *shares, after)


def as_column(row):
    size = row.shape[1]
    return jnp.broadcast_to(row.astype(jnp.float32), (size, size)).T.astype(jnp.int32)


def pick_columns(wide, column):
    out = jnp.zeros((wide.shape[0], LANES), jnp.float32)
    for c in range(wide.shape[1] // LANES):
        out += jnp.where(column == c, wide[:, c * LANES : (c + 1) * LANES], 0.0)
    return out


def early_kernel(per_row, slot_row, count, fb, after, fbk, keep, token):
    token[...] = jnp.zeros_like(token)
    depth, kw = fb.shape
    cap = slot_row.shape[1]
    slot = as_column(slot_row[...])[:, 0:1]
    hot = slot // per_row == lax.broadcasted_iota(jnp.int32, (cap, depth), 1)
    hot = hot.astype(jnp.float32).astype(jnp.bfloat16)
    used = lax.broadcasted_iota(jnp.int32, (cap, 1), 0) < count[0, 0]
    wide = jnp.dot(hot, fb[...], preferred_element_type=jnp.float32)
    fbk[...] = jnp.where(used, pick_columns(wide, slot % per_row), 0.0)
    group = lax.broadcasted_iota(jnp.int32, (cap, kw), 1) // LANES
    mark = jnp.where(used & (slot % per_row == group), 1.0, 0.0).astype(jnp.bfloat16)
    tile = min(depth, 512)
    for t in range(depth // tile):
        line = lax.broadcasted_iota(jnp.int32, (tile, cap), 0) + t * tile
        hot = (slot_row[...] // per_row == line).astype(jnp.float32).astype(jnp.bfloat16)
        mask = jnp.dot(hot, mark, preferred_element_type=jnp.float32)
        keep[t * tile : (t + 1) * tile, :] = (1.0 - mask).astype(jnp.bfloat16)


def early(slot_row, count, fb, after):
    depth, kw = fb.shape
    cap = slot_row.shape[1]
    return pl.pallas_call(
        functools.partial(early_kernel, kw // LANES),
        out_shape=[
            jax.ShapeDtypeStruct((cap, LANES), jnp.float32),
            jax.ShapeDtypeStruct((depth, kw), jnp.bfloat16),
            TOKEN,
        ],
        in_specs=[VMEM, SMEM, VMEM, ANY],
        compiler_params=params(14),
        cost_estimate=BRIEF,
        name="early",
    )(slot_row, count, fb, after)


def prepare_kernel(per_row, n, *refs):
    xs, (slot_row, count), (xg, xt, token) = refs[:n], refs[n : n + 2], refs[-3:]
    token[...] = jnp.zeros_like(token)
    depth = xs[0].shape[1]
    cap = slot_row.shape[1]
    used = lax.broadcasted_iota(jnp.int32, (cap, 1), 0) < count[0, 0]
    line = jnp.where(used, as_column(slot_row[...])[:, 0:1] // per_row, depth)
    hot = line == lax.broadcasted_iota(jnp.int32, (cap, depth), 1)
    hot = hot.astype(jnp.float32).astype(jnp.bfloat16)
    start = 0
    for x in xs:
        rows = x.shape[0]
        xg[:, start : start + rows] = lax.dot_general(
            hot, x[...], (((1,), (1,)), ((), ())), preferred_element_type=jnp.float32
        ).astype(jnp.bfloat16)
        xt[:, start : start + rows] = x[...].T
        start += rows


def prepare(xs, slot_row, count, per_row, after):
    rows, depth = sum(x.shape[0] for x in xs), xs[0].shape[1]
    cap = slot_row.shape[1]
    return pl.pallas_call(
        functools.partial(prepare_kernel, per_row, len(xs)),
        out_shape=[
            jax.ShapeDtypeStruct((cap, rows), jnp.bfloat16),
            jax.ShapeDtypeStruct((depth, rows), jnp.bfloat16),
            TOKEN,
        ],
        in_specs=[VMEM] * (len(xs) + 1) + [SMEM] + [ANY] * len(after),
        compiler_params=params(14),
        cost_estimate=BRIEF,
        name="prepare",
    )(*xs, slot_row, count, *after)


def stack(slopes, order, s):
    start = 0
    for k, low, high in order:
        s[start : start + high - low, :] = slopes[k][low:high, :]
        start += high - low


def gather_kernel(order, *refs):
    slopes, (xg, out, s) = refs[:-3], refs[-3:]
    stack(slopes, order, s)
    out[...] = jnp.dot(xg[...], s[...], preferred_element_type=jnp.float32)


def gather(slopes, order, xg):
    kw = slopes[0].shape[1]
    return pl.pallas_call(
        functools.partial(gather_kernel, order),
        out_shape=jax.ShapeDtypeStruct((xg.shape[0], kw), jnp.float32),
        scratch_shapes=[pltpu.VMEM((xg.shape[1], kw), jnp.bfloat16)],
        compiler_params=params(8),
        cost_estimate=BRIEF,
        name="gather",
    )(*slopes, xg)


def kept_kernel(per_row, order, *refs):
    slopes, (wide, xg, fbk, slot_row, out, s) = refs[:-6], refs[-6:]
    cap = slot_row.shape[1]
    stack(slopes, order, s)
    total = wide[...] + jnp.dot(xg[...], s[...], preferred_element_type=jnp.float32)
    value = pick_columns(total, as_column(slot_row[...])[:, 0:1] % per_row) + fbk[...]
    out[:cap, :] = value.astype(jnp.bfloat16)
    tail = out.shape[0] - cap
    number = jnp.broadcast_to(slot_row[...], (tail, cap))
    line = lax.broadcasted_iota(jnp.int32, (tail, cap), 0)
    number = jnp.where(line == 0, number // LANES, number % LANES)
    out[cap:, :] = number.astype(jnp.float32).astype(jnp.bfloat16)


def kept(slopes, order, wide, xg, fbk, slot_row):
    cap, kw = wide.shape
    return pl.pallas_call(
        functools.partial(kept_kernel, kw // LANES, order),
        out_shape=jax.ShapeDtypeStruct((cap + 16, LANES), jnp.bfloat16),
        scratch_shapes=[pltpu.VMEM((xg.shape[1], kw), jnp.bfloat16)],
        compiler_params=params(8),
        cost_estimate=BRIEF,
        name="kept",
    )(*slopes, wide, xg, fbk, slot_row)


def send_out(held, out, sems, t, tile):
    rows = pl.ds(t * tile, tile)
    return pltpu.make_async_copy(held.at[rows, :], out.at[rows, :], sems.at[t])


def residue_kernel(order, tile, *refs):
    n = len({k for k, _, _ in order})
    slopes, xts, (fb, keep, out, token, s, held, sems) = refs[:n], refs[n:-7], refs[-7:]
    token[...] = jnp.zeros_like(token)
    stack(slopes, order, s)
    tiles = out.shape[0] // tile
    for t in range(tiles):
        rows = slice(t * tile, (t + 1) * tile)
        pseudo, start = fb[rows, :].astype(jnp.float32), 0
        for xt in xts:
            part = s[start : start + xt.shape[1], :]
            pseudo += jnp.dot(xt[rows, :], part, preferred_element_type=jnp.float32)
            start += xt.shape[1]
        held[rows, :] = jnp.where(keep[rows, :] > 0, pseudo, 0.0).astype(jnp.bfloat16)
        send_out(held, out, sems, t, tile).start()
    for t in range(tiles):
        send_out(held, out, sems, t, tile).wait()


def residue(slopes, order, xts, fb, keep):
    depth, kw = fb.shape
    total = sum(xt.shape[1] for xt in xts)
    tile = min(depth, 512)
    return pl.pallas_call(
        functools.partial(residue_kernel, order, tile),
        out_shape=[
            jax.ShapeDtypeStruct((depth, kw), jnp.bfloat16),
            TOKEN,
        ],
        in_specs=[VMEM] * (len(slopes) + len(xts) + 2),
        out_specs=[ANY, VMEM],
        scratch_shapes=[
            pltpu.VMEM((total, kw), jnp.bfloat16),
            pltpu.VMEM((depth, kw), jnp.bfloat16),
            pltpu.SemaphoreType.DMA((depth // tile,)),
        ],
        compiler_params=params(14),
        cost_estimate=BRIEF,
        name="residue",
    )(*slopes, *xts, fb, keep)


def join_kernel(n, *refs):
    out, start = refs[-1], 0
    for part in refs[:n]:
        out[start : start + part.shape[0], :] = part[...]
        start += part.shape[0]


def join(parts, after):
    rows, lanes = sum(part.shape[0] for part in parts), parts[0].shape[1]
    return pl.pallas_call(
        functools.partial(join_kernel, len(parts)),
        out_shape=jax.ShapeDtypeStruct((rows, lanes), jnp.bfloat16),
        in_specs=[VMEM] * len(parts) + [ANY] * len(after),
        compiler_params=params(8),
        cost_estimate=BRIEF,
        name="join",
    )(*parts, *after)


def spread(group, wide, lines, cap, per_row):
    size = cap + 16
    for k in range(group.shape[0] // size):
        start = k * size
        tail = group[start + cap : start + size, :].astype(jnp.float32)
        number = (tail[0:1, :] * LANES + tail[1:2, :]).astype(jnp.int32)
        lines[:, k * cap : (k + 1) * cap] = jnp.broadcast_to(number // per_row, (8, cap))
        column = jnp.broadcast_to((number % per_row).astype(jnp.float32), (LANES, cap)).T
        value = group[start : start + cap, :].astype(jnp.float32)
        for c in range(per_row):
            wide[k * cap : (k + 1) * cap, c * LANES : (c + 1) * LANES] = jnp.where(
                column == c, value, 0.0
            ).astype(jnp.bfloat16)


def place(lines, wide, t, tile):
    line = lax.broadcasted_iota(jnp.int32, (tile, lines.shape[1]), 0) + t * tile
    hot = (lines[0:1, :] == line).astype(jnp.float32).astype(jnp.bfloat16)
    return jnp.dot(hot, wide[...], preferred_element_type=jnp.float32)


def half_kernel(cap, per_row, tile, group, out, wide, lines):
    spread(group, wide, lines, cap, per_row)
    for t in range(out.shape[0] // tile):
        out[t * tile : (t + 1) * tile, :] = place(lines, wide, t, tile)


def outer_kernel(cap, per_row, tile, n, group, half, out, wide, lines, held, sems):
    spread(group, wide, lines, cap, per_row)
    tiles = out.shape[0] // tile
    for t in range(tiles):
        rows = slice(t * tile, (t + 1) * tile)
        held[rows, :] = (half[rows, :] + place(lines, wide, t, tile)) * (1.0 / n)
        send_out(held, out, sems, t, tile).start()
    for t in range(tiles):
        send_out(held, out, sems, t, tile).wait()


def outer(groups, cap, depth, kw):
    slots = groups[0].shape[0] // (cap + 16) * cap
    n = 2 * slots // cap
    tile = min(depth, 512)
    shape = jax.ShapeDtypeStruct((depth, kw), jnp.float32)
    scratch = [pltpu.VMEM((slots, kw), jnp.bfloat16), pltpu.VMEM((8, slots), jnp.int32)]
    half = pl.pallas_call(
        functools.partial(half_kernel, cap, kw // LANES, tile),
        out_shape=shape,
        scratch_shapes=scratch,
        compiler_params=params(14),
        cost_estimate=BRIEF,
        name="half",
    )(groups[0])
    return pl.pallas_call(
        functools.partial(outer_kernel, cap, kw // LANES, tile, n),
        out_shape=shape,
        out_specs=ANY,
        scratch_shapes=scratch
        + [pltpu.VMEM((depth, kw), jnp.float32), pltpu.SemaphoreType.DMA((depth // tile,))],
        compiler_params=params(14),
        cost_estimate=BRIEF,
        name="outer",
    )(groups[1], half)


def on_device(inputs, target, weights, feedback, counts, blocks):
    tokens, w, fb = inputs[0], weights[0], feedback[0]
    n_shard, n_rep = lax.axis_size("shard"), lax.axis_size("rep")
    tok_dev = tokens.shape[0]
    depth, kw = w.shape
    early_rows = tok_dev * 3 // 4
    spans = [(0, early_rows), (early_rows, tok_dev)]
    per_row = kw // LANES
    slot_row = blocks[0]
    near = [d for d in range(1, n_shard) if d & (d - 1) == 0]
    far = [d for d in range(1, n_shard) if d & (d - 1) != 0]

    me = lax.axis_index("shard")
    first = tok_dev // 4
    far_out, rest = [], tokens
    for low, high in [(0, first), (first, tok_dev)]:
        out = [lax.dynamic_slice(rest, (low, (me ^ d) * depth), (high - low, depth)) for d in far]
        rest, *out = lax.optimization_barrier((rest, *out))
        far_out.append(out)
    far_in = [[swap(x, "shard", n_shard, d) for x in xs] for d, xs in zip(far, zip(*far_out))]
    near_out, token = [], far_out[1][0]
    for low, high in spans:
        *out, token = cut(tokens, depth, [(d, low, high - low) for d in near], [token])
        near_out.append(out)
        if low == 0:
            fbk, keep, token = early(slot_row, counts, fb, token)
    near_in = [[swap(x, "shard", n_shard, d) for x, d in zip(out, near)] for out in near_out]

    own, _ = cut(tokens, depth, [(0, 0, tok_dev)], [token])

    brief, wide = jnp.bfloat16, jnp.float32
    outs = [(tok_dev, wide)] + [(tok_dev, brief)] * len(far)
    (mine, *products), x_far = project([own] + sum(far_in, []), outs, w, [])
    whole = [swap(p, "shard", n_shard, d) for p, d in zip(products, far)]
    xg_far, xt_far, token = prepare([x_far], slot_row, counts, per_row, [])
    after, shares, x_near = [token], [], []
    for part, (low, high) in enumerate(spans):
        outs = [(high - low, brief)] * len(near)
        products, x = project(near_in[part], outs, w, after)
        shares.append([swap(p, "shard", n_shard, d) for p, d in zip(products, near)])
        x_near.append(x)
        after = products[-1:]
    xg_near, xt_near, token = prepare(x_near, slot_row, counts, per_row, [products[0]])
    shares = [share[k] for k in range(len(near)) for share in shares]
    slopes = slope(target[0], mine, whole, shares, spans, token)
    slopes = [slopes] + [swap(slopes, "shard", n_shard, d) for d in far + near]

    n_far = 1 + len(far)
    order_far = [(k, 0, tok_dev) for k in range(n_far)]
    order_near = [(k, low, high) for low, high in spans for k in range(len(near))]
    wide = gather(slopes[:n_far], order_far, xg_far)
    message = kept(slopes[n_far:], order_near, wide, xg_near, fbk, slot_row)
    same_core = [swap(message, "rep", n_rep, d) for d in range(n_rep - 2, 0, -2)]
    order = order_far + [(n_far + k, low, high) for k, low, high in order_near]
    new_feedback, token = residue(slopes, order, [xt_far, xt_near], fb, keep)
    joined, after = message, [token]
    for received in same_core:
        joined, after = join([joined, received], after), []
    groups = [joined, swap(joined, "rep", n_rep, 1)]
    return outer(groups, message.shape[0] - 16, depth, kw), new_feedback[None]


def solution(mesh):
    placed = (
        P("rep", "shard", None),
        P("rep", "shard", None),
        P("rep", "shard", None),
        P("rep", "shard", None),
        P("rep", "shard"),
        P("rep", "shard", None),
    )
    return jax.shard_map(
        on_device,
        mesh=mesh,
        in_specs=placed,
        out_specs=(P("shard", None), P("rep", "shard", None)),
        check_vma=False,
    )
```

```python
import functools

import jax
import jax.numpy as jnp
from jax import lax
from jax.experimental import pallas as pl
from jax.experimental.pallas import tpu as pltpu
from jax.sharding import PartitionSpec as P

LANES = 128
ANY = pl.BlockSpec(memory_space=pl.ANY)
BRIEF = pl.CostEstimate(flops=1000, bytes_accessed=1000, transcendentals=0)
VMEM = pl.BlockSpec(memory_space=pltpu.VMEM)
SMEM = pl.BlockSpec(memory_space=pltpu.SMEM)
MIB = 1024 * 1024
TOKEN = jax.ShapeDtypeStruct((8, LANES), jnp.float32)


def params(mib):
    return pltpu.CompilerParams(vmem_limit_bytes=mib * MIB)


def swap(x, axis, n, d):
    return lax.ppermute(x, axis, [(i, i ^ d) for i in range(n)])


def cut_kernel(cuts, tokens, *refs):
    outs, (token, sems) = refs[-len(cuts) - 2 : -2], refs[-2:]
    token[...] = jnp.zeros_like(token)
    me = lax.axis_index("shard")
    copies = []
    for k, (d, low, rows) in enumerate(cuts):
        depth = outs[k].shape[1]
        columns = pl.ds(pl.multiple_of((me ^ d) * depth, LANES), depth)
        copy = pltpu.make_async_copy(tokens.at[pl.ds(low, rows), columns], outs[k], sems.at[k])
        copy.start()
        copies.append(copy)
    for copy in copies:
        copy.wait()


def cut(tokens, depth, cuts, after):
    return pl.pallas_call(
        functools.partial(cut_kernel, cuts),
        out_shape=[jax.ShapeDtypeStruct((rows, depth), tokens.dtype) for _, _, rows in cuts]
        + [TOKEN],
        in_specs=[ANY] * (1 + len(after)),
        out_specs=[ANY] * len(cuts) + [VMEM],
        scratch_shapes=[pltpu.SemaphoreType.DMA((len(cuts),))],
        compiler_params=params(6),
        cost_estimate=BRIEF,
        name="cut",
    )(tokens, *after)


def project_kernel(n, *refs):
    pieces, w, outs, x = refs[:n], refs[n], refs[-n - 1 : -1], refs[-1]
    start = 0
    for piece in pieces:
        x[start : start + piece.shape[0], :] = piece[...]
        start += piece.shape[0]
    full = jnp.dot(x[...], w[...], preferred_element_type=jnp.float32)
    start = 0
    for out in outs:
        out[...] = full[start : start + out.shape[0], :].astype(out.dtype)
        start += out.shape[0]


def project(pieces, types, w, after):
    n = len(pieces)
    rows, depth = sum(p.shape[0] for p in pieces), pieces[0].shape[1]
    kw = w.shape[1]
    result = pl.pallas_call(
        functools.partial(project_kernel, n),
        out_shape=[jax.ShapeDtypeStruct((p.shape[0], kw), t) for p, t in zip(pieces, types)]
        + [jax.ShapeDtypeStruct((rows, depth), jnp.bfloat16)],
        in_specs=[VMEM] * (n + 1) + [ANY] * len(after),
        compiler_params=params(14),
        cost_estimate=BRIEF,
        name="project",
    )(*pieces, w, *after)
    return result[:n], result[n]


def slope_kernel(tok_dev, n, spans, *refs):
    goal, mine, out = refs[0], refs[1], refs[-1]
    whole = refs[2 : 2 + n]
    shares = refs[2 + n : -2]
    for part, (low, high) in enumerate(spans):
        key_proj = mine[low:high, :]
        for product in whole:
            key_proj += product[low:high, :].astype(jnp.float32)
        for product in shares[part :: len(spans)]:
            key_proj += product[...].astype(jnp.float32)
        gap = key_proj - goal[low:high, :].astype(jnp.float32)
        out[low:high, :] = (gap / tok_dev).astype(jnp.bfloat16)


def slope(goal, mine, whole, shares, spans, after):
    return pl.pallas_call(
        functools.partial(slope_kernel, goal.shape[0], len(whole), spans),
        out_shape=jax.ShapeDtypeStruct(mine.shape, jnp.bfloat16),
        in_specs=[VMEM] * (2 + len(whole) + len(shares)) + [ANY],
        compiler_params=params(8),
        cost_estimate=BRIEF,
        name="slope",
    )(goal, mine, *whole, *shares, after)


def as_column(row):
    size = row.shape[1]
    return jnp.broadcast_to(row.astype(jnp.float32), (size, size)).T.astype(jnp.int32)


def pick_columns(wide, column):
    out = jnp.zeros((wide.shape[0], LANES), jnp.float32)
    for c in range(wide.shape[1] // LANES):
        out += jnp.where(column == c, wide[:, c * LANES : (c + 1) * LANES], 0.0)
    return out


def early_kernel(per_row, slot_row, count, fb, after, fbk, keep, token):
    token[...] = jnp.zeros_like(token)
    depth, kw = fb.shape
    cap = slot_row.shape[1]
    slot = as_column(slot_row[...])[:, 0:1]
    hot = slot // per_row == lax.broadcasted_iota(jnp.int32, (cap, depth), 1)
    hot = hot.astype(jnp.float32).astype(jnp.bfloat16)
    used = lax.broadcasted_iota(jnp.int32, (cap, 1), 0) < count[0, 0]
    wide = jnp.dot(hot, fb[...], preferred_element_type=jnp.float32)
    fbk[...] = jnp.where(used, pick_columns(wide, slot % per_row), 0.0)
    group = lax.broadcasted_iota(jnp.int32, (cap, kw), 1) // LANES
    mark = jnp.where(used & (slot % per_row == group), 1.0, 0.0).astype(jnp.bfloat16)
    tile = min(depth, 512)
    for t in range(depth // tile):
        line = lax.broadcasted_iota(jnp.int32, (tile, cap), 0) + t * tile
        hot = (slot_row[...] // per_row == line).astype(jnp.float32).astype(jnp.bfloat16)
        mask = jnp.dot(hot, mark, preferred_element_type=jnp.float32)
        keep[t * tile : (t + 1) * tile, :] = (1.0 - mask).astype(jnp.bfloat16)


def early(slot_row, count, fb, after):
    depth, kw = fb.shape
    cap = slot_row.shape[1]
    return pl.pallas_call(
        functools.partial(early_kernel, kw // LANES),
        out_shape=[
            jax.ShapeDtypeStruct((cap, LANES), jnp.float32),
            jax.ShapeDtypeStruct((depth, kw), jnp.bfloat16),
            TOKEN,
        ],
        in_specs=[VMEM, SMEM, VMEM, ANY],
        compiler_params=params(14),
        cost_estimate=BRIEF,
        name="early",
    )(slot_row, count, fb, after)


def prepare_kernel(per_row, n, *refs):
    xs, (slot_row, count), (xg, xt, token) = refs[:n], refs[n : n + 2], refs[-3:]
    token[...] = jnp.zeros_like(token)
    depth = xs[0].shape[1]
    cap = slot_row.shape[1]
    used = lax.broadcasted_iota(jnp.int32, (cap, 1), 0) < count[0, 0]
    line = jnp.where(used, as_column(slot_row[...])[:, 0:1] // per_row, depth)
    hot = line == lax.broadcasted_iota(jnp.int32, (cap, depth), 1)
    hot = hot.astype(jnp.float32).astype(jnp.bfloat16)
    start = 0
    for x in xs:
        rows = x.shape[0]
        xg[:, start : start + rows] = lax.dot_general(
            hot, x[...], (((1,), (1,)), ((), ())), preferred_element_type=jnp.float32
        ).astype(jnp.bfloat16)
        xt[:, start : start + rows] = x[...].T
        start += rows


def prepare(xs, slot_row, count, per_row, after):
    rows, depth = sum(x.shape[0] for x in xs), xs[0].shape[1]
    cap = slot_row.shape[1]
    return pl.pallas_call(
        functools.partial(prepare_kernel, per_row, len(xs)),
        out_shape=[
            jax.ShapeDtypeStruct((cap, rows), jnp.bfloat16),
            jax.ShapeDtypeStruct((depth, rows), jnp.bfloat16),
            TOKEN,
        ],
        in_specs=[VMEM] * (len(xs) + 1) + [SMEM] + [ANY] * len(after),
        compiler_params=params(14),
        cost_estimate=BRIEF,
        name="prepare",
    )(*xs, slot_row, count, *after)


def stack(slopes, order, s):
    start = 0
    for k, low, high in order:
        s[start : start + high - low, :] = slopes[k][low:high, :]
        start += high - low


def gather_kernel(order, *refs):
    slopes, (xg, out, s) = refs[:-3], refs[-3:]
    stack(slopes, order, s)
    out[...] = jnp.dot(xg[...], s[...], preferred_element_type=jnp.float32)


def gather(slopes, order, xg):
    kw = slopes[0].shape[1]
    return pl.pallas_call(
        functools.partial(gather_kernel, order),
        out_shape=jax.ShapeDtypeStruct((xg.shape[0], kw), jnp.float32),
        scratch_shapes=[pltpu.VMEM((xg.shape[1], kw), jnp.bfloat16)],
        compiler_params=params(8),
        cost_estimate=BRIEF,
        name="gather",
    )(*slopes, xg)


def kept_kernel(per_row, order, *refs):
    slopes, (wide, xg, fbk, slot_row, out, s) = refs[:-6], refs[-6:]
    cap = slot_row.shape[1]
    stack(slopes, order, s)
    total = wide[...] + jnp.dot(xg[...], s[...], preferred_element_type=jnp.float32)
    value = pick_columns(total, as_column(slot_row[...])[:, 0:1] % per_row) + fbk[...]
    out[:cap, :] = value.astype(jnp.bfloat16)
    tail = out.shape[0] - cap
    number = jnp.broadcast_to(slot_row[...], (tail, cap))
    line = lax.broadcasted_iota(jnp.int32, (tail, cap), 0)
    number = jnp.where(line == 0, number // LANES, number % LANES)
    out[cap:, :] = number.astype(jnp.float32).astype(jnp.bfloat16)


def kept(slopes, order, wide, xg, fbk, slot_row):
    cap, kw = wide.shape
    return pl.pallas_call(
        functools.partial(kept_kernel, kw // LANES, order),
        out_shape=jax.ShapeDtypeStruct((cap + 16, LANES), jnp.bfloat16),
        scratch_shapes=[pltpu.VMEM((xg.shape[1], kw), jnp.bfloat16)],
        compiler_params=params(8),
        cost_estimate=BRIEF,
        name="kept",
    )(*slopes, wide, xg, fbk, slot_row)


def send_out(held, out, sems, t, tile):
    rows = pl.ds(t * tile, tile)
    return pltpu.make_async_copy(held.at[rows, :], out.at[rows, :], sems.at[t])


def residue_kernel(order, tile, *refs):
    n = len({k for k, _, _ in order})
    slopes, xts, (fb, keep, out, token, s, held, sems) = refs[:n], refs[n:-7], refs[-7:]
    token[...] = jnp.zeros_like(token)
    stack(slopes, order, s)
    tiles = out.shape[0] // tile
    for t in range(tiles):
        rows = slice(t * tile, (t + 1) * tile)
        pseudo, start = fb[rows, :].astype(jnp.float32), 0
        for xt in xts:
            part = s[start : start + xt.shape[1], :]
            pseudo += jnp.dot(xt[rows, :], part, preferred_element_type=jnp.float32)
            start += xt.shape[1]
        held[rows, :] = jnp.where(keep[rows, :] > 0, pseudo, 0.0).astype(jnp.bfloat16)
        send_out(held, out, sems, t, tile).start()
    for t in range(tiles):
        send_out(held, out, sems, t, tile).wait()


def residue(slopes, order, xts, fb, keep):
    depth, kw = fb.shape
    total = sum(xt.shape[1] for xt in xts)
    tile = min(depth, 512)
    return pl.pallas_call(
        functools.partial(residue_kernel, order, tile),
        out_shape=[
            jax.ShapeDtypeStruct((depth, kw), jnp.bfloat16),
            TOKEN,
        ],
        in_specs=[VMEM] * (len(slopes) + len(xts) + 2),
        out_specs=[ANY, VMEM],
        scratch_shapes=[
            pltpu.VMEM((total, kw), jnp.bfloat16),
            pltpu.VMEM((depth, kw), jnp.bfloat16),
            pltpu.SemaphoreType.DMA((depth // tile,)),
        ],
        compiler_params=params(14),
        cost_estimate=BRIEF,
        name="residue",
    )(*slopes, *xts, fb, keep)


def join_kernel(n, *refs):
    out, start = refs[-1], 0
    for part in refs[:n]:
        out[start : start + part.shape[0], :] = part[...]
        start += part.shape[0]


def join(parts, after):
    rows, lanes = sum(part.shape[0] for part in parts), parts[0].shape[1]
    return pl.pallas_call(
        functools.partial(join_kernel, len(parts)),
        out_shape=jax.ShapeDtypeStruct((rows, lanes), jnp.bfloat16),
        in_specs=[VMEM] * len(parts) + [ANY] * len(after),
        compiler_params=params(8),
        cost_estimate=BRIEF,
        name="join",
    )(*parts, *after)


def spread(group, wide, lines, cap, per_row):
    size = cap + 16
    for k in range(group.shape[0] // size):
        start = k * size
        tail = group[start + cap : start + size, :].astype(jnp.float32)
        number = (tail[0:1, :] * LANES + tail[1:2, :]).astype(jnp.int32)
        lines[:, k * cap : (k + 1) * cap] = jnp.broadcast_to(number // per_row, (8, cap))
        column = jnp.broadcast_to((number % per_row).astype(jnp.float32), (LANES, cap)).T
        value = group[start : start + cap, :].astype(jnp.float32)
        for c in range(per_row):
            wide[k * cap : (k + 1) * cap, c * LANES : (c + 1) * LANES] = jnp.where(
                column == c, value, 0.0
            ).astype(jnp.bfloat16)


def place(lines, wide, t, tile):
    line = lax.broadcasted_iota(jnp.int32, (tile, lines.shape[1]), 0) + t * tile
    hot = (lines[0:1, :] == line).astype(jnp.float32).astype(jnp.bfloat16)
    return jnp.dot(hot, wide[...], preferred_element_type=jnp.float32)


def half_kernel(cap, per_row, tile, group, out, wide, lines):
    spread(group, wide, lines, cap, per_row)
    for t in range(out.shape[0] // tile):
        out[t * tile : (t + 1) * tile, :] = place(lines, wide, t, tile)


def outer_kernel(cap, per_row, tile, n, group, half, out, wide, lines, held, sems):
    spread(group, wide, lines, cap, per_row)
    tiles = out.shape[0] // tile
    for t in range(tiles):
        rows = slice(t * tile, (t + 1) * tile)
        held[rows, :] = (half[rows, :] + place(lines, wide, t, tile)) * (1.0 / n)
        send_out(held, out, sems, t, tile).start()
    for t in range(tiles):
        send_out(held, out, sems, t, tile).wait()


def outer(groups, cap, depth, kw):
    slots = groups[0].shape[0] // (cap + 16) * cap
    n = 2 * slots // cap
    tile = min(depth, 256)
    shape = jax.ShapeDtypeStruct((depth, kw), jnp.float32)
    scratch = [pltpu.VMEM((slots, kw), jnp.bfloat16), pltpu.VMEM((8, slots), jnp.int32)]
    half = pl.pallas_call(
        functools.partial(half_kernel, cap, kw // LANES, tile),
        out_shape=shape,
        scratch_shapes=scratch,
        compiler_params=params(14),
        cost_estimate=BRIEF,
        name="half",
    )(groups[0])
    return pl.pallas_call(
        functools.partial(outer_kernel, cap, kw // LANES, tile, n),
        out_shape=shape,
        out_specs=ANY,
        scratch_shapes=scratch
        + [pltpu.VMEM((depth, kw), jnp.float32), pltpu.SemaphoreType.DMA((depth // tile,))],
        compiler_params=params(14),
        cost_estimate=BRIEF,
        name="outer",
    )(groups[1], half)


def on_device(inputs, target, weights, feedback, counts, blocks):
    tokens, w, fb = inputs[0], weights[0], feedback[0]
    n_shard, n_rep = lax.axis_size("shard"), lax.axis_size("rep")
    tok_dev = tokens.shape[0]
    depth, kw = w.shape
    early_rows = tok_dev * 3 // 4
    spans = [(0, early_rows), (early_rows, tok_dev)]
    per_row = kw // LANES
    slot_row = blocks[0]
    near = [d for d in range(1, n_shard) if d & (d - 1) == 0]
    far = [d for d in range(1, n_shard) if d & (d - 1) != 0]

    me = lax.axis_index("shard")
    far_out = [lax.dynamic_slice(tokens, (0, (me ^ d) * depth), (tok_dev, depth)) for d in far]
    far_in = [swap(x, "shard", n_shard, d) for x, d in zip(far_out, far)]
    near_out, token = [], far_out[0]
    for low, high in spans:
        *out, token = cut(tokens, depth, [(d, low, high - low) for d in near], [token])
        near_out.append(out)
        if low == 0:
            fbk, keep, token = early(slot_row, counts, fb, token)
    near_in = [[swap(x, "shard", n_shard, d) for x, d in zip(out, near)] for out in near_out]

    own, _ = cut(tokens, depth, [(0, 0, tok_dev)], [token])

    brief, wide = jnp.bfloat16, jnp.float32
    (mine, *products), x_far = project([own] + far_in, [wide] + [brief] * len(far), w, [])
    whole = [swap(p, "shard", n_shard, d) for p, d in zip(products, far)]
    xg_far, xt_far, token = prepare([x_far], slot_row, counts, per_row, [])
    after, shares, x_near = [token], [], []
    for part in range(len(spans)):
        products, x = project(near_in[part], [brief] * len(near), w, after)
        shares.append([swap(p, "shard", n_shard, d) for p, d in zip(products, near)])
        x_near.append(x)
        after = products[-1:]
    xg_near, xt_near, token = prepare(x_near, slot_row, counts, per_row, [products[0]])
    shares = [share[k] for k in range(len(near)) for share in shares]
    slopes = slope(target[0], mine, whole, shares, spans, token)
    slopes = [slopes] + [swap(slopes, "shard", n_shard, d) for d in far + near]

    n_far = 1 + len(far)
    order_far = [(k, 0, tok_dev) for k in range(n_far)]
    order_near = [(k, low, high) for low, high in spans for k in range(len(near))]
    wide = gather(slopes[:n_far], order_far, xg_far)
    message = kept(slopes[n_far:], order_near, wide, xg_near, fbk, slot_row)
    chips = [4, *range(n_rep - 2, 4, -2), 2] if n_rep > 4 else list(range(2, n_rep, 2))
    same_core = [swap(message, "rep", n_rep, d) for d in chips]
    order = order_far + [(n_far + k, low, high) for k, low, high in order_near]
    new_feedback, token = residue(slopes, order, [xt_far, xt_near], fb, keep)
    joined, after = message, [token]
    for received in same_core:
        joined, after = join([joined, received], after), []
    groups = [joined, swap(joined, "rep", n_rep, 1)]
    return outer(groups, message.shape[0] - 16, depth, kw), new_feedback[None]


def solution(mesh):
    placed = (
        P("rep", "shard", None),
        P("rep", "shard", None),
        P("rep", "shard", None),
        P("rep", "shard", None),
        P("rep", "shard"),
        P("rep", "shard", None),
    )
    return jax.shard_map(
        on_device,
        mesh=mesh,
        in_specs=placed,
        out_specs=(P("shard", None), P("rep", "shard", None)),
        check_vma=False,
    )
```

```python
import functools

import jax
import jax.numpy as jnp
from jax import lax
from jax.experimental import pallas as pl
from jax.experimental.pallas import tpu as pltpu
from jax.sharding import PartitionSpec as P

LANES = 128
ANY = pl.BlockSpec(memory_space=pl.ANY)
BRIEF = pl.CostEstimate(flops=1000, bytes_accessed=1000, transcendentals=0)
VMEM = pl.BlockSpec(memory_space=pltpu.VMEM)
SMEM = pl.BlockSpec(memory_space=pltpu.SMEM)
MIB = 1024 * 1024
TOKEN = jax.ShapeDtypeStruct((8, LANES), jnp.float32)


def params(mib):
    return pltpu.CompilerParams(vmem_limit_bytes=mib * MIB)


def swap(x, axis, n, d):
    return lax.ppermute(x, axis, [(i, i ^ d) for i in range(n)])


def cut_kernel(cuts, tokens, *refs):
    outs, (token, sems) = refs[-len(cuts) - 2 : -2], refs[-2:]
    token[...] = jnp.zeros_like(token)
    me = lax.axis_index("shard")
    copies = []
    for k, (d, low, rows) in enumerate(cuts):
        depth = outs[k].shape[1]
        columns = pl.ds(pl.multiple_of((me ^ d) * depth, LANES), depth)
        copy = pltpu.make_async_copy(tokens.at[pl.ds(low, rows), columns], outs[k], sems.at[k])
        copy.start()
        copies.append(copy)
    for copy in copies:
        copy.wait()


def cut(tokens, depth, cuts, after):
    return pl.pallas_call(
        functools.partial(cut_kernel, cuts),
        out_shape=[jax.ShapeDtypeStruct((rows, depth), tokens.dtype) for _, _, rows in cuts]
        + [TOKEN],
        in_specs=[ANY] * (1 + len(after)),
        out_specs=[ANY] * len(cuts) + [VMEM],
        scratch_shapes=[pltpu.SemaphoreType.DMA((len(cuts),))],
        compiler_params=params(6),
        cost_estimate=BRIEF,
        name="cut",
    )(tokens, *after)


def project_kernel(n, *refs):
    pieces, w, outs, x = refs[:n], refs[n], refs[-n - 1 : -1], refs[-1]
    start = 0
    for piece in pieces:
        x[start : start + piece.shape[0], :] = piece[...]
        start += piece.shape[0]
    full = jnp.dot(x[...], w[...], preferred_element_type=jnp.float32)
    start = 0
    for out in outs:
        out[...] = full[start : start + out.shape[0], :].astype(out.dtype)
        start += out.shape[0]


def project(pieces, types, w, after):
    n = len(pieces)
    rows, depth = sum(p.shape[0] for p in pieces), pieces[0].shape[1]
    kw = w.shape[1]
    result = pl.pallas_call(
        functools.partial(project_kernel, n),
        out_shape=[jax.ShapeDtypeStruct((p.shape[0], kw), t) for p, t in zip(pieces, types)]
        + [jax.ShapeDtypeStruct((rows, depth), jnp.bfloat16)],
        in_specs=[VMEM] * (n + 1) + [ANY] * len(after),
        compiler_params=params(14),
        cost_estimate=BRIEF,
        name="project",
    )(*pieces, w, *after)
    return result[:n], result[n]


def slope_kernel(tok_dev, n, spans, *refs):
    goal, mine, out = refs[0], refs[1], refs[-1]
    whole = refs[2 : 2 + n]
    shares = refs[2 + n : -2]
    for part, (low, high) in enumerate(spans):
        key_proj = mine[low:high, :]
        for product in whole:
            key_proj += product[low:high, :].astype(jnp.float32)
        for product in shares[part :: len(spans)]:
            key_proj += product[...].astype(jnp.float32)
        gap = key_proj - goal[low:high, :].astype(jnp.float32)
        out[low:high, :] = (gap / tok_dev).astype(jnp.bfloat16)


def slope(goal, mine, whole, shares, spans, after):
    return pl.pallas_call(
        functools.partial(slope_kernel, goal.shape[0], len(whole), spans),
        out_shape=jax.ShapeDtypeStruct(mine.shape, jnp.bfloat16),
        in_specs=[VMEM] * (2 + len(whole) + len(shares)) + [ANY],
        compiler_params=params(8),
        cost_estimate=BRIEF,
        name="slope",
    )(goal, mine, *whole, *shares, after)


def as_column(row):
    size = row.shape[1]
    return jnp.broadcast_to(row.astype(jnp.float32), (size, size)).T.astype(jnp.int32)


def pick_columns(wide, column):
    out = jnp.zeros((wide.shape[0], LANES), jnp.float32)
    for c in range(wide.shape[1] // LANES):
        out += jnp.where(column == c, wide[:, c * LANES : (c + 1) * LANES], 0.0)
    return out


def early_kernel(per_row, slot_row, count, fb, after, fbk, keep, token):
    token[...] = jnp.zeros_like(token)
    depth, kw = fb.shape
    cap = slot_row.shape[1]
    slot = as_column(slot_row[...])[:, 0:1]
    hot = slot // per_row == lax.broadcasted_iota(jnp.int32, (cap, depth), 1)
    hot = hot.astype(jnp.float32).astype(jnp.bfloat16)
    used = lax.broadcasted_iota(jnp.int32, (cap, 1), 0) < count[0, 0]
    wide = jnp.dot(hot, fb[...], preferred_element_type=jnp.float32)
    fbk[...] = jnp.where(used, pick_columns(wide, slot % per_row), 0.0)
    group = lax.broadcasted_iota(jnp.int32, (cap, kw), 1) // LANES
    mark = jnp.where(used & (slot % per_row == group), 1.0, 0.0).astype(jnp.bfloat16)
    tile = min(depth, 512)
    for t in range(depth // tile):
        line = lax.broadcasted_iota(jnp.int32, (tile, cap), 0) + t * tile
        hot = (slot_row[...] // per_row == line).astype(jnp.float32).astype(jnp.bfloat16)
        mask = jnp.dot(hot, mark, preferred_element_type=jnp.float32)
        keep[t * tile : (t + 1) * tile, :] = (1.0 - mask).astype(jnp.bfloat16)


def early(slot_row, count, fb, after):
    depth, kw = fb.shape
    cap = slot_row.shape[1]
    return pl.pallas_call(
        functools.partial(early_kernel, kw // LANES),
        out_shape=[
            jax.ShapeDtypeStruct((cap, LANES), jnp.float32),
            jax.ShapeDtypeStruct((depth, kw), jnp.bfloat16),
            TOKEN,
        ],
        in_specs=[VMEM, SMEM, VMEM, ANY],
        compiler_params=params(14),
        cost_estimate=BRIEF,
        name="early",
    )(slot_row, count, fb, after)


def prepare_kernel(per_row, n, *refs):
    xs, (slot_row, count), (xg, xt, token) = refs[:n], refs[n : n + 2], refs[-3:]
    token[...] = jnp.zeros_like(token)
    depth = xs[0].shape[1]
    cap = slot_row.shape[1]
    used = lax.broadcasted_iota(jnp.int32, (cap, 1), 0) < count[0, 0]
    line = jnp.where(used, as_column(slot_row[...])[:, 0:1] // per_row, depth)
    hot = line == lax.broadcasted_iota(jnp.int32, (cap, depth), 1)
    hot = hot.astype(jnp.float32).astype(jnp.bfloat16)
    start = 0
    for x in xs:
        rows = x.shape[0]
        xg[:, start : start + rows] = lax.dot_general(
            hot, x[...], (((1,), (1,)), ((), ())), preferred_element_type=jnp.float32
        ).astype(jnp.bfloat16)
        xt[:, start : start + rows] = x[...].T
        start += rows


def prepare(xs, slot_row, count, per_row, after):
    rows, depth = sum(x.shape[0] for x in xs), xs[0].shape[1]
    cap = slot_row.shape[1]
    return pl.pallas_call(
        functools.partial(prepare_kernel, per_row, len(xs)),
        out_shape=[
            jax.ShapeDtypeStruct((cap, rows), jnp.bfloat16),
            jax.ShapeDtypeStruct((depth, rows), jnp.bfloat16),
            TOKEN,
        ],
        in_specs=[VMEM] * (len(xs) + 1) + [SMEM] + [ANY] * len(after),
        compiler_params=params(14),
        cost_estimate=BRIEF,
        name="prepare",
    )(*xs, slot_row, count, *after)


def stack(slopes, order, s):
    start = 0
    for k, low, high in order:
        s[start : start + high - low, :] = slopes[k][low:high, :]
        start += high - low


def gather_kernel(order, *refs):
    slopes, (xg, out, s) = refs[:-3], refs[-3:]
    stack(slopes, order, s)
    out[...] = jnp.dot(xg[...], s[...], preferred_element_type=jnp.float32)


def gather(slopes, order, xg):
    kw = slopes[0].shape[1]
    return pl.pallas_call(
        functools.partial(gather_kernel, order),
        out_shape=jax.ShapeDtypeStruct((xg.shape[0], kw), jnp.float32),
        scratch_shapes=[pltpu.VMEM((xg.shape[1], kw), jnp.bfloat16)],
        compiler_params=params(8),
        cost_estimate=BRIEF,
        name="gather",
    )(*slopes, xg)


def kept_kernel(per_row, order, *refs):
    slopes, (wide, xg, fbk, slot_row, out, s) = refs[:-6], refs[-6:]
    cap = slot_row.shape[1]
    stack(slopes, order, s)
    total = wide[...] + jnp.dot(xg[...], s[...], preferred_element_type=jnp.float32)
    value = pick_columns(total, as_column(slot_row[...])[:, 0:1] % per_row) + fbk[...]
    out[:cap, :] = value.astype(jnp.bfloat16)
    tail = out.shape[0] - cap
    number = jnp.broadcast_to(slot_row[...], (tail, cap))
    line = lax.broadcasted_iota(jnp.int32, (tail, cap), 0)
    number = jnp.where(line == 0, number // LANES, number % LANES)
    out[cap:, :] = number.astype(jnp.float32).astype(jnp.bfloat16)


def kept(slopes, order, wide, xg, fbk, slot_row):
    cap, kw = wide.shape
    return pl.pallas_call(
        functools.partial(kept_kernel, kw // LANES, order),
        out_shape=jax.ShapeDtypeStruct((cap + 16, LANES), jnp.bfloat16),
        scratch_shapes=[pltpu.VMEM((xg.shape[1], kw), jnp.bfloat16)],
        compiler_params=params(8),
        cost_estimate=BRIEF,
        name="kept",
    )(*slopes, wide, xg, fbk, slot_row)


def send_out(held, out, sems, t, tile):
    rows = pl.ds(t * tile, tile)
    return pltpu.make_async_copy(held.at[rows, :], out.at[rows, :], sems.at[t])


def residue_kernel(order, tile, *refs):
    n = len({k for k, _, _ in order})
    slopes, xts, (fb, keep, out, token, s, held, sems) = refs[:n], refs[n:-7], refs[-7:]
    token[...] = jnp.zeros_like(token)
    stack(slopes, order, s)
    tiles = out.shape[0] // tile
    for t in range(tiles):
        rows = slice(t * tile, (t + 1) * tile)
        pseudo, start = fb[rows, :].astype(jnp.float32), 0
        for xt in xts:
            part = s[start : start + xt.shape[1], :]
            pseudo += jnp.dot(xt[rows, :], part, preferred_element_type=jnp.float32)
            start += xt.shape[1]
        held[rows, :] = jnp.where(keep[rows, :] > 0, pseudo, 0.0).astype(jnp.bfloat16)
        send_out(held, out, sems, t, tile).start()
    for t in range(tiles):
        send_out(held, out, sems, t, tile).wait()


def residue(slopes, order, xts, fb, keep):
    depth, kw = fb.shape
    total = sum(xt.shape[1] for xt in xts)
    tile = min(depth, 256)
    return pl.pallas_call(
        functools.partial(residue_kernel, order, tile),
        out_shape=[
            jax.ShapeDtypeStruct((depth, kw), jnp.bfloat16),
            TOKEN,
        ],
        in_specs=[VMEM] * (len(slopes) + len(xts) + 2),
        out_specs=[ANY, VMEM],
        scratch_shapes=[
            pltpu.VMEM((total, kw), jnp.bfloat16),
            pltpu.VMEM((depth, kw), jnp.bfloat16),
            pltpu.SemaphoreType.DMA((depth // tile,)),
        ],
        compiler_params=params(14),
        cost_estimate=BRIEF,
        name="residue",
    )(*slopes, *xts, fb, keep)


def join_kernel(n, *refs):
    out, start = refs[-1], 0
    for part in refs[:n]:
        out[start : start + part.shape[0], :] = part[...]
        start += part.shape[0]


def join(parts, after):
    rows, lanes = sum(part.shape[0] for part in parts), parts[0].shape[1]
    return pl.pallas_call(
        functools.partial(join_kernel, len(parts)),
        out_shape=jax.ShapeDtypeStruct((rows, lanes), jnp.bfloat16),
        in_specs=[VMEM] * len(parts) + [ANY] * len(after),
        compiler_params=params(8),
        cost_estimate=BRIEF,
        name="join",
    )(*parts, *after)


def spread(group, wide, lines, cap, per_row):
    size = cap + 16
    for k in range(group.shape[0] // size):
        start = k * size
        tail = group[start + cap : start + size, :].astype(jnp.float32)
        number = (tail[0:1, :] * LANES + tail[1:2, :]).astype(jnp.int32)
        lines[:, k * cap : (k + 1) * cap] = jnp.broadcast_to(number // per_row, (8, cap))
        column = jnp.broadcast_to((number % per_row).astype(jnp.float32), (LANES, cap)).T
        value = group[start : start + cap, :].astype(jnp.float32)
        for c in range(per_row):
            wide[k * cap : (k + 1) * cap, c * LANES : (c + 1) * LANES] = jnp.where(
                column == c, value, 0.0
            ).astype(jnp.bfloat16)


def place(lines, wide, t, tile):
    line = lax.broadcasted_iota(jnp.int32, (tile, lines.shape[1]), 0) + t * tile
    hot = (lines[0:1, :] == line).astype(jnp.float32).astype(jnp.bfloat16)
    return jnp.dot(hot, wide[...], preferred_element_type=jnp.float32)


def half_kernel(cap, per_row, tile, group, out, wide, lines):
    spread(group, wide, lines, cap, per_row)
    for t in range(out.shape[0] // tile):
        out[t * tile : (t + 1) * tile, :] = place(lines, wide, t, tile)


def outer_kernel(cap, per_row, tile, n, group, half, out, wide, lines, held, sems):
    spread(group, wide, lines, cap, per_row)
    tiles = out.shape[0] // tile
    for t in range(tiles):
        rows = slice(t * tile, (t + 1) * tile)
        held[rows, :] = (half[rows, :] + place(lines, wide, t, tile)) * (1.0 / n)
        send_out(held, out, sems, t, tile).start()
    for t in range(tiles):
        send_out(held, out, sems, t, tile).wait()


def outer(groups, cap, depth, kw):
    slots = groups[0].shape[0] // (cap + 16) * cap
    n = 2 * slots // cap
    tile = min(depth, 256)
    shape = jax.ShapeDtypeStruct((depth, kw), jnp.float32)
    scratch = [pltpu.VMEM((slots, kw), jnp.bfloat16), pltpu.VMEM((8, slots), jnp.int32)]
    half = pl.pallas_call(
        functools.partial(half_kernel, cap, kw // LANES, tile),
        out_shape=shape,
        scratch_shapes=scratch,
        compiler_params=params(14),
        cost_estimate=BRIEF,
        name="half",
    )(groups[0])
    return pl.pallas_call(
        functools.partial(outer_kernel, cap, kw // LANES, tile, n),
        out_shape=shape,
        out_specs=ANY,
        scratch_shapes=scratch
        + [pltpu.VMEM((depth, kw), jnp.float32), pltpu.SemaphoreType.DMA((depth // tile,))],
        compiler_params=params(14),
        cost_estimate=BRIEF,
        name="outer",
    )(groups[1], half)


def on_device(inputs, target, weights, feedback, counts, blocks):
    tokens, w, fb = inputs[0], weights[0], feedback[0]
    n_shard, n_rep = lax.axis_size("shard"), lax.axis_size("rep")
    tok_dev = tokens.shape[0]
    depth, kw = w.shape
    early_rows = tok_dev * 3 // 4
    spans = [(0, early_rows), (early_rows, tok_dev)]
    per_row = kw // LANES
    slot_row = blocks[0]
    near = [d for d in range(1, n_shard) if d & (d - 1) == 0]
    far = [d for d in range(1, n_shard) if d & (d - 1) != 0]

    me = lax.axis_index("shard")
    far_out = [lax.dynamic_slice(tokens, (0, (me ^ d) * depth), (tok_dev, depth)) for d in far]
    far_in = [swap(x, "shard", n_shard, d) for x, d in zip(far_out, far)]
    near_out, token = [], far_out[0]
    for low, high in spans:
        *out, token = cut(tokens, depth, [(d, low, high - low) for d in near], [token])
        near_out.append(out)
        if low == 0:
            fbk, keep, token = early(slot_row, counts, fb, token)
    near_in = [[swap(x, "shard", n_shard, d) for x, d in zip(out, near)] for out in near_out]

    own, _ = cut(tokens, depth, [(0, 0, tok_dev)], [token])

    brief, wide = jnp.bfloat16, jnp.float32
    (mine, *products), x_far = project([own] + far_in, [wide] + [brief] * len(far), w, [])
    whole = [swap(p, "shard", n_shard, d) for p, d in zip(products, far)]
    xg_far, xt_far, token = prepare([x_far], slot_row, counts, per_row, [])
    after, shares, x_near = [token], [], []
    for part in range(len(spans)):
        products, x = project(near_in[part], [brief] * len(near), w, after)
        shares.append([swap(p, "shard", n_shard, d) for p, d in zip(products, near)])
        x_near.append(x)
        after = products[-1:]
    xg_near, xt_near, token = prepare(x_near, slot_row, counts, per_row, [products[0]])
    shares = [share[k] for k in range(len(near)) for share in shares]
    slopes = slope(target[0], mine, whole, shares, spans, token)
    slopes = [slopes] + [swap(slopes, "shard", n_shard, d) for d in far + near]

    n_far = 1 + len(far)
    order_far = [(k, 0, tok_dev) for k in range(n_far)]
    order_near = [(k, low, high) for low, high in spans for k in range(len(near))]
    wide = gather(slopes[:n_far], order_far, xg_far)
    message = kept(slopes[n_far:], order_near, wide, xg_near, fbk, slot_row)
    same_core = [swap(message, "rep", n_rep, d) for d in range(n_rep - 2, 0, -2)]
    order = order_far + [(n_far + k, low, high) for k, low, high in order_near]
    new_feedback, token = residue(slopes, order, [xt_far, xt_near], fb, keep)
    joined, after = message, [token]
    for received in same_core:
        joined, after = join([joined, received], after), []
    groups = [joined, swap(joined, "rep", n_rep, 1)]
    return outer(groups, message.shape[0] - 16, depth, kw), new_feedback[None]


def solution(mesh):
    placed = (
        P("rep", "shard", None),
        P("rep", "shard", None),
        P("rep", "shard", None),
        P("rep", "shard", None),
        P("rep", "shard"),
        P("rep", "shard", None),
    )
    return jax.shard_map(
        on_device,
        mesh=mesh,
        in_specs=placed,
        out_specs=(P("shard", None), P("rep", "shard", None)),
        check_vma=False,
    )
```

```python
import functools

import jax
import jax.numpy as jnp
from jax import lax
from jax.experimental import pallas as pl
from jax.experimental.pallas import tpu as pltpu
from jax.sharding import PartitionSpec as P

LANES = 128
ANY = pl.BlockSpec(memory_space=pl.ANY)
BRIEF = pl.CostEstimate(flops=1000, bytes_accessed=1000, transcendentals=0)
VMEM = pl.BlockSpec(memory_space=pltpu.VMEM)
SMEM = pl.BlockSpec(memory_space=pltpu.SMEM)
MIB = 1024 * 1024
TOKEN = jax.ShapeDtypeStruct((8, LANES), jnp.float32)


def params(mib):
    return pltpu.CompilerParams(vmem_limit_bytes=mib * MIB)


def swap(x, axis, n, d):
    return lax.ppermute(x, axis, [(i, i ^ d) for i in range(n)])


def cut_kernel(cuts, tokens, *refs):
    outs, (token, sems) = refs[-len(cuts) - 2 : -2], refs[-2:]
    token[...] = jnp.zeros_like(token)
    me = lax.axis_index("shard")
    copies = []
    for k, (d, low, rows) in enumerate(cuts):
        depth = outs[k].shape[1]
        columns = pl.ds(pl.multiple_of((me ^ d) * depth, LANES), depth)
        copy = pltpu.make_async_copy(tokens.at[pl.ds(low, rows), columns], outs[k], sems.at[k])
        copy.start()
        copies.append(copy)
    for copy in copies:
        copy.wait()


def cut(tokens, depth, cuts, after):
    return pl.pallas_call(
        functools.partial(cut_kernel, cuts),
        out_shape=[jax.ShapeDtypeStruct((rows, depth), tokens.dtype) for _, _, rows in cuts]
        + [TOKEN],
        in_specs=[ANY] * (1 + len(after)),
        out_specs=[ANY] * len(cuts) + [VMEM],
        scratch_shapes=[pltpu.SemaphoreType.DMA((len(cuts),))],
        compiler_params=params(6),
        cost_estimate=BRIEF,
        name="cut",
    )(tokens, *after)


def project_kernel(n, *refs):
    pieces, w, outs, x = refs[:n], refs[n], refs[-n - 1 : -1], refs[-1]
    start = 0
    for piece in pieces:
        x[start : start + piece.shape[0], :] = piece[...]
        start += piece.shape[0]
    full = jnp.dot(x[...], w[...], preferred_element_type=jnp.float32)
    start = 0
    for out in outs:
        out[...] = full[start : start + out.shape[0], :].astype(out.dtype)
        start += out.shape[0]


def project(pieces, types, w, after):
    n = len(pieces)
    rows, depth = sum(p.shape[0] for p in pieces), pieces[0].shape[1]
    kw = w.shape[1]
    result = pl.pallas_call(
        functools.partial(project_kernel, n),
        out_shape=[jax.ShapeDtypeStruct((p.shape[0], kw), t) for p, t in zip(pieces, types)]
        + [jax.ShapeDtypeStruct((rows, depth), jnp.bfloat16)],
        in_specs=[VMEM] * (n + 1) + [ANY] * len(after),
        compiler_params=params(14),
        cost_estimate=BRIEF,
        name="project",
    )(*pieces, w, *after)
    return result[:n], result[n]


def slope_kernel(tok_dev, n, spans, *refs):
    goal, mine, out = refs[0], refs[1], refs[-1]
    whole = refs[2 : 2 + n]
    shares = refs[2 + n : -2]
    for part, (low, high) in enumerate(spans):
        key_proj = mine[low:high, :]
        for product in whole:
            key_proj += product[low:high, :].astype(jnp.float32)
        for product in shares[part :: len(spans)]:
            key_proj += product[...].astype(jnp.float32)
        gap = key_proj - goal[low:high, :].astype(jnp.float32)
        out[low:high, :] = (gap / tok_dev).astype(jnp.bfloat16)


def slope(goal, mine, whole, shares, spans, after):
    return pl.pallas_call(
        functools.partial(slope_kernel, goal.shape[0], len(whole), spans),
        out_shape=jax.ShapeDtypeStruct(mine.shape, jnp.bfloat16),
        in_specs=[VMEM] * (2 + len(whole) + len(shares)) + [ANY],
        compiler_params=params(8),
        cost_estimate=BRIEF,
        name="slope",
    )(goal, mine, *whole, *shares, after)


def as_column(row):
    size = row.shape[1]
    return jnp.broadcast_to(row.astype(jnp.float32), (size, size)).T.astype(jnp.int32)


def pick_columns(wide, column):
    out = jnp.zeros((wide.shape[0], LANES), jnp.float32)
    for c in range(wide.shape[1] // LANES):
        out += jnp.where(column == c, wide[:, c * LANES : (c + 1) * LANES], 0.0)
    return out


def early_kernel(per_row, slot_row, count, fb, after, fbk, keep, token):
    token[...] = jnp.zeros_like(token)
    depth, kw = fb.shape
    cap = slot_row.shape[1]
    slot = as_column(slot_row[...])[:, 0:1]
    hot = slot // per_row == lax.broadcasted_iota(jnp.int32, (cap, depth), 1)
    hot = hot.astype(jnp.float32).astype(jnp.bfloat16)
    used = lax.broadcasted_iota(jnp.int32, (cap, 1), 0) < count[0, 0]
    wide = jnp.dot(hot, fb[...], preferred_element_type=jnp.float32)
    fbk[...] = jnp.where(used, pick_columns(wide, slot % per_row), 0.0)
    group = lax.broadcasted_iota(jnp.int32, (cap, kw), 1) // LANES
    mark = jnp.where(used & (slot % per_row == group), 1.0, 0.0).astype(jnp.bfloat16)
    tile = min(depth, 512)
    for t in range(depth // tile):
        line = lax.broadcasted_iota(jnp.int32, (tile, cap), 0) + t * tile
        hot = (slot_row[...] // per_row == line).astype(jnp.float32).astype(jnp.bfloat16)
        mask = jnp.dot(hot, mark, preferred_element_type=jnp.float32)
        keep[t * tile : (t + 1) * tile, :] = (1.0 - mask).astype(jnp.bfloat16)


def early(slot_row, count, fb, after):
    depth, kw = fb.shape
    cap = slot_row.shape[1]
    return pl.pallas_call(
        functools.partial(early_kernel, kw // LANES),
        out_shape=[
            jax.ShapeDtypeStruct((cap, LANES), jnp.float32),
            jax.ShapeDtypeStruct((depth, kw), jnp.bfloat16),
            TOKEN,
        ],
        in_specs=[VMEM, SMEM, VMEM, ANY],
        compiler_params=params(14),
        cost_estimate=BRIEF,
        name="early",
    )(slot_row, count, fb, after)


def prepare_kernel(per_row, n, *refs):
    xs, (slot_row, count), (xg, xt, token) = refs[:n], refs[n : n + 2], refs[-3:]
    token[...] = jnp.zeros_like(token)
    depth = xs[0].shape[1]
    cap = slot_row.shape[1]
    used = lax.broadcasted_iota(jnp.int32, (cap, 1), 0) < count[0, 0]
    line = jnp.where(used, as_column(slot_row[...])[:, 0:1] // per_row, depth)
    hot = line == lax.broadcasted_iota(jnp.int32, (cap, depth), 1)
    hot = hot.astype(jnp.float32).astype(jnp.bfloat16)
    start = 0
    for x in xs:
        rows = x.shape[0]
        xg[:, start : start + rows] = lax.dot_general(
            hot, x[...], (((1,), (1,)), ((), ())), preferred_element_type=jnp.float32
        ).astype(jnp.bfloat16)
        xt[:, start : start + rows] = x[...].T
        start += rows


def prepare(xs, slot_row, count, per_row, after):
    rows, depth = sum(x.shape[0] for x in xs), xs[0].shape[1]
    cap = slot_row.shape[1]
    return pl.pallas_call(
        functools.partial(prepare_kernel, per_row, len(xs)),
        out_shape=[
            jax.ShapeDtypeStruct((cap, rows), jnp.bfloat16),
            jax.ShapeDtypeStruct((depth, rows), jnp.bfloat16),
            TOKEN,
        ],
        in_specs=[VMEM] * (len(xs) + 1) + [SMEM] + [ANY] * len(after),
        compiler_params=params(14),
        cost_estimate=BRIEF,
        name="prepare",
    )(*xs, slot_row, count, *after)


def stack(slopes, order, s):
    start = 0
    for k, low, high in order:
        s[start : start + high - low, :] = slopes[k][low:high, :]
        start += high - low


def gather_kernel(order, *refs):
    slopes, (xg, out, s) = refs[:-3], refs[-3:]
    stack(slopes, order, s)
    out[...] = jnp.dot(xg[...], s[...], preferred_element_type=jnp.float32)


def gather(slopes, order, xg):
    kw = slopes[0].shape[1]
    return pl.pallas_call(
        functools.partial(gather_kernel, order),
        out_shape=jax.ShapeDtypeStruct((xg.shape[0], kw), jnp.float32),
        scratch_shapes=[pltpu.VMEM((xg.shape[1], kw), jnp.bfloat16)],
        compiler_params=params(8),
        cost_estimate=BRIEF,
        name="gather",
    )(*slopes, xg)


def kept_kernel(per_row, order, *refs):
    slopes, (wide, xg, fbk, slot_row, after, out, s) = refs[:-7], refs[-7:]
    stack(slopes, order, s)
    total = wide[...] + jnp.dot(xg[...], s[...], preferred_element_type=jnp.float32)
    value = pick_columns(total, as_column(slot_row[...])[:, 0:1] % per_row) + fbk[...]
    out[...] = value.astype(jnp.bfloat16)


def kept(slopes, order, wide, xg, fbk, slot_row, after):
    cap, kw = wide.shape
    return pl.pallas_call(
        functools.partial(kept_kernel, kw // LANES, order),
        out_shape=jax.ShapeDtypeStruct((cap, LANES), jnp.bfloat16),
        in_specs=[VMEM] * (len(slopes) + 4) + [ANY],
        scratch_shapes=[pltpu.VMEM((xg.shape[1], kw), jnp.bfloat16)],
        compiler_params=params(8),
        cost_estimate=BRIEF,
        name="kept",
    )(*slopes, wide, xg, fbk, slot_row, after)


def send_out(held, out, sems, t, tile):
    rows = pl.ds(t * tile, tile)
    return pltpu.make_async_copy(held.at[rows, :], out.at[rows, :], sems.at[t])


def residue_kernel(order, tile, *refs):
    n = len({k for k, _, _ in order})
    slopes, xts, (fb, keep, out, token, s, held, sems) = refs[:n], refs[n:-7], refs[-7:]
    token[...] = jnp.zeros_like(token)
    stack(slopes, order, s)
    tiles = out.shape[0] // tile
    for t in range(tiles):
        rows = slice(t * tile, (t + 1) * tile)
        pseudo, start = fb[rows, :].astype(jnp.float32), 0
        for xt in xts:
            part = s[start : start + xt.shape[1], :]
            pseudo += jnp.dot(xt[rows, :], part, preferred_element_type=jnp.float32)
            start += xt.shape[1]
        held[rows, :] = jnp.where(keep[rows, :] > 0, pseudo, 0.0).astype(jnp.bfloat16)
        send_out(held, out, sems, t, tile).start()
    for t in range(tiles):
        send_out(held, out, sems, t, tile).wait()


def residue(slopes, order, xts, fb, keep):
    depth, kw = fb.shape
    total = sum(xt.shape[1] for xt in xts)
    tile = min(depth, 256)
    return pl.pallas_call(
        functools.partial(residue_kernel, order, tile),
        out_shape=[
            jax.ShapeDtypeStruct((depth, kw), jnp.bfloat16),
            TOKEN,
        ],
        in_specs=[VMEM] * (len(slopes) + len(xts) + 2),
        out_specs=[ANY, VMEM],
        scratch_shapes=[
            pltpu.VMEM((total, kw), jnp.bfloat16),
            pltpu.VMEM((depth, kw), jnp.bfloat16),
            pltpu.SemaphoreType.DMA((depth // tile,)),
        ],
        compiler_params=params(14),
        cost_estimate=BRIEF,
        name="residue",
    )(*slopes, *xts, fb, keep)


def join_kernel(n, *refs):
    out, start = refs[-1], 0
    for part in refs[:n]:
        out[start : start + part.shape[0], :] = part[...]
        start += part.shape[0]


def join(parts, after):
    rows, lanes = sum(part.shape[0] for part in parts), parts[0].shape[1]
    return pl.pallas_call(
        functools.partial(join_kernel, len(parts)),
        out_shape=jax.ShapeDtypeStruct((rows, lanes), jnp.bfloat16),
        in_specs=[VMEM] * len(parts) + [ANY] * len(after),
        compiler_params=params(8),
        cost_estimate=BRIEF,
        name="join",
    )(*parts, *after)


def number_kernel(row, after, out):
    out[...] = row[...]


def number(row, after):
    return pl.pallas_call(
        number_kernel,
        out_shape=jax.ShapeDtypeStruct(row.shape, row.dtype),
        in_specs=[VMEM, ANY],
        compiler_params=params(4),
        cost_estimate=BRIEF,
        name="number",
    )(row, after)


def places_kernel(per_row, tile, order, numbers, after, *refs):
    hots, columns, (token, lines) = refs[:2], refs[2:4], refs[4:]
    token[...] = jnp.zeros_like(token)
    cap = numbers.shape[1]
    rep = lax.axis_index("rep")
    for core in range(2):
        for k, d in enumerate(order):
            row = numbers[pl.ds(rep ^ d ^ core, 1), :]
            lines[:, k * cap : (k + 1) * cap] = jnp.broadcast_to(row // per_row, (8, cap))
            column = as_column(row % per_row).astype(jnp.float32)
            columns[core][k * cap : (k + 1) * cap, :] = column.astype(jnp.bfloat16)
        for t in range(hots[core].shape[0] // tile):
            line = lax.broadcasted_iota(jnp.int32, (tile, lines.shape[1]), 0) + t * tile
            hot = (lines[0:1, :] == line).astype(jnp.float32).astype(jnp.bfloat16)
            hots[core][t * tile : (t + 1) * tile, :] = hot


def places(numbers, order, depth, per_row, after):
    cap = numbers.shape[1]
    slots = len(order) * cap
    return pl.pallas_call(
        functools.partial(places_kernel, per_row, min(depth, 256), order),
        out_shape=[jax.ShapeDtypeStruct((depth, slots), jnp.bfloat16)] * 2
        + [jax.ShapeDtypeStruct((slots, LANES), jnp.bfloat16)] * 2
        + [TOKEN],
        in_specs=[VMEM, ANY],
        scratch_shapes=[pltpu.VMEM((8, slots), jnp.int32)],
        compiler_params=params(14),
        cost_estimate=BRIEF,
        name="places",
    )(numbers, after)


def spread(group, columns, wide):
    column, value = columns[...].astype(jnp.float32), group[...].astype(jnp.float32)
    for c in range(wide.shape[1] // LANES):
        wide[:, c * LANES : (c + 1) * LANES] = jnp.where(column == c, value, 0.0).astype(
            jnp.bfloat16
        )


def half_kernel(tile, group, hot, columns, out, wide):
    spread(group, columns, wide)
    for t in range(out.shape[0] // tile):
        rows = slice(t * tile, (t + 1) * tile)
        out[rows, :] = jnp.dot(hot[rows, :], wide[...], preferred_element_type=jnp.float32)


def outer_kernel(tile, n, group, hot, columns, half, out, wide, held, sems):
    spread(group, columns, wide)
    tiles = out.shape[0] // tile
    for t in range(tiles):
        rows = slice(t * tile, (t + 1) * tile)
        rest = jnp.dot(hot[rows, :], wide[...], preferred_element_type=jnp.float32)
        held[rows, :] = (half[rows, :] + rest) * (1.0 / n)
        send_out(held, out, sems, t, tile).start()
    for t in range(tiles):
        send_out(held, out, sems, t, tile).wait()


def outer(groups, hots, columns, kw, n):
    depth, slots = hots[0].shape
    tile = min(depth, 256)
    shape = jax.ShapeDtypeStruct((depth, kw), jnp.float32)
    wide = pltpu.VMEM((slots, kw), jnp.bfloat16)
    half = pl.pallas_call(
        functools.partial(half_kernel, min(depth, 512)),
        out_shape=shape,
        scratch_shapes=[wide],
        compiler_params=params(14),
        cost_estimate=BRIEF,
        name="half",
    )(groups[0], hots[0], columns[0])
    return pl.pallas_call(
        functools.partial(outer_kernel, tile, n),
        out_shape=shape,
        in_specs=[VMEM] * 4,
        out_specs=ANY,
        scratch_shapes=[
            wide,
            pltpu.VMEM((depth, kw), jnp.float32),
            pltpu.SemaphoreType.DMA((depth // tile,)),
        ],
        compiler_params=params(16),
        cost_estimate=BRIEF,
        name="outer",
    )(groups[1], hots[1], columns[1], half)


def on_device(inputs, target, weights, feedback, counts, blocks):
    tokens, w, fb = inputs[0], weights[0], feedback[0]
    n_shard, n_rep = lax.axis_size("shard"), lax.axis_size("rep")
    tok_dev = tokens.shape[0]
    depth, kw = w.shape
    early_rows = tok_dev * 3 // 4
    spans = [(0, early_rows), (early_rows, tok_dev)]
    per_row = kw // LANES
    slot_row = blocks[0]
    near = [d for d in range(1, n_shard) if d & (d - 1) == 0]
    far = [d for d in range(1, n_shard) if d & (d - 1) != 0]

    me = lax.axis_index("shard")
    far_out = [lax.dynamic_slice(tokens, (0, (me ^ d) * depth), (tok_dev, depth)) for d in far]
    far_in = [swap(x, "shard", n_shard, d) for x, d in zip(far_out, far)]
    near_out, token = [], far_out[0]
    for low, high in spans:
        *out, token = cut(tokens, depth, [(d, low, high - low) for d in near], [token])
        near_out.append(out)
        if low == 0:
            numbers = lax.all_gather(number(slot_row, token), "rep", axis=0, tiled=True)
            fbk, keep, token = early(slot_row, counts, fb, numbers)
    near_in = [[swap(x, "shard", n_shard, d) for x, d in zip(out, near)] for out in near_out]

    own, _ = cut(tokens, depth, [(0, 0, tok_dev)], [token])

    brief, wide = jnp.bfloat16, jnp.float32
    (mine, *products), x_far = project([own] + far_in, [wide] + [brief] * len(far), w, [])
    whole = [swap(p, "shard", n_shard, d) for p, d in zip(products, far)]
    xg_far, xt_far, token = prepare([x_far], slot_row, counts, per_row, [])
    after, shares, x_near = [token], [], []
    for part in range(len(spans)):
        products, x = project(near_in[part], [brief] * len(near), w, after)
        shares.append([swap(p, "shard", n_shard, d) for p, d in zip(products, near)])
        x_near.append(x)
        after = products[-1:]
    xg_near, xt_near, token = prepare(x_near, slot_row, counts, per_row, [products[0]])
    shares = [share[k] for k in range(len(near)) for share in shares]
    slopes = slope(target[0], mine, whole, shares, spans, token)
    chips = [0, *range(n_rep - 2, 0, -2)]
    *where, token = places(numbers, chips, depth, per_row, slopes)
    slopes = [slopes] + [swap(slopes, "shard", n_shard, d) for d in far + near]

    n_far = 1 + len(far)
    order_far = [(k, 0, tok_dev) for k in range(n_far)]
    order_near = [(k, low, high) for low, high in spans for k in range(len(near))]
    wide = gather(slopes[:n_far], order_far, xg_far)
    message = kept(slopes[n_far:], order_near, wide, xg_near, fbk, slot_row, token)
    same_core = [swap(message, "rep", n_rep, d) for d in chips[1:]]
    order = order_far + [(n_far + k, low, high) for k, low, high in order_near]
    new_feedback, token = residue(slopes, order, [xt_far, xt_near], fb, keep)
    joined, after = message, [token]
    for received in same_core:
        joined, after = join([joined, received], after), []
    groups = [joined, swap(joined, "rep", n_rep, 1)]
    return outer(groups, where[:2], where[2:], kw, n_rep), new_feedback[None]


def solution(mesh):
    placed = (
        P("rep", "shard", None),
        P("rep", "shard", None),
        P("rep", "shard", None),
        P("rep", "shard", None),
        P("rep", "shard"),
        P("rep", "shard", None),
    )
    return jax.shard_map(
        on_device,
        mesh=mesh,
        in_specs=placed,
        out_specs=(P("shard", None), P("rep", "shard", None)),
        check_vma=False,
    )
```

```python
import functools

import jax
import jax.numpy as jnp
from jax import lax
from jax.experimental import pallas as pl
from jax.experimental.pallas import tpu as pltpu
from jax.sharding import PartitionSpec as P

LANES = 128
ANY = pl.BlockSpec(memory_space=pl.ANY)
BRIEF = pl.CostEstimate(flops=1000, bytes_accessed=1000, transcendentals=0)
VMEM = pl.BlockSpec(memory_space=pltpu.VMEM)
SMEM = pl.BlockSpec(memory_space=pltpu.SMEM)
MIB = 1024 * 1024
TOKEN = jax.ShapeDtypeStruct((8, LANES), jnp.float32)


def params(mib):
    return pltpu.CompilerParams(vmem_limit_bytes=mib * MIB)


def swap(x, axis, n, d):
    return lax.ppermute(x, axis, [(i, i ^ d) for i in range(n)])


def cut_kernel(cuts, tokens, *refs):
    outs, (token, sems) = refs[-len(cuts) - 2 : -2], refs[-2:]
    token[...] = jnp.zeros_like(token)
    me = lax.axis_index("shard")
    copies = []
    for k, (d, low, rows) in enumerate(cuts):
        depth = outs[k].shape[1]
        columns = pl.ds(pl.multiple_of((me ^ d) * depth, LANES), depth)
        copy = pltpu.make_async_copy(tokens.at[pl.ds(low, rows), columns], outs[k], sems.at[k])
        copy.start()
        copies.append(copy)
    for copy in copies:
        copy.wait()


def cut(tokens, depth, cuts, after):
    return pl.pallas_call(
        functools.partial(cut_kernel, cuts),
        out_shape=[jax.ShapeDtypeStruct((rows, depth), tokens.dtype) for _, _, rows in cuts]
        + [TOKEN],
        in_specs=[ANY] * (1 + len(after)),
        out_specs=[ANY] * len(cuts) + [VMEM],
        scratch_shapes=[pltpu.SemaphoreType.DMA((len(cuts),))],
        compiler_params=params(6),
        cost_estimate=BRIEF,
        name="cut",
    )(tokens, *after)


def project_kernel(n, *refs):
    pieces, w, outs, x = refs[:n], refs[n], refs[-n - 1 : -1], refs[-1]
    start = 0
    for piece in pieces:
        x[start : start + piece.shape[0], :] = piece[...]
        start += piece.shape[0]
    full = jnp.dot(x[...], w[...], preferred_element_type=jnp.float32)
    start = 0
    for out in outs:
        out[...] = full[start : start + out.shape[0], :].astype(out.dtype)
        start += out.shape[0]


def project(pieces, types, w, after):
    n = len(pieces)
    rows, depth = sum(p.shape[0] for p in pieces), pieces[0].shape[1]
    kw = w.shape[1]
    result = pl.pallas_call(
        functools.partial(project_kernel, n),
        out_shape=[jax.ShapeDtypeStruct((p.shape[0], kw), t) for p, t in zip(pieces, types)]
        + [jax.ShapeDtypeStruct((rows, depth), jnp.bfloat16)],
        in_specs=[VMEM] * (n + 1) + [ANY] * len(after),
        compiler_params=params(14),
        cost_estimate=BRIEF,
        name="project",
    )(*pieces, w, *after)
    return result[:n], result[n]


def slope_kernel(tok_dev, n, spans, *refs):
    goal, mine, out = refs[0], refs[1], refs[-1]
    whole = refs[2 : 2 + n]
    shares = refs[2 + n : -2]
    for part, (low, high) in enumerate(spans):
        key_proj = mine[low:high, :]
        for product in whole:
            key_proj += product[low:high, :].astype(jnp.float32)
        for product in shares[part :: len(spans)]:
            key_proj += product[...].astype(jnp.float32)
        gap = key_proj - goal[low:high, :].astype(jnp.float32)
        for k in range(out.shape[0]):
            out[k, low:high, :] = (gap / tok_dev).astype(jnp.bfloat16)


def slope(goal, mine, whole, shares, spans, after, copies):
    return pl.pallas_call(
        functools.partial(slope_kernel, goal.shape[0], len(whole), spans),
        out_shape=jax.ShapeDtypeStruct((copies, *mine.shape), jnp.bfloat16),
        in_specs=[VMEM] * (2 + len(whole) + len(shares)) + [ANY],
        compiler_params=params(8),
        cost_estimate=BRIEF,
        name="slope",
    )(goal, mine, *whole, *shares, after)


def as_column(row):
    size = row.shape[1]
    return jnp.broadcast_to(row.astype(jnp.float32), (size, size)).T.astype(jnp.int32)


def pick_columns(wide, column):
    out = jnp.zeros((wide.shape[0], LANES), jnp.float32)
    for c in range(wide.shape[1] // LANES):
        out += jnp.where(column == c, wide[:, c * LANES : (c + 1) * LANES], 0.0)
    return out


def early_kernel(per_row, slot_row, count, fb, after, fbk, keep, token):
    token[...] = jnp.zeros_like(token)
    depth, kw = fb.shape
    cap = slot_row.shape[1]
    slot = as_column(slot_row[...])[:, 0:1]
    hot = slot // per_row == lax.broadcasted_iota(jnp.int32, (cap, depth), 1)
    hot = hot.astype(jnp.float32).astype(jnp.bfloat16)
    used = lax.broadcasted_iota(jnp.int32, (cap, 1), 0) < count[0, 0]
    wide = jnp.dot(hot, fb[...], preferred_element_type=jnp.float32)
    fbk[...] = jnp.where(used, pick_columns(wide, slot % per_row), 0.0)
    group = lax.broadcasted_iota(jnp.int32, (cap, kw), 1) // LANES
    mark = jnp.where(used & (slot % per_row == group), 1.0, 0.0).astype(jnp.bfloat16)
    tile = min(depth, 512)
    for t in range(depth // tile):
        line = lax.broadcasted_iota(jnp.int32, (tile, cap), 0) + t * tile
        hot = (slot_row[...] // per_row == line).astype(jnp.float32).astype(jnp.bfloat16)
        mask = jnp.dot(hot, mark, preferred_element_type=jnp.float32)
        keep[t * tile : (t + 1) * tile, :] = (1.0 - mask).astype(jnp.bfloat16)


def early(slot_row, count, fb, after):
    depth, kw = fb.shape
    cap = slot_row.shape[1]
    return pl.pallas_call(
        functools.partial(early_kernel, kw // LANES),
        out_shape=[
            jax.ShapeDtypeStruct((cap, LANES), jnp.float32),
            jax.ShapeDtypeStruct((depth, kw), jnp.bfloat16),
            TOKEN,
        ],
        in_specs=[VMEM, SMEM, VMEM, ANY],
        compiler_params=params(14),
        cost_estimate=BRIEF,
        name="early",
    )(slot_row, count, fb, after)


def prepare_kernel(per_row, n, *refs):
    xs, (slot_row, count), (xg, xt, token) = refs[:n], refs[n : n + 2], refs[-3:]
    token[...] = jnp.zeros_like(token)
    depth = xs[0].shape[1]
    cap = slot_row.shape[1]
    used = lax.broadcasted_iota(jnp.int32, (cap, 1), 0) < count[0, 0]
    line = jnp.where(used, as_column(slot_row[...])[:, 0:1] // per_row, depth)
    hot = line == lax.broadcasted_iota(jnp.int32, (cap, depth), 1)
    hot = hot.astype(jnp.float32).astype(jnp.bfloat16)
    start = 0
    for x in xs:
        rows = x.shape[0]
        xg[:, start : start + rows] = lax.dot_general(
            hot, x[...], (((1,), (1,)), ((), ())), preferred_element_type=jnp.float32
        ).astype(jnp.bfloat16)
        xt[:, start : start + rows] = x[...].T
        start += rows


def prepare(xs, slot_row, count, per_row, after):
    rows, depth = sum(x.shape[0] for x in xs), xs[0].shape[1]
    cap = slot_row.shape[1]
    return pl.pallas_call(
        functools.partial(prepare_kernel, per_row, len(xs)),
        out_shape=[
            jax.ShapeDtypeStruct((cap, rows), jnp.bfloat16),
            jax.ShapeDtypeStruct((depth, rows), jnp.bfloat16),
            TOKEN,
        ],
        in_specs=[VMEM] * (len(xs) + 1) + [SMEM] + [ANY] * len(after),
        compiler_params=params(14),
        cost_estimate=BRIEF,
        name="prepare",
    )(*xs, slot_row, count, *after)


def kept_kernel(per_row, order, slopes, *refs):
    xgs, (fbk, slot_row, out, s) = refs[:-4], refs[-4:]
    cap = slot_row.shape[1]
    me = lax.axis_index("shard")
    tok_dev = slopes.shape[0] // lax.axis_size("shard")
    start = 0
    for d, low, high in order:
        rows = pl.ds(pl.multiple_of((me ^ d) * tok_dev + low, 16), high - low)
        s[start : start + high - low, :] = slopes[rows, :]
        start += high - low
    total, start = 0.0, 0
    for xg in xgs:
        part = s[start : start + xg.shape[1], :]
        total += jnp.dot(xg[...], part, preferred_element_type=jnp.float32)
        start += xg.shape[1]
    value = pick_columns(total, as_column(slot_row[...])[:, 0:1] % per_row) + fbk[...]
    out[:cap, :] = value.astype(jnp.bfloat16)
    tail = out.shape[0] - cap
    number = jnp.broadcast_to(slot_row[...], (tail, cap))
    line = lax.broadcasted_iota(jnp.int32, (tail, cap), 0)
    number = jnp.where(line == 0, number // LANES, number % LANES)
    out[cap:, :] = number.astype(jnp.float32).astype(jnp.bfloat16)


def kept(slopes, order, xgs, fbk, slot_row):
    cap = slot_row.shape[1]
    return pl.pallas_call(
        functools.partial(kept_kernel, slopes.shape[1] // LANES, order),
        out_shape=[
            jax.ShapeDtypeStruct((cap + 16, LANES), jnp.bfloat16),
            jax.ShapeDtypeStruct(slopes.shape, jnp.bfloat16),
        ],
        compiler_params=params(8),
        cost_estimate=BRIEF,
        name="kept",
    )(slopes, *xgs, fbk, slot_row)


def send_out(held, out, sems, t, tile):
    rows = pl.ds(t * tile, tile)
    return pltpu.make_async_copy(held.at[rows, :], out.at[rows, :], sems.at[t])


def residue_kernel(tile, s, *refs):
    xts, (fb, keep, out, token, held, sems) = refs[:-6], refs[-6:]
    token[...] = jnp.zeros_like(token)
    tiles = out.shape[0] // tile
    for t in range(tiles):
        rows = slice(t * tile, (t + 1) * tile)
        pseudo, start = fb[rows, :].astype(jnp.float32), 0
        for xt in xts:
            part = s[start : start + xt.shape[1], :]
            pseudo += jnp.dot(xt[rows, :], part, preferred_element_type=jnp.float32)
            start += xt.shape[1]
        held[rows, :] = jnp.where(keep[rows, :] > 0, pseudo, 0.0).astype(jnp.bfloat16)
        send_out(held, out, sems, t, tile).start()
    for t in range(tiles):
        send_out(held, out, sems, t, tile).wait()


def residue(s, xts, fb, keep):
    depth, kw = fb.shape
    tile = min(depth, 256)
    return pl.pallas_call(
        functools.partial(residue_kernel, tile),
        out_shape=[jax.ShapeDtypeStruct((depth, kw), jnp.bfloat16), TOKEN],
        in_specs=[VMEM] * (len(xts) + 3),
        out_specs=[ANY, VMEM],
        scratch_shapes=[
            pltpu.VMEM((depth, kw), jnp.bfloat16),
            pltpu.SemaphoreType.DMA((depth // tile,)),
        ],
        compiler_params=params(14),
        cost_estimate=BRIEF,
        name="residue",
    )(s, *xts, fb, keep)


def join_kernel(n, *refs):
    out, start = refs[-1], 0
    for part in refs[:n]:
        out[start : start + part.shape[0], :] = part[...]
        start += part.shape[0]


def join(parts, after):
    rows, lanes = sum(part.shape[0] for part in parts), parts[0].shape[1]
    return pl.pallas_call(
        functools.partial(join_kernel, len(parts)),
        out_shape=jax.ShapeDtypeStruct((rows, lanes), jnp.bfloat16),
        in_specs=[VMEM] * len(parts) + [ANY] * len(after),
        compiler_params=params(8),
        cost_estimate=BRIEF,
        name="join",
    )(*parts, *after)


def spread(group, wide, lines, cap, per_row):
    size = cap + 16
    for k in range(group.shape[0] // size):
        start = k * size
        tail = group[start + cap : start + size, :].astype(jnp.float32)
        number = (tail[0:1, :] * LANES + tail[1:2, :]).astype(jnp.int32)
        lines[:, k * cap : (k + 1) * cap] = jnp.broadcast_to(number // per_row, (8, cap))
        column = jnp.broadcast_to((number % per_row).astype(jnp.float32), (LANES, cap)).T
        value = group[start : start + cap, :].astype(jnp.float32)
        for c in range(per_row):
            wide[k * cap : (k + 1) * cap, c * LANES : (c + 1) * LANES] = jnp.where(
                column == c, value, 0.0
            ).astype(jnp.bfloat16)


def place(lines, wide, t, tile):
    line = lax.broadcasted_iota(jnp.int32, (tile, lines.shape[1]), 0) + t * tile
    hot = (lines[0:1, :] == line).astype(jnp.float32).astype(jnp.bfloat16)
    return jnp.dot(hot, wide[...], preferred_element_type=jnp.float32)


def half_kernel(cap, per_row, tile, group, out, wide, lines):
    spread(group, wide, lines, cap, per_row)
    for t in range(out.shape[0] // tile):
        out[t * tile : (t + 1) * tile, :] = place(lines, wide, t, tile)


def outer_kernel(cap, per_row, tile, n, group, half, out, wide, lines, held, sems):
    spread(group, wide, lines, cap, per_row)
    tiles = out.shape[0] // tile
    for t in range(tiles):
        rows = slice(t * tile, (t + 1) * tile)
        held[rows, :] = (half[rows, :] + place(lines, wide, t, tile)) * (1.0 / n)
        send_out(held, out, sems, t, tile).start()
    for t in range(tiles):
        send_out(held, out, sems, t, tile).wait()


def outer(groups, cap, depth, kw):
    slots = groups[0].shape[0] // (cap + 16) * cap
    n = 2 * slots // cap
    tile = min(depth, 256)
    shape = jax.ShapeDtypeStruct((depth, kw), jnp.float32)
    scratch = [pltpu.VMEM((slots, kw), jnp.bfloat16), pltpu.VMEM((8, slots), jnp.int32)]
    half = pl.pallas_call(
        functools.partial(half_kernel, cap, kw // LANES, tile),
        out_shape=shape,
        scratch_shapes=scratch,
        compiler_params=params(14),
        cost_estimate=BRIEF,
        name="half",
    )(groups[0])
    return pl.pallas_call(
        functools.partial(outer_kernel, cap, kw // LANES, tile, n),
        out_shape=shape,
        out_specs=ANY,
        scratch_shapes=scratch
        + [pltpu.VMEM((depth, kw), jnp.float32), pltpu.SemaphoreType.DMA((depth // tile,))],
        compiler_params=params(14),
        cost_estimate=BRIEF,
        name="outer",
    )(groups[1], half)


def on_device(inputs, target, weights, feedback, counts, blocks):
    tokens, w, fb = inputs[0], weights[0], feedback[0]
    n_shard, n_rep = lax.axis_size("shard"), lax.axis_size("rep")
    tok_dev = tokens.shape[0]
    depth, kw = w.shape
    early_rows = tok_dev * 3 // 4
    spans = [(0, early_rows), (early_rows, tok_dev)]
    per_row = kw // LANES
    slot_row = blocks[0]
    near = [d for d in range(1, n_shard) if d & (d - 1) == 0]
    far = [d for d in range(1, n_shard) if d & (d - 1) != 0]

    me = lax.axis_index("shard")
    far_out = [lax.dynamic_slice(tokens, (0, (me ^ d) * depth), (tok_dev, depth)) for d in far]
    far_in = [swap(x, "shard", n_shard, d) for x, d in zip(far_out, far)]
    near_out, token = [], far_out[0]
    for low, high in spans:
        *out, token = cut(tokens, depth, [(d, low, high - low) for d in near], [token])
        near_out.append(out)
        if low == 0:
            fbk, keep, token = early(slot_row, counts, fb, token)
    near_in = [[swap(x, "shard", n_shard, d) for x, d in zip(out, near)] for out in near_out]

    own, _ = cut(tokens, depth, [(0, 0, tok_dev)], [token])

    brief, wide = jnp.bfloat16, jnp.float32
    (mine, *products), x_far = project([own] + far_in, [wide] + [brief] * len(far), w, [])
    whole = [swap(p, "shard", n_shard, d) for p, d in zip(products, far)]
    xg_far, xt_far, token = prepare([x_far], slot_row, counts, per_row, [])
    after, shares, x_near = [token], [], []
    for part in range(len(spans)):
        products, x = project(near_in[part], [brief] * len(near), w, after)
        shares.append([swap(p, "shard", n_shard, d) for p, d in zip(products, near)])
        x_near.append(x)
        after = products[-1:]
    xg_near, xt_near, token = prepare(x_near, slot_row, counts, per_row, [products[0]])
    shares = [share[k] for k in range(len(near)) for share in shares]
    slopes = slope(target[0], mine, whole, shares, spans, token, n_shard)
    slopes = lax.all_to_all(slopes, "shard", 0, 0).reshape(-1, kw)

    order = [(d, 0, tok_dev) for d in [0] + far]
    order += [(d, low, high) for low, high in spans for d in near]
    message, slopes = kept(slopes, order, [xg_far, xg_near], fbk, slot_row)
    same_core = [swap(message, "rep", n_rep, d) for d in range(n_rep - 2, 0, -2)]
    new_feedback, token = residue(slopes, [xt_far, xt_near], fb, keep)
    joined, after = message, [token]
    for received in same_core:
        joined, after = join([joined, received], after), []
    groups = [joined, swap(joined, "rep", n_rep, 1)]
    return outer(groups, message.shape[0] - 16, depth, kw), new_feedback[None]


def solution(mesh):
    placed = (
        P("rep", "shard", None),
        P("rep", "shard", None),
        P("rep", "shard", None),
        P("rep", "shard", None),
        P("rep", "shard"),
        P("rep", "shard", None),
    )
    return jax.shard_map(
        on_device,
        mesh=mesh,
        in_specs=placed,
        out_specs=(P("shard", None), P("rep", "shard", None)),
        check_vma=False,
    )
```

```python
import functools

import jax
import jax.numpy as jnp
from jax import lax
from jax.experimental import pallas as pl
from jax.experimental.pallas import tpu as pltpu
from jax.sharding import PartitionSpec as P

LANES = 128
ANY = pl.BlockSpec(memory_space=pl.ANY)
BRIEF = pl.CostEstimate(flops=1000, bytes_accessed=1000, transcendentals=0)
VMEM = pl.BlockSpec(memory_space=pltpu.VMEM)
SMEM = pl.BlockSpec(memory_space=pltpu.SMEM)
MIB = 1024 * 1024
TOKEN = jax.ShapeDtypeStruct((8, LANES), jnp.float32)


def params(mib):
    return pltpu.CompilerParams(vmem_limit_bytes=mib * MIB)


def swap(x, axis, n, d):
    return lax.ppermute(x, axis, [(i, i ^ d) for i in range(n)])


def cut_kernel(cuts, tokens, *refs):
    outs, (token, sems) = refs[-len(cuts) - 2 : -2], refs[-2:]
    token[...] = jnp.zeros_like(token)
    me = lax.axis_index("shard")
    copies = []
    for k, (d, low, rows) in enumerate(cuts):
        depth = outs[k].shape[1]
        columns = pl.ds(pl.multiple_of((me ^ d) * depth, LANES), depth)
        copy = pltpu.make_async_copy(tokens.at[pl.ds(low, rows), columns], outs[k], sems.at[k])
        copy.start()
        copies.append(copy)
    for copy in copies:
        copy.wait()


def cut(tokens, depth, cuts, after):
    return pl.pallas_call(
        functools.partial(cut_kernel, cuts),
        out_shape=[jax.ShapeDtypeStruct((rows, depth), tokens.dtype) for _, _, rows in cuts]
        + [TOKEN],
        in_specs=[ANY] * (1 + len(after)),
        out_specs=[ANY] * len(cuts) + [VMEM],
        scratch_shapes=[pltpu.SemaphoreType.DMA((len(cuts),))],
        compiler_params=params(6),
        cost_estimate=BRIEF,
        name="cut",
    )(tokens, *after)


def project_kernel(n, m, *refs):
    pieces, w, outs, x = refs[:n], refs[n], refs[-m - 1 : -1], refs[-1]
    start = 0
    for piece in pieces:
        x[start : start + piece.shape[0], :] = piece[...]
        start += piece.shape[0]
    full = jnp.dot(x[...], w[...], preferred_element_type=jnp.float32)
    start = 0
    for out in outs:
        out[...] = full[start : start + out.shape[0], :].astype(out.dtype)
        start += out.shape[0]


def project(pieces, outs, w, after):
    n = len(pieces)
    rows, depth = sum(p.shape[0] for p in pieces), pieces[0].shape[1]
    kw = w.shape[1]
    result = pl.pallas_call(
        functools.partial(project_kernel, n, len(outs)),
        out_shape=[jax.ShapeDtypeStruct((r, kw), t) for r, t in outs]
        + [jax.ShapeDtypeStruct((rows, depth), jnp.bfloat16)],
        in_specs=[VMEM] * (n + 1) + [ANY] * len(after),
        compiler_params=params(14),
        cost_estimate=BRIEF,
        name="project",
    )(*pieces, w, *after)
    return result[:-1], result[-1]


def slope_kernel(tok_dev, n, spans, *refs):
    goal, mine, out = refs[0], refs[1], refs[-1]
    whole = refs[2 : 2 + n]
    shares = refs[2 + n : -2]
    for part, (low, high) in enumerate(spans):
        key_proj = mine[low:high, :]
        for product in whole:
            key_proj += product[low:high, :].astype(jnp.float32)
        for product in shares[part :: len(spans)]:
            key_proj += product[...].astype(jnp.float32)
        gap = key_proj - goal[low:high, :].astype(jnp.float32)
        out[low:high, :] = (gap / tok_dev).astype(jnp.bfloat16)


def slope(goal, mine, whole, shares, spans, after):
    return pl.pallas_call(
        functools.partial(slope_kernel, goal.shape[0], len(whole), spans),
        out_shape=jax.ShapeDtypeStruct(mine.shape, jnp.bfloat16),
        in_specs=[VMEM] * (2 + len(whole) + len(shares)) + [ANY],
        compiler_params=params(8),
        cost_estimate=BRIEF,
        name="slope",
    )(goal, mine, *whole, *shares, after)


def as_column(row):
    size = row.shape[1]
    return jnp.broadcast_to(row.astype(jnp.float32), (size, size)).T.astype(jnp.int32)


def pick_columns(wide, column):
    out = jnp.zeros((wide.shape[0], LANES), jnp.float32)
    for c in range(wide.shape[1] // LANES):
        out += jnp.where(column == c, wide[:, c * LANES : (c + 1) * LANES], 0.0)
    return out


def early_kernel(per_row, slot_row, count, fb, after, fbk, keep, token):
    token[...] = jnp.zeros_like(token)
    depth, kw = fb.shape
    cap = slot_row.shape[1]
    slot = as_column(slot_row[...])[:, 0:1]
    hot = slot // per_row == lax.broadcasted_iota(jnp.int32, (cap, depth), 1)
    hot = hot.astype(jnp.float32).astype(jnp.bfloat16)
    used = lax.broadcasted_iota(jnp.int32, (cap, 1), 0) < count[0, 0]
    wide = jnp.dot(hot, fb[...], preferred_element_type=jnp.float32)
    fbk[...] = jnp.where(used, pick_columns(wide, slot % per_row), 0.0)
    group = lax.broadcasted_iota(jnp.int32, (cap, kw), 1) // LANES
    mark = jnp.where(used & (slot % per_row == group), 1.0, 0.0).astype(jnp.bfloat16)
    tile = min(depth, 512)
    for t in range(depth // tile):
        line = lax.broadcasted_iota(jnp.int32, (tile, cap), 0) + t * tile
        hot = (slot_row[...] // per_row == line).astype(jnp.float32).astype(jnp.bfloat16)
        mask = jnp.dot(hot, mark, preferred_element_type=jnp.float32)
        keep[t * tile : (t + 1) * tile, :] = (1.0 - mask).astype(jnp.bfloat16)


def early(slot_row, count, fb, after):
    depth, kw = fb.shape
    cap = slot_row.shape[1]
    return pl.pallas_call(
        functools.partial(early_kernel, kw // LANES),
        out_shape=[
            jax.ShapeDtypeStruct((cap, LANES), jnp.float32),
            jax.ShapeDtypeStruct((depth, kw), jnp.bfloat16),
            TOKEN,
        ],
        in_specs=[VMEM, SMEM, VMEM, ANY],
        compiler_params=params(14),
        cost_estimate=BRIEF,
        name="early",
    )(slot_row, count, fb, after)


def prepare_kernel(per_row, n, *refs):
    xs, (slot_row, count), (xg, xt, token) = refs[:n], refs[n : n + 2], refs[-3:]
    token[...] = jnp.zeros_like(token)
    depth = xs[0].shape[1]
    cap = slot_row.shape[1]
    used = lax.broadcasted_iota(jnp.int32, (cap, 1), 0) < count[0, 0]
    line = jnp.where(used, as_column(slot_row[...])[:, 0:1] // per_row, depth)
    hot = line == lax.broadcasted_iota(jnp.int32, (cap, depth), 1)
    hot = hot.astype(jnp.float32).astype(jnp.bfloat16)
    start = 0
    for x in xs:
        rows = x.shape[0]
        xg[:, start : start + rows] = lax.dot_general(
            hot, x[...], (((1,), (1,)), ((), ())), preferred_element_type=jnp.float32
        ).astype(jnp.bfloat16)
        xt[:, start : start + rows] = x[...].T
        start += rows


def prepare(xs, slot_row, count, per_row, after):
    rows, depth = sum(x.shape[0] for x in xs), xs[0].shape[1]
    cap = slot_row.shape[1]
    return pl.pallas_call(
        functools.partial(prepare_kernel, per_row, len(xs)),
        out_shape=[
            jax.ShapeDtypeStruct((cap, rows), jnp.bfloat16),
            jax.ShapeDtypeStruct((depth, rows), jnp.bfloat16),
            TOKEN,
        ],
        in_specs=[VMEM] * (len(xs) + 1) + [SMEM] + [ANY] * len(after),
        compiler_params=params(14),
        cost_estimate=BRIEF,
        name="prepare",
    )(*xs, slot_row, count, *after)


def stack(slopes, order, s):
    start = 0
    for k, low, high in order:
        s[start : start + high - low, :] = slopes[k][low:high, :]
        start += high - low


def gather_kernel(order, *refs):
    slopes, (xg, out, s) = refs[:-3], refs[-3:]
    stack(slopes, order, s)
    out[...] = jnp.dot(xg[...], s[...], preferred_element_type=jnp.float32)


def gather(slopes, order, xg):
    kw = slopes[0].shape[1]
    return pl.pallas_call(
        functools.partial(gather_kernel, order),
        out_shape=jax.ShapeDtypeStruct((xg.shape[0], kw), jnp.float32),
        scratch_shapes=[pltpu.VMEM((xg.shape[1], kw), jnp.bfloat16)],
        compiler_params=params(8),
        cost_estimate=BRIEF,
        name="gather",
    )(*slopes, xg)


def kept_kernel(per_row, order, *refs):
    slopes, (wide, xg, fbk, slot_row, out, s) = refs[:-6], refs[-6:]
    cap = slot_row.shape[1]
    stack(slopes, order, s)
    total = wide[...] + jnp.dot(xg[...], s[...], preferred_element_type=jnp.float32)
    value = pick_columns(total, as_column(slot_row[...])[:, 0:1] % per_row) + fbk[...]
    out[:cap, :] = value.astype(jnp.bfloat16)
    tail = out.shape[0] - cap
    number = jnp.broadcast_to(slot_row[...], (tail, cap))
    line = lax.broadcasted_iota(jnp.int32, (tail, cap), 0)
    number = jnp.where(line == 0, number // LANES, number % LANES)
    out[cap:, :] = number.astype(jnp.float32).astype(jnp.bfloat16)


def kept(slopes, order, wide, xg, fbk, slot_row):
    cap, kw = wide.shape
    return pl.pallas_call(
        functools.partial(kept_kernel, kw // LANES, order),
        out_shape=jax.ShapeDtypeStruct((cap + 16, LANES), jnp.bfloat16),
        scratch_shapes=[pltpu.VMEM((xg.shape[1], kw), jnp.bfloat16)],
        compiler_params=params(8),
        cost_estimate=BRIEF,
        name="kept",
    )(*slopes, wide, xg, fbk, slot_row)


def send_out(held, out, sems, t, tile):
    rows = pl.ds(t * tile, tile)
    return pltpu.make_async_copy(held.at[rows, :], out.at[rows, :], sems.at[t])


def residue_kernel(order, tile, *refs):
    n = len({k for k, _, _ in order})
    slopes, xts, (fb, keep, out, token, s, held, sems) = refs[:n], refs[n:-7], refs[-7:]
    token[...] = jnp.zeros_like(token)
    stack(slopes, order, s)
    tiles = out.shape[0] // tile
    for t in range(tiles):
        rows = slice(t * tile, (t + 1) * tile)
        pseudo, start = fb[rows, :].astype(jnp.float32), 0
        for xt in xts:
            part = s[start : start + xt.shape[1], :]
            pseudo += jnp.dot(xt[rows, :], part, preferred_element_type=jnp.float32)
            start += xt.shape[1]
        held[rows, :] = jnp.where(keep[rows, :] > 0, pseudo, 0.0).astype(jnp.bfloat16)
        send_out(held, out, sems, t, tile).start()
    for t in range(tiles):
        send_out(held, out, sems, t, tile).wait()


def residue(slopes, order, xts, fb, keep):
    depth, kw = fb.shape
    total = sum(xt.shape[1] for xt in xts)
    tile = min(depth, 256)
    return pl.pallas_call(
        functools.partial(residue_kernel, order, tile),
        out_shape=[
            jax.ShapeDtypeStruct((depth, kw), jnp.bfloat16),
            TOKEN,
        ],
        in_specs=[VMEM] * (len(slopes) + len(xts) + 2),
        out_specs=[ANY, VMEM],
        scratch_shapes=[
            pltpu.VMEM((total, kw), jnp.bfloat16),
            pltpu.VMEM((depth, kw), jnp.bfloat16),
            pltpu.SemaphoreType.DMA((depth // tile,)),
        ],
        compiler_params=params(14),
        cost_estimate=BRIEF,
        name="residue",
    )(*slopes, *xts, fb, keep)


def join_kernel(n, *refs):
    out, start = refs[-1], 0
    for part in refs[:n]:
        out[start : start + part.shape[0], :] = part[...]
        start += part.shape[0]


def join(parts, after):
    rows, lanes = sum(part.shape[0] for part in parts), parts[0].shape[1]
    return pl.pallas_call(
        functools.partial(join_kernel, len(parts)),
        out_shape=jax.ShapeDtypeStruct((rows, lanes), jnp.bfloat16),
        in_specs=[VMEM] * len(parts) + [ANY] * len(after),
        compiler_params=params(8),
        cost_estimate=BRIEF,
        name="join",
    )(*parts, *after)


def spread(group, wide, lines, cap, per_row):
    size = cap + 16
    for k in range(group.shape[0] // size):
        start = k * size
        tail = group[start + cap : start + size, :].astype(jnp.float32)
        number = (tail[0:1, :] * LANES + tail[1:2, :]).astype(jnp.int32)
        lines[:, k * cap : (k + 1) * cap] = jnp.broadcast_to(number // per_row, (8, cap))
        column = jnp.broadcast_to((number % per_row).astype(jnp.float32), (LANES, cap)).T
        value = group[start : start + cap, :].astype(jnp.float32)
        for c in range(per_row):
            wide[k * cap : (k + 1) * cap, c * LANES : (c + 1) * LANES] = jnp.where(
                column == c, value, 0.0
            ).astype(jnp.bfloat16)


def place(lines, wide, t, tile):
    line = lax.broadcasted_iota(jnp.int32, (tile, lines.shape[1]), 0) + t * tile
    hot = (lines[0:1, :] == line).astype(jnp.float32).astype(jnp.bfloat16)
    return jnp.dot(hot, wide[...], preferred_element_type=jnp.float32)


def half_kernel(cap, per_row, tile, group, out, wide, lines):
    spread(group, wide, lines, cap, per_row)
    for t in range(out.shape[0] // tile):
        out[t * tile : (t + 1) * tile, :] = place(lines, wide, t, tile)


def outer_kernel(cap, per_row, tile, n, group, half, out, wide, lines, held, sems):
    spread(group, wide, lines, cap, per_row)
    tiles = out.shape[0] // tile
    for t in range(tiles):
        rows = slice(t * tile, (t + 1) * tile)
        held[rows, :] = (half[rows, :] + place(lines, wide, t, tile)) * (1.0 / n)
        send_out(held, out, sems, t, tile).start()
    for t in range(tiles):
        send_out(held, out, sems, t, tile).wait()


def outer(groups, cap, depth, kw):
    slots = groups[0].shape[0] // (cap + 16) * cap
    n = 2 * slots // cap
    tile = min(depth, 256)
    shape = jax.ShapeDtypeStruct((depth, kw), jnp.float32)
    scratch = [pltpu.VMEM((slots, kw), jnp.bfloat16), pltpu.VMEM((8, slots), jnp.int32)]
    half = pl.pallas_call(
        functools.partial(half_kernel, cap, kw // LANES, tile),
        out_shape=shape,
        scratch_shapes=scratch,
        compiler_params=params(14),
        cost_estimate=BRIEF,
        name="half",
    )(groups[0])
    return pl.pallas_call(
        functools.partial(outer_kernel, cap, kw // LANES, tile, n),
        out_shape=shape,
        out_specs=ANY,
        scratch_shapes=scratch
        + [pltpu.VMEM((depth, kw), jnp.float32), pltpu.SemaphoreType.DMA((depth // tile,))],
        compiler_params=params(14),
        cost_estimate=BRIEF,
        name="outer",
    )(groups[1], half)


def on_device(inputs, target, weights, feedback, counts, blocks):
    tokens, w, fb = inputs[0], weights[0], feedback[0]
    n_shard, n_rep = lax.axis_size("shard"), lax.axis_size("rep")
    tok_dev = tokens.shape[0]
    depth, kw = w.shape
    early_rows = tok_dev // 2
    spans = [(0, early_rows), (early_rows, tok_dev)]
    per_row = kw // LANES
    slot_row = blocks[0]
    near = [d for d in range(1, n_shard) if d & (d - 1) == 0]
    far = [d for d in range(1, n_shard) if d & (d - 1) != 0]

    me = lax.axis_index("shard")
    rows = tok_dev // 2 if n_shard == 4 else tok_dev
    far_out = [
        [
            lax.dynamic_slice(tokens, (low, (me ^ d) * depth), (rows, depth))
            for low in range(0, tok_dev, rows)
        ]
        for d in far
    ]
    if n_shard == 4:
        ((by_x, by_y),) = far_out
        by_x, by_y = swap(by_x, "shard", n_shard, 1), swap(by_y, "shard", n_shard, 2)
        hops = [by_x, by_y]
        far_in = [swap(by_x, "shard", n_shard, 2), swap(by_y, "shard", n_shard, 1)]
    else:
        hops = []
        far_in = [swap(x, "shard", n_shard, d) for (x,), d in zip(far_out, far)]
    near_out, after = [], [far_out[0][0]]
    for low, high in spans:
        *out, token = cut(tokens, depth, [(d, low, high - low) for d in near], after)
        near_out.append(out)
        if low == 0:
            fbk, keep, token = early(slot_row, counts, fb, token)
            after = [token] + hops
    near_in = [[swap(x, "shard", n_shard, d) for x, d in zip(out, near)] for out in near_out]

    own, _ = cut(tokens, depth, [(0, 0, tok_dev)], [token])

    brief, wide = jnp.bfloat16, jnp.float32
    near_outs = [[(high - low, brief)] * len(near) for low, high in spans]
    early_near, x_early = project(near_in[0], near_outs[0], w, [])
    outs = [(tok_dev, wide)] + [(tok_dev, brief)] * len(far)
    (mine, *products), x_far = project([own] + far_in, outs, w, early_near[-1:])
    whole = [swap(p, "shard", n_shard, d) for p, d in zip(products, far)]
    xg_far, xt_far, token = prepare([x_far], slot_row, counts, per_row, products)
    late_near, x_late = project(near_in[1], near_outs[1], w, [token])
    shares = [
        [swap(p, "shard", n_shard, d) for p, d in zip(part, near)]
        for part in (early_near, late_near)
    ]
    x_near = [x_early, x_late]
    xg_near, xt_near, token = prepare(x_near, slot_row, counts, per_row, late_near[:1])
    shares = [share[k] for k in range(len(near)) for share in shares]
    slopes = slope(target[0], mine, whole, shares, spans, token)
    slopes = [slopes] + [swap(slopes, "shard", n_shard, d) for d in far + near]

    n_far = 1 + len(far)
    order_far = [(k, 0, tok_dev) for k in range(n_far)]
    order_near = [(k, low, high) for low, high in spans for k in range(len(near))]
    wide = gather(slopes[:n_far], order_far, xg_far)
    message = kept(slopes[n_far:], order_near, wide, xg_near, fbk, slot_row)
    same_core = [swap(message, "rep", n_rep, d) for d in range(n_rep - 2, 0, -2)]
    order = order_far + [(n_far + k, low, high) for k, low, high in order_near]
    new_feedback, token = residue(slopes, order, [xt_far, xt_near], fb, keep)
    joined, after = message, [token]
    for received in same_core:
        joined, after = join([joined, received], after), []
    groups = [joined, swap(joined, "rep", n_rep, 1)]
    return outer(groups, message.shape[0] - 16, depth, kw), new_feedback[None]


def solution(mesh):
    placed = (
        P("rep", "shard", None),
        P("rep", "shard", None),
        P("rep", "shard", None),
        P("rep", "shard", None),
        P("rep", "shard"),
        P("rep", "shard", None),
    )
    return jax.shard_map(
        on_device,
        mesh=mesh,
        in_specs=placed,
        out_specs=(P("shard", None), P("rep", "shard", None)),
        check_vma=False,
    )
```

```python
import functools

import jax
import jax.numpy as jnp
from jax import lax
from jax.experimental import pallas as pl
from jax.experimental.pallas import tpu as pltpu
from jax.sharding import PartitionSpec as P

LANES = 128
ANY = pl.BlockSpec(memory_space=pl.ANY)
BRIEF = pl.CostEstimate(flops=1000, bytes_accessed=1000, transcendentals=0)
VMEM = pl.BlockSpec(memory_space=pltpu.VMEM)
SMEM = pl.BlockSpec(memory_space=pltpu.SMEM)
MIB = 1024 * 1024
TOKEN = jax.ShapeDtypeStruct((8, LANES), jnp.float32)


def params(mib):
    return pltpu.CompilerParams(vmem_limit_bytes=mib * MIB)


def swap(x, axis, n, d):
    return lax.ppermute(x, axis, [(i, i ^ d) for i in range(n)])


def cut_kernel(cuts, tokens, *refs):
    outs, (token, sems) = refs[-len(cuts) - 2 : -2], refs[-2:]
    token[...] = jnp.zeros_like(token)
    me = lax.axis_index("shard")
    copies = []
    for k, (d, low, rows) in enumerate(cuts):
        depth = outs[k].shape[1]
        columns = pl.ds(pl.multiple_of((me ^ d) * depth, LANES), depth)
        copy = pltpu.make_async_copy(tokens.at[pl.ds(low, rows), columns], outs[k], sems.at[k])
        copy.start()
        copies.append(copy)
    for copy in copies:
        copy.wait()


def cut(tokens, depth, cuts, after):
    return pl.pallas_call(
        functools.partial(cut_kernel, cuts),
        out_shape=[jax.ShapeDtypeStruct((rows, depth), tokens.dtype) for _, _, rows in cuts]
        + [TOKEN],
        in_specs=[ANY] * (1 + len(after)),
        out_specs=[ANY] * len(cuts) + [VMEM],
        scratch_shapes=[pltpu.SemaphoreType.DMA((len(cuts),))],
        compiler_params=params(6),
        cost_estimate=BRIEF,
        name="cut",
    )(tokens, *after)


def project_kernel(n, m, *refs):
    pieces, w, outs, x = refs[:n], refs[n], refs[-m - 1 : -1], refs[-1]
    start = 0
    for piece in pieces:
        x[start : start + piece.shape[0], :] = piece[...]
        start += piece.shape[0]
    full = jnp.dot(x[...], w[...], preferred_element_type=jnp.float32)
    start = 0
    for out in outs:
        out[...] = full[start : start + out.shape[0], :].astype(out.dtype)
        start += out.shape[0]


def project(pieces, outs, w, after):
    n = len(pieces)
    rows, depth = sum(p.shape[0] for p in pieces), pieces[0].shape[1]
    kw = w.shape[1]
    result = pl.pallas_call(
        functools.partial(project_kernel, n, len(outs)),
        out_shape=[jax.ShapeDtypeStruct((r, kw), t) for r, t in outs]
        + [jax.ShapeDtypeStruct((rows, depth), jnp.bfloat16)],
        in_specs=[VMEM] * (n + 1) + [ANY] * len(after),
        compiler_params=params(14),
        cost_estimate=BRIEF,
        name="project",
    )(*pieces, w, *after)
    return result[:-1], result[-1]


def slope_kernel(tok_dev, n, spans, *refs):
    goal, mine, out = refs[0], refs[1], refs[-1]
    whole = refs[2 : 2 + n]
    shares = refs[2 + n : -2]
    for part, (low, high) in enumerate(spans):
        key_proj = mine[low:high, :]
        for product in whole:
            key_proj += product[low:high, :].astype(jnp.float32)
        for product in shares[part :: len(spans)]:
            key_proj += product[...].astype(jnp.float32)
        gap = key_proj - goal[low:high, :].astype(jnp.float32)
        out[low:high, :] = (gap / tok_dev).astype(jnp.bfloat16)


def slope(goal, mine, whole, shares, spans, after):
    return pl.pallas_call(
        functools.partial(slope_kernel, goal.shape[0], len(whole), spans),
        out_shape=jax.ShapeDtypeStruct(mine.shape, jnp.bfloat16),
        in_specs=[VMEM] * (2 + len(whole) + len(shares)) + [ANY],
        compiler_params=params(8),
        cost_estimate=BRIEF,
        name="slope",
    )(goal, mine, *whole, *shares, after)


def as_column(row):
    size = row.shape[1]
    return jnp.broadcast_to(row.astype(jnp.float32), (size, size)).T.astype(jnp.int32)


def pick_columns(wide, column):
    out = jnp.zeros((wide.shape[0], LANES), jnp.float32)
    for c in range(wide.shape[1] // LANES):
        out += jnp.where(column == c, wide[:, c * LANES : (c + 1) * LANES], 0.0)
    return out


def early_kernel(per_row, slot_row, count, fb, after, fbk, keep, token):
    token[...] = jnp.zeros_like(token)
    depth, kw = fb.shape
    cap = slot_row.shape[1]
    slot = as_column(slot_row[...])[:, 0:1]
    hot = slot // per_row == lax.broadcasted_iota(jnp.int32, (cap, depth), 1)
    hot = hot.astype(jnp.float32).astype(jnp.bfloat16)
    used = lax.broadcasted_iota(jnp.int32, (cap, 1), 0) < count[0, 0]
    wide = jnp.dot(hot, fb[...], preferred_element_type=jnp.float32)
    fbk[...] = jnp.where(used, pick_columns(wide, slot % per_row), 0.0)
    group = lax.broadcasted_iota(jnp.int32, (cap, kw), 1) // LANES
    mark = jnp.where(used & (slot % per_row == group), 1.0, 0.0).astype(jnp.bfloat16)
    tile = min(depth, 512)
    for t in range(depth // tile):
        line = lax.broadcasted_iota(jnp.int32, (tile, cap), 0) + t * tile
        hot = (slot_row[...] // per_row == line).astype(jnp.float32).astype(jnp.bfloat16)
        mask = jnp.dot(hot, mark, preferred_element_type=jnp.float32)
        keep[t * tile : (t + 1) * tile, :] = (1.0 - mask).astype(jnp.bfloat16)


def early(slot_row, count, fb, after):
    depth, kw = fb.shape
    cap = slot_row.shape[1]
    return pl.pallas_call(
        functools.partial(early_kernel, kw // LANES),
        out_shape=[
            jax.ShapeDtypeStruct((cap, LANES), jnp.float32),
            jax.ShapeDtypeStruct((depth, kw), jnp.bfloat16),
            TOKEN,
        ],
        in_specs=[VMEM, SMEM, VMEM, ANY],
        compiler_params=params(14),
        cost_estimate=BRIEF,
        name="early",
    )(slot_row, count, fb, after)


def prepare_kernel(per_row, n, *refs):
    xs, (slot_row, count), (xg, xt, token) = refs[:n], refs[n : n + 2], refs[-3:]
    token[...] = jnp.zeros_like(token)
    depth = xs[0].shape[1]
    cap = slot_row.shape[1]
    used = lax.broadcasted_iota(jnp.int32, (cap, 1), 0) < count[0, 0]
    line = jnp.where(used, as_column(slot_row[...])[:, 0:1] // per_row, depth)
    hot = line == lax.broadcasted_iota(jnp.int32, (cap, depth), 1)
    hot = hot.astype(jnp.float32).astype(jnp.bfloat16)
    start = 0
    for x in xs:
        rows = x.shape[0]
        xg[:, start : start + rows] = lax.dot_general(
            hot, x[...], (((1,), (1,)), ((), ())), preferred_element_type=jnp.float32
        ).astype(jnp.bfloat16)
        xt[:, start : start + rows] = x[...].T
        start += rows


def prepare(xs, slot_row, count, per_row, after):
    rows, depth = sum(x.shape[0] for x in xs), xs[0].shape[1]
    cap = slot_row.shape[1]
    return pl.pallas_call(
        functools.partial(prepare_kernel, per_row, len(xs)),
        out_shape=[
            jax.ShapeDtypeStruct((cap, rows), jnp.bfloat16),
            jax.ShapeDtypeStruct((depth, rows), jnp.bfloat16),
            TOKEN,
        ],
        in_specs=[VMEM] * (len(xs) + 1) + [SMEM] + [ANY] * len(after),
        compiler_params=params(14),
        cost_estimate=BRIEF,
        name="prepare",
    )(*xs, slot_row, count, *after)


def stack(slopes, order, s):
    start = 0
    for k, low, high in order:
        s[start : start + high - low, :] = slopes[k][low:high, :]
        start += high - low


def gather_kernel(order, *refs):
    slopes, (xg, out, s) = refs[:-3], refs[-3:]
    stack(slopes, order, s)
    out[...] = jnp.dot(xg[...], s[...], preferred_element_type=jnp.float32)


def gather(slopes, order, xg):
    kw = slopes[0].shape[1]
    return pl.pallas_call(
        functools.partial(gather_kernel, order),
        out_shape=jax.ShapeDtypeStruct((xg.shape[0], kw), jnp.float32),
        scratch_shapes=[pltpu.VMEM((xg.shape[1], kw), jnp.bfloat16)],
        compiler_params=params(8),
        cost_estimate=BRIEF,
        name="gather",
    )(*slopes, xg)


def kept_kernel(per_row, order, *refs):
    slopes, (wide, xg, fbk, slot_row, out, s) = refs[:-6], refs[-6:]
    cap = slot_row.shape[1]
    stack(slopes, order, s)
    total = wide[...] + jnp.dot(xg[...], s[...], preferred_element_type=jnp.float32)
    value = pick_columns(total, as_column(slot_row[...])[:, 0:1] % per_row) + fbk[...]
    out[:cap, :] = value.astype(jnp.bfloat16)
    tail = out.shape[0] - cap
    number = jnp.broadcast_to(slot_row[...], (tail, cap))
    line = lax.broadcasted_iota(jnp.int32, (tail, cap), 0)
    number = jnp.where(line == 0, number // LANES, number % LANES)
    out[cap:, :] = number.astype(jnp.float32).astype(jnp.bfloat16)


def kept(slopes, order, wide, xg, fbk, slot_row):
    cap, kw = wide.shape
    return pl.pallas_call(
        functools.partial(kept_kernel, kw // LANES, order),
        out_shape=jax.ShapeDtypeStruct((cap + 16, LANES), jnp.bfloat16),
        scratch_shapes=[pltpu.VMEM((xg.shape[1], kw), jnp.bfloat16)],
        compiler_params=params(8),
        cost_estimate=BRIEF,
        name="kept",
    )(*slopes, wide, xg, fbk, slot_row)


def send_out(held, out, sems, t, tile):
    rows = pl.ds(t * tile, tile)
    return pltpu.make_async_copy(held.at[rows, :], out.at[rows, :], sems.at[t])


def residue_kernel(order, tile, *refs):
    n = len({k for k, _, _ in order})
    slopes, xts, (fb, keep, out, token, s, held, sems) = refs[:n], refs[n:-7], refs[-7:]
    token[...] = jnp.zeros_like(token)
    stack(slopes, order, s)
    tiles = out.shape[0] // tile
    for t in range(tiles):
        rows = slice(t * tile, (t + 1) * tile)
        pseudo, start = fb[rows, :].astype(jnp.float32), 0
        for xt in xts:
            part = s[start : start + xt.shape[1], :]
            pseudo += jnp.dot(xt[rows, :], part, preferred_element_type=jnp.float32)
            start += xt.shape[1]
        held[rows, :] = jnp.where(keep[rows, :] > 0, pseudo, 0.0).astype(jnp.bfloat16)
        send_out(held, out, sems, t, tile).start()
    for t in range(tiles):
        send_out(held, out, sems, t, tile).wait()


def residue(slopes, order, xts, fb, keep):
    depth, kw = fb.shape
    total = sum(xt.shape[1] for xt in xts)
    tile = min(depth, 256)
    return pl.pallas_call(
        functools.partial(residue_kernel, order, tile),
        out_shape=[
            jax.ShapeDtypeStruct((depth, kw), jnp.bfloat16),
            TOKEN,
        ],
        in_specs=[VMEM] * (len(slopes) + len(xts) + 2),
        out_specs=[ANY, VMEM],
        scratch_shapes=[
            pltpu.VMEM((total, kw), jnp.bfloat16),
            pltpu.VMEM((depth, kw), jnp.bfloat16),
            pltpu.SemaphoreType.DMA((depth // tile,)),
        ],
        compiler_params=params(14),
        cost_estimate=BRIEF,
        name="residue",
    )(*slopes, *xts, fb, keep)


def join_kernel(n, *refs):
    out, start = refs[-1], 0
    for part in refs[:n]:
        out[start : start + part.shape[0], :] = part[...]
        start += part.shape[0]


def join(parts, after):
    rows, lanes = sum(part.shape[0] for part in parts), parts[0].shape[1]
    return pl.pallas_call(
        functools.partial(join_kernel, len(parts)),
        out_shape=jax.ShapeDtypeStruct((rows, lanes), jnp.bfloat16),
        in_specs=[VMEM] * len(parts) + [ANY] * len(after),
        compiler_params=params(8),
        cost_estimate=BRIEF,
        name="join",
    )(*parts, *after)


def spread(group, wide, lines, cap, per_row):
    size = cap + 16
    for k in range(group.shape[0] // size):
        start = k * size
        tail = group[start + cap : start + size, :].astype(jnp.float32)
        number = (tail[0:1, :] * LANES + tail[1:2, :]).astype(jnp.int32)
        lines[:, k * cap : (k + 1) * cap] = jnp.broadcast_to(number // per_row, (8, cap))
        column = jnp.broadcast_to((number % per_row).astype(jnp.float32), (LANES, cap)).T
        value = group[start : start + cap, :].astype(jnp.float32)
        for c in range(per_row):
            wide[k * cap : (k + 1) * cap, c * LANES : (c + 1) * LANES] = jnp.where(
                column == c, value, 0.0
            ).astype(jnp.bfloat16)


def place(lines, wide, t, tile):
    line = lax.broadcasted_iota(jnp.int32, (tile, lines.shape[1]), 0) + t * tile
    hot = (lines[0:1, :] == line).astype(jnp.float32).astype(jnp.bfloat16)
    return jnp.dot(hot, wide[...], preferred_element_type=jnp.float32)


def half_kernel(cap, per_row, tile, group, out, wide, lines):
    spread(group, wide, lines, cap, per_row)
    for t in range(out.shape[0] // tile):
        out[t * tile : (t + 1) * tile, :] = place(lines, wide, t, tile)


def outer_kernel(cap, per_row, tile, n, group, half, out, wide, lines, held, sems):
    spread(group, wide, lines, cap, per_row)
    tiles = out.shape[0] // tile
    for t in range(tiles):
        rows = slice(t * tile, (t + 1) * tile)
        held[rows, :] = (half[rows, :] + place(lines, wide, t, tile)) * (1.0 / n)
        send_out(held, out, sems, t, tile).start()
    for t in range(tiles):
        send_out(held, out, sems, t, tile).wait()


def outer(groups, cap, depth, kw):
    slots = groups[0].shape[0] // (cap + 16) * cap
    n = 2 * slots // cap
    tile = min(depth, 256)
    shape = jax.ShapeDtypeStruct((depth, kw), jnp.float32)
    scratch = [pltpu.VMEM((slots, kw), jnp.bfloat16), pltpu.VMEM((8, slots), jnp.int32)]
    half = pl.pallas_call(
        functools.partial(half_kernel, cap, kw // LANES, tile),
        out_shape=shape,
        scratch_shapes=scratch,
        compiler_params=params(14),
        cost_estimate=BRIEF,
        name="half",
    )(groups[0])
    return pl.pallas_call(
        functools.partial(outer_kernel, cap, kw // LANES, tile, n),
        out_shape=shape,
        out_specs=ANY,
        scratch_shapes=scratch
        + [pltpu.VMEM((depth, kw), jnp.float32), pltpu.SemaphoreType.DMA((depth // tile,))],
        compiler_params=params(14),
        cost_estimate=BRIEF,
        name="outer",
    )(groups[1], half)


def on_device(inputs, target, weights, feedback, counts, blocks):
    tokens, w, fb = inputs[0], weights[0], feedback[0]
    n_shard, n_rep = lax.axis_size("shard"), lax.axis_size("rep")
    tok_dev = tokens.shape[0]
    depth, kw = w.shape
    early_rows = tok_dev * 5 // 8
    spans = [(0, early_rows), (early_rows, tok_dev)]
    per_row = kw // LANES
    slot_row = blocks[0]
    near = [d for d in range(1, n_shard) if d & (d - 1) == 0]
    far = [d for d in range(1, n_shard) if d & (d - 1) != 0]

    me = lax.axis_index("shard")
    rows = tok_dev // 2 if n_shard == 4 else tok_dev
    far_out = [
        [
            lax.dynamic_slice(tokens, (low, (me ^ d) * depth), (rows, depth))
            for low in range(0, tok_dev, rows)
        ]
        for d in far
    ]
    if n_shard == 4:
        ((by_x, by_y),) = far_out
        by_x, by_y = swap(by_x, "shard", n_shard, 1), swap(by_y, "shard", n_shard, 2)
        hops = [by_x, by_y]
        far_in = [swap(by_x, "shard", n_shard, 2), swap(by_y, "shard", n_shard, 1)]
    else:
        hops = []
        far_in = [swap(x, "shard", n_shard, d) for (x,), d in zip(far_out, far)]
    near_out, after = [], [far_out[0][0]]
    for low, high in spans:
        *out, token = cut(tokens, depth, [(d, low, high - low) for d in near], after)
        near_out.append(out)
        if low == 0:
            fbk, keep, token = early(slot_row, counts, fb, token)
            after = [token] + hops
    near_in = [[swap(x, "shard", n_shard, d) for x, d in zip(out, near)] for out in near_out]

    own, _ = cut(tokens, depth, [(0, 0, tok_dev)], [token])

    brief, wide = jnp.bfloat16, jnp.float32
    near_outs = [[(high - low, brief)] * len(near) for low, high in spans]
    early_near, x_early = project(near_in[0], near_outs[0], w, [])
    outs = [(tok_dev, wide)] + [(tok_dev, brief)] * len(far)
    (mine, *products), x_far = project([own] + far_in, outs, w, early_near[-1:])
    whole = [swap(p, "shard", n_shard, d) for p, d in zip(products, far)]
    xg_far, xt_far, token = prepare([x_far], slot_row, counts, per_row, products)
    late_near, x_late = project(near_in[1], near_outs[1], w, [token])
    shares = [
        [swap(p, "shard", n_shard, d) for p, d in zip(part, near)]
        for part in (early_near, late_near)
    ]
    x_near = [x_early, x_late]
    xg_near, xt_near, token = prepare(x_near, slot_row, counts, per_row, late_near[:1])
    shares = [share[k] for k in range(len(near)) for share in shares]
    slopes = slope(target[0], mine, whole, shares, spans, token)
    slopes = [slopes] + [swap(slopes, "shard", n_shard, d) for d in far + near]

    n_far = 1 + len(far)
    order_far = [(k, 0, tok_dev) for k in range(n_far)]
    order_near = [(k, low, high) for low, high in spans for k in range(len(near))]
    wide = gather(slopes[:n_far], order_far, xg_far)
    message = kept(slopes[n_far:], order_near, wide, xg_near, fbk, slot_row)
    same_core = [swap(message, "rep", n_rep, d) for d in range(n_rep - 2, 0, -2)]
    order = order_far + [(n_far + k, low, high) for k, low, high in order_near]
    new_feedback, token = residue(slopes, order, [xt_far, xt_near], fb, keep)
    joined, after = message, [token]
    for received in same_core:
        joined, after = join([joined, received], after), []
    groups = [joined, swap(joined, "rep", n_rep, 1)]
    return outer(groups, message.shape[0] - 16, depth, kw), new_feedback[None]


def solution(mesh):
    placed = (
        P("rep", "shard", None),
        P("rep", "shard", None),
        P("rep", "shard", None),
        P("rep", "shard", None),
        P("rep", "shard"),
        P("rep", "shard", None),
    )
    return jax.shard_map(
        on_device,
        mesh=mesh,
        in_specs=placed,
        out_specs=(P("shard", None), P("rep", "shard", None)),
        check_vma=False,
    )
```

```python
import functools

import jax
import jax.numpy as jnp
from jax import lax
from jax.experimental import pallas as pl
from jax.experimental.pallas import tpu as pltpu
from jax.sharding import PartitionSpec as P

LANES = 128
ANY = pl.BlockSpec(memory_space=pl.ANY)
BRIEF = pl.CostEstimate(flops=1000, bytes_accessed=1000, transcendentals=0)
VMEM = pl.BlockSpec(memory_space=pltpu.VMEM)
SMEM = pl.BlockSpec(memory_space=pltpu.SMEM)
MIB = 1024 * 1024
TOKEN = jax.ShapeDtypeStruct((8, LANES), jnp.float32)


def params(mib):
    return pltpu.CompilerParams(vmem_limit_bytes=mib * MIB)


def swap(x, axis, n, d):
    return lax.ppermute(x, axis, [(i, i ^ d) for i in range(n)])


def cut_kernel(cuts, tokens, *refs):
    outs, (token, sems) = refs[-len(cuts) - 2 : -2], refs[-2:]
    token[...] = jnp.zeros_like(token)
    me = lax.axis_index("shard")
    copies = []
    for k, (d, low, rows) in enumerate(cuts):
        depth = outs[k].shape[1]
        columns = pl.ds(pl.multiple_of((me ^ d) * depth, LANES), depth)
        copy = pltpu.make_async_copy(tokens.at[pl.ds(low, rows), columns], outs[k], sems.at[k])
        copy.start()
        copies.append(copy)
    for copy in copies:
        copy.wait()


def cut(tokens, depth, cuts, after):
    return pl.pallas_call(
        functools.partial(cut_kernel, cuts),
        out_shape=[jax.ShapeDtypeStruct((rows, depth), tokens.dtype) for _, _, rows in cuts]
        + [TOKEN],
        in_specs=[ANY] * (1 + len(after)),
        out_specs=[ANY] * len(cuts) + [VMEM],
        scratch_shapes=[pltpu.SemaphoreType.DMA((len(cuts),))],
        compiler_params=params(6),
        cost_estimate=BRIEF,
        name="cut",
    )(tokens, *after)


def project_kernel(n, m, *refs):
    pieces, w, outs, x = refs[:n], refs[n], refs[-m - 1 : -1], refs[-1]
    start = 0
    for piece in pieces:
        x[start : start + piece.shape[0], :] = piece[...]
        start += piece.shape[0]
    full = jnp.dot(x[...], w[...], preferred_element_type=jnp.float32)
    start = 0
    for out in outs:
        out[...] = full[start : start + out.shape[0], :].astype(out.dtype)
        start += out.shape[0]


def project(pieces, outs, w, after):
    n = len(pieces)
    rows, depth = sum(p.shape[0] for p in pieces), pieces[0].shape[1]
    kw = w.shape[1]
    result = pl.pallas_call(
        functools.partial(project_kernel, n, len(outs)),
        out_shape=[jax.ShapeDtypeStruct((r, kw), t) for r, t in outs]
        + [jax.ShapeDtypeStruct((rows, depth), jnp.bfloat16)],
        in_specs=[VMEM] * (n + 1) + [ANY] * len(after),
        compiler_params=params(14),
        cost_estimate=BRIEF,
        name="project",
    )(*pieces, w, *after)
    return result[:-1], result[-1]


def slope_kernel(tok_dev, n, spans, *refs):
    goal, mine, out = refs[0], refs[1], refs[-1]
    whole = refs[2 : 2 + n]
    shares = refs[2 + n : -2]
    for part, (low, high) in enumerate(spans):
        key_proj = mine[low:high, :]
        for product in whole:
            key_proj += product[low:high, :].astype(jnp.float32)
        for product in shares[part :: len(spans)]:
            key_proj += product[...].astype(jnp.float32)
        gap = key_proj - goal[low:high, :].astype(jnp.float32)
        out[low:high, :] = (gap / tok_dev).astype(jnp.bfloat16)


def slope(goal, mine, whole, shares, spans, after):
    return pl.pallas_call(
        functools.partial(slope_kernel, goal.shape[0], len(whole), spans),
        out_shape=jax.ShapeDtypeStruct(mine.shape, jnp.bfloat16),
        in_specs=[VMEM] * (2 + len(whole) + len(shares)) + [ANY],
        compiler_params=params(8),
        cost_estimate=BRIEF,
        name="slope",
    )(goal, mine, *whole, *shares, after)


def as_column(row):
    size = row.shape[1]
    return jnp.broadcast_to(row.astype(jnp.float32), (size, size)).T.astype(jnp.int32)


def pick_columns(wide, column):
    out = jnp.zeros((wide.shape[0], LANES), jnp.float32)
    for c in range(wide.shape[1] // LANES):
        out += jnp.where(column == c, wide[:, c * LANES : (c + 1) * LANES], 0.0)
    return out


def early_kernel(per_row, slot_row, count, fb, after, fbk, keep, token):
    token[...] = jnp.zeros_like(token)
    depth, kw = fb.shape
    cap = slot_row.shape[1]
    slot = as_column(slot_row[...])[:, 0:1]
    hot = slot // per_row == lax.broadcasted_iota(jnp.int32, (cap, depth), 1)
    hot = hot.astype(jnp.float32).astype(jnp.bfloat16)
    used = lax.broadcasted_iota(jnp.int32, (cap, 1), 0) < count[0, 0]
    wide = jnp.dot(hot, fb[...], preferred_element_type=jnp.float32)
    fbk[...] = jnp.where(used, pick_columns(wide, slot % per_row), 0.0)
    group = lax.broadcasted_iota(jnp.int32, (cap, kw), 1) // LANES
    mark = jnp.where(used & (slot % per_row == group), 1.0, 0.0).astype(jnp.bfloat16)
    tile = min(depth, 512)
    for t in range(depth // tile):
        line = lax.broadcasted_iota(jnp.int32, (tile, cap), 0) + t * tile
        hot = (slot_row[...] // per_row == line).astype(jnp.float32).astype(jnp.bfloat16)
        mask = jnp.dot(hot, mark, preferred_element_type=jnp.float32)
        keep[t * tile : (t + 1) * tile, :] = (1.0 - mask).astype(jnp.bfloat16)


def early(slot_row, count, fb, after):
    depth, kw = fb.shape
    cap = slot_row.shape[1]
    return pl.pallas_call(
        functools.partial(early_kernel, kw // LANES),
        out_shape=[
            jax.ShapeDtypeStruct((cap, LANES), jnp.float32),
            jax.ShapeDtypeStruct((depth, kw), jnp.bfloat16),
            TOKEN,
        ],
        in_specs=[VMEM, SMEM, VMEM, ANY],
        compiler_params=params(14),
        cost_estimate=BRIEF,
        name="early",
    )(slot_row, count, fb, after)


def prepare_kernel(per_row, n, *refs):
    xs, (slot_row, count), (xg, xt, token) = refs[:n], refs[n : n + 2], refs[-3:]
    token[...] = jnp.zeros_like(token)
    depth = xs[0].shape[1]
    cap = slot_row.shape[1]
    used = lax.broadcasted_iota(jnp.int32, (cap, 1), 0) < count[0, 0]
    line = jnp.where(used, as_column(slot_row[...])[:, 0:1] // per_row, depth)
    hot = line == lax.broadcasted_iota(jnp.int32, (cap, depth), 1)
    hot = hot.astype(jnp.float32).astype(jnp.bfloat16)
    start = 0
    for x in xs:
        rows = x.shape[0]
        xg[:, start : start + rows] = lax.dot_general(
            hot, x[...], (((1,), (1,)), ((), ())), preferred_element_type=jnp.float32
        ).astype(jnp.bfloat16)
        xt[:, start : start + rows] = x[...].T
        start += rows


def prepare(xs, slot_row, count, per_row, after):
    rows, depth = sum(x.shape[0] for x in xs), xs[0].shape[1]
    cap = slot_row.shape[1]
    return pl.pallas_call(
        functools.partial(prepare_kernel, per_row, len(xs)),
        out_shape=[
            jax.ShapeDtypeStruct((cap, rows), jnp.bfloat16),
            jax.ShapeDtypeStruct((depth, rows), jnp.bfloat16),
            TOKEN,
        ],
        in_specs=[VMEM] * (len(xs) + 1) + [SMEM] + [ANY] * len(after),
        compiler_params=params(14),
        cost_estimate=BRIEF,
        name="prepare",
    )(*xs, slot_row, count, *after)


def stack(slopes, order, s):
    start = 0
    for k, low, high in order:
        s[start : start + high - low, :] = slopes[k][low:high, :]
        start += high - low


def gather_kernel(order, *refs):
    slopes, (xg, out, s) = refs[:-3], refs[-3:]
    stack(slopes, order, s)
    out[...] = jnp.dot(xg[...], s[...], preferred_element_type=jnp.float32)


def gather(slopes, order, xg):
    kw = slopes[0].shape[1]
    return pl.pallas_call(
        functools.partial(gather_kernel, order),
        out_shape=jax.ShapeDtypeStruct((xg.shape[0], kw), jnp.float32),
        scratch_shapes=[pltpu.VMEM((xg.shape[1], kw), jnp.bfloat16)],
        compiler_params=params(8),
        cost_estimate=BRIEF,
        name="gather",
    )(*slopes, xg)


def kept_kernel(per_row, order, *refs):
    slopes, (wide, xg, fbk, slot_row, out, s) = refs[:-6], refs[-6:]
    cap = slot_row.shape[1]
    stack(slopes, order, s)
    total = wide[...] + jnp.dot(xg[...], s[...], preferred_element_type=jnp.float32)
    value = pick_columns(total, as_column(slot_row[...])[:, 0:1] % per_row) + fbk[...]
    out[:cap, :] = value.astype(jnp.bfloat16)
    tail = out.shape[0] - cap
    number = jnp.broadcast_to(slot_row[...], (tail, cap))
    line = lax.broadcasted_iota(jnp.int32, (tail, cap), 0)
    number = jnp.where(line == 0, number // LANES, number % LANES)
    out[cap:, :] = number.astype(jnp.float32).astype(jnp.bfloat16)


def kept(slopes, order, wide, xg, fbk, slot_row):
    cap, kw = wide.shape
    return pl.pallas_call(
        functools.partial(kept_kernel, kw // LANES, order),
        out_shape=jax.ShapeDtypeStruct((cap + 16, LANES), jnp.bfloat16),
        scratch_shapes=[pltpu.VMEM((xg.shape[1], kw), jnp.bfloat16)],
        compiler_params=params(8),
        cost_estimate=BRIEF,
        name="kept",
    )(*slopes, wide, xg, fbk, slot_row)


def send_out(held, out, sems, t, tile):
    rows = pl.ds(t * tile, tile)
    return pltpu.make_async_copy(held.at[rows, :], out.at[rows, :], sems.at[t])


def residue_kernel(order, tile, *refs):
    n = len({k for k, _, _ in order})
    slopes, xts, (fb, keep, out, token, s, held, sems) = refs[:n], refs[n:-7], refs[-7:]
    token[...] = jnp.zeros_like(token)
    stack(slopes, order, s)
    tiles = out.shape[0] // tile
    for t in range(tiles):
        rows = slice(t * tile, (t + 1) * tile)
        pseudo, start = fb[rows, :].astype(jnp.float32), 0
        for xt in xts:
            part = s[start : start + xt.shape[1], :]
            pseudo += jnp.dot(xt[rows, :], part, preferred_element_type=jnp.float32)
            start += xt.shape[1]
        held[rows, :] = jnp.where(keep[rows, :] > 0, pseudo, 0.0).astype(jnp.bfloat16)
        send_out(held, out, sems, t, tile).start()
    for t in range(tiles):
        send_out(held, out, sems, t, tile).wait()


def residue(slopes, order, xts, fb, keep):
    depth, kw = fb.shape
    total = sum(xt.shape[1] for xt in xts)
    tile = min(depth, 256)
    return pl.pallas_call(
        functools.partial(residue_kernel, order, tile),
        out_shape=[
            jax.ShapeDtypeStruct((depth, kw), jnp.bfloat16),
            TOKEN,
        ],
        in_specs=[VMEM] * (len(slopes) + len(xts) + 2),
        out_specs=[ANY, VMEM],
        scratch_shapes=[
            pltpu.VMEM((total, kw), jnp.bfloat16),
            pltpu.VMEM((depth, kw), jnp.bfloat16),
            pltpu.SemaphoreType.DMA((depth // tile,)),
        ],
        compiler_params=params(14),
        cost_estimate=BRIEF,
        name="residue",
    )(*slopes, *xts, fb, keep)


def join_kernel(n, *refs):
    out, start = refs[-1], 0
    for part in refs[:n]:
        out[start : start + part.shape[0], :] = part[...]
        start += part.shape[0]


def join(parts, after):
    rows, lanes = sum(part.shape[0] for part in parts), parts[0].shape[1]
    return pl.pallas_call(
        functools.partial(join_kernel, len(parts)),
        out_shape=jax.ShapeDtypeStruct((rows, lanes), jnp.bfloat16),
        in_specs=[VMEM] * len(parts) + [ANY] * len(after),
        compiler_params=params(8),
        cost_estimate=BRIEF,
        name="join",
    )(*parts, *after)


def spread(group, wide, lines, cap, per_row):
    size = cap + 16
    for k in range(group.shape[0] // size):
        start = k * size
        tail = group[start + cap : start + size, :].astype(jnp.float32)
        number = (tail[0:1, :] * LANES + tail[1:2, :]).astype(jnp.int32)
        lines[:, k * cap : (k + 1) * cap] = jnp.broadcast_to(number // per_row, (8, cap))
        column = jnp.broadcast_to((number % per_row).astype(jnp.float32), (LANES, cap)).T
        value = group[start : start + cap, :].astype(jnp.float32)
        for c in range(per_row):
            wide[k * cap : (k + 1) * cap, c * LANES : (c + 1) * LANES] = jnp.where(
                column == c, value, 0.0
            ).astype(jnp.bfloat16)


def place(lines, wide, t, tile):
    line = lax.broadcasted_iota(jnp.int32, (tile, lines.shape[1]), 0) + t * tile
    hot = (lines[0:1, :] == line).astype(jnp.float32).astype(jnp.bfloat16)
    return jnp.dot(hot, wide[...], preferred_element_type=jnp.float32)


def half_kernel(cap, per_row, tile, group, out, wide, lines):
    spread(group, wide, lines, cap, per_row)
    for t in range(out.shape[0] // tile):
        out[t * tile : (t + 1) * tile, :] = place(lines, wide, t, tile)


def outer_kernel(cap, per_row, tile, n, group, half, out, wide, lines, held, sems):
    spread(group, wide, lines, cap, per_row)
    tiles = out.shape[0] // tile
    for t in range(tiles):
        rows = slice(t * tile, (t + 1) * tile)
        held[rows, :] = (half[rows, :] + place(lines, wide, t, tile)) * (1.0 / n)
        send_out(held, out, sems, t, tile).start()
    for t in range(tiles):
        send_out(held, out, sems, t, tile).wait()


def outer(groups, cap, depth, kw):
    slots = groups[0].shape[0] // (cap + 16) * cap
    n = 2 * slots // cap
    tile = min(depth, 256)
    shape = jax.ShapeDtypeStruct((depth, kw), jnp.float32)
    scratch = [pltpu.VMEM((slots, kw), jnp.bfloat16), pltpu.VMEM((8, slots), jnp.int32)]
    half = pl.pallas_call(
        functools.partial(half_kernel, cap, kw // LANES, tile),
        out_shape=shape,
        scratch_shapes=scratch,
        compiler_params=params(14),
        cost_estimate=BRIEF,
        name="half",
    )(groups[0])
    return pl.pallas_call(
        functools.partial(outer_kernel, cap, kw // LANES, tile, n),
        out_shape=shape,
        out_specs=ANY,
        scratch_shapes=scratch
        + [pltpu.VMEM((depth, kw), jnp.float32), pltpu.SemaphoreType.DMA((depth // tile,))],
        compiler_params=params(14),
        cost_estimate=BRIEF,
        name="outer",
    )(groups[1], half)


def on_device(inputs, target, weights, feedback, counts, blocks):
    tokens, w, fb = inputs[0], weights[0], feedback[0]
    n_shard, n_rep = lax.axis_size("shard"), lax.axis_size("rep")
    tok_dev = tokens.shape[0]
    depth, kw = w.shape
    early_rows = tok_dev * 3 // 8
    spans = [(0, early_rows), (early_rows, tok_dev)]
    per_row = kw // LANES
    slot_row = blocks[0]
    near = [d for d in range(1, n_shard) if d & (d - 1) == 0]
    far = [d for d in range(1, n_shard) if d & (d - 1) != 0]

    me = lax.axis_index("shard")
    rows = tok_dev // 2 if n_shard == 4 else tok_dev
    far_out = [
        [
            lax.dynamic_slice(tokens, (low, (me ^ d) * depth), (rows, depth))
            for low in range(0, tok_dev, rows)
        ]
        for d in far
    ]
    if n_shard == 4:
        ((by_x, by_y),) = far_out
        by_x, by_y = swap(by_x, "shard", n_shard, 1), swap(by_y, "shard", n_shard, 2)
        hops = [by_x, by_y]
        far_in = [swap(by_x, "shard", n_shard, 2), swap(by_y, "shard", n_shard, 1)]
    else:
        hops = []
        far_in = [swap(x, "shard", n_shard, d) for (x,), d in zip(far_out, far)]
    near_out, after = [], [far_out[0][0]]
    for low, high in spans:
        *out, token = cut(tokens, depth, [(d, low, high - low) for d in near], after)
        near_out.append(out)
        if low == 0:
            fbk, keep, token = early(slot_row, counts, fb, token)
            after = [token] + hops
    near_in = [[swap(x, "shard", n_shard, d) for x, d in zip(out, near)] for out in near_out]

    own, _ = cut(tokens, depth, [(0, 0, tok_dev)], [token])

    brief, wide = jnp.bfloat16, jnp.float32
    near_outs = [[(high - low, brief)] * len(near) for low, high in spans]
    early_near, x_early = project(near_in[0], near_outs[0], w, [])
    outs = [(tok_dev, wide)] + [(tok_dev, brief)] * len(far)
    (mine, *products), x_far = project([own] + far_in, outs, w, early_near[-1:])
    whole = [swap(p, "shard", n_shard, d) for p, d in zip(products, far)]
    xg_far, xt_far, token = prepare([x_far], slot_row, counts, per_row, products)
    late_near, x_late = project(near_in[1], near_outs[1], w, [token])
    shares = [
        [swap(p, "shard", n_shard, d) for p, d in zip(part, near)]
        for part in (early_near, late_near)
    ]
    x_near = [x_early, x_late]
    xg_near, xt_near, token = prepare(x_near, slot_row, counts, per_row, late_near[:1])
    shares = [share[k] for k in range(len(near)) for share in shares]
    slopes = slope(target[0], mine, whole, shares, spans, token)
    slopes = [slopes] + [swap(slopes, "shard", n_shard, d) for d in far + near]

    n_far = 1 + len(far)
    order_far = [(k, 0, tok_dev) for k in range(n_far)]
    order_near = [(k, low, high) for low, high in spans for k in range(len(near))]
    wide = gather(slopes[:n_far], order_far, xg_far)
    message = kept(slopes[n_far:], order_near, wide, xg_near, fbk, slot_row)
    same_core = [swap(message, "rep", n_rep, d) for d in range(n_rep - 2, 0, -2)]
    order = order_far + [(n_far + k, low, high) for k, low, high in order_near]
    new_feedback, token = residue(slopes, order, [xt_far, xt_near], fb, keep)
    joined, after = message, [token]
    for received in same_core:
        joined, after = join([joined, received], after), []
    groups = [joined, swap(joined, "rep", n_rep, 1)]
    return outer(groups, message.shape[0] - 16, depth, kw), new_feedback[None]


def solution(mesh):
    placed = (
        P("rep", "shard", None),
        P("rep", "shard", None),
        P("rep", "shard", None),
        P("rep", "shard", None),
        P("rep", "shard"),
        P("rep", "shard", None),
    )
    return jax.shard_map(
        on_device,
        mesh=mesh,
        in_specs=placed,
        out_specs=(P("shard", None), P("rep", "shard", None)),
        check_vma=False,
    )
```

```python
import functools

import jax
import jax.numpy as jnp
from jax import lax
from jax.experimental import pallas as pl
from jax.experimental.pallas import tpu as pltpu
from jax.sharding import PartitionSpec as P

LANES = 128
ANY = pl.BlockSpec(memory_space=pl.ANY)
BRIEF = pl.CostEstimate(flops=1000, bytes_accessed=1000, transcendentals=0)
VMEM = pl.BlockSpec(memory_space=pltpu.VMEM)
SMEM = pl.BlockSpec(memory_space=pltpu.SMEM)
MIB = 1024 * 1024
TOKEN = jax.ShapeDtypeStruct((8, LANES), jnp.float32)


def params(mib):
    return pltpu.CompilerParams(vmem_limit_bytes=mib * MIB)


def swap(x, axis, n, d):
    return lax.ppermute(x, axis, [(i, i ^ d) for i in range(n)])


def cut_kernel(cuts, tokens, *refs):
    outs, (token, sems) = refs[-len(cuts) - 2 : -2], refs[-2:]
    token[...] = jnp.zeros_like(token)
    me = lax.axis_index("shard")
    copies = []
    for k, (d, low, rows) in enumerate(cuts):
        depth = outs[k].shape[1]
        columns = pl.ds(pl.multiple_of((me ^ d) * depth, LANES), depth)
        copy = pltpu.make_async_copy(tokens.at[pl.ds(low, rows), columns], outs[k], sems.at[k])
        copy.start()
        copies.append(copy)
    for copy in copies:
        copy.wait()


def cut(tokens, depth, cuts, after):
    return pl.pallas_call(
        functools.partial(cut_kernel, cuts),
        out_shape=[jax.ShapeDtypeStruct((rows, depth), tokens.dtype) for _, _, rows in cuts]
        + [TOKEN],
        in_specs=[ANY] * (1 + len(after)),
        out_specs=[ANY] * len(cuts) + [VMEM],
        scratch_shapes=[pltpu.SemaphoreType.DMA((len(cuts),))],
        compiler_params=params(6),
        cost_estimate=BRIEF,
        name="cut",
    )(tokens, *after)


def project_kernel(n, m, *refs):
    pieces, w, outs, x = refs[:n], refs[n], refs[-m - 1 : -1], refs[-1]
    start = 0
    for piece in pieces:
        x[start : start + piece.shape[0], :] = piece[...]
        start += piece.shape[0]
    full = jnp.dot(x[...], w[...], preferred_element_type=jnp.float32)
    start = 0
    for out in outs:
        out[...] = full[start : start + out.shape[0], :].astype(out.dtype)
        start += out.shape[0]


def project(pieces, outs, w, after):
    n = len(pieces)
    rows, depth = sum(p.shape[0] for p in pieces), pieces[0].shape[1]
    kw = w.shape[1]
    result = pl.pallas_call(
        functools.partial(project_kernel, n, len(outs)),
        out_shape=[jax.ShapeDtypeStruct((r, kw), t) for r, t in outs]
        + [jax.ShapeDtypeStruct((rows, depth), jnp.bfloat16)],
        in_specs=[VMEM] * (n + 1) + [ANY] * len(after),
        compiler_params=params(14),
        cost_estimate=BRIEF,
        name="project",
    )(*pieces, w, *after)
    return result[:-1], result[-1]


def slope_kernel(tok_dev, n, spans, *refs):
    goal, mine, out = refs[0], refs[1], refs[-1]
    whole = refs[2 : 2 + n]
    shares = refs[2 + n : -2]
    for part, (low, high) in enumerate(spans):
        key_proj = mine[low:high, :]
        for product in whole:
            key_proj += product[low:high, :].astype(jnp.float32)
        for product in shares[part :: len(spans)]:
            key_proj += product[...].astype(jnp.float32)
        gap = key_proj - goal[low:high, :].astype(jnp.float32)
        out[low:high, :] = (gap / tok_dev).astype(jnp.bfloat16)


def slope(goal, mine, whole, shares, spans, after):
    return pl.pallas_call(
        functools.partial(slope_kernel, goal.shape[0], len(whole), spans),
        out_shape=jax.ShapeDtypeStruct(mine.shape, jnp.bfloat16),
        in_specs=[VMEM] * (2 + len(whole) + len(shares)) + [ANY],
        compiler_params=params(8),
        cost_estimate=BRIEF,
        name="slope",
    )(goal, mine, *whole, *shares, after)


def as_column(row):
    size = row.shape[1]
    return jnp.broadcast_to(row.astype(jnp.float32), (size, size)).T.astype(jnp.int32)


def pick_columns(wide, column):
    out = jnp.zeros((wide.shape[0], LANES), jnp.float32)
    for c in range(wide.shape[1] // LANES):
        out += jnp.where(column == c, wide[:, c * LANES : (c + 1) * LANES], 0.0)
    return out


def early_kernel(per_row, slot_row, count, fb, after, fbk, keep, token):
    token[...] = jnp.zeros_like(token)
    depth, kw = fb.shape
    cap = slot_row.shape[1]
    slot = as_column(slot_row[...])[:, 0:1]
    hot = slot // per_row == lax.broadcasted_iota(jnp.int32, (cap, depth), 1)
    hot = hot.astype(jnp.float32).astype(jnp.bfloat16)
    used = lax.broadcasted_iota(jnp.int32, (cap, 1), 0) < count[0, 0]
    wide = jnp.dot(hot, fb[...], preferred_element_type=jnp.float32)
    fbk[...] = jnp.where(used, pick_columns(wide, slot % per_row), 0.0)
    group = lax.broadcasted_iota(jnp.int32, (cap, kw), 1) // LANES
    mark = jnp.where(used & (slot % per_row == group), 1.0, 0.0).astype(jnp.bfloat16)
    tile = min(depth, 512)
    for t in range(depth // tile):
        line = lax.broadcasted_iota(jnp.int32, (tile, cap), 0) + t * tile
        hot = (slot_row[...] // per_row == line).astype(jnp.float32).astype(jnp.bfloat16)
        mask = jnp.dot(hot, mark, preferred_element_type=jnp.float32)
        keep[t * tile : (t + 1) * tile, :] = (1.0 - mask).astype(jnp.bfloat16)


def early(slot_row, count, fb, after):
    depth, kw = fb.shape
    cap = slot_row.shape[1]
    return pl.pallas_call(
        functools.partial(early_kernel, kw // LANES),
        out_shape=[
            jax.ShapeDtypeStruct((cap, LANES), jnp.float32),
            jax.ShapeDtypeStruct((depth, kw), jnp.bfloat16),
            TOKEN,
        ],
        in_specs=[VMEM, SMEM, VMEM, ANY],
        compiler_params=params(14),
        cost_estimate=BRIEF,
        name="early",
    )(slot_row, count, fb, after)


def prepare_kernel(per_row, n, *refs):
    xs, (slot_row, count), (xg, xt, token) = refs[:n], refs[n : n + 2], refs[-3:]
    token[...] = jnp.zeros_like(token)
    depth = xs[0].shape[1]
    cap = slot_row.shape[1]
    used = lax.broadcasted_iota(jnp.int32, (cap, 1), 0) < count[0, 0]
    line = jnp.where(used, as_column(slot_row[...])[:, 0:1] // per_row, depth)
    hot = line == lax.broadcasted_iota(jnp.int32, (cap, depth), 1)
    hot = hot.astype(jnp.float32).astype(jnp.bfloat16)
    start = 0
    for x in xs:
        rows = x.shape[0]
        xg[:, start : start + rows] = lax.dot_general(
            hot, x[...], (((1,), (1,)), ((), ())), preferred_element_type=jnp.float32
        ).astype(jnp.bfloat16)
        xt[:, start : start + rows] = x[...].T
        start += rows


def prepare(xs, slot_row, count, per_row, after):
    rows, depth = sum(x.shape[0] for x in xs), xs[0].shape[1]
    cap = slot_row.shape[1]
    return pl.pallas_call(
        functools.partial(prepare_kernel, per_row, len(xs)),
        out_shape=[
            jax.ShapeDtypeStruct((cap, rows), jnp.bfloat16),
            jax.ShapeDtypeStruct((depth, rows), jnp.bfloat16),
            TOKEN,
        ],
        in_specs=[VMEM] * (len(xs) + 1) + [SMEM] + [ANY] * len(after),
        compiler_params=params(14),
        cost_estimate=BRIEF,
        name="prepare",
    )(*xs, slot_row, count, *after)


def stack(slopes, order, s):
    start = 0
    for k, low, high in order:
        s[start : start + high - low, :] = slopes[k][low:high, :]
        start += high - low


def gather_kernel(order, *refs):
    slopes, (xg, out, s) = refs[:-3], refs[-3:]
    stack(slopes, order, s)
    out[...] = jnp.dot(xg[...], s[...], preferred_element_type=jnp.float32)


def gather(slopes, order, xg):
    kw = slopes[0].shape[1]
    return pl.pallas_call(
        functools.partial(gather_kernel, order),
        out_shape=jax.ShapeDtypeStruct((xg.shape[0], kw), jnp.float32),
        scratch_shapes=[pltpu.VMEM((xg.shape[1], kw), jnp.bfloat16)],
        compiler_params=params(8),
        cost_estimate=BRIEF,
        name="gather",
    )(*slopes, xg)


def kept_kernel(per_row, order, *refs):
    slopes, (wide, xg, fbk, slot_row, out, s) = refs[:-6], refs[-6:]
    cap = slot_row.shape[1]
    stack(slopes, order, s)
    total = wide[...] + jnp.dot(xg[...], s[...], preferred_element_type=jnp.float32)
    value = pick_columns(total, as_column(slot_row[...])[:, 0:1] % per_row) + fbk[...]
    out[:cap, :] = value.astype(jnp.bfloat16)
    tail = out.shape[0] - cap
    number = jnp.broadcast_to(slot_row[...], (tail, cap))
    line = lax.broadcasted_iota(jnp.int32, (tail, cap), 0)
    number = jnp.where(line == 0, number // LANES, number % LANES)
    out[cap:, :] = number.astype(jnp.float32).astype(jnp.bfloat16)


def kept(slopes, order, wide, xg, fbk, slot_row):
    cap, kw = wide.shape
    return pl.pallas_call(
        functools.partial(kept_kernel, kw // LANES, order),
        out_shape=jax.ShapeDtypeStruct((cap + 16, LANES), jnp.bfloat16),
        scratch_shapes=[pltpu.VMEM((xg.shape[1], kw), jnp.bfloat16)],
        compiler_params=params(8),
        cost_estimate=BRIEF,
        name="kept",
    )(*slopes, wide, xg, fbk, slot_row)


def send_out(held, out, sems, t, tile):
    rows = pl.ds(t * tile, tile)
    return pltpu.make_async_copy(held.at[rows, :], out.at[rows, :], sems.at[t])


def residue_kernel(order, tile, *refs):
    n = len({k for k, _, _ in order})
    slopes, xts, (fb, keep, out, token, s, held, sems) = refs[:n], refs[n:-7], refs[-7:]
    token[...] = jnp.zeros_like(token)
    stack(slopes, order, s)
    tiles = out.shape[0] // tile
    for t in range(tiles):
        rows = slice(t * tile, (t + 1) * tile)
        pseudo, start = fb[rows, :].astype(jnp.float32), 0
        for xt in xts:
            part = s[start : start + xt.shape[1], :]
            pseudo += jnp.dot(xt[rows, :], part, preferred_element_type=jnp.float32)
            start += xt.shape[1]
        held[rows, :] = jnp.where(keep[rows, :] > 0, pseudo, 0.0).astype(jnp.bfloat16)
        send_out(held, out, sems, t, tile).start()
    for t in range(tiles):
        send_out(held, out, sems, t, tile).wait()


def residue(slopes, order, xts, fb, keep):
    depth, kw = fb.shape
    total = sum(xt.shape[1] for xt in xts)
    tile = min(depth, 256)
    return pl.pallas_call(
        functools.partial(residue_kernel, order, tile),
        out_shape=[
            jax.ShapeDtypeStruct((depth, kw), jnp.bfloat16),
            TOKEN,
        ],
        in_specs=[VMEM] * (len(slopes) + len(xts) + 2),
        out_specs=[ANY, VMEM],
        scratch_shapes=[
            pltpu.VMEM((total, kw), jnp.bfloat16),
            pltpu.VMEM((depth, kw), jnp.bfloat16),
            pltpu.SemaphoreType.DMA((depth // tile,)),
        ],
        compiler_params=params(14),
        cost_estimate=BRIEF,
        name="residue",
    )(*slopes, *xts, fb, keep)


def join_kernel(n, *refs):
    out, start = refs[-1], 0
    for part in refs[:n]:
        out[start : start + part.shape[0], :] = part[...]
        start += part.shape[0]


def join(parts, after):
    rows, lanes = sum(part.shape[0] for part in parts), parts[0].shape[1]
    return pl.pallas_call(
        functools.partial(join_kernel, len(parts)),
        out_shape=jax.ShapeDtypeStruct((rows, lanes), jnp.bfloat16),
        in_specs=[VMEM] * len(parts) + [ANY] * len(after),
        compiler_params=params(8),
        cost_estimate=BRIEF,
        name="join",
    )(*parts, *after)


def spread(group, wide, lines, cap, per_row):
    size = cap + 16
    for k in range(group.shape[0] // size):
        start = k * size
        tail = group[start + cap : start + size, :].astype(jnp.float32)
        number = (tail[0:1, :] * LANES + tail[1:2, :]).astype(jnp.int32)
        lines[:, k * cap : (k + 1) * cap] = jnp.broadcast_to(number // per_row, (8, cap))
        column = jnp.broadcast_to((number % per_row).astype(jnp.float32), (LANES, cap)).T
        value = group[start : start + cap, :].astype(jnp.float32)
        for c in range(per_row):
            wide[k * cap : (k + 1) * cap, c * LANES : (c + 1) * LANES] = jnp.where(
                column == c, value, 0.0
            ).astype(jnp.bfloat16)


def place(lines, wide, t, tile):
    line = lax.broadcasted_iota(jnp.int32, (tile, lines.shape[1]), 0) + t * tile
    hot = (lines[0:1, :] == line).astype(jnp.float32).astype(jnp.bfloat16)
    return jnp.dot(hot, wide[...], preferred_element_type=jnp.float32)


def half_kernel(cap, per_row, tile, group, out, wide, lines):
    spread(group, wide, lines, cap, per_row)
    for t in range(out.shape[0] // tile):
        out[t * tile : (t + 1) * tile, :] = place(lines, wide, t, tile)


def outer_kernel(cap, per_row, tile, n, group, half, out, wide, lines, held, sems):
    spread(group, wide, lines, cap, per_row)
    tiles = out.shape[0] // tile
    for t in range(tiles):
        rows = slice(t * tile, (t + 1) * tile)
        held[rows, :] = (half[rows, :] + place(lines, wide, t, tile)) * (1.0 / n)
        send_out(held, out, sems, t, tile).start()
    for t in range(tiles):
        send_out(held, out, sems, t, tile).wait()


def outer(groups, cap, depth, kw):
    slots = groups[0].shape[0] // (cap + 16) * cap
    n = 2 * slots // cap
    tile = min(depth, 256)
    shape = jax.ShapeDtypeStruct((depth, kw), jnp.float32)
    scratch = [pltpu.VMEM((slots, kw), jnp.bfloat16), pltpu.VMEM((8, slots), jnp.int32)]
    half = pl.pallas_call(
        functools.partial(half_kernel, cap, kw // LANES, tile),
        out_shape=shape,
        scratch_shapes=scratch,
        compiler_params=params(14),
        cost_estimate=BRIEF,
        name="half",
    )(groups[0])
    return pl.pallas_call(
        functools.partial(outer_kernel, cap, kw // LANES, tile, n),
        out_shape=shape,
        out_specs=ANY,
        scratch_shapes=scratch
        + [pltpu.VMEM((depth, kw), jnp.float32), pltpu.SemaphoreType.DMA((depth // tile,))],
        compiler_params=params(14),
        cost_estimate=BRIEF,
        name="outer",
    )(groups[1], half)


def on_device(inputs, target, weights, feedback, counts, blocks):
    tokens, w, fb = inputs[0], weights[0], feedback[0]
    n_shard, n_rep = lax.axis_size("shard"), lax.axis_size("rep")
    tok_dev = tokens.shape[0]
    depth, kw = w.shape
    early_rows = tok_dev // 2
    spans = [(0, early_rows), (early_rows, tok_dev)]
    per_row = kw // LANES
    slot_row = blocks[0]
    near = [d for d in range(1, n_shard) if d & (d - 1) == 0]
    far = [d for d in range(1, n_shard) if d & (d - 1) != 0]

    me = lax.axis_index("shard")
    rows = tok_dev // 2 if n_shard == 4 else tok_dev
    far_out = [
        [
            lax.dynamic_slice(tokens, (low, (me ^ d) * depth), (rows, depth))
            for low in range(0, tok_dev, rows)
        ]
        for d in far
    ]
    if n_shard == 4:
        ((by_x, by_y),) = far_out
        by_x, by_y = swap(by_x, "shard", n_shard, 1), swap(by_y, "shard", n_shard, 2)
        hops = [by_x, by_y]
        far_in = [swap(by_x, "shard", n_shard, 2), swap(by_y, "shard", n_shard, 1)]
    else:
        hops = []
        far_in = [swap(x, "shard", n_shard, d) for (x,), d in zip(far_out, far)]
    near_out, after = [], [far_out[0][0]]
    for low, high in spans:
        *out, token = cut(tokens, depth, [(d, low, high - low) for d in near], after)
        near_out.append(out)
        if low == 0:
            fbk, keep, token = early(slot_row, counts, fb, token)
            after = [token] + hops
    near_in = [[swap(x, "shard", n_shard, d) for x, d in zip(out, near)] for out in near_out]

    own, _ = cut(tokens, depth, [(0, 0, tok_dev)], [token])

    brief, wide = jnp.bfloat16, jnp.float32
    near_outs = [[(high - low, brief)] * len(near) for low, high in spans]
    early_near, x_early = project(near_in[0], near_outs[0], w, [])
    outs = [(tok_dev, wide)] + [(tok_dev, brief)] * len(far)
    (mine, *products), x_far = project([own] + far_in, outs, w, early_near[-1:])
    whole = [swap(p, "shard", n_shard, d) for p, d in zip(products, far)]
    xg_far, xt_far, token = prepare([x_far], slot_row, counts, per_row, products)
    late_near, x_late = project(near_in[1], near_outs[1], w, [token])
    shares = [
        [swap(p, "shard", n_shard, d) for p, d in zip(part, near)]
        for part in (early_near, late_near)
    ]
    x_near = [x_early, x_late]
    xg_near, xt_near, token = prepare(x_near, slot_row, counts, per_row, late_near[:1])
    shares = [share[k] for k in range(len(near)) for share in shares]
    slopes = slope(target[0], mine, whole, shares, spans, token)
    slopes = [slopes] + [swap(slopes, "shard", n_shard, d) for d in far + near]

    n_far = 1 + len(far)
    order_far = [(k, 0, tok_dev) for k in range(n_far)]
    order_near = [(k, low, high) for low, high in spans for k in range(len(near))]
    wide = gather(slopes[:n_far], order_far, xg_far)
    message = kept(slopes[n_far:], order_near, wide, xg_near, fbk, slot_row)
    chips = [4, *range(n_rep - 2, 4, -2), 2] if n_rep > 4 else list(range(2, n_rep, 2))
    same_core = [swap(message, "rep", n_rep, d) for d in chips]
    order = order_far + [(n_far + k, low, high) for k, low, high in order_near]
    new_feedback, token = residue(slopes, order, [xt_far, xt_near], fb, keep)
    joined, after = message, [token]
    for received in same_core:
        joined, after = join([joined, received], after), []
    groups = [joined, swap(joined, "rep", n_rep, 1)]
    return outer(groups, message.shape[0] - 16, depth, kw), new_feedback[None]


def solution(mesh):
    placed = (
        P("rep", "shard", None),
        P("rep", "shard", None),
        P("rep", "shard", None),
        P("rep", "shard", None),
        P("rep", "shard"),
        P("rep", "shard", None),
    )
    return jax.shard_map(
        on_device,
        mesh=mesh,
        in_specs=placed,
        out_specs=(P("shard", None), P("rep", "shard", None)),
        check_vma=False,
    )
```

```python
import functools

import jax
import jax.numpy as jnp
from jax import lax
from jax.experimental import pallas as pl
from jax.experimental.pallas import tpu as pltpu
from jax.sharding import PartitionSpec as P

LANES = 128
ANY = pl.BlockSpec(memory_space=pl.ANY)
BRIEF = pl.CostEstimate(flops=1000, bytes_accessed=1000, transcendentals=0)
VMEM = pl.BlockSpec(memory_space=pltpu.VMEM)
SMEM = pl.BlockSpec(memory_space=pltpu.SMEM)
MIB = 1024 * 1024
TOKEN = jax.ShapeDtypeStruct((8, LANES), jnp.float32)


def params(mib):
    return pltpu.CompilerParams(vmem_limit_bytes=mib * MIB)


def swap(x, axis, n, d):
    return lax.ppermute(x, axis, [(i, i ^ d) for i in range(n)])


def cut_kernel(cuts, tokens, *refs):
    outs, (token, sems) = refs[-len(cuts) - 2 : -2], refs[-2:]
    token[...] = jnp.zeros_like(token)
    me = lax.axis_index("shard")
    copies = []
    for k, (d, low, rows) in enumerate(cuts):
        depth = outs[k].shape[1]
        columns = pl.ds(pl.multiple_of((me ^ d) * depth, LANES), depth)
        copy = pltpu.make_async_copy(tokens.at[pl.ds(low, rows), columns], outs[k], sems.at[k])
        copy.start()
        copies.append(copy)
    for copy in copies:
        copy.wait()


def cut(tokens, depth, cuts, after):
    return pl.pallas_call(
        functools.partial(cut_kernel, cuts),
        out_shape=[jax.ShapeDtypeStruct((rows, depth), tokens.dtype) for _, _, rows in cuts]
        + [TOKEN],
        in_specs=[ANY] * (1 + len(after)),
        out_specs=[ANY] * len(cuts) + [VMEM],
        scratch_shapes=[pltpu.SemaphoreType.DMA((len(cuts),))],
        compiler_params=params(6),
        cost_estimate=BRIEF,
        name="cut",
    )(tokens, *after)


def project_kernel(n, m, *refs):
    pieces, w, outs, x = refs[:n], refs[n], refs[-m - 1 : -1], refs[-1]
    start = 0
    for piece in pieces:
        x[start : start + piece.shape[0], :] = piece[...]
        start += piece.shape[0]
    full = jnp.dot(x[...], w[...], preferred_element_type=jnp.float32)
    start = 0
    for out in outs:
        out[...] = full[start : start + out.shape[0], :].astype(out.dtype)
        start += out.shape[0]


def project(pieces, outs, w, after):
    n = len(pieces)
    rows, depth = sum(p.shape[0] for p in pieces), pieces[0].shape[1]
    kw = w.shape[1]
    result = pl.pallas_call(
        functools.partial(project_kernel, n, len(outs)),
        out_shape=[jax.ShapeDtypeStruct((r, kw), t) for r, t in outs]
        + [jax.ShapeDtypeStruct((rows, depth), jnp.bfloat16)],
        in_specs=[VMEM] * (n + 1) + [ANY] * len(after),
        compiler_params=params(14),
        cost_estimate=BRIEF,
        name="project",
    )(*pieces, w, *after)
    return result[:-1], result[-1]


def slope_kernel(tok_dev, n, spans, *refs):
    goal, mine, out = refs[0], refs[1], refs[-1]
    whole = refs[2 : 2 + n]
    shares = refs[2 + n : -2]
    for part, (low, high) in enumerate(spans):
        key_proj = mine[low:high, :]
        for product in whole:
            key_proj += product[low:high, :].astype(jnp.float32)
        for product in shares[part :: len(spans)]:
            key_proj += product[...].astype(jnp.float32)
        gap = key_proj - goal[low:high, :].astype(jnp.float32)
        out[low:high, :] = (gap / tok_dev).astype(jnp.bfloat16)


def slope(goal, mine, whole, shares, spans, after):
    return pl.pallas_call(
        functools.partial(slope_kernel, goal.shape[0], len(whole), spans),
        out_shape=jax.ShapeDtypeStruct(mine.shape, jnp.bfloat16),
        in_specs=[VMEM] * (2 + len(whole) + len(shares)) + [ANY],
        compiler_params=params(8),
        cost_estimate=BRIEF,
        name="slope",
    )(goal, mine, *whole, *shares, after)


def as_column(row):
    size = row.shape[1]
    return jnp.broadcast_to(row.astype(jnp.float32), (size, size)).T.astype(jnp.int32)


def pick_columns(wide, column):
    out = jnp.zeros((wide.shape[0], LANES), jnp.float32)
    for c in range(wide.shape[1] // LANES):
        out += jnp.where(column == c, wide[:, c * LANES : (c + 1) * LANES], 0.0)
    return out


def early_kernel(per_row, slot_row, count, fb, after, fbk, keep, token):
    token[...] = jnp.zeros_like(token)
    depth, kw = fb.shape
    cap = slot_row.shape[1]
    slot = as_column(slot_row[...])[:, 0:1]
    hot = slot // per_row == lax.broadcasted_iota(jnp.int32, (cap, depth), 1)
    hot = hot.astype(jnp.float32).astype(jnp.bfloat16)
    used = lax.broadcasted_iota(jnp.int32, (cap, 1), 0) < count[0, 0]
    wide = jnp.dot(hot, fb[...], preferred_element_type=jnp.float32)
    fbk[...] = jnp.where(used, pick_columns(wide, slot % per_row), 0.0)
    group = lax.broadcasted_iota(jnp.int32, (cap, kw), 1) // LANES
    mark = jnp.where(used & (slot % per_row == group), 1.0, 0.0).astype(jnp.bfloat16)
    tile = min(depth, 512)
    for t in range(depth // tile):
        line = lax.broadcasted_iota(jnp.int32, (tile, cap), 0) + t * tile
        hot = (slot_row[...] // per_row == line).astype(jnp.float32).astype(jnp.bfloat16)
        mask = jnp.dot(hot, mark, preferred_element_type=jnp.float32)
        keep[t * tile : (t + 1) * tile, :] = (1.0 - mask).astype(jnp.bfloat16)


def early(slot_row, count, fb, after):
    depth, kw = fb.shape
    cap = slot_row.shape[1]
    return pl.pallas_call(
        functools.partial(early_kernel, kw // LANES),
        out_shape=[
            jax.ShapeDtypeStruct((cap, LANES), jnp.float32),
            jax.ShapeDtypeStruct((depth, kw), jnp.bfloat16),
            TOKEN,
        ],
        in_specs=[VMEM, SMEM, VMEM, ANY],
        compiler_params=params(14),
        cost_estimate=BRIEF,
        name="early",
    )(slot_row, count, fb, after)


def prepare_kernel(per_row, n, *refs):
    xs, (slot_row, count), (xg, xt, token) = refs[:n], refs[n : n + 2], refs[-3:]
    token[...] = jnp.zeros_like(token)
    depth = xs[0].shape[1]
    cap = slot_row.shape[1]
    used = lax.broadcasted_iota(jnp.int32, (cap, 1), 0) < count[0, 0]
    line = jnp.where(used, as_column(slot_row[...])[:, 0:1] // per_row, depth)
    hot = line == lax.broadcasted_iota(jnp.int32, (cap, depth), 1)
    hot = hot.astype(jnp.float32).astype(jnp.bfloat16)
    start = 0
    for x in xs:
        rows = x.shape[0]
        xg[:, start : start + rows] = lax.dot_general(
            hot, x[...], (((1,), (1,)), ((), ())), preferred_element_type=jnp.float32
        ).astype(jnp.bfloat16)
        xt[:, start : start + rows] = x[...].T
        start += rows


def prepare(xs, slot_row, count, per_row, after):
    rows, depth = sum(x.shape[0] for x in xs), xs[0].shape[1]
    cap = slot_row.shape[1]
    return pl.pallas_call(
        functools.partial(prepare_kernel, per_row, len(xs)),
        out_shape=[
            jax.ShapeDtypeStruct((cap, rows), jnp.bfloat16),
            jax.ShapeDtypeStruct((depth, rows), jnp.bfloat16),
            TOKEN,
        ],
        in_specs=[VMEM] * (len(xs) + 1) + [SMEM] + [ANY] * len(after),
        compiler_params=params(14),
        cost_estimate=BRIEF,
        name="prepare",
    )(*xs, slot_row, count, *after)


def stack(slopes, order, s):
    start = 0
    for k, low, high in order:
        s[start : start + high - low, :] = slopes[k][low:high, :]
        start += high - low


def gather_kernel(order, *refs):
    slopes, (xg, out, s) = refs[:-3], refs[-3:]
    stack(slopes, order, s)
    out[...] = jnp.dot(xg[...], s[...], preferred_element_type=jnp.float32)


def gather(slopes, order, xg):
    kw = slopes[0].shape[1]
    return pl.pallas_call(
        functools.partial(gather_kernel, order),
        out_shape=jax.ShapeDtypeStruct((xg.shape[0], kw), jnp.float32),
        scratch_shapes=[pltpu.VMEM((xg.shape[1], kw), jnp.bfloat16)],
        compiler_params=params(8),
        cost_estimate=BRIEF,
        name="gather",
    )(*slopes, xg)


def kept_kernel(per_row, order, *refs):
    slopes, (wide, xg, fbk, slot_row, out, s) = refs[:-6], refs[-6:]
    cap = slot_row.shape[1]
    stack(slopes, order, s)
    total = wide[...] + jnp.dot(xg[...], s[...], preferred_element_type=jnp.float32)
    value = pick_columns(total, as_column(slot_row[...])[:, 0:1] % per_row) + fbk[...]
    out[:cap, :] = value.astype(jnp.bfloat16)
    tail = out.shape[0] - cap
    number = jnp.broadcast_to(slot_row[...], (tail, cap))
    line = lax.broadcasted_iota(jnp.int32, (tail, cap), 0)
    number = jnp.where(line == 0, number // LANES, number % LANES)
    out[cap:, :] = number.astype(jnp.float32).astype(jnp.bfloat16)


def kept(slopes, order, wide, xg, fbk, slot_row):
    cap, kw = wide.shape
    return pl.pallas_call(
        functools.partial(kept_kernel, kw // LANES, order),
        out_shape=jax.ShapeDtypeStruct((cap + 16, LANES), jnp.bfloat16),
        scratch_shapes=[pltpu.VMEM((xg.shape[1], kw), jnp.bfloat16)],
        compiler_params=params(8),
        cost_estimate=BRIEF,
        name="kept",
    )(*slopes, wide, xg, fbk, slot_row)


def send_out(held, out, sems, t, tile):
    rows = pl.ds(t * tile, tile)
    return pltpu.make_async_copy(held.at[rows, :], out.at[rows, :], sems.at[t])


def residue_kernel(order, tile, *refs):
    n = len({k for k, _, _ in order})
    slopes, xts, (fb, keep, out, token, s, held, sems) = refs[:n], refs[n:-7], refs[-7:]
    token[...] = jnp.zeros_like(token)
    stack(slopes, order, s)
    tiles = out.shape[0] // tile
    for t in range(tiles):
        rows = slice(t * tile, (t + 1) * tile)
        pseudo, start = fb[rows, :].astype(jnp.float32), 0
        for xt in xts:
            part = s[start : start + xt.shape[1], :]
            pseudo += jnp.dot(xt[rows, :], part, preferred_element_type=jnp.float32)
            start += xt.shape[1]
        held[rows, :] = jnp.where(keep[rows, :] > 0, pseudo, 0.0).astype(jnp.bfloat16)
        send_out(held, out, sems, t, tile).start()
    for t in range(tiles):
        send_out(held, out, sems, t, tile).wait()


def residue(slopes, order, xts, fb, keep):
    depth, kw = fb.shape
    total = sum(xt.shape[1] for xt in xts)
    tile = min(depth, 256)
    return pl.pallas_call(
        functools.partial(residue_kernel, order, tile),
        out_shape=[
            jax.ShapeDtypeStruct((depth, kw), jnp.bfloat16),
            TOKEN,
        ],
        in_specs=[VMEM] * (len(slopes) + len(xts) + 2),
        out_specs=[ANY, VMEM],
        scratch_shapes=[
            pltpu.VMEM((total, kw), jnp.bfloat16),
            pltpu.VMEM((depth, kw), jnp.bfloat16),
            pltpu.SemaphoreType.DMA((depth // tile,)),
        ],
        compiler_params=params(14),
        cost_estimate=BRIEF,
        name="residue",
    )(*slopes, *xts, fb, keep)


def join_kernel(n, *refs):
    out, start = refs[-1], 0
    for part in refs[:n]:
        out[start : start + part.shape[0], :] = part[...]
        start += part.shape[0]


def join(parts, after):
    rows, lanes = sum(part.shape[0] for part in parts), parts[0].shape[1]
    return pl.pallas_call(
        functools.partial(join_kernel, len(parts)),
        out_shape=jax.ShapeDtypeStruct((rows, lanes), jnp.bfloat16),
        in_specs=[VMEM] * len(parts) + [ANY] * len(after),
        compiler_params=params(8),
        cost_estimate=BRIEF,
        name="join",
    )(*parts, *after)


def spread(group, wide, lines, cap, per_row):
    size = cap + 16
    for k in range(group.shape[0] // size):
        start = k * size
        tail = group[start + cap : start + size, :].astype(jnp.float32)
        number = (tail[0:1, :] * LANES + tail[1:2, :]).astype(jnp.int32)
        lines[:, k * cap : (k + 1) * cap] = jnp.broadcast_to(number // per_row, (8, cap))
        column = jnp.broadcast_to((number % per_row).astype(jnp.float32), (LANES, cap)).T
        value = group[start : start + cap, :].astype(jnp.float32)
        for c in range(per_row):
            wide[k * cap : (k + 1) * cap, c * LANES : (c + 1) * LANES] = jnp.where(
                column == c, value, 0.0
            ).astype(jnp.bfloat16)


def place(lines, wide, t, tile):
    line = lax.broadcasted_iota(jnp.int32, (tile, lines.shape[1]), 0) + t * tile
    hot = (lines[0:1, :] == line).astype(jnp.float32).astype(jnp.bfloat16)
    return jnp.dot(hot, wide[...], preferred_element_type=jnp.float32)


def half_kernel(cap, per_row, tile, group, out, wide, lines):
    spread(group, wide, lines, cap, per_row)
    for t in range(out.shape[0] // tile):
        out[t * tile : (t + 1) * tile, :] = place(lines, wide, t, tile)


def outer_kernel(cap, per_row, tile, n, group, half, out, wide, lines, held, sems):
    spread(group, wide, lines, cap, per_row)
    tiles = out.shape[0] // tile
    for t in range(tiles):
        rows = slice(t * tile, (t + 1) * tile)
        held[rows, :] = (half[rows, :] + place(lines, wide, t, tile)) * (1.0 / n)
        send_out(held, out, sems, t, tile).start()
    for t in range(tiles):
        send_out(held, out, sems, t, tile).wait()


def outer(groups, cap, depth, kw):
    slots = groups[0].shape[0] // (cap + 16) * cap
    n = 2 * slots // cap
    tile = min(depth, 256)
    shape = jax.ShapeDtypeStruct((depth, kw), jnp.float32)
    scratch = [pltpu.VMEM((slots, kw), jnp.bfloat16), pltpu.VMEM((8, slots), jnp.int32)]
    half = pl.pallas_call(
        functools.partial(half_kernel, cap, kw // LANES, tile),
        out_shape=shape,
        scratch_shapes=scratch,
        compiler_params=params(14),
        cost_estimate=BRIEF,
        name="half",
    )(groups[0])
    return pl.pallas_call(
        functools.partial(outer_kernel, cap, kw // LANES, tile, n),
        out_shape=shape,
        out_specs=ANY,
        scratch_shapes=scratch
        + [pltpu.VMEM((depth, kw), jnp.float32), pltpu.SemaphoreType.DMA((depth // tile,))],
        compiler_params=params(14),
        cost_estimate=BRIEF,
        name="outer",
    )(groups[1], half)


def on_device(inputs, target, weights, feedback, counts, blocks):
    tokens, w, fb = inputs[0], weights[0], feedback[0]
    n_shard, n_rep = lax.axis_size("shard"), lax.axis_size("rep")
    tok_dev = tokens.shape[0]
    depth, kw = w.shape
    early_rows = tok_dev // 2
    spans = [(0, early_rows), (early_rows, tok_dev)]
    per_row = kw // LANES
    slot_row = blocks[0]
    near = [d for d in range(1, n_shard) if d & (d - 1) == 0]
    far = [d for d in range(1, n_shard) if d & (d - 1) != 0]

    me = lax.axis_index("shard")
    rows = tok_dev // 2 if n_shard == 4 else tok_dev
    far_out = [
        [
            lax.dynamic_slice(tokens, (low, (me ^ d) * depth), (rows, depth))
            for low in range(0, tok_dev, rows)
        ]
        for d in far
    ]
    if n_shard == 4:
        ((by_x, by_y),) = far_out
        by_x, by_y = swap(by_x, "shard", n_shard, 1), swap(by_y, "shard", n_shard, 2)
        hops = [by_x, by_y]
        far_in = [swap(by_x, "shard", n_shard, 2), swap(by_y, "shard", n_shard, 1)]
    else:
        hops = []
        far_in = [swap(x, "shard", n_shard, d) for (x,), d in zip(far_out, far)]
    near_out, after = [], [far_out[0][0]]
    for low, high in spans:
        *out, token = cut(tokens, depth, [(d, low, high - low) for d in near], after)
        near_out.append(out)
        after = [token] + hops
    near_in = [[swap(x, "shard", n_shard, d) for x, d in zip(out, near)] for out in near_out]

    own, _ = cut(tokens, depth, [(0, 0, tok_dev)], [token])

    brief, wide = jnp.bfloat16, jnp.float32
    near_outs = [[(high - low, brief)] * len(near) for low, high in spans]
    early_near, x_early = project(near_in[0], near_outs[0], w, [])
    outs = [(tok_dev, wide)] + [(tok_dev, brief)] * len(far)
    (mine, *products), x_far = project([own] + far_in, outs, w, early_near[-1:])
    whole = [swap(p, "shard", n_shard, d) for p, d in zip(products, far)]
    xg_far, xt_far, token = prepare([x_far], slot_row, counts, per_row, products)
    late_near, x_late = project(near_in[1], near_outs[1], w, [token])
    shares = [
        [swap(p, "shard", n_shard, d) for p, d in zip(part, near)]
        for part in (early_near, late_near)
    ]
    x_near = [x_early, x_late]
    xg_near, xt_near, token = prepare(x_near, slot_row, counts, per_row, late_near[:1])
    shares = [share[k] for k in range(len(near)) for share in shares]
    slopes = slope(target[0], mine, whole, shares, spans, token)
    fbk, keep, _ = early(slot_row, counts, fb, slopes)
    slopes = [slopes] + [swap(slopes, "shard", n_shard, d) for d in far + near]

    n_far = 1 + len(far)
    order_far = [(k, 0, tok_dev) for k in range(n_far)]
    order_near = [(k, low, high) for low, high in spans for k in range(len(near))]
    wide = gather(slopes[:n_far], order_far, xg_far)
    message = kept(slopes[n_far:], order_near, wide, xg_near, fbk, slot_row)
    chips = [4, *range(n_rep - 2, 4, -2), 2] if n_rep > 4 else list(range(2, n_rep, 2))
    same_core = [swap(message, "rep", n_rep, d) for d in chips]
    order = order_far + [(n_far + k, low, high) for k, low, high in order_near]
    new_feedback, token = residue(slopes, order, [xt_far, xt_near], fb, keep)
    joined, after = message, [token]
    for received in same_core:
        joined, after = join([joined, received], after), []
    groups = [joined, swap(joined, "rep", n_rep, 1)]
    return outer(groups, message.shape[0] - 16, depth, kw), new_feedback[None]


def solution(mesh):
    placed = (
        P("rep", "shard", None),
        P("rep", "shard", None),
        P("rep", "shard", None),
        P("rep", "shard", None),
        P("rep", "shard"),
        P("rep", "shard", None),
    )
    return jax.shard_map(
        on_device,
        mesh=mesh,
        in_specs=placed,
        out_specs=(P("shard", None), P("rep", "shard", None)),
        check_vma=False,
    )
```

```python
import functools

import jax
import jax.numpy as jnp
from jax import lax
from jax.experimental import pallas as pl
from jax.experimental.pallas import tpu as pltpu
from jax.sharding import PartitionSpec as P

LANES = 128
ANY = pl.BlockSpec(memory_space=pl.ANY)
BRIEF = pl.CostEstimate(flops=1000, bytes_accessed=1000, transcendentals=0)
VMEM = pl.BlockSpec(memory_space=pltpu.VMEM)
SMEM = pl.BlockSpec(memory_space=pltpu.SMEM)
MIB = 1024 * 1024
TOKEN = jax.ShapeDtypeStruct((8, LANES), jnp.float32)


def params(mib):
    return pltpu.CompilerParams(vmem_limit_bytes=mib * MIB)


def swap(x, axis, n, d):
    return lax.ppermute(x, axis, [(i, i ^ d) for i in range(n)])


def cut_kernel(cuts, tokens, *refs):
    outs, (token, sems) = refs[-len(cuts) - 2 : -2], refs[-2:]
    token[...] = jnp.zeros_like(token)
    me = lax.axis_index("shard")
    copies = []
    for k, (d, low, rows) in enumerate(cuts):
        depth = outs[k].shape[1]
        columns = pl.ds(pl.multiple_of((me ^ d) * depth, LANES), depth)
        copy = pltpu.make_async_copy(tokens.at[pl.ds(low, rows), columns], outs[k], sems.at[k])
        copy.start()
        copies.append(copy)
    for copy in copies:
        copy.wait()


def cut(tokens, depth, cuts, after):
    return pl.pallas_call(
        functools.partial(cut_kernel, cuts),
        out_shape=[jax.ShapeDtypeStruct((rows, depth), tokens.dtype) for _, _, rows in cuts]
        + [TOKEN],
        in_specs=[ANY] * (1 + len(after)),
        out_specs=[ANY] * len(cuts) + [VMEM],
        scratch_shapes=[pltpu.SemaphoreType.DMA((len(cuts),))],
        compiler_params=params(6),
        cost_estimate=BRIEF,
        name="cut",
    )(tokens, *after)


def project_kernel(n, m, *refs):
    pieces, w, outs, x = refs[:n], refs[n], refs[-m - 1 : -1], refs[-1]
    start = 0
    for piece in pieces:
        x[start : start + piece.shape[0], :] = piece[...]
        start += piece.shape[0]
    full = jnp.dot(x[...], w[...], preferred_element_type=jnp.float32)
    start = 0
    for out in outs:
        out[...] = full[start : start + out.shape[0], :].astype(out.dtype)
        start += out.shape[0]


def project(pieces, outs, w, after):
    n = len(pieces)
    rows, depth = sum(p.shape[0] for p in pieces), pieces[0].shape[1]
    kw = w.shape[1]
    result = pl.pallas_call(
        functools.partial(project_kernel, n, len(outs)),
        out_shape=[jax.ShapeDtypeStruct((r, kw), t) for r, t in outs]
        + [jax.ShapeDtypeStruct((rows, depth), jnp.bfloat16)],
        in_specs=[VMEM] * (n + 1) + [ANY] * len(after),
        compiler_params=params(14),
        cost_estimate=BRIEF,
        name="project",
    )(*pieces, w, *after)
    return result[:-1], result[-1]


def slope_kernel(tok_dev, n, spans, *refs):
    goal, mine, out = refs[0], refs[1], refs[-1]
    whole = refs[2 : 2 + n]
    shares = refs[2 + n : -2]
    for part, (low, high) in enumerate(spans):
        key_proj = mine[low:high, :]
        for product in whole:
            key_proj += product[low:high, :].astype(jnp.float32)
        for product in shares[part :: len(spans)]:
            key_proj += product[...].astype(jnp.float32)
        gap = key_proj - goal[low:high, :].astype(jnp.float32)
        out[low:high, :] = (gap / tok_dev).astype(jnp.bfloat16)


def slope(goal, mine, whole, shares, spans, after):
    return pl.pallas_call(
        functools.partial(slope_kernel, goal.shape[0], len(whole), spans),
        out_shape=jax.ShapeDtypeStruct(mine.shape, jnp.bfloat16),
        in_specs=[VMEM] * (2 + len(whole) + len(shares)) + [ANY],
        compiler_params=params(8),
        cost_estimate=BRIEF,
        name="slope",
    )(goal, mine, *whole, *shares, after)


def as_column(row):
    size = row.shape[1]
    return jnp.broadcast_to(row.astype(jnp.float32), (size, size)).T.astype(jnp.int32)


def pick_columns(wide, column):
    out = jnp.zeros((wide.shape[0], LANES), jnp.float32)
    for c in range(wide.shape[1] // LANES):
        out += jnp.where(column == c, wide[:, c * LANES : (c + 1) * LANES], 0.0)
    return out


def early_kernel(per_row, slot_row, count, fb, after, fbk, keep, token):
    token[...] = jnp.zeros_like(token)
    depth, kw = fb.shape
    cap = slot_row.shape[1]
    slot = as_column(slot_row[...])[:, 0:1]
    hot = slot // per_row == lax.broadcasted_iota(jnp.int32, (cap, depth), 1)
    hot = hot.astype(jnp.float32).astype(jnp.bfloat16)
    used = lax.broadcasted_iota(jnp.int32, (cap, 1), 0) < count[0, 0]
    wide = jnp.dot(hot, fb[...], preferred_element_type=jnp.float32)
    fbk[...] = jnp.where(used, pick_columns(wide, slot % per_row), 0.0)
    group = lax.broadcasted_iota(jnp.int32, (cap, kw), 1) // LANES
    mark = jnp.where(used & (slot % per_row == group), 1.0, 0.0).astype(jnp.bfloat16)
    tile = min(depth, 512)
    for t in range(depth // tile):
        line = lax.broadcasted_iota(jnp.int32, (tile, cap), 0) + t * tile
        hot = (slot_row[...] // per_row == line).astype(jnp.float32).astype(jnp.bfloat16)
        mask = jnp.dot(hot, mark, preferred_element_type=jnp.float32)
        keep[t * tile : (t + 1) * tile, :] = (1.0 - mask).astype(jnp.bfloat16)


def early(slot_row, count, fb, after):
    depth, kw = fb.shape
    cap = slot_row.shape[1]
    return pl.pallas_call(
        functools.partial(early_kernel, kw // LANES),
        out_shape=[
            jax.ShapeDtypeStruct((cap, LANES), jnp.float32),
            jax.ShapeDtypeStruct((depth, kw), jnp.bfloat16),
            TOKEN,
        ],
        in_specs=[VMEM, SMEM, VMEM, ANY],
        compiler_params=params(14),
        cost_estimate=BRIEF,
        name="early",
    )(slot_row, count, fb, after)


def prepare_kernel(per_row, n, *refs):
    xs, (slot_row, count), (xg, xt, token) = refs[:n], refs[n : n + 2], refs[-3:]
    token[...] = jnp.zeros_like(token)
    depth = xs[0].shape[1]
    cap = slot_row.shape[1]
    used = lax.broadcasted_iota(jnp.int32, (cap, 1), 0) < count[0, 0]
    line = jnp.where(used, as_column(slot_row[...])[:, 0:1] // per_row, depth)
    hot = line == lax.broadcasted_iota(jnp.int32, (cap, depth), 1)
    hot = hot.astype(jnp.float32).astype(jnp.bfloat16)
    start = 0
    for x in xs:
        rows = x.shape[0]
        xg[:, start : start + rows] = lax.dot_general(
            hot, x[...], (((1,), (1,)), ((), ())), preferred_element_type=jnp.float32
        ).astype(jnp.bfloat16)
        xt[:, start : start + rows] = x[...].T
        start += rows


def prepare(xs, slot_row, count, per_row, after):
    rows, depth = sum(x.shape[0] for x in xs), xs[0].shape[1]
    cap = slot_row.shape[1]
    return pl.pallas_call(
        functools.partial(prepare_kernel, per_row, len(xs)),
        out_shape=[
            jax.ShapeDtypeStruct((cap, rows), jnp.bfloat16),
            jax.ShapeDtypeStruct((depth, rows), jnp.bfloat16),
            TOKEN,
        ],
        in_specs=[VMEM] * (len(xs) + 1) + [SMEM] + [ANY] * len(after),
        compiler_params=params(14),
        cost_estimate=BRIEF,
        name="prepare",
    )(*xs, slot_row, count, *after)


def stack(slopes, order, s):
    start = 0
    for k, low, high in order:
        s[start : start + high - low, :] = slopes[k][low:high, :]
        start += high - low


def gather_kernel(order, *refs):
    slopes, (xg, out, s) = refs[:-3], refs[-3:]
    stack(slopes, order, s)
    out[...] = jnp.dot(xg[...], s[...], preferred_element_type=jnp.float32)


def gather(slopes, order, xg):
    kw = slopes[0].shape[1]
    return pl.pallas_call(
        functools.partial(gather_kernel, order),
        out_shape=jax.ShapeDtypeStruct((xg.shape[0], kw), jnp.float32),
        scratch_shapes=[pltpu.VMEM((xg.shape[1], kw), jnp.bfloat16)],
        compiler_params=params(8),
        cost_estimate=BRIEF,
        name="gather",
    )(*slopes, xg)


def kept_kernel(per_row, order, *refs):
    slopes, (wide, xg, fbk, slot_row, out, s) = refs[:-6], refs[-6:]
    cap = slot_row.shape[1]
    stack(slopes, order, s)
    total = wide[...] + jnp.dot(xg[...], s[...], preferred_element_type=jnp.float32)
    value = pick_columns(total, as_column(slot_row[...])[:, 0:1] % per_row) + fbk[...]
    out[:cap, :] = value.astype(jnp.bfloat16)
    tail = out.shape[0] - cap
    number = jnp.broadcast_to(slot_row[...], (tail, cap))
    line = lax.broadcasted_iota(jnp.int32, (tail, cap), 0)
    number = jnp.where(line == 0, number // LANES, number % LANES)
    out[cap:, :] = number.astype(jnp.float32).astype(jnp.bfloat16)


def kept(slopes, order, wide, xg, fbk, slot_row):
    cap, kw = wide.shape
    return pl.pallas_call(
        functools.partial(kept_kernel, kw // LANES, order),
        out_shape=jax.ShapeDtypeStruct((cap + 16, LANES), jnp.bfloat16),
        scratch_shapes=[pltpu.VMEM((xg.shape[1], kw), jnp.bfloat16)],
        compiler_params=params(8),
        cost_estimate=BRIEF,
        name="kept",
    )(*slopes, wide, xg, fbk, slot_row)


def send_out(held, out, sems, t, tile):
    rows = pl.ds(t * tile, tile)
    return pltpu.make_async_copy(held.at[rows, :], out.at[rows, :], sems.at[t])


def residue_kernel(order, tile, *refs):
    n = len({k for k, _, _ in order})
    slopes, xts, (fb, keep, out, token, s, held, sems) = refs[:n], refs[n:-7], refs[-7:]
    token[...] = jnp.zeros_like(token)
    stack(slopes, order, s)
    tiles = out.shape[0] // tile
    for t in range(tiles):
        rows = slice(t * tile, (t + 1) * tile)
        pseudo, start = fb[rows, :].astype(jnp.float32), 0
        for xt in xts:
            part = s[start : start + xt.shape[1], :]
            pseudo += jnp.dot(xt[rows, :], part, preferred_element_type=jnp.float32)
            start += xt.shape[1]
        held[rows, :] = jnp.where(keep[rows, :] > 0, pseudo, 0.0).astype(jnp.bfloat16)
        send_out(held, out, sems, t, tile).start()
    for t in range(tiles):
        send_out(held, out, sems, t, tile).wait()


def residue(slopes, order, xts, fb, keep):
    depth, kw = fb.shape
    total = sum(xt.shape[1] for xt in xts)
    tile = min(depth, 256)
    return pl.pallas_call(
        functools.partial(residue_kernel, order, tile),
        out_shape=[
            jax.ShapeDtypeStruct((depth, kw), jnp.bfloat16),
            TOKEN,
        ],
        in_specs=[VMEM] * (len(slopes) + len(xts) + 2),
        out_specs=[ANY, VMEM],
        scratch_shapes=[
            pltpu.VMEM((total, kw), jnp.bfloat16),
            pltpu.VMEM((depth, kw), jnp.bfloat16),
            pltpu.SemaphoreType.DMA((depth // tile,)),
        ],
        compiler_params=params(14),
        cost_estimate=BRIEF,
        name="residue",
    )(*slopes, *xts, fb, keep)


def join_kernel(n, *refs):
    out, start = refs[-1], 0
    for part in refs[:n]:
        out[start : start + part.shape[0], :] = part[...]
        start += part.shape[0]


def join(parts, after):
    rows, lanes = sum(part.shape[0] for part in parts), parts[0].shape[1]
    return pl.pallas_call(
        functools.partial(join_kernel, len(parts)),
        out_shape=jax.ShapeDtypeStruct((rows, lanes), jnp.bfloat16),
        in_specs=[VMEM] * len(parts) + [ANY] * len(after),
        compiler_params=params(8),
        cost_estimate=BRIEF,
        name="join",
    )(*parts, *after)


def spread(group, wide, lines, cap, per_row):
    size = cap + 16
    for k in range(group.shape[0] // size):
        start = k * size
        tail = group[start + cap : start + size, :].astype(jnp.float32)
        number = (tail[0:1, :] * LANES + tail[1:2, :]).astype(jnp.int32)
        lines[:, k * cap : (k + 1) * cap] = jnp.broadcast_to(number // per_row, (8, cap))
        column = jnp.broadcast_to((number % per_row).astype(jnp.float32), (LANES, cap)).T
        value = group[start : start + cap, :].astype(jnp.float32)
        for c in range(per_row):
            wide[k * cap : (k + 1) * cap, c * LANES : (c + 1) * LANES] = jnp.where(
                column == c, value, 0.0
            ).astype(jnp.bfloat16)


def place(lines, wide, t, tile):
    line = lax.broadcasted_iota(jnp.int32, (tile, lines.shape[1]), 0) + t * tile
    hot = (lines[0:1, :] == line).astype(jnp.float32).astype(jnp.bfloat16)
    return jnp.dot(hot, wide[...], preferred_element_type=jnp.float32)


def unpack_kernel(cap, per_row, message, *refs):
    wide, lines = refs[-2:]
    spread(message, wide, lines, cap, per_row)


def unpack(message, cap, kw, after):
    return pl.pallas_call(
        functools.partial(unpack_kernel, cap, kw // LANES),
        out_shape=[
            jax.ShapeDtypeStruct((cap, kw), jnp.bfloat16),
            jax.ShapeDtypeStruct((8, cap), jnp.int32),
        ],
        in_specs=[VMEM] + [ANY] * len(after),
        compiler_params=params(4),
        cost_estimate=BRIEF,
        name="unpack",
    )(message, *after)


def half_kernel(tile, n, *refs):
    wides, rows_of, (out, wide, lines) = refs[:n], refs[n : 2 * n], refs[2 * n :]
    cap = wides[0].shape[0]
    for k in range(n):
        wide[k * cap : (k + 1) * cap, :] = wides[k][...]
        lines[:, k * cap : (k + 1) * cap] = rows_of[k][...]
    for t in range(out.shape[0] // tile):
        out[t * tile : (t + 1) * tile, :] = place(lines, wide, t, tile)


def outer_kernel(cap, per_row, tile, n, group, half, out, wide, lines, held, sems):
    spread(group, wide, lines, cap, per_row)
    tiles = out.shape[0] // tile
    for t in range(tiles):
        rows = slice(t * tile, (t + 1) * tile)
        held[rows, :] = (half[rows, :] + place(lines, wide, t, tile)) * (1.0 / n)
        send_out(held, out, sems, t, tile).start()
    for t in range(tiles):
        send_out(held, out, sems, t, tile).wait()


def outer(group, unpacked, cap, depth, kw):
    slots = len(unpacked) * cap
    n = 2 * slots // cap
    tile = min(depth, 256)
    shape = jax.ShapeDtypeStruct((depth, kw), jnp.float32)
    scratch = [pltpu.VMEM((slots, kw), jnp.bfloat16), pltpu.VMEM((8, slots), jnp.int32)]
    half = pl.pallas_call(
        functools.partial(half_kernel, min(depth, 512), len(unpacked)),
        out_shape=shape,
        scratch_shapes=scratch,
        compiler_params=params(14),
        cost_estimate=BRIEF,
        name="half",
    )(*[wide for wide, _ in unpacked], *[lines for _, lines in unpacked])
    return pl.pallas_call(
        functools.partial(outer_kernel, cap, kw // LANES, tile, n),
        out_shape=shape,
        out_specs=ANY,
        scratch_shapes=scratch
        + [pltpu.VMEM((depth, kw), jnp.float32), pltpu.SemaphoreType.DMA((depth // tile,))],
        compiler_params=params(14),
        cost_estimate=BRIEF,
        name="outer",
    )(group, half)


def on_device(inputs, target, weights, feedback, counts, blocks):
    tokens, w, fb = inputs[0], weights[0], feedback[0]
    n_shard, n_rep = lax.axis_size("shard"), lax.axis_size("rep")
    tok_dev = tokens.shape[0]
    depth, kw = w.shape
    early_rows = tok_dev // 2
    spans = [(0, early_rows), (early_rows, tok_dev)]
    per_row = kw // LANES
    slot_row = blocks[0]
    near = [d for d in range(1, n_shard) if d & (d - 1) == 0]
    far = [d for d in range(1, n_shard) if d & (d - 1) != 0]

    me = lax.axis_index("shard")
    rows = tok_dev // 2 if n_shard == 4 else tok_dev
    far_out = [
        [
            lax.dynamic_slice(tokens, (low, (me ^ d) * depth), (rows, depth))
            for low in range(0, tok_dev, rows)
        ]
        for d in far
    ]
    if n_shard == 4:
        ((by_x, by_y),) = far_out
        by_x, by_y = swap(by_x, "shard", n_shard, 1), swap(by_y, "shard", n_shard, 2)
        hops = [by_x, by_y]
        far_in = [swap(by_x, "shard", n_shard, 2), swap(by_y, "shard", n_shard, 1)]
    else:
        hops = []
        far_in = [swap(x, "shard", n_shard, d) for (x,), d in zip(far_out, far)]
    near_out, after = [], [far_out[0][0]]
    for low, high in spans:
        *out, token = cut(tokens, depth, [(d, low, high - low) for d in near], after)
        near_out.append(out)
        after = [token] + hops
    near_in = [[swap(x, "shard", n_shard, d) for x, d in zip(out, near)] for out in near_out]

    own, _ = cut(tokens, depth, [(0, 0, tok_dev)], [token])

    brief, wide = jnp.bfloat16, jnp.float32
    near_outs = [[(high - low, brief)] * len(near) for low, high in spans]
    early_near, x_early = project(near_in[0], near_outs[0], w, [])
    outs = [(tok_dev, wide)] + [(tok_dev, brief)] * len(far)
    (mine, *products), x_far = project([own] + far_in, outs, w, early_near[-1:])
    whole = [swap(p, "shard", n_shard, d) for p, d in zip(products, far)]
    xg_far, xt_far, token = prepare([x_far], slot_row, counts, per_row, products)
    late_near, x_late = project(near_in[1], near_outs[1], w, [token])
    shares = [
        [swap(p, "shard", n_shard, d) for p, d in zip(part, near)]
        for part in (early_near, late_near)
    ]
    x_near = [x_early, x_late]
    xg_near, xt_near, token = prepare(x_near, slot_row, counts, per_row, late_near[:1])
    shares = [share[k] for k in range(len(near)) for share in shares]
    slopes = slope(target[0], mine, whole, shares, spans, token)
    fbk, keep, _ = early(slot_row, counts, fb, slopes)
    slopes = [slopes] + [swap(slopes, "shard", n_shard, d) for d in far + near]

    n_far = 1 + len(far)
    order_far = [(k, 0, tok_dev) for k in range(n_far)]
    order_near = [(k, low, high) for low, high in spans for k in range(len(near))]
    wide = gather(slopes[:n_far], order_far, xg_far)
    message = kept(slopes[n_far:], order_near, wide, xg_near, fbk, slot_row)
    chips = [4, *range(n_rep - 2, 4, -2), 2] if n_rep > 4 else list(range(2, n_rep, 2))
    same_core = [swap(message, "rep", n_rep, d) for d in chips]
    order = order_far + [(n_far + k, low, high) for k, low, high in order_near]
    new_feedback, token = residue(slopes, order, [xt_far, xt_near], fb, keep)
    cap = slot_row.shape[1]
    joined, after, unpacked = message, [token], [unpack(message, cap, kw, [token])]
    for received in same_core:
        joined, after = join([joined, received], after + [unpacked[-1][1]]), []
        unpacked.append(unpack(received, cap, kw, [token]))
    group = swap(joined, "rep", n_rep, 1)
    return outer(group, unpacked, cap, depth, kw), new_feedback[None]


def solution(mesh):
    placed = (
        P("rep", "shard", None),
        P("rep", "shard", None),
        P("rep", "shard", None),
        P("rep", "shard", None),
        P("rep", "shard"),
        P("rep", "shard", None),
    )
    return jax.shard_map(
        on_device,
        mesh=mesh,
        in_specs=placed,
        out_specs=(P("shard", None), P("rep", "shard", None)),
        check_vma=False,
    )
```

```python
import functools

import jax
import jax.numpy as jnp
from jax import lax
from jax.experimental import pallas as pl
from jax.experimental.pallas import tpu as pltpu
from jax.sharding import PartitionSpec as P

LANES = 128
ANY = pl.BlockSpec(memory_space=pl.ANY)
BRIEF = pl.CostEstimate(flops=1000, bytes_accessed=1000, transcendentals=0)
VMEM = pl.BlockSpec(memory_space=pltpu.VMEM)
SMEM = pl.BlockSpec(memory_space=pltpu.SMEM)
MIB = 1024 * 1024
TOKEN = jax.ShapeDtypeStruct((8, LANES), jnp.float32)


def params(mib):
    return pltpu.CompilerParams(vmem_limit_bytes=mib * MIB)


def swap(x, axis, n, d):
    return lax.ppermute(x, axis, [(i, i ^ d) for i in range(n)])


def cut_kernel(cuts, tokens, *refs):
    outs, (token, sems) = refs[-len(cuts) - 2 : -2], refs[-2:]
    token[...] = jnp.zeros_like(token)
    me = lax.axis_index("shard")
    copies = []
    for k, (d, low, rows) in enumerate(cuts):
        depth = outs[k].shape[1]
        columns = pl.ds(pl.multiple_of((me ^ d) * depth, LANES), depth)
        copy = pltpu.make_async_copy(tokens.at[pl.ds(low, rows), columns], outs[k], sems.at[k])
        copy.start()
        copies.append(copy)
    for copy in copies:
        copy.wait()


def cut(tokens, depth, cuts, after):
    return pl.pallas_call(
        functools.partial(cut_kernel, cuts),
        out_shape=[jax.ShapeDtypeStruct((rows, depth), tokens.dtype) for _, _, rows in cuts]
        + [TOKEN],
        in_specs=[ANY] * (1 + len(after)),
        out_specs=[ANY] * len(cuts) + [VMEM],
        scratch_shapes=[pltpu.SemaphoreType.DMA((len(cuts),))],
        compiler_params=params(6),
        cost_estimate=BRIEF,
        name="cut",
    )(tokens, *after)


def project_kernel(n, m, *refs):
    pieces, w, outs, x = refs[:n], refs[n], refs[-m - 1 : -1], refs[-1]
    start = 0
    for piece in pieces:
        x[start : start + piece.shape[0], :] = piece[...]
        start += piece.shape[0]
    full = jnp.dot(x[...], w[...], preferred_element_type=jnp.float32)
    start = 0
    for out in outs:
        out[...] = full[start : start + out.shape[0], :].astype(out.dtype)
        start += out.shape[0]


def project(pieces, outs, w, after):
    n = len(pieces)
    rows, depth = sum(p.shape[0] for p in pieces), pieces[0].shape[1]
    kw = w.shape[1]
    result = pl.pallas_call(
        functools.partial(project_kernel, n, len(outs)),
        out_shape=[jax.ShapeDtypeStruct((r, kw), t) for r, t in outs]
        + [jax.ShapeDtypeStruct((rows, depth), jnp.bfloat16)],
        in_specs=[VMEM] * (n + 1) + [ANY] * len(after),
        compiler_params=params(14),
        cost_estimate=BRIEF,
        name="project",
    )(*pieces, w, *after)
    return result[:-1], result[-1]


def slope_kernel(tok_dev, n, spans, *refs):
    goal, mine, out = refs[0], refs[1], refs[-1]
    whole = refs[2 : 2 + n]
    shares = refs[2 + n : -2]
    for part, (low, high) in enumerate(spans):
        key_proj = mine[low:high, :]
        for product in whole:
            key_proj += product[low:high, :].astype(jnp.float32)
        for product in shares[part :: len(spans)]:
            key_proj += product[...].astype(jnp.float32)
        gap = key_proj - goal[low:high, :].astype(jnp.float32)
        out[low:high, :] = (gap / tok_dev).astype(jnp.bfloat16)


def slope(goal, mine, whole, shares, spans, after):
    return pl.pallas_call(
        functools.partial(slope_kernel, goal.shape[0], len(whole), spans),
        out_shape=jax.ShapeDtypeStruct(mine.shape, jnp.bfloat16),
        in_specs=[VMEM] * (2 + len(whole) + len(shares)) + [ANY],
        compiler_params=params(8),
        cost_estimate=BRIEF,
        name="slope",
    )(goal, mine, *whole, *shares, after)


def as_column(row):
    size = row.shape[1]
    return jnp.broadcast_to(row.astype(jnp.float32), (size, size)).T.astype(jnp.int32)


def pick_columns(wide, column):
    out = jnp.zeros((wide.shape[0], LANES), jnp.float32)
    for c in range(wide.shape[1] // LANES):
        out += jnp.where(column == c, wide[:, c * LANES : (c + 1) * LANES], 0.0)
    return out


def early_kernel(per_row, slot_row, count, fb, after, fbk, keep, token):
    token[...] = jnp.zeros_like(token)
    depth, kw = fb.shape
    cap = slot_row.shape[1]
    slot = as_column(slot_row[...])[:, 0:1]
    hot = slot // per_row == lax.broadcasted_iota(jnp.int32, (cap, depth), 1)
    hot = hot.astype(jnp.float32).astype(jnp.bfloat16)
    used = lax.broadcasted_iota(jnp.int32, (cap, 1), 0) < count[0, 0]
    wide = jnp.dot(hot, fb[...], preferred_element_type=jnp.float32)
    fbk[...] = jnp.where(used, pick_columns(wide, slot % per_row), 0.0)
    group = lax.broadcasted_iota(jnp.int32, (cap, kw), 1) // LANES
    mark = jnp.where(used & (slot % per_row == group), 1.0, 0.0).astype(jnp.bfloat16)
    tile = min(depth, 512)
    for t in range(depth // tile):
        line = lax.broadcasted_iota(jnp.int32, (tile, cap), 0) + t * tile
        hot = (slot_row[...] // per_row == line).astype(jnp.float32).astype(jnp.bfloat16)
        mask = jnp.dot(hot, mark, preferred_element_type=jnp.float32)
        keep[t * tile : (t + 1) * tile, :] = (1.0 - mask).astype(jnp.bfloat16)


def early(slot_row, count, fb, after):
    depth, kw = fb.shape
    cap = slot_row.shape[1]
    return pl.pallas_call(
        functools.partial(early_kernel, kw // LANES),
        out_shape=[
            jax.ShapeDtypeStruct((cap, LANES), jnp.float32),
            jax.ShapeDtypeStruct((depth, kw), jnp.bfloat16),
            TOKEN,
        ],
        in_specs=[VMEM, SMEM, VMEM, ANY],
        compiler_params=params(14),
        cost_estimate=BRIEF,
        name="early",
    )(slot_row, count, fb, after)


def prepare_kernel(per_row, n, *refs):
    xs, (slot_row, count), (xg, xt, token) = refs[:n], refs[n : n + 2], refs[-3:]
    token[...] = jnp.zeros_like(token)
    depth = xs[0].shape[1]
    cap = slot_row.shape[1]
    used = lax.broadcasted_iota(jnp.int32, (cap, 1), 0) < count[0, 0]
    line = jnp.where(used, as_column(slot_row[...])[:, 0:1] // per_row, depth)
    hot = line == lax.broadcasted_iota(jnp.int32, (cap, depth), 1)
    hot = hot.astype(jnp.float32).astype(jnp.bfloat16)
    start = 0
    for x in xs:
        rows = x.shape[0]
        xg[:, start : start + rows] = lax.dot_general(
            hot, x[...], (((1,), (1,)), ((), ())), preferred_element_type=jnp.float32
        ).astype(jnp.bfloat16)
        xt[:, start : start + rows] = x[...].T
        start += rows


def prepare(xs, slot_row, count, per_row, after):
    rows, depth = sum(x.shape[0] for x in xs), xs[0].shape[1]
    cap = slot_row.shape[1]
    return pl.pallas_call(
        functools.partial(prepare_kernel, per_row, len(xs)),
        out_shape=[
            jax.ShapeDtypeStruct((cap, rows), jnp.bfloat16),
            jax.ShapeDtypeStruct((depth, rows), jnp.bfloat16),
            TOKEN,
        ],
        in_specs=[VMEM] * (len(xs) + 1) + [SMEM] + [ANY] * len(after),
        compiler_params=params(14),
        cost_estimate=BRIEF,
        name="prepare",
    )(*xs, slot_row, count, *after)


def stack(slopes, order, s):
    start = 0
    for k, low, high in order:
        s[start : start + high - low, :] = slopes[k][low:high, :]
        start += high - low


def gather_kernel(order, *refs):
    slopes, (xg, out, s) = refs[:-3], refs[-3:]
    stack(slopes, order, s)
    out[...] = jnp.dot(xg[...], s[...], preferred_element_type=jnp.float32)


def gather(slopes, order, xg):
    kw = slopes[0].shape[1]
    return pl.pallas_call(
        functools.partial(gather_kernel, order),
        out_shape=jax.ShapeDtypeStruct((xg.shape[0], kw), jnp.float32),
        scratch_shapes=[pltpu.VMEM((xg.shape[1], kw), jnp.bfloat16)],
        compiler_params=params(8),
        cost_estimate=BRIEF,
        name="gather",
    )(*slopes, xg)


def kept_kernel(per_row, order, *refs):
    slopes, (wide, xg, fbk, slot_row, out, s) = refs[:-6], refs[-6:]
    cap = slot_row.shape[1]
    stack(slopes, order, s)
    total = wide[...] + jnp.dot(xg[...], s[...], preferred_element_type=jnp.float32)
    value = pick_columns(total, as_column(slot_row[...])[:, 0:1] % per_row) + fbk[...]
    out[:cap, :] = value.astype(jnp.bfloat16)
    tail = out.shape[0] - cap
    number = jnp.broadcast_to(slot_row[...], (tail, cap))
    line = lax.broadcasted_iota(jnp.int32, (tail, cap), 0)
    number = jnp.where(line == 0, number // LANES, number % LANES)
    out[cap:, :] = number.astype(jnp.float32).astype(jnp.bfloat16)


def kept(slopes, order, wide, xg, fbk, slot_row):
    cap, kw = wide.shape
    return pl.pallas_call(
        functools.partial(kept_kernel, kw // LANES, order),
        out_shape=jax.ShapeDtypeStruct((cap + 16, LANES), jnp.bfloat16),
        scratch_shapes=[pltpu.VMEM((xg.shape[1], kw), jnp.bfloat16)],
        compiler_params=params(8),
        cost_estimate=BRIEF,
        name="kept",
    )(*slopes, wide, xg, fbk, slot_row)


def send_out(held, out, sems, t, tile):
    rows = pl.ds(t * tile, tile)
    return pltpu.make_async_copy(held.at[rows, :], out.at[rows, :], sems.at[t])


def residue_kernel(order, tile, *refs):
    n = len({k for k, _, _ in order})
    slopes, xts, (fb, keep, out, token, s, held, sems) = refs[:n], refs[n:-7], refs[-7:]
    token[...] = jnp.zeros_like(token)
    stack(slopes, order, s)
    tiles = out.shape[0] // tile
    for t in range(tiles):
        rows = slice(t * tile, (t + 1) * tile)
        pseudo, start = fb[rows, :].astype(jnp.float32), 0
        for xt in xts:
            part = s[start : start + xt.shape[1], :]
            pseudo += jnp.dot(xt[rows, :], part, preferred_element_type=jnp.float32)
            start += xt.shape[1]
        held[rows, :] = jnp.where(keep[rows, :] > 0, pseudo, 0.0).astype(jnp.bfloat16)
        send_out(held, out, sems, t, tile).start()
    for t in range(tiles):
        send_out(held, out, sems, t, tile).wait()


def residue(slopes, order, xts, fb, keep):
    depth, kw = fb.shape
    total = sum(xt.shape[1] for xt in xts)
    tile = min(depth, 256)
    return pl.pallas_call(
        functools.partial(residue_kernel, order, tile),
        out_shape=[
            jax.ShapeDtypeStruct((depth, kw), jnp.bfloat16),
            TOKEN,
        ],
        in_specs=[VMEM] * (len(slopes) + len(xts) + 2),
        out_specs=[ANY, VMEM],
        scratch_shapes=[
            pltpu.VMEM((total, kw), jnp.bfloat16),
            pltpu.VMEM((depth, kw), jnp.bfloat16),
            pltpu.SemaphoreType.DMA((depth // tile,)),
        ],
        compiler_params=params(14),
        cost_estimate=BRIEF,
        name="residue",
    )(*slopes, *xts, fb, keep)


def join_kernel(n, *refs):
    out, start = refs[-1], 0
    for part in refs[:n]:
        out[start : start + part.shape[0], :] = part[...]
        start += part.shape[0]


def join(parts, after):
    rows, lanes = sum(part.shape[0] for part in parts), parts[0].shape[1]
    return pl.pallas_call(
        functools.partial(join_kernel, len(parts)),
        out_shape=jax.ShapeDtypeStruct((rows, lanes), jnp.bfloat16),
        in_specs=[VMEM] * len(parts) + [ANY] * len(after),
        compiler_params=params(8),
        cost_estimate=BRIEF,
        name="join",
    )(*parts, *after)


def spread(group, wide, lines, cap, per_row):
    size = cap + 16
    for k in range(group.shape[0] // size):
        start = k * size
        tail = group[start + cap : start + size, :].astype(jnp.float32)
        number = (tail[0:1, :] * LANES + tail[1:2, :]).astype(jnp.int32)
        lines[:, k * cap : (k + 1) * cap] = jnp.broadcast_to(number // per_row, (8, cap))
        column = jnp.broadcast_to((number % per_row).astype(jnp.float32), (LANES, cap)).T
        value = group[start : start + cap, :].astype(jnp.float32)
        for c in range(per_row):
            wide[k * cap : (k + 1) * cap, c * LANES : (c + 1) * LANES] = jnp.where(
                column == c, value, 0.0
            ).astype(jnp.bfloat16)


def place(lines, wide, t, tile):
    line = lax.broadcasted_iota(jnp.int32, (tile, lines.shape[1]), 0) + t * tile
    hot = (lines[0:1, :] == line).astype(jnp.float32).astype(jnp.bfloat16)
    return jnp.dot(hot, wide[...], preferred_element_type=jnp.float32)


def half_kernel(cap, per_row, tile, group, out, wide, lines):
    spread(group, wide, lines, cap, per_row)
    for t in range(out.shape[0] // tile):
        out[t * tile : (t + 1) * tile, :] = place(lines, wide, t, tile)


def outer_kernel(cap, per_row, tile, n, group, half, out, wide, lines, held, sems):
    spread(group, wide, lines, cap, per_row)
    tiles = out.shape[0] // tile
    for t in range(tiles):
        rows = slice(t * tile, (t + 1) * tile)
        held[rows, :] = (half[rows, :] + place(lines, wide, t, tile)) * (1.0 / n)
        send_out(held, out, sems, t, tile).start()
    for t in range(tiles):
        send_out(held, out, sems, t, tile).wait()


def outer(groups, cap, depth, kw):
    slots = groups[0].shape[0] // (cap + 16) * cap
    n = 2 * slots // cap
    tile = min(depth, 128)
    shape = jax.ShapeDtypeStruct((depth, kw), jnp.float32)
    scratch = [pltpu.VMEM((slots, kw), jnp.bfloat16), pltpu.VMEM((8, slots), jnp.int32)]
    half = pl.pallas_call(
        functools.partial(half_kernel, cap, kw // LANES, tile),
        out_shape=shape,
        scratch_shapes=scratch,
        compiler_params=params(14),
        cost_estimate=BRIEF,
        name="half",
    )(groups[0])
    return pl.pallas_call(
        functools.partial(outer_kernel, cap, kw // LANES, tile, n),
        out_shape=shape,
        out_specs=ANY,
        scratch_shapes=scratch
        + [pltpu.VMEM((depth, kw), jnp.float32), pltpu.SemaphoreType.DMA((depth // tile,))],
        compiler_params=params(14),
        cost_estimate=BRIEF,
        name="outer",
    )(groups[1], half)


def on_device(inputs, target, weights, feedback, counts, blocks):
    tokens, w, fb = inputs[0], weights[0], feedback[0]
    n_shard, n_rep = lax.axis_size("shard"), lax.axis_size("rep")
    tok_dev = tokens.shape[0]
    depth, kw = w.shape
    early_rows = tok_dev // 2
    spans = [(0, early_rows), (early_rows, tok_dev)]
    per_row = kw // LANES
    slot_row = blocks[0]
    near = [d for d in range(1, n_shard) if d & (d - 1) == 0]
    far = [d for d in range(1, n_shard) if d & (d - 1) != 0]

    me = lax.axis_index("shard")
    rows = tok_dev // 2 if n_shard == 4 else tok_dev
    far_out = [
        [
            lax.dynamic_slice(tokens, (low, (me ^ d) * depth), (rows, depth))
            for low in range(0, tok_dev, rows)
        ]
        for d in far
    ]
    if n_shard == 4:
        ((by_x, by_y),) = far_out
        by_x, by_y = swap(by_x, "shard", n_shard, 1), swap(by_y, "shard", n_shard, 2)
        hops = [by_x, by_y]
        far_in = [swap(by_x, "shard", n_shard, 2), swap(by_y, "shard", n_shard, 1)]
    else:
        hops = []
        far_in = [swap(x, "shard", n_shard, d) for (x,), d in zip(far_out, far)]
    near_out, after = [], [far_out[0][0]]
    for low, high in spans:
        *out, token = cut(tokens, depth, [(d, low, high - low) for d in near], after)
        near_out.append(out)
        after = [token] + hops
    near_in = [[swap(x, "shard", n_shard, d) for x, d in zip(out, near)] for out in near_out]

    own, _ = cut(tokens, depth, [(0, 0, tok_dev)], [token])

    brief, wide = jnp.bfloat16, jnp.float32
    near_outs = [[(high - low, brief)] * len(near) for low, high in spans]
    early_near, x_early = project(near_in[0], near_outs[0], w, [])
    outs = [(tok_dev, wide)] + [(tok_dev, brief)] * len(far)
    (mine, *products), x_far = project([own] + far_in, outs, w, early_near[-1:])
    whole = [swap(p, "shard", n_shard, d) for p, d in zip(products, far)]
    xg_far, xt_far, token = prepare([x_far], slot_row, counts, per_row, products)
    late_near, x_late = project(near_in[1], near_outs[1], w, [token])
    shares = [
        [swap(p, "shard", n_shard, d) for p, d in zip(part, near)]
        for part in (early_near, late_near)
    ]
    x_near = [x_early, x_late]
    xg_near, xt_near, token = prepare(x_near, slot_row, counts, per_row, late_near[:1])
    shares = [share[k] for k in range(len(near)) for share in shares]
    slopes = slope(target[0], mine, whole, shares, spans, token)
    fbk, keep, _ = early(slot_row, counts, fb, slopes)
    slopes = [slopes] + [swap(slopes, "shard", n_shard, d) for d in far + near]

    n_far = 1 + len(far)
    order_far = [(k, 0, tok_dev) for k in range(n_far)]
    order_near = [(k, low, high) for low, high in spans for k in range(len(near))]
    wide = gather(slopes[:n_far], order_far, xg_far)
    message = kept(slopes[n_far:], order_near, wide, xg_near, fbk, slot_row)
    chips = [4, *range(n_rep - 2, 4, -2), 2] if n_rep > 4 else list(range(2, n_rep, 2))
    same_core = [swap(message, "rep", n_rep, d) for d in chips]
    order = order_far + [(n_far + k, low, high) for k, low, high in order_near]
    new_feedback, token = residue(slopes, order, [xt_far, xt_near], fb, keep)
    joined, after = message, [token]
    for received in same_core:
        joined, after = join([joined, received], after), []
    groups = [joined, swap(joined, "rep", n_rep, 1)]
    return outer(groups, message.shape[0] - 16, depth, kw), new_feedback[None]


def solution(mesh):
    placed = (
        P("rep", "shard", None),
        P("rep", "shard", None),
        P("rep", "shard", None),
        P("rep", "shard", None),
        P("rep", "shard"),
        P("rep", "shard", None),
    )
    return jax.shard_map(
        on_device,
        mesh=mesh,
        in_specs=placed,
        out_specs=(P("shard", None), P("rep", "shard", None)),
        check_vma=False,
    )
```
